32 devices in a mesh: expert: 4 (over y, x), dp: 8 (over z, core).
Axes of the slice: x: 2, y: 2, z: 4, core: 2. Of those that a mesh axis runs over, the one named last changes fastest.
Arguments:
- residual_in: bfloat16 [4096, 2048], P(('expert', 'dp')), may hold values from -6 to 6
- cotangent: bfloat16 [4096, 2048], P(('expert', 'dp')), may hold values from -6 to 6
- lengths: int32 [4], P('expert'), may hold values from 512 to 1024, as said below
- routes: int32 [4096, 8], P(('expert', 'dp')), may hold values from 0 to 15, all different within a row; in each aligned block of 128 rows (0 to 127, 128 to 255, ...) at most 128 rows name the same one
- attn_qkv: float32 [3, 2048, 2048], P(None, ('expert', 'dp')), may hold values from -0.125 to 0.125
- attn_out: float32 [2048, 2048], P(('expert', 'dp')), may hold values from -2 to 2
- gains: float32 [4, 2048], P(None, ('expert', 'dp')), may hold values from 0.5 to 1.5
- router: float32 [2048, 16], P(('expert', 'dp')), may hold values from -0.0625 to 0.0625
- expert_in: float32 [2048, 16, 2, 1024], P('dp', 'expert'), may hold values from -0.125 to 0.125
- expert_down: float32 [2048, 16, 1024], P('dp', 'expert'), may hold values from -0.5 to 0.5
Outputs:
- output: float32 [4096, 2048], P(('expert', 'dp'))
- grad_input: float32 [4096, 2048], P(('expert', 'dp'))
- grad_qkv: float32 [3, 2048, 2048], P(None, ('expert', 'dp'))
- grad_out: float32 [2048, 2048], P(('expert', 'dp'))
- grad_gains: float32 [4, 2048], P(None, ('expert', 'dp'))
- grad_router: float32 [2048, 16], P(('expert', 'dp'))
- grad_expert_in: float32 [2048, 16, 2, 1024], P('dp', 'expert')
- grad_expert_down: float32 [2048, 16, 1024], P('dp', 'expert')
The draws below stay inside these ranges and needn't reach their ends.
Inputs may be any that keep to these rules, and one draw needn't show every extreme that they name: `routes`: each token names 8 different experts. Among the 128 tokens of one device no expert is named by more than 128 tokens, and in every draw some expert is named by exactly 128 tokens of some device. `lengths`: in every draw some sequence is full.
All inputs are finite; a program needn't handle non-finite values.
Results may differ from the reference program's by a relative error of at most 0.019.
The reference program's roundings to bfloat16 on the way count: a program that leaves them out, or rounds other values in their place, can miss the bound.
Values may be sent and summed in bfloat16 or wider, within the bound.
A program may use at most 512 MiB of HBM per device.

```python
import math
import jax
import jax.numpy as jnp
import numpy as np
from jax import lax

D = 2048
HEADS = 16
HD = 128
FF = 1024
TOP = 8
TOK_DEV = 128
EXPERTS = 16
MOST = 128
SEQ_LEN = 1024
SEQS = 4
TOKENS = 4096
N_DP = 8


def draw_lengths(key, part):
    base_lengths = jax.random.randint(key, (SEQS,), SEQ_LEN // 2, SEQ_LEN + 1)
    full_index = jax.random.randint(jax.random.fold_in(key, 7), (), 0, SEQS)
    return jnp.where(jnp.arange(SEQS) == full_index, SEQ_LEN, base_lengths).astype(jnp.int32)


def steps_of(key, extent, cuts, least, high):
    level = 1.0
    for axis_at, parts in cuts:
        heights = jax.random.uniform(jax.random.fold_in(jax.random.fold_in(key, 6), axis_at), (parts,), jnp.float32, least / len(cuts), high / len(cuts))
        level = level * jnp.repeat(jnp.exp(heights), extent[axis_at] // parts).reshape((-1,) + (1,) * (len(extent) - 1 - axis_at))
    return level


def assign_block(own_key, own, number, rows, number_of, top, reach, slope):
    sequence = jax.random.permutation(own_key, number_of)
    packed, usual = load_shares(number_of, rows * top, reach, slope, True), load_shares(number_of, rows * top, reach, slope, False)
    places = jnp.arange(number_of)

    def named(sizes, rotation):
        used = int((sizes > 0).sum())
        fixed = max(1, used // 4)
        moved = fixed + (places - fixed + rotation * (used - fixed)) % max(1, number_of - fixed)
        return jnp.zeros((number_of,), jnp.int32).at[sequence[jnp.where(places < fixed, places, moved)]].set(jnp.asarray(sizes, jnp.int32))

    sizes = jnp.where(number % 4 == 0, named(packed, number // 4), named(usual, number - number // 4 - 1))
    mixed = jax.random.permutation(jax.random.fold_in(own, 3), number_of)
    source_of, taker = mixed[0:number_of // 2 * 2:2], mixed[1:number_of // 2 * 2:2]
    margin = jnp.minimum(sizes[source_of] - 1, reach - sizes[taker]) // 2
    margin = jnp.where((source_of == sequence[0]) | (taker == sequence[0]) | (sizes[taker] == 0), 0, jnp.maximum(margin, 0))
    moved = jax.random.randint(jax.random.fold_in(own, 4), (number_of // 2,), 0, 1 << 20) % (margin + 1)
    sizes = sizes.at[source_of].add(-moved).at[taker].add(moved)
    items = jnp.searchsorted(jnp.cumsum(sizes), jnp.arange(rows * top), side="right").astype(jnp.int32)
    table = items.reshape(top, rows).T
    table = table[jax.random.permutation(jax.random.fold_in(own, 1), rows)]
    rotation = jax.random.randint(jax.random.fold_in(own, 2), (rows, 1), 0, top)
    return jnp.take_along_axis(table, (jnp.arange(top)[None, :] + rotation) % top, axis=1)


def load_shares(number_of, total, limit, skew, full):
    loads = [(1 << 20) // math.isqrt(rank ** skew) + 1 for rank in range(1, number_of + 1)]
    largest = limit if full else min(limit, max(-(-total // number_of), total * loads[0] // sum(loads)))
    least = 1 if total - largest >= number_of - 1 else 0
    counts, surplus = [largest] + [least] * (number_of - 1), total - largest - least * (number_of - 1)
    while surplus > 0:
        free = [i for i in range(1, number_of) if counts[i] < largest] or [i for i in range(1, number_of) if counts[i] < limit]
        pool, budget = sum([loads[i] for i in free]), surplus
        for i in free:
            more = min(limit - counts[i], max(1, budget * loads[i] // pool), surplus)
            counts[i] = counts[i] + more
            surplus = surplus - more
    return np.array(counts)


def noise(key, shape, deviation, most, shards=(), kind=jnp.bfloat16):
    result = jax.random.normal(key, shape, jnp.float32) * deviation
    if len(shards) > 0:
        result = steps_of(key, shape, shards, -0.22, 0.18) * result
    return jnp.clip(result, min=-most, max=most).astype(kind)


def setup_inputs(seed: int = 0) -> dict:
    key_of = jax.random.split(jax.random.key(seed), 11)
    residual_in = noise(key_of[0], (TOKENS, D), 1.0, 6.0, ((0, 32),))
    cotangent = noise(key_of[1], (TOKENS, D), 1.0, 6.0, ((0, 32),))
    lengths = draw_lengths(jax.random.fold_in(key_of[10], 71), 0)
    routes_keys = jax.random.split(jax.random.fold_in(key_of[3], 1), TOKENS // TOK_DEV)
    routes_turns = jax.random.permutation(jax.random.fold_in(key_of[3], 3), TOKENS // TOK_DEV)
    routes = jax.vmap(lambda own, number: assign_block(jax.random.fold_in(key_of[3], 2), own, number, TOK_DEV, EXPERTS, TOP, MOST, 1))(routes_keys, routes_turns).reshape((TOKENS, TOP))
    attn_qkv = noise(key_of[4], (3, D, D), D ** -0.5, 0.125, ((1, 32),), jnp.float32)
    attn_out = noise(key_of[5], (D, D), (max(1, 4 * D // (TOK_DEV * N_DP))) ** -0.5, 2.0, ((0, 32),), jnp.float32)
    gains = jnp.clip(1.0 + 0.1 * jax.random.normal(key_of[6], (4, D), jnp.float32), 0.5, 1.5)
    router = noise(key_of[7], (D, EXPERTS), (4 * D) ** -0.5, 0.0625, ((0, 32),), jnp.float32)
    expert_in = noise(key_of[8], (D, EXPERTS, 2, FF), D ** -0.5, 0.125, ((0, 8), (1, 4)), jnp.float32)
    expert_down = noise(key_of[9], (D, EXPERTS, FF), (FF // 8) ** -0.5, 0.5, ((0, 8), (1, 4)), jnp.float32)
    return dict(residual_in=residual_in, cotangent=cotangent, lengths=lengths, routes=routes, attn_qkv=attn_qkv, attn_out=attn_out, gains=gains, router=router, expert_in=expert_in, expert_down=expert_down)


epsilon = 1e-05
rope_base = 10000.0
masked_score = -1000000000.0

@jax.custom_vjp
def low(v):
    return lax.optimization_barrier(v.astype(jnp.bfloat16)).astype(jnp.float32)

@jax.custom_vjp
def low_back(v):
    return v

def low_keep(v):
    return (low(v), None)

def low_pass(kept, grad):
    return (grad,)

def back_keep(v):
    return (v, None)

def back_low(kept, grad):
    return (low(grad),)
low.defvjp(low_keep, low_pass)
low_back.defvjp(back_keep, back_low)

def matmul_high(left, right):
    return jnp.dot(left, right, precision=lax.Precision.HIGHEST, preferred_element_type=jnp.float32)

def rms_scale(values):
    return lax.rsqrt(lax.optimization_barrier(jnp.mean(values * values, axis=-1, keepdims=True)) + epsilon)

def angle_tables(positions):
    frequency = rope_base ** (-2.0 * jnp.arange(HD // 2, dtype=jnp.float32) / HD)
    angles = positions.astype(jnp.float32)[:, None] * frequency[None, :]
    return (jnp.cos(angles), jnp.sin(angles))

def rotate(values, cosine, sine_table):
    row_count = values.shape[0]
    shaped = values.reshape(row_count, HEADS, 2, HD // 2)
    first_half = shaped[:, :, 0, :]
    second_half = shaped[:, :, 1, :]
    cos_rows = cosine[:, None, :]
    sin_rows = sine_table[:, None, :]
    turned = jnp.stack([first_half * cos_rows - second_half * sin_rows, second_half * cos_rows + first_half * sin_rows], axis=2)
    return turned.reshape(row_count, HEADS * HD)

def attend(block_item):
    query_rows, key_rows, value_rows, length = block_item
    seq_rows = query_rows.shape[0]
    query_heads = query_rows.reshape(seq_rows, HEADS, HD)
    key_heads = key_rows.reshape(seq_rows, HEADS, HD)
    value_heads = value_rows.reshape(seq_rows, HEADS, HD)
    raw_scores = jnp.einsum('qhd,khd->hqk', query_heads, key_heads, precision=lax.Precision.HIGHEST) * HD ** (-0.5)
    scores = low_back(raw_scores)
    key_live = jnp.arange(seq_rows) < length
    scores = jnp.where(key_live[None, None, :], scores, masked_score)
    weights_low = low(jax.nn.softmax(scores, axis=-1))
    attended = jnp.einsum('hqk,khd->qhd', weights_low, value_heads, precision=lax.Precision.HIGHEST)
    return low(low_back(attended.reshape(seq_rows, HEADS * HD)))

def slot_index(route_rows):
    flat_routes = route_rows.reshape(-1)
    onehot = (flat_routes[:, None] == jnp.arange(EXPERTS, dtype=jnp.int32)[None, :]).astype(jnp.int32)
    rank_rows = lax.optimization_barrier(jnp.sum((jnp.cumsum(onehot, axis=0) - onehot) * onehot, axis=1))
    return (flat_routes * MOST + rank_rows).astype(jnp.int32)

def experts_block(normed_rows, route_rows, gate_rows, weights_in, weights_down):
    slot_rows = slot_index(route_rows)
    token_of = jnp.arange(slot_rows.shape[0], dtype=jnp.int32) // TOP
    buffer = jnp.zeros((EXPERTS * MOST, D), jnp.float32).at[slot_rows].set(normed_rows[token_of])
    buffer = low_back(buffer).reshape(EXPERTS, MOST, D)
    both_parts = jnp.einsum('emd,dekf->emkf', buffer, weights_in, precision=lax.Precision.HIGHEST)
    gate_part = low_back(both_parts[:, :, 0, :])
    up_part = low_back(both_parts[:, :, 1, :])
    hidden = low(jax.nn.silu(gate_part) * up_part)
    produced = jnp.einsum('emf,def->emd', hidden, weights_down, precision=lax.Precision.HIGHEST)
    produced = low(low_back(produced)).reshape(EXPERTS * MOST, D)
    picked = produced[slot_rows].reshape(TOK_DEV, TOP, D)
    return lax.optimization_barrier(jnp.sum(gate_rows[:, :, None] * picked, axis=1))

def layer(residual_in, lengths, routes, attn_qkv, attn_out, gains, router, expert_in, expert_down):
    tokens = residual_in.shape[0]
    gain_rows = low(gains)
    qkv_weights = low(attn_qkv)
    normed_in = low(residual_in * rms_scale(residual_in) * gain_rows[0])
    query_raw = low_back(matmul_high(normed_in, qkv_weights[0]))
    key_raw = low_back(matmul_high(normed_in, qkv_weights[1]))
    value_rows = low(low_back(matmul_high(normed_in, qkv_weights[2])))
    positions = jnp.arange(tokens, dtype=jnp.int32) % SEQ_LEN
    cosine, sine_table = angle_tables(positions)
    query_rot = low(rotate(query_raw * rms_scale(query_raw) * gain_rows[1], cosine, sine_table))
    key_rot = low(rotate(key_raw * rms_scale(key_raw) * gain_rows[2], cosine, sine_table))
    per_seq = (SEQS, SEQ_LEN, D)
    attended = lax.map(jax.checkpoint(attend), (query_rot.reshape(per_seq), key_rot.reshape(per_seq), value_rows.reshape(per_seq), lengths))
    attended = attended.reshape(tokens, D)
    live_rows = (positions < jnp.repeat(lengths, SEQ_LEN)).astype(jnp.float32)[:, None]
    branch = low_back(matmul_high(attended, low(attn_out)))
    middle = residual_in + live_rows * branch
    normed_mid = low(middle * rms_scale(middle) * gain_rows[3])
    logits = low_back(matmul_high(normed_mid, low(router)))
    chosen = jnp.take_along_axis(logits, routes, axis=1)
    gate_weights = jax.nn.softmax(chosen, axis=-1)
    weights_in = low(expert_in)
    weights_down = low(expert_down)
    blocks = tokens // TOK_DEV

    def expert_mix(block_item):
        return experts_block(block_item[0], block_item[1], block_item[2], weights_in, weights_down)
    combined = lax.map(jax.checkpoint(expert_mix), (normed_mid.reshape(blocks, TOK_DEV, D), routes.reshape(blocks, TOK_DEV, TOP), gate_weights.reshape(blocks, TOK_DEV, TOP)))
    return middle + live_rows * combined.reshape(tokens, D)

def reference(residual_in, cotangent, lengths, routes, attn_qkv, attn_out, gains, router, expert_in, expert_down):

    def forward(inputs, qkv_all, out_all, gain_all, router_all, in_all, down_all):
        return layer(inputs, lengths, routes, qkv_all, out_all, gain_all, router_all, in_all, down_all)
    output, pullback = jax.vjp(forward, residual_in.astype(jnp.float32), attn_qkv, attn_out, gains, router, expert_in, expert_down)
    gradients = pullback(cotangent.astype(jnp.float32))
    return (output, gradients[0], gradients[1], gradients[2], gradients[3], gradients[4], gradients[5], gradients[6])
```

```python
import jax
import jax.numpy as jnp
import numpy as np
from jax import lax
from jax.sharding import Mesh
from jax.sharding import PartitionSpec as P

HEADS = 16
HD = 128

epsilon = 1e-05
rope_base = 10000.0
masked_score = -1000000000.0

low_type = jnp.bfloat16
high_type = jnp.float32


def rms_scale(values):
    return lax.rsqrt(jnp.mean(values * values, axis=-1, keepdims=True) + epsilon)


def angle_tables(positions):
    frequency = rope_base ** (-2.0 * jnp.arange(HD // 2, dtype=jnp.float32) / HD)
    angles = positions.astype(jnp.float32)[:, None] * frequency[None, :]
    return (jnp.cos(angles), jnp.sin(angles))


def rotate(values, cosine, sine_table):
    row_count, width = values.shape
    shaped = values.reshape(row_count, width // HD, 2, HD // 2)
    first_half = shaped[:, :, 0, :]
    second_half = shaped[:, :, 1, :]
    cos_rows = cosine[:, None, :]
    sin_rows = sine_table[:, None, :]
    turned = jnp.stack(
        [
            first_half * cos_rows - second_half * sin_rows,
            second_half * cos_rows + first_half * sin_rows,
        ],
        axis=2,
    )
    return turned.reshape(row_count, width)


def rms_back(grad_rows, normed, scale, gain):
    grad_normed = grad_rows * gain
    inner = jnp.mean(grad_normed * normed, axis=-1, keepdims=True)
    return (scale * grad_normed - normed * scale * inner, jnp.sum(grad_rows * normed, axis=0))


def dot(left, right):
    return jnp.dot(left, right, preferred_element_type=high_type)


def dot_t(left, right):
    return lax.dot_general(left, right, (((1,), (1,)), ((), ())), preferred_element_type=high_type)


def t_dot(left, right):
    return lax.dot_general(left, right, (((0,), (0,)), ((), ())), preferred_element_type=high_type)


GRID = ("ey", "ex", "dz", "dc")
SEQ = ("dz", "dc")


class Moves:
    def __init__(self, depth):
        self.depth = depth
        self.count = 2 * 2 * depth * 2

    def pairs(self, move):
        result = []
        for index in range(self.count):
            c = index % 2
            z = index // 2 % self.depth
            x = index // (2 * self.depth) % 2
            y = index // (4 * self.depth)
            y, x, z, c = move(y, x, z, c)
            result.append((index, ((y * 2 + x) * self.depth + z) * 2 + c))
        return result

    def send(self, values, move):
        return lax.ppermute(values, GRID, self.pairs(move))

    def core(self, values):
        return self.send(values, lambda y, x, z, c: (y, x, z, 1 - c))

    def from_z(self, values, step):
        return self.send(values, lambda y, x, z, c: (y, x, (z - step) % self.depth, c))

    def to_z(self, values, step):
        return self.send(values, lambda y, x, z, c: (y, x, (z + step) % self.depth, c))

    def near(self, values):
        return self.send(
            values, lambda y, x, z, c: (y, 1 - x, z, c) if c == 0 else (1 - y, x, z, c)
        )

    def far(self, values):
        return self.send(
            values, lambda y, x, z, c: (1 - y, x, z, c) if c == 0 else (y, 1 - x, z, c)
        )

    def sum_seq(self, values):
        values = values + self.core(values)
        total = values
        for step in range(1, self.depth):
            total = total + self.from_z(values, step)
        return total

    def spread(self, rows):
        own = jnp.concatenate(
            [rows] + [self.from_z(rows, step) for step in range(1, self.depth)], axis=0
        )
        near = self.near(own)
        far = self.far(jnp.concatenate([own, near], axis=0))
        return [jnp.concatenate([v, self.core(v)], axis=0) for v in (own, near, far)]

    def collect(self, chunks, rows):
        def both(chunk):
            half = chunk.shape[0] // 2
            arrived = self.core(chunk[half:])
            return chunk[:half].astype(high_type) + arrived.astype(high_type)

        far = self.far(both(chunks[2]).astype(low_type)).astype(high_type)
        half = far.shape[0] // 2
        near = self.near((both(chunks[1]) + far[half:]).astype(low_type))
        own = (both(chunks[0]) + far[:half] + near.astype(high_type)).astype(low_type)
        total = own[:rows].astype(high_type)
        for step in range(1, self.depth):
            total = total + self.to_z(own[step * rows : (step + 1) * rows], step).astype(high_type)
        return total

    def block_order(self):
        y, x, z, c = (lax.axis_index(name) for name in GRID)

        def at(y, x, step, c):
            return ((y * 2 + x) * self.depth + (z + step) % self.depth) * 2 + c

        order = []
        for dy, dx in ((0, 0),):
            for core in (c, 1 - c):
                order += [at(y, x, k, core) for k in range(self.depth)]
        for core in (c, 1 - c):
            order += [at(y ^ core, x ^ (1 - core), k, core) for k in range(self.depth)]
        for core in (c, 1 - c):
            order += [at(y ^ (1 - core), x ^ core, k, core) for k in range(self.depth)]
            order += [at(1 - y, 1 - x, k, core) for k in range(self.depth)]
        return jnp.stack(order)


def grid_shards(
    residual_in,
    cotangent,
    lengths,
    routes,
    attn_qkv,
    attn_out,
    gains,
    router,
    expert_in,
    expert_down,
):
    rows, width = residual_in.shape
    depth = lax.axis_size("dz")
    move = Moves(depth)
    ranks = 2 * depth
    columns = 4
    seq_rows = rows * ranks
    local_experts = expert_in.shape[1]
    experts = local_experts * columns
    hidden_width = expert_in.shape[3]
    part = hidden_width // ranks
    span = local_experts * part
    chunk_rows = expert_in.shape[0]
    weight_rows = attn_qkv.shape[1]
    score_scale = HD ** (-0.5)
    y, x, z, c = (lax.axis_index(name) for name in GRID)
    column = y * 2 + x
    own_heads = HEADS // ranks
    own_width = own_heads * HD

    def by_rank(values):
        lead = values.shape[:-1]
        shaped = values.reshape(lead + (2, own_heads, depth, HD))
        n = len(lead)
        return shaped.transpose((n + 2, n) + tuple(range(n)) + (n + 1, n + 3)).reshape(
            (ranks,) + lead + (own_width,)
        )

    def by_head(values):
        lead = values.shape[1:-1]
        shaped = values.reshape((depth, 2) + lead + (own_heads, HD))
        n = len(lead)
        return shaped.transpose(tuple(range(2, n + 2)) + (1, n + 2, 0, n + 3)).reshape(
            lead + (width,)
        )

    small = jnp.concatenate([gains.T, router], axis=1).astype(low_type)
    small = lax.all_gather(small, GRID, axis=0, tiled=True)
    gain_rows = small[:, :4].T.astype(high_type)
    router_weight = small[:, 4:]
    gain_own = [
        lax.dynamic_index_in_dim(by_rank(gain_rows[i]), z * 2 + c, 0, keepdims=False)
        for i in (1, 2)
    ]

    held = [residual_in] + [move.from_z(residual_in, k) for k in range(1, depth)]
    crossed = [move.core(block) for block in held]
    normed_in = jnp.zeros((depth, 2, rows, width), low_type)
    for k in range(depth):
        for block, core in ((held[k], c), (crossed[k], 1 - c)):
            block = block.astype(high_type)
            block = (block * rms_scale(block) * gain_rows[0]).astype(low_type)
            normed_in = lax.dynamic_update_slice(
                normed_in, block[None, None], ((z + k) % depth, core, 0, 0)
            )
    normed_in = normed_in.reshape(seq_rows, width)

    packed = attn_qkv.astype(low_type).transpose(1, 0, 2)
    packed = by_rank(packed).reshape(ranks, weight_rows, 3 * own_width)
    packed = lax.all_to_all(packed, SEQ, 0, 0, tiled=True).reshape(-1, 3 * own_width)
    near = move.near(packed)
    far = move.far(jnp.stack([packed, near]))
    in_x = jnp.where(c == 0, near, far[0])
    in_y = jnp.where(c == 0, far[0], near)
    in_row = [jnp.where(x == 0, packed, in_x), jnp.where(x == 0, in_x, packed)]
    out_row = [jnp.where(x == 0, in_y, far[1]), jnp.where(x == 0, far[1], in_y)]
    qkv_weight = jnp.concatenate(
        [jnp.where(y == 0, a, b) for a, b in zip(in_row, out_row)]
        + [jnp.where(y == 0, b, a) for a, b in zip(in_row, out_row)],
        axis=0,
    )
    out_weight = lax.all_gather(attn_out.astype(low_type), GRID, axis=0, tiled=True)

    sliced_in = expert_in.astype(low_type).reshape(chunk_rows, local_experts, 2, ranks, part)
    sliced_in = sliced_in.transpose(3, 0, 2, 1, 4).reshape(ranks, chunk_rows, 2 * span)
    weights_in = lax.all_to_all(sliced_in, SEQ, 0, 0, tiled=True).reshape(width, 2 * span)
    sliced_down = expert_down.astype(low_type).reshape(chunk_rows, local_experts, ranks, part)
    sliced_down = sliced_down.transpose(2, 0, 1, 3).reshape(ranks, chunk_rows, span)
    weights_down = lax.all_to_all(sliced_down, SEQ, 0, 0, tiled=True).reshape(width, span)

    raw = dot(normed_in, qkv_weight)
    query_raw, key_raw = raw[:, :own_width], raw[:, own_width : 2 * own_width]
    value_rows = raw[:, 2 * own_width :].astype(low_type)
    squares = jnp.stack(
        [jnp.sum(query_raw * query_raw, axis=1), jnp.sum(key_raw * key_raw, axis=1)]
    )
    scales = lax.rsqrt(move.sum_seq(squares) / width + epsilon)
    query_scale, key_scale = scales[0][:, None], scales[1][:, None]
    positions = jnp.arange(seq_rows, dtype=jnp.int32)
    length_now = lengths[0]
    key_live = positions < length_now
    cosine, sine_table = angle_tables(positions)
    query_normed = query_raw * query_scale
    key_normed = key_raw * key_scale
    query_rot = rotate(query_normed * gain_own[0], cosine, sine_table).astype(low_type)
    key_rot = rotate(key_normed * gain_own[1], cosine, sine_table).astype(low_type)
    query_heads = query_rot.reshape(seq_rows, own_heads, HD)
    key_heads = key_rot.reshape(seq_rows, own_heads, HD)
    value_heads = value_rows.reshape(seq_rows, own_heads, HD)

    def per_head(spec, left, right):
        return jnp.einsum(spec, left, right, preferred_element_type=high_type)

    scores = per_head("qhd,khd->hqk", query_heads, key_heads) * score_scale
    scores = jnp.where(key_live[None, None, :], scores, masked_score)
    probs = jax.nn.softmax(scores, axis=-1)
    probs_low = probs.astype(low_type)
    attended = per_head("hqk,khd->qhd", probs_low, value_heads).astype(low_type)
    attended = lax.all_to_all(attended.reshape(ranks, rows, own_width), SEQ, 0, 0, tiled=True)
    attended = by_head(attended)

    own_positions = (z * 2 + c) * rows + jnp.arange(rows, dtype=jnp.int32)
    live_rows = (own_positions < length_now).astype(high_type)[:, None]
    input_rows = residual_in.astype(high_type)
    middle = input_rows + live_rows * dot(attended, out_weight)
    scale_mid = rms_scale(middle)
    normed_mid_f = middle * scale_mid
    normed_mid = (normed_mid_f * gain_rows[3]).astype(low_type)

    logits = dot(normed_mid, router_weight)
    named = jnp.any(
        routes[:, :, None] == jnp.arange(experts, dtype=jnp.int32)[None, None, :], axis=1
    )
    top = jnp.max(jnp.where(named, logits, -jnp.inf), axis=1, keepdims=True)
    weight_of = jnp.where(named, jnp.exp(jnp.where(named, logits - top, 0.0)), 0.0)
    gates = weight_of / jnp.sum(weight_of, axis=1, keepdims=True)

    grad_rows = cotangent.astype(high_type)
    grad_comb = live_rows * grad_rows
    order = move.block_order()
    gates_all = lax.all_gather(gates.T[None], GRID, axis=0, tiled=True)
    gates_all = lax.dynamic_slice_in_dim(gates_all, column * local_experts, local_experts, 1)
    chosen_block = (order[:, None] == jnp.arange(4 * ranks, dtype=jnp.int32)[None, :]).astype(
        high_type
    )

    def permuted(spec, blocks):
        return jnp.einsum(
            spec,
            chosen_block,
            blocks,
            precision=lax.Precision.HIGHEST,
            preferred_element_type=high_type,
        )

    gates_all = permuted("ij,jer->ier", gates_all).transpose(0, 2, 1).reshape(-1, local_experts)
    grad_chunks = move.spread(grad_comb.astype(low_type))
    token_chunks = move.spread(normed_mid)
    back_chunks, mixed_chunks, gate_sums = [], [], []
    grad_in = jnp.zeros((width, 2 * span), high_type)
    grad_down = jnp.zeros((width, span), high_type)
    start = 0
    for tokens, grads in zip(token_chunks, grad_chunks):
        count = tokens.shape[0]
        gate = gates_all[start : start + count]
        start += count
        wide = jnp.repeat(gate, part, axis=1)
        both_parts = dot(tokens, weights_in)
        gate_part, up_part = both_parts[:, :span], both_parts[:, span:]
        down_grad = dot(grads, weights_down)
        sigma = jax.nn.sigmoid(gate_part)
        hidden = (gate_part * sigma * up_part).astype(low_type).astype(high_type)
        gate_sums.append(
            jnp.sum((hidden * down_grad).reshape(count, local_experts, part), axis=2)
        )
        weighted = (wide * hidden).astype(low_type)
        grad_hidden = wide * down_grad
        grad_gate = grad_hidden * up_part * sigma * (1.0 + gate_part * (1.0 - sigma))
        grad_up = grad_hidden * gate_part * sigma
        grad_both = jnp.concatenate([grad_gate, grad_up], axis=1).astype(low_type)
        back_chunks.append(dot_t(grad_both, weights_in).astype(low_type))
        mixed_chunks.append(dot_t(weighted, weights_down).astype(low_type))
        grad_in = grad_in + t_dot(tokens, grad_both)
        grad_down = grad_down + t_dot(grads, weighted)
    grad_mid_norm = move.collect(back_chunks, rows)
    combined = move.collect(mixed_chunks, rows)
    output = middle + live_rows * combined

    sliced = grad_in.astype(low_type).reshape(ranks, chunk_rows, 2 * span)
    sliced = lax.all_to_all(sliced, SEQ, 0, 0, tiled=True)
    sliced = sliced.reshape(ranks, chunk_rows, 2, local_experts, part).transpose(1, 3, 2, 0, 4)
    grad_expert_in = sliced.reshape(expert_in.shape).astype(high_type)
    sliced = grad_down.astype(low_type).reshape(ranks, chunk_rows, span)
    sliced = lax.all_to_all(sliced, SEQ, 0, 0, tiled=True)
    sliced = sliced.reshape(ranks, chunk_rows, local_experts, part).transpose(1, 2, 0, 3)
    grad_expert_down = sliced.reshape(expert_down.shape).astype(high_type)

    sums = jnp.concatenate(gate_sums, axis=0).reshape(-1, rows, local_experts).transpose(0, 2, 1)
    placed = jnp.zeros((4 * ranks, columns, local_experts, rows), high_type)
    sums = permuted("ij,ier->jer", sums)
    placed = lax.dynamic_update_slice(placed, sums[:, None], (0, column, 0, 0))
    grad_gates = lax.psum_scatter(
        placed.reshape(4 * ranks, experts, rows), GRID, scatter_dimension=0, tiled=True
    )[0].T
    grad_chosen = gates * (grad_gates - jnp.sum(gates * grad_gates, axis=1, keepdims=True))
    grad_logits = grad_chosen.astype(low_type)
    grad_mid_norm = grad_mid_norm + dot_t(grad_logits, router_weight)
    grad_router = t_dot(normed_mid, grad_logits)

    grad_mid_rows, grad_gain_mid = rms_back(grad_mid_norm, normed_mid_f, scale_mid, gain_rows[3])
    grad_middle = grad_rows + grad_mid_rows
    grad_branch = (live_rows * grad_middle).astype(low_type)
    grad_out = lax.psum_scatter(
        t_dot(attended, grad_branch).astype(low_type), GRID, scatter_dimension=0, tiled=True
    ).astype(high_type)

    grad_attended = by_rank(dot_t(grad_branch, out_weight).astype(low_type))
    grad_attended = lax.all_to_all(grad_attended, SEQ, 0, 0, tiled=True)
    grad_heads = grad_attended.reshape(seq_rows, own_heads, HD)
    grad_probs = per_head("qhd,khd->hqk", grad_heads, value_heads)
    inner_rows = jnp.sum(probs * grad_probs, axis=-1, keepdims=True)
    grad_scores = (probs * (grad_probs - inner_rows)).astype(low_type)
    grad_query = per_head("hqk,khd->qhd", grad_scores, key_heads) * score_scale
    grad_key = per_head("hqk,qhd->khd", grad_scores, query_heads) * score_scale
    grad_value = per_head("hqk,qhd->khd", probs_low, grad_heads).astype(low_type)
    grad_query = rotate(grad_query.reshape(seq_rows, own_width), cosine, -sine_table)
    grad_key = rotate(grad_key.reshape(seq_rows, own_width), cosine, -sine_table)
    query_inner = grad_query * gain_own[0]
    key_inner = grad_key * gain_own[1]
    inner = jnp.stack(
        [
            jnp.sum(query_inner * query_normed, axis=1),
            jnp.sum(key_inner * key_normed, axis=1),
        ]
    )
    inner = move.sum_seq(inner) / width
    query_back = query_scale * (query_inner - query_normed * inner[0][:, None])
    key_back = key_scale * (key_inner - key_normed * inner[1][:, None])
    grad_raw = jnp.concatenate(
        [
            query_back.astype(low_type),
            key_back.astype(low_type),
            grad_value.reshape(seq_rows, own_width),
        ],
        axis=1,
    )

    by_core = grad_raw.reshape(depth, 2, rows, 3 * own_width)
    other = lax.dynamic_index_in_dim(by_core, 1 - c, 1, keepdims=False)
    mine = lax.dynamic_index_in_dim(by_core, c, 1, keepdims=False)
    other = dot_t(other.reshape(depth * rows, -1), qkv_weight).astype(low_type)
    mine = dot_t(mine.reshape(depth * rows, -1), qkv_weight)
    share = (mine + move.core(other).astype(high_type)).astype(low_type)
    share = share.reshape(depth, rows, width)
    grad_norm_in = lax.dynamic_index_in_dim(share, z, 0, keepdims=False).astype(high_type)
    for step in range(1, depth):
        piece = lax.dynamic_index_in_dim(share, (z + step) % depth, 0, keepdims=False)
        grad_norm_in = grad_norm_in + move.to_z(piece, step).astype(high_type)

    grad_qkv = t_dot(normed_in, grad_raw).astype(low_type).reshape(columns, -1, 3 * own_width)

    def for_column(index):
        return lax.dynamic_index_in_dim(grad_qkv, index, 0, keepdims=False)

    far_x, far_y = x ^ c, y ^ (1 - c)
    near_x, near_y = x ^ (1 - c), y ^ c
    arrived = move.far(
        jnp.stack([for_column(far_y * 2 + far_x), for_column(3 - column)])
    ).astype(high_type)
    near = (for_column(near_y * 2 + near_x).astype(high_type) + arrived[1]).astype(low_type)
    total = for_column(column).astype(high_type) + arrived[0] + move.near(near).astype(high_type)
    total = total.astype(low_type).reshape(ranks, weight_rows, 3 * own_width)
    total = lax.all_to_all(total, SEQ, 0, 0, tiled=True)
    grad_qkv = by_head(total.reshape(ranks, weight_rows, 3, own_width))
    grad_qkv = grad_qkv.transpose(1, 0, 2).astype(high_type)

    scale_in = rms_scale(input_rows)
    grad_in_rows, grad_gain_in = rms_back(
        grad_norm_in, input_rows * scale_in, scale_in, gain_rows[0]
    )
    grad_input = grad_middle + grad_in_rows

    def at_heads(values):
        whole = jnp.zeros((2, own_heads, depth, HD), high_type)
        values = values.reshape(1, own_heads, 1, HD)
        return lax.dynamic_update_slice(whole, values, (c, 0, z, 0)).reshape(width)

    grad_small = jnp.concatenate(
        [
            jnp.stack(
                [
                    grad_gain_in,
                    at_heads(jnp.sum(grad_query * query_normed, axis=0)),
                    at_heads(jnp.sum(grad_key * key_normed, axis=0)),
                    grad_gain_mid,
                ]
            ).T,
            grad_router,
        ],
        axis=1,
    )
    grad_small = lax.psum_scatter(grad_small, GRID, scatter_dimension=0, tiled=True)
    return (
        output,
        grad_input,
        grad_qkv,
        grad_out,
        grad_small[:, :4].T,
        grad_small[:, 4:],
        grad_expert_in,
        grad_expert_down,
    )


def slot_index(route_rows, experts, capacity):
    flat_routes = route_rows.reshape(-1)
    onehot = (flat_routes[:, None] == jnp.arange(experts, dtype=jnp.int32)[None, :]).astype(
        jnp.int32
    )
    rows = jnp.arange(flat_routes.shape[0], dtype=jnp.int32)
    earlier = (rows[None, :] < rows[:, None]).astype(jnp.bfloat16)
    before = jnp.dot(
        earlier, onehot.astype(jnp.bfloat16), preferred_element_type=jnp.float32
    ).astype(jnp.int32)
    rank_rows = jnp.sum(before * onehot, axis=1)
    return flat_routes * capacity + rank_rows


def head_scores(query_rot, key_all, key_live):
    row_count = query_rot.shape[0]
    query_heads = query_rot.reshape(row_count, HEADS, HD)
    key_heads = key_all.reshape(key_all.shape[0], HEADS, HD)
    raw_scores = jnp.einsum(
        "qhd,khd->hqk", query_heads, key_heads, preferred_element_type=jnp.float32
    ) * HD ** (-0.5)
    return jnp.where(key_live[None, None, :], raw_scores, masked_score)


def to_owners(buffer):
    return lax.all_to_all(buffer, "expert", split_axis=0, concat_axis=0, tiled=True)


def from_owners(buffer):
    return lax.all_to_all(buffer, "expert", split_axis=0, concat_axis=0, tiled=True)


def shards(
    residual_in,
    cotangent,
    lengths,
    routes,
    attn_qkv,
    attn_out,
    gains,
    router,
    expert_in,
    expert_down,
):
    tok_rows, model_width = residual_in.shape
    top_count = routes.shape[1]
    owners = lax.axis_size("expert")
    local_experts = expert_in.shape[1]
    experts = local_experts * owners
    capacity = tok_rows * top_count * 2 // experts
    local_slots = local_experts * capacity
    seq_rows = tok_rows * lax.axis_size("dp")
    score_scale = HD ** (-0.5)
    qkv_weights, out_weight, gain_low, router_weight = (
        lax.all_gather(attn_qkv.astype(low_type), ("expert", "dp"), axis=1, tiled=True),
        lax.all_gather(attn_out.astype(low_type), ("expert", "dp"), axis=0, tiled=True),
        lax.all_gather(gains.astype(low_type), ("expert", "dp"), axis=1, tiled=True),
        lax.all_gather(router.astype(low_type), ("expert", "dp"), axis=0, tiled=True),
    )
    gain_rows = gain_low.astype(high_type)
    input_rows = residual_in.astype(high_type)
    scale_in = rms_scale(input_rows)
    normed_in_f = input_rows * scale_in
    normed_in = (normed_in_f * gain_rows[0]).astype(low_type)
    query_raw = jnp.dot(normed_in, qkv_weights[0], preferred_element_type=high_type)
    key_raw = jnp.dot(normed_in, qkv_weights[1], preferred_element_type=high_type)
    value_rows = jnp.dot(normed_in, qkv_weights[2], preferred_element_type=high_type).astype(
        low_type
    )
    positions = lax.axis_index("dp") * tok_rows + jnp.arange(tok_rows, dtype=jnp.int32)
    length_now = lengths[0]
    live_rows = (positions < length_now).astype(high_type)[:, None]
    key_live = jnp.arange(seq_rows, dtype=jnp.int32) < length_now
    cosine, sine_table = angle_tables(positions)
    query_scale = rms_scale(query_raw)
    query_normed = query_raw * query_scale
    query_rot = rotate(query_normed * gain_rows[1], cosine, sine_table).astype(low_type)
    key_scale = rms_scale(key_raw)
    key_normed = key_raw * key_scale
    key_rot = rotate(key_normed * gain_rows[2], cosine, sine_table).astype(low_type)
    key_all = lax.all_gather(key_rot, "dp", axis=0, tiled=True)
    value_all = lax.all_gather(value_rows, "dp", axis=0, tiled=True)
    scores = head_scores(query_rot, key_all, key_live)
    top_score = jnp.max(scores, axis=-1, keepdims=True)
    exp_scores = jnp.exp(scores - top_score)
    row_total = jnp.sum(exp_scores, axis=-1, keepdims=True)
    weights_low = (exp_scores / row_total).astype(low_type)
    log_total = top_score + jnp.log(row_total)
    value_heads = value_all.reshape(seq_rows, HEADS, HD)
    attended = jnp.einsum(
        "hqk,khd->qhd", weights_low, value_heads, preferred_element_type=high_type
    )
    attended = attended.reshape(tok_rows, model_width).astype(low_type)
    branch = jnp.dot(attended, out_weight, preferred_element_type=high_type)
    middle = input_rows + live_rows * branch
    scale_mid = rms_scale(middle)
    normed_mid_f = middle * scale_mid
    normed_mid = (normed_mid_f * gain_rows[3]).astype(low_type)
    logits = jnp.dot(normed_mid, router_weight, preferred_element_type=high_type)
    selector = (routes[:, :, None] == jnp.arange(experts, dtype=jnp.int32)[None, None, :]).astype(
        high_type
    )
    chosen = jnp.einsum("te,tje->tj", logits, selector)
    gate_weights = jax.nn.softmax(chosen, axis=-1)
    slot_rows = slot_index(routes, experts, capacity)
    token_of = jnp.arange(slot_rows.shape[0], dtype=jnp.int32) // top_count
    send_rows = (
        jnp.zeros((experts * capacity, model_width), low_type)
        .at[slot_rows]
        .set(normed_mid[token_of])
    )
    rows_recv = lax.all_to_all(
        send_rows.reshape(owners, local_slots, model_width),
        "expert",
        split_axis=0,
        concat_axis=0,
        tiled=True,
    )
    rows_recv = rows_recv.reshape(owners, local_experts, capacity, model_width)
    weights_in, weights_down = (
        lax.all_gather(expert_in.astype(low_type), "dp", axis=0, tiled=True),
        lax.all_gather(expert_down.astype(low_type), "dp", axis=0, tiled=True),
    )
    both_parts = jnp.einsum(
        "sxmd,dxkf->sxmkf", rows_recv, weights_in, preferred_element_type=high_type
    )
    gate_part = both_parts[:, :, :, 0, :]
    up_part = both_parts[:, :, :, 1, :]
    hidden = (jax.nn.silu(gate_part) * up_part).astype(low_type)
    produced = jnp.einsum(
        "sxmf,dxf->sxmd", hidden, weights_down, preferred_element_type=high_type
    ).astype(low_type)
    returned = from_owners(produced.reshape(owners, local_slots, model_width))
    returned = returned.reshape(experts * capacity, model_width)
    picked = returned[slot_rows].reshape(tok_rows, top_count, model_width).astype(high_type)
    combined = jnp.sum(gate_weights[:, :, None] * picked, axis=1)
    output = middle + live_rows * combined
    grad_rows = cotangent.astype(high_type)
    grad_comb = live_rows * grad_rows
    grad_gates = jnp.einsum("tjd,td->tj", picked, grad_comb)
    grad_chosen = gate_weights * (
        grad_gates - jnp.sum(gate_weights * grad_gates, axis=-1, keepdims=True)
    )
    grad_logits = jnp.einsum("tj,tje->te", grad_chosen, selector).astype(low_type)
    grad_send = (
        (gate_weights[:, :, None] * grad_comb[:, None, :]).astype(low_type).reshape(-1, model_width)
    )
    grad_buffer = (
        jnp.zeros((experts * capacity, model_width), low_type).at[slot_rows].set(grad_send)
    )
    grad_recv = to_owners(grad_buffer.reshape(owners, local_slots, model_width))
    grad_recv = grad_recv.reshape(owners, local_experts, capacity, model_width)
    grad_hidden = jnp.einsum(
        "sxmd,dxf->sxmf", grad_recv, weights_down, preferred_element_type=high_type
    )
    sigma_gate = jax.nn.sigmoid(gate_part)
    grad_gate = grad_hidden * up_part * sigma_gate * (1.0 + gate_part * (1.0 - sigma_gate))
    grad_up = grad_hidden * gate_part * sigma_gate
    grad_both = jnp.stack([grad_gate, grad_up], axis=3).astype(low_type)
    grad_rows_out = jnp.einsum(
        "sxmkf,dxkf->sxmd", grad_both, weights_in, preferred_element_type=high_type
    ).astype(low_type)
    grad_back = from_owners(grad_rows_out.reshape(owners, local_slots, model_width))
    grad_back = grad_back.reshape(experts * capacity, model_width)
    grad_mid_norm = jnp.sum(
        grad_back[slot_rows].reshape(tok_rows, top_count, model_width).astype(high_type), axis=1
    )
    grad_mid_norm = grad_mid_norm + jnp.dot(
        grad_logits, router_weight.T, preferred_element_type=high_type
    )
    grad_router = jnp.dot(normed_mid.T, grad_logits, preferred_element_type=high_type)
    row_piece = rows_recv
    grad_expert_in = lax.psum_scatter(
        jnp.einsum(
            "sxmd,sxmkf->dxkf", row_piece, grad_both, preferred_element_type=high_type
        ).astype(jnp.bfloat16),
        "dp",
        scatter_dimension=0,
        tiled=True,
    ).astype(jnp.float32)
    row_piece = grad_recv
    grad_expert_down = lax.psum_scatter(
        jnp.einsum("sxmd,sxmf->dxf", row_piece, hidden, preferred_element_type=high_type).astype(
            jnp.bfloat16
        ),
        "dp",
        scatter_dimension=0,
        tiled=True,
    ).astype(jnp.float32)
    grad_mid_rows, grad_gain_mid = rms_back(grad_mid_norm, normed_mid_f, scale_mid, gain_rows[3])
    grad_middle = grad_rows + grad_mid_rows
    grad_branch = (live_rows * grad_middle).astype(low_type)
    grad_out_weight = jnp.dot(attended.T, grad_branch, preferred_element_type=high_type)
    grad_attended = jnp.dot(grad_branch, out_weight.T, preferred_element_type=high_type).astype(
        low_type
    )
    scores = head_scores(query_rot, key_all, key_live)
    probs_full = jnp.exp(scores - log_total)
    grad_heads = grad_attended.reshape(tok_rows, HEADS, HD)
    value_heads = value_all.reshape(seq_rows, HEADS, HD)
    key_heads = key_all.reshape(seq_rows, HEADS, HD)
    query_heads = query_rot.reshape(tok_rows, HEADS, HD)
    grad_probs = jnp.einsum(
        "qhd,khd->hqk", grad_heads, value_heads, preferred_element_type=high_type
    )
    inner_rows = jnp.sum(probs_full * grad_probs, axis=-1, keepdims=True)
    grad_scores = (probs_full * (grad_probs - inner_rows)).astype(low_type)
    grad_query = (
        jnp.einsum(
            "hqk,khd->qhd", grad_scores, key_heads, preferred_element_type=high_type
        ).reshape(tok_rows, model_width)
        * score_scale
    )
    grad_key_part = (
        jnp.einsum(
            "hqk,qhd->khd", grad_scores, query_heads, preferred_element_type=high_type
        ).reshape(seq_rows, model_width)
        * score_scale
    )
    grad_value_part = jnp.einsum(
        "hqk,qhd->khd", probs_full.astype(low_type), grad_heads, preferred_element_type=high_type
    ).reshape(seq_rows, model_width)
    grad_key_sum, grad_value_sum = (
        lax.psum_scatter(
            grad_key_part.astype(jnp.bfloat16), "dp", scatter_dimension=0, tiled=True
        ).astype(jnp.float32),
        lax.psum_scatter(
            grad_value_part.astype(jnp.bfloat16), "dp", scatter_dimension=0, tiled=True
        ).astype(jnp.float32),
    )
    grad_value = grad_value_sum.astype(low_type)
    grad_key_raw, grad_key_gain = rms_back(
        rotate(grad_key_sum, cosine, -sine_table), key_normed, key_scale, gain_rows[2]
    )
    grad_query_raw, grad_query_gain = rms_back(
        rotate(grad_query, cosine, -sine_table), query_normed, query_scale, gain_rows[1]
    )
    grad_key_raw = grad_key_raw.astype(low_type)
    grad_query_raw = grad_query_raw.astype(low_type)
    grad_norm_in = jnp.dot(grad_query_raw, qkv_weights[0].T, preferred_element_type=high_type)
    grad_norm_in = grad_norm_in + jnp.dot(
        grad_key_raw, qkv_weights[1].T, preferred_element_type=high_type
    )
    grad_norm_in = grad_norm_in + jnp.dot(
        grad_value, qkv_weights[2].T, preferred_element_type=high_type
    )
    grad_qkv_local = jnp.stack(
        [
            jnp.dot(normed_in.T, grad_query_raw, preferred_element_type=high_type),
            jnp.dot(normed_in.T, grad_key_raw, preferred_element_type=high_type),
            jnp.dot(normed_in.T, grad_value, preferred_element_type=high_type),
        ]
    )
    grad_in_rows, grad_gain_in = rms_back(grad_norm_in, normed_in_f, scale_in, gain_rows[0])
    grad_input = grad_middle + grad_in_rows
    grad_gains_local = jnp.stack([grad_gain_in, grad_query_gain, grad_key_gain, grad_gain_mid])
    summed = (
        lax.psum_scatter(grad_qkv_local, ("expert", "dp"), scatter_dimension=1, tiled=True),
        lax.psum_scatter(grad_out_weight, ("expert", "dp"), scatter_dimension=0, tiled=True),
        lax.psum_scatter(grad_gains_local, ("expert", "dp"), scatter_dimension=1, tiled=True),
        lax.psum_scatter(grad_router, ("expert", "dp"), scatter_dimension=0, tiled=True),
    )
    return (
        output,
        grad_input,
        summed[0],
        summed[1],
        summed[2],
        summed[3],
        grad_expert_in,
        grad_expert_down,
    )


def solution(mesh):
    column_count, rank_count = mesh.shape["expert"], mesh.shape["dp"]
    depth = rank_count // 2
    tiled = column_count == 4 and rank_count % 2 == 0 and HEADS == column_count * depth
    if tiled:
        mesh = Mesh(mesh.devices.reshape(2, 2, depth, 2), GRID)
        column, rank, body = ("ey", "ex"), SEQ, grid_shards
    else:
        column, rank, body = ("expert",), ("dp",), shards
    device = column + rank
    placed = (
        P(device, None),
        P(device, None),
        P(column),
        P(device, None),
        P(None, device, None),
        P(device, None),
        P(None, device),
        P(device, None),
        P(rank, column, None, None),
        P(rank, column, None),
    )
    return jax.shard_map(
        body,
        mesh=mesh,
        in_specs=placed,
        out_specs=placed[:1] * 2 + placed[4:],
        check_vma=False,
    )
```

```python
import functools

import jax
import jax.numpy as jnp
from jax import lax
from jax.experimental import pallas as pl
from jax.experimental.pallas import tpu as pltpu
from jax.sharding import Mesh
from jax.sharding import PartitionSpec as P

HEADS = 16
HD = 128

epsilon = 1e-05
rope_base = 10000.0
masked_score = -1000000000.0

low_type = jnp.bfloat16
high_type = jnp.float32


def rms_scale(values):
    return lax.rsqrt(jnp.mean(values * values, axis=-1, keepdims=True) + epsilon)


def angle_tables(positions):
    frequency = rope_base ** (-2.0 * jnp.arange(HD // 2, dtype=jnp.float32) / HD)
    angles = positions.astype(jnp.float32)[:, None] * frequency[None, :]
    return (jnp.cos(angles), jnp.sin(angles))


def rotate(values, cosine, sine_table):
    row_count, width = values.shape
    shaped = values.reshape(row_count, width // HD, 2, HD // 2)
    first_half = shaped[:, :, 0, :]
    second_half = shaped[:, :, 1, :]
    cos_rows = cosine[:, None, :]
    sin_rows = sine_table[:, None, :]
    turned = jnp.stack(
        [
            first_half * cos_rows - second_half * sin_rows,
            second_half * cos_rows + first_half * sin_rows,
        ],
        axis=2,
    )
    return turned.reshape(row_count, width)


def rms_back(grad_rows, normed, scale, gain):
    grad_normed = grad_rows * gain
    inner = jnp.mean(grad_normed * normed, axis=-1, keepdims=True)
    return (scale * grad_normed - normed * scale * inner, jnp.sum(grad_rows * normed, axis=0))


def dot(left, right):
    return jnp.dot(left, right, preferred_element_type=high_type)


def dot_t(left, right):
    return lax.dot_general(left, right, (((1,), (1,)), ((), ())), preferred_element_type=high_type)


def t_dot(left, right):
    return lax.dot_general(left, right, (((0,), (0,)), ((), ())), preferred_element_type=high_type)


GRID = ("ey", "ex", "dz", "dc")
SEQ = ("dz", "dc")


MESH_ID = pl.DeviceIdType.MESH


class Place:
    def __init__(self, depth):
        self.depth = depth
        self.y, self.x, self.z, self.c = (lax.axis_index(name) for name in GRID)

    def near_of(self, core):
        return self.y + core * (1 - 2 * self.y), self.x + (1 - core) * (1 - 2 * self.x)

    def far_of(self, core):
        return self.near_of(1 - core)

    def along(self, step):
        return lax.rem(self.z + step, self.depth)

    def block(self, column, z, core):
        return ((column[0] * 2 + column[1]) * self.depth + z) * 2 + core

    @property
    def own_column(self):
        return self.y, self.x

    @property
    def other_column(self):
        return 1 - self.y, 1 - self.x

    def core(self):
        return self.y, self.x, self.z, 1 - self.c

    def chip(self, step, core=None):
        return self.y, self.x, self.along(step), self.c if core is None else core

    def near(self):
        return (*self.near_of(self.c), self.z, self.c)

    def far(self):
        return (*self.far_of(self.c), self.z, self.c)


def meet(partners):
    barrier = pltpu.get_barrier_semaphore()
    for partner in partners:
        pl.semaphore_signal(barrier, inc=1, device_id=partner, device_id_type=MESH_ID)
    pl.semaphore_wait(barrier, len(partners))


def remote(source, target, sems, slot, partner):
    return pltpu.make_async_remote_copy(
        src_ref=source,
        dst_ref=target,
        send_sem=sems[0].at[slot],
        recv_sem=sems[1].at[slot],
        device_id=partner,
        device_id_type=MESH_ID,
    )


def pair(count):
    return [pltpu.SemaphoreType.DMA((count,)), pltpu.SemaphoreType.DMA((count,))]


def in_hbm(count):
    return [pl.BlockSpec(memory_space=pl.ANY)] * count


def spread_kernel(depth, count, extra, *refs):
    whole = count + extra
    sources, targets, sems = refs[:count], refs[whole : whole + count], refs[2 * whole :]
    extra_sources, extra_targets = refs[count:whole], refs[whole + count : 2 * whole]
    extra_sems = sems[9 * count :]
    at = Place(depth)
    others = range(1, depth)
    ranks = [(k, core) for k in range(depth) for core in range(2) if k or core]
    peers = [at.chip(k, lax.rem(at.c + core, 2)) for k, core in ranks]
    meet([at.near(), at.far()] + peers)
    started, local = [], []

    def push(n, source, index, kind, slot, partner):
        copy = remote(source, targets[n].at[index], sems[9 * n + 2 * kind :], slot, partner)
        copy.start()
        started.append(copy)

    def arrive(n, index, kind, slot):
        target = targets[n].at[index]
        remote(target, target, sems[9 * n + 2 * kind :], slot, at.core()).wait_recv()

    z_kind, near_kind, far_kind, core_kind = range(4)
    own = at.block(at.own_column, at.z, at.c)
    for n in range(count):
        for k in others:
            push(n, sources[n], own, z_kind, k - 1, at.chip(k))
        push(n, sources[n], own, near_kind, 0, at.near())
        push(n, sources[n], own, far_kind, 0, at.far())
        push(n, sources[n], own, core_kind, 0, at.core())
        copy = pltpu.make_async_copy(sources[n], targets[n].at[own], sems[9 * n + 8])
        copy.start()
        local.append(copy)
    own_rank = at.z * 2 + at.c
    for n in range(extra):
        for slot, there in enumerate(peers):
            copy = remote(
                extra_sources[n].at[there[2] * 2 + there[3]],
                extra_targets[n].at[own_rank],
                extra_sems[3 * n :],
                slot,
                there,
            )
            copy.start()
            started.append(copy)
        copy = pltpu.make_async_copy(
            extra_sources[n].at[own_rank], extra_targets[n].at[own_rank], extra_sems[3 * n + 2]
        )
        copy.start()
        local.append(copy)
    for k in others:
        index = at.block(at.own_column, at.along(depth - k), at.c)
        for n in range(count):
            arrive(n, index, z_kind, k - 1)
            push(n, targets[n].at[index], index, near_kind, k, at.near())
            push(n, targets[n].at[index], index, far_kind, k, at.far())
            push(n, targets[n].at[index], index, core_kind, k, at.core())
    for k in range(depth):
        index = at.block(at.near_of(at.c), at.along(depth - k), at.c)
        for n in range(count):
            arrive(n, index, near_kind, k)
            push(n, targets[n].at[index], index, far_kind, depth + k, at.far())
            push(n, targets[n].at[index], index, core_kind, depth + k, at.core())
    for j in range(2 * depth):
        column = at.far_of(at.c) if j < depth else at.other_column
        index = at.block(column, at.along(depth - j % depth), at.c)
        for n in range(count):
            arrive(n, index, far_kind, j)
            push(n, targets[n].at[index], index, core_kind, 2 * depth + j, at.core())
    core = 1 - at.c
    columns = [at.own_column, at.near_of(core), at.far_of(core), at.other_column]
    for j in range(4 * depth):
        index = at.block(columns[j // depth], at.along(depth - j % depth), core)
        for n in range(count):
            arrive(n, index, core_kind, j)
    for n in range(extra):
        for slot, (k, core) in enumerate(ranks):
            target = extra_targets[n].at[at.along(depth - k) * 2 + lax.rem(at.c + core, 2)]
            remote(target, target, extra_sems[3 * n :], slot, at.core()).wait_recv()
    for copy in started:
        copy.wait_send()
    for copy in local:
        copy.wait()


def spread(depth, ident, arrays, extras=()):
    sems = []
    for _ in arrays:
        sems += pair(depth - 1) + pair(depth) + pair(2 * depth) + pair(4 * depth)
        sems.append(pltpu.SemaphoreType.DMA)
    for _ in extras:
        sems += pair(2 * depth - 1) + [pltpu.SemaphoreType.DMA]
    count = len(arrays) + len(extras)
    shapes = [((8 * depth,) + a.shape, a.dtype) for a in arrays]
    shapes += [(a.shape, a.dtype) for a in extras]
    return pl.pallas_call(
        functools.partial(spread_kernel, depth, len(arrays), len(extras)),
        out_shape=[jax.ShapeDtypeStruct(*shape) for shape in shapes],
        in_specs=in_hbm(count),
        out_specs=in_hbm(count),
        scratch_shapes=sems,
        compiler_params=pltpu.CompilerParams(
            collective_id=ident, has_side_effects=True, vmem_limit_bytes=16 << 20
        ),
        cost_estimate=pl.CostEstimate(
            flops=0,
            bytes_accessed=sum(64 * depth * a.size * a.dtype.itemsize for a in arrays),
            transcendentals=0,
        ),
    )(*arrays, *extras)


def sum_rows(target, lead, terms):
    rows = target.shape[-2]
    tile = min(rows, 16)

    def body(i, carry):
        at = pl.ds(pl.multiple_of(i * tile, tile), tile)
        total = terms[0][0][(*terms[0][1], at, slice(None))].astype(high_type)
        for ref, where in terms[1:]:
            total = total + ref[(*where, at, slice(None))].astype(high_type)
        target[(*lead, at, slice(None))] = total.astype(target.dtype)
        return carry

    lax.fori_loop(0, rows // tile, body, 0)


def collect_kernel(depth, count, shared, *refs):
    whole = count + shared
    parts, totals = refs[:count], refs[whole : whole + count]
    scratch, sems = refs[2 * whole : 2 * whole + 5 * count], refs[2 * whole + 5 * count :]
    at = Place(depth)
    ranks = [(k, core) for k in range(depth) for core in range(2) if k or core]
    peers = [at.chip(k, lax.rem(at.c + core, 2)) for k, core in ranks]
    meet([at.near(), at.far()] + peers)
    started = []
    groups = (3, 2, 1, 0)
    per = 9

    def block(slot, core):
        column = (at.own_column, at.near_of(core), at.far_of(core), at.other_column)[
            groups[slot // depth]
        ]
        return at.block(column, at.along(1 + slot % depth), core)

    def push(copy):
        copy.start()
        started.append(copy)

    def arrive(buffer, pair_of, slot):
        remote(buffer.at[slot], buffer.at[slot], pair_of, slot, at.core()).wait_recv()

    def load(n, slot):
        return pltpu.make_async_copy(
            parts[n].at[block(slot, at.c)], scratch[5 * n].at[slot], sems[per * n + 8].at[slot]
        )

    def number(column):
        return column[0] * 2 + column[1]

    if shared:
        part, arrived = refs[count], refs[whole + count]
        mine, far_in, near_in, local = refs[-10:-6]
        far_sems, near_sems, out_sems = refs[-6:-4], refs[-4:-2], refs[-2:]
        columns = [at.other_column, at.far_of(at.c), at.near_of(at.c), at.own_column]
        for i in range(2):
            push(remote(part.at[number(columns[i])], far_in.at[i], far_sems, i, at.far()))
            pltpu.make_async_copy(
                part.at[number(columns[2 + i])], mine.at[i], local.at[i]
            ).start()
    for slot in range(4 * depth):
        for n in range(count):
            push(
                remote(
                    parts[n].at[block(slot, 1 - at.c)],
                    scratch[5 * n + 1].at[slot],
                    sems[per * n :],
                    slot,
                    at.core(),
                )
            )
            load(n, slot).start()

    def add(n, slot, more):
        mine, crossed = scratch[5 * n : 5 * n + 2]
        load(n, slot).wait()
        arrive(crossed, sems[per * n :], slot)
        terms = [(mine, (slot,)), (crossed, (slot,))] + more
        if slot < 4 * depth - 1:
            sum_rows(mine, (slot,), terms)
        else:
            sum_rows(totals[n], (), terms)
        return mine.at[slot]

    for n in range(count):
        for slot in range(2 * depth):
            total = add(n, slot, [])
            far_in = scratch[5 * n + 2]
            push(remote(total, far_in.at[slot], sems[per * n + 2 :], slot, at.far()))
    if shared:
        mine, far_in, near_in, local = refs[-10:-6]
        pltpu.make_async_copy(part.at[number(columns[2])], mine.at[0], local.at[0]).wait()
        arrive(far_in, far_sems, 0)
        sum_rows(mine, (0,), [(mine, (0,)), (far_in, (0,))])
        push(remote(mine.at[0], near_in.at[0], near_sems, 0, at.near()))
    for n in range(count):
        far_in, near_in = scratch[5 * n + 2 : 5 * n + 4]
        for k in range(depth):
            arrive(far_in, sems[per * n + 2 :], k)
            total = add(n, 2 * depth + k, [(far_in, (k,))])
            push(remote(total, near_in.at[k], sems[per * n + 4 :], k, at.near()))
    if shared:
        mine, far_in, near_in, local = refs[-10:-6]
        pltpu.make_async_copy(part.at[number(columns[3])], mine.at[1], local.at[1]).wait()
        arrive(far_in, far_sems, 1)
        arrive(near_in, near_sems, 0)
        sum_rows(mine, (1,), [(mine, (1,)), (far_in, (1,)), (near_in, (0,))])
        rows = arrived.shape[0] // (2 * depth)

        def piece(ref, rank):
            return ref.at[pl.ds(pl.multiple_of(rank * rows, rows), rows)]

        own_rank = at.z * 2 + at.c
        for slot, there in enumerate(peers):
            source = piece(mine.at[1], there[2] * 2 + there[3])
            push(remote(source, piece(arrived, own_rank), out_sems, slot, there))
        kept = pltpu.make_async_copy(
            piece(mine.at[1], own_rank), piece(arrived, own_rank), local.at[2]
        )
        kept.start()
    for n in range(count):
        far_in, near_in, z_in = scratch[5 * n + 2 : 5 * n + 5]
        for k in range(depth):
            arrive(far_in, sems[per * n + 2 :], depth + k)
            arrive(near_in, sems[per * n + 4 :], k)
            total = add(n, 3 * depth + k, [(far_in, (depth + k,)), (near_in, (k,))])
            if k < depth - 1:
                push(remote(total, z_in.at[k], sems[per * n + 6 :], k, at.chip(1 + k)))
    for n in range(count):
        z_in = scratch[5 * n + 4]
        for k in range(depth - 1):
            arrive(z_in, sems[per * n + 6 :], k)
        sum_rows(totals[n], (), [(totals[n], ())] + [(z_in, (k,)) for k in range(depth - 1)])
    if shared:
        for slot, (k, core) in enumerate(ranks):
            target = piece(arrived, at.along(depth - k) * 2 + lax.rem(at.c + core, 2))
            remote(target, target, out_sems, slot, at.core()).wait_recv()
        kept.wait()
    for copy in started:
        copy.wait_send()


def collect(depth, ident, *arrays, shared=None):
    count = len(arrays)
    buffers, sems, shapes = [], [], []
    for a in arrays:
        for slots in (4 * depth, 4 * depth, 2 * depth, depth, depth - 1):
            buffers.append(pltpu.VMEM((slots,) + a.shape[1:], a.dtype))
        sems += pair(4 * depth) + pair(2 * depth) + pair(depth) + pair(depth - 1)
        sems.append(pltpu.SemaphoreType.DMA((4 * depth,)))
        shapes.append(jax.ShapeDtypeStruct(a.shape[1:], high_type))
    specs = [pl.BlockSpec(memory_space=pltpu.VMEM)] * count
    if shared is not None:
        block = shared.shape[1:]
        arrays += (shared,)
        specs += in_hbm(1)
        shapes.append(jax.ShapeDtypeStruct(block, shared.dtype))
        sems += [pltpu.VMEM((slots,) + block, shared.dtype) for slots in (2, 2, 1)]
        sems.append(pltpu.SemaphoreType.DMA((3,)))
        sems += pair(2) + pair(1) + pair(2 * depth - 1)
    return pl.pallas_call(
        functools.partial(collect_kernel, depth, count, shared is not None),
        out_shape=shapes,
        in_specs=in_hbm(len(arrays)),
        out_specs=specs,
        scratch_shapes=buffers + sems,
        compiler_params=pltpu.CompilerParams(
            collective_id=ident, has_side_effects=True, vmem_limit_bytes=56 << 20
        ),
        cost_estimate=pl.CostEstimate(
            flops=0,
            bytes_accessed=sum(16 * a.size * a.dtype.itemsize for a in arrays),
            transcendentals=0,
        ),
    )(*arrays)


def gather_kernel(depth, x_ref, w_ref, s_ref, x_out, w_out, s_out, *sems):
    at = Place(depth)
    ranks = [(k, core) for k in range(depth) for core in range(2) if k or core]

    def peer(k, core):
        return at.chip(k, lax.rem(at.c + core, 2))

    meet([peer(k, core) for k, core in ranks] + [at.near(), at.far()])
    started, local = [], []

    def push(copy):
        copy.start()
        started.append(copy)

    def rank(z, c):
        return z * 2 + c

    own, column = rank(at.z, at.c), at.y * 2 + at.x
    x_z, x_core, w_sems, s_sems, w_side, s_side = (sems[2 * i : 2 * i + 2] for i in range(6))
    for slot, (k, core) in enumerate(ranks):
        there = peer(k, core)
        push(remote(s_ref, s_out.at[column, own], s_sems, slot, there))
        push(
            remote(
                w_ref.at[rank(there[2], there[3])], w_out.at[column, own], w_sems, slot, there
            )
        )
    for k in range(1, depth):
        push(remote(x_ref, x_out.at[own], x_z, k - 1, at.chip(k)))
    push(remote(x_ref, x_out.at[own], x_core, 0, at.core()))
    for i, (source, target) in enumerate(
        ((x_ref, x_out.at[own]), (w_ref.at[own], w_out.at[column, own]), (s_ref, s_out.at[column, own]))
    ):
        copy = pltpu.make_async_copy(source, target, sems[12].at[i])
        copy.start()
        local.append(copy)

    def arrive(target, pair_of, slot):
        remote(target, target, pair_of, slot, at.core()).wait_recv()

    for slot, (k, core) in enumerate(ranks):
        source = rank(at.along(depth - k), lax.rem(at.c + core, 2))
        arrive(s_out.at[column, source], s_sems, slot)
        arrive(w_out.at[column, source], w_sems, slot)
    for copy in local:
        copy.wait()
    near_y, near_x = at.near_of(at.c)
    far_y, far_x = at.far_of(at.c)
    beside, across = near_y * 2 + near_x, far_y * 2 + far_x
    for target, pair_of in ((s_out, s_side), (w_out, w_side)):
        push(remote(target.at[column], target.at[column], pair_of, 0, at.near()))
        push(remote(target.at[column], target.at[column], pair_of, 1, at.far()))
    for k in range(1, depth):
        source = rank(at.along(depth - k), at.c)
        arrive(x_out.at[source], x_z, k - 1)
        push(remote(x_out.at[source], x_out.at[source], x_core, k, at.core()))
    for target, pair_of in ((s_out, s_side), (w_out, w_side)):
        arrive(target.at[beside], pair_of, 0)
        push(remote(target.at[beside], target.at[beside], pair_of, 2, at.far()))
    for k in range(depth):
        arrive(x_out.at[rank(at.along(depth - k), 1 - at.c)], x_core, k)
    for target, pair_of in ((s_out, s_side), (w_out, w_side)):
        arrive(target.at[across], pair_of, 1)
        arrive(target.at[3 - column], pair_of, 2)
    for copy in started:
        copy.wait_send()


def gather(depth, ident, x, w, s):
    ranks = 2 * depth
    sems = pair(depth - 1) + pair(depth) + pair(ranks - 1) * 2 + pair(3) * 2
    sems.append(pltpu.SemaphoreType.DMA((3,)))
    return pl.pallas_call(
        functools.partial(gather_kernel, depth),
        out_shape=[
            jax.ShapeDtypeStruct((ranks,) + x.shape, x.dtype),
            jax.ShapeDtypeStruct((4,) + w.shape, w.dtype),
            jax.ShapeDtypeStruct((4, ranks) + s.shape, s.dtype),
        ],
        in_specs=in_hbm(3),
        out_specs=in_hbm(3),
        scratch_shapes=sems,
        compiler_params=pltpu.CompilerParams(
            collective_id=ident, has_side_effects=True, vmem_limit_bytes=16 << 20
        ),
        cost_estimate=pl.CostEstimate(
            flops=0, bytes_accessed=64 * depth * x.size, transcendentals=0
        ),
    )(x, w, s)


def exchange_kernel(depth, same, x_ref, out_ref, send_sems, recv_sems, local_sem):
    at = Place(depth)
    ranks = [(k, core) for k in range(depth) for core in range(2) if k or core]
    peers = [at.chip(k, lax.rem(at.c + core, 2)) for k, core in ranks]
    meet(peers)
    own = at.z * 2 + at.c
    copies = []
    for slot, there in enumerate(peers):
        source = x_ref if same else x_ref.at[there[2] * 2 + there[3]]
        copy = remote(source, out_ref.at[own], (send_sems, recv_sems), slot, there)
        copy.start()
        copies.append(copy)
    local = pltpu.make_async_copy(x_ref if same else x_ref.at[own], out_ref.at[own], local_sem)
    local.start()
    for slot, (k, core) in enumerate(ranks):
        target = out_ref.at[at.along(depth - k) * 2 + lax.rem(at.c + core, 2)]
        remote(target, target, (send_sems, recv_sems), slot, at.core()).wait_recv()
    for copy in copies:
        copy.wait_send()
    local.wait()


def exchange(depth, ident, x, same=False):
    ranks = 2 * depth
    return pl.pallas_call(
        functools.partial(exchange_kernel, depth, same),
        out_shape=jax.ShapeDtypeStruct((ranks,) + x.shape if same else x.shape, x.dtype),
        in_specs=in_hbm(1),
        out_specs=in_hbm(1)[0],
        scratch_shapes=pair(ranks - 1) + [pltpu.SemaphoreType.DMA],
        compiler_params=pltpu.CompilerParams(
            collective_id=ident, has_side_effects=True, vmem_limit_bytes=16 << 20
        ),
        cost_estimate=pl.CostEstimate(
            flops=0, bytes_accessed=16 * x.size * x.dtype.itemsize, transcendentals=0
        ),
    )(x)


def column_kernel(depth, part, total, mine, crossed, z_in, z_out, *sems):
    at = Place(depth)
    meet([at.core()] + [at.chip(k) for k in range(1, depth)])
    started = []

    def push(copy):
        copy.start()
        started.append(copy)

    def local(k):
        return pltpu.make_async_copy(
            part.at[at.along(1 + k) * 2 + at.c], mine.at[k], sems[4].at[k]
        )

    def arrive(buffer, pair_of, slot):
        remote(buffer.at[slot], buffer.at[slot], pair_of, slot, at.core()).wait_recv()

    for k in range(depth):
        push(
            remote(
                part.at[at.along(1 + k) * 2 + 1 - at.c], crossed.at[k], sems[0:2], k, at.core()
            )
        )
        local(k).start()
    for k in range(depth):
        local(k).wait()
        arrive(crossed, sems[0:2], k)
        terms = [(mine, (k,)), (crossed, (k,))]
        if k < depth - 1:
            sum_rows(z_out, (k,), terms)
            push(remote(z_out.at[k], z_in.at[k], sems[2:4], k, at.chip(1 + k)))
        else:
            sum_rows(total, (), terms)
    for k in range(depth - 1):
        arrive(z_in, sems[2:4], k)
    sum_rows(total, (), [(total, ())] + [(z_in, (k,)) for k in range(depth - 1)])
    for copy in started:
        copy.wait_send()


def collect_column(depth, ident, part):
    block = part.shape[1:]
    return pl.pallas_call(
        functools.partial(column_kernel, depth),
        out_shape=jax.ShapeDtypeStruct(block, high_type),
        in_specs=in_hbm(1),
        out_specs=pl.BlockSpec(memory_space=pltpu.VMEM),
        scratch_shapes=[pltpu.VMEM((depth,) + block, part.dtype)] * 2
        + [pltpu.VMEM((depth - 1,) + block, part.dtype)] * 2
        + pair(depth)
        + pair(depth - 1)
        + [pltpu.SemaphoreType.DMA((depth,))],
        compiler_params=pltpu.CompilerParams(
            collective_id=ident, has_side_effects=True, vmem_limit_bytes=32 << 20
        ),
        cost_estimate=pl.CostEstimate(
            flops=0, bytes_accessed=16 * part.size * part.dtype.itemsize, transcendentals=0
        ),
    )(part)


def lines_in(values):
    rows, local, two, hidden = values.shape
    values = values.reshape(rows, local, two, hidden // 128, 128)
    return values.transpose(0, 1, 3, 2, 4).reshape(-1, 128)


def lines_down(values):
    rows, local, hidden = values.shape
    return values.reshape(rows, local, hidden // 128, 128).transpose(0, 2, 1, 3).reshape(-1, 128)


def places(ranks, local):
    for rank in range(ranks):
        for x in range(local):
            for k in range(2):
                yield rank, (k * local + x) * 128, (x * ranks + rank) * 2 + k, None
            yield rank, x * 128, None, rank * local + x


def pack_kernel(ranks, local, step, in_ref, down_ref, in_out, down_out):
    for rank, column, of_in, of_down in places(ranks, local):
        if of_down is None:
            value = in_ref[pl.ds(of_in, step, stride=2 * local * ranks), :]
            in_out[rank, :, column : column + 128] = value.astype(low_type)
        else:
            value = down_ref[pl.ds(of_down, step, stride=local * ranks), :]
            down_out[rank, :, column : column + 128] = value.astype(low_type)


def pack(ranks, expert_in, expert_down):
    rows, local = expert_in.shape[:2]
    step = 32
    lines = step * local * ranks
    span = local * 128
    return pl.pallas_call(
        functools.partial(pack_kernel, ranks, local, step),
        grid=(rows // step,),
        in_specs=[
            pl.BlockSpec((2 * lines, 128), lambda i: (i, 0)),
            pl.BlockSpec((lines, 128), lambda i: (i, 0)),
        ],
        out_specs=[
            pl.BlockSpec((ranks, step, 2 * span), lambda i: (0, i, 0)),
            pl.BlockSpec((ranks, step, span), lambda i: (0, i, 0)),
        ],
        out_shape=[
            jax.ShapeDtypeStruct((ranks, rows, 2 * span), low_type),
            jax.ShapeDtypeStruct((ranks, rows, span), low_type),
        ],
        compiler_params=pltpu.CompilerParams(vmem_limit_bytes=32 << 20),
    )(lines_in(expert_in), lines_down(expert_down))


def unpack_kernel(ranks, local, step, in_ref, out_ref):
    for rank, column, of_in, of_down in places(ranks, local):
        down = in_ref.shape[2] == local * 128
        if down == (of_in is None):
            first = of_down if down else of_in
            stride = (1 if down else 2) * local * ranks
            value = in_ref[rank, :, column : column + 128].astype(high_type)
            out_ref[pl.ds(first, step, stride=stride), :] = value


def unpack(local, sliced):
    ranks, rows, span = sliced.shape
    step = 32
    lines = step * ranks * span // 128
    return pl.pallas_call(
        functools.partial(unpack_kernel, ranks, local, step),
        grid=(rows // step,),
        in_specs=[pl.BlockSpec((ranks, step, span), lambda i: (0, i, 0))],
        out_specs=pl.BlockSpec((lines, 128), lambda i: (i, 0)),
        out_shape=jax.ShapeDtypeStruct((rows * ranks * span // 128, 128), high_type),
        compiler_params=pltpu.CompilerParams(vmem_limit_bytes=32 << 20),
    )(sliced)


def grid_shards(
    residual_in,
    cotangent,
    lengths,
    routes,
    attn_qkv,
    attn_out,
    gains,
    router,
    expert_in,
    expert_down,
):
    rows, width = residual_in.shape
    depth = lax.axis_size("dz")
    ranks = 2 * depth
    columns = 4
    seq_rows = rows * ranks
    local_experts = expert_in.shape[1]
    experts = local_experts * columns
    hidden_width = expert_in.shape[3]
    part = hidden_width // ranks
    span = local_experts * part
    chunk_rows = expert_in.shape[0]
    weight_rows = attn_qkv.shape[1]
    score_scale = HD ** (-0.5)
    y, x, z, c = (lax.axis_index(name) for name in GRID)
    column = y * 2 + x
    own_heads = HEADS // ranks
    own_width = own_heads * HD

    def sum_column(ident, pairs):
        flat = exchange(depth, ident, pairs.reshape(-1, 128), same=True)
        return jnp.sum(flat, axis=0).reshape(pairs.shape)

    def by_rank(values):
        lead = values.shape[:-1]
        shaped = values.reshape(lead + (2, own_heads, depth, HD))
        n = len(lead)
        return shaped.transpose((n + 2, n) + tuple(range(n)) + (n + 1, n + 3)).reshape(
            (ranks,) + lead + (own_width,)
        )

    def by_head(values):
        lead = values.shape[1:-1]
        shaped = values.reshape((depth, 2) + lead + (own_heads, HD))
        n = len(lead)
        return shaped.transpose(tuple(range(2, n + 2)) + (1, n + 2, 0, n + 3)).reshape(
            lead + (width,)
        )

    small = jnp.concatenate([gains.T, router], axis=1).astype(low_type)
    small = jnp.pad(small, ((0, 0), (0, 128 - small.shape[1])))
    packed = attn_qkv.astype(low_type).transpose(1, 0, 2)
    packed = by_rank(packed).reshape(ranks, weight_rows, 3 * own_width)
    seq_input, qkv_weight, small = gather(depth, 0, residual_in, packed, small)
    qkv_weight = qkv_weight.reshape(width, 3 * own_width)
    small = small.reshape(width, 128)
    gain_rows = small[:, :4].T.astype(high_type)
    router_weight = small[:, 4 : 4 + experts]
    gain_own = [
        lax.dynamic_index_in_dim(by_rank(gain_rows[i]), z * 2 + c, 0, keepdims=False)
        for i in (1, 2)
    ]
    normed_in = seq_input.reshape(seq_rows, width).astype(high_type)
    normed_in = (normed_in * rms_scale(normed_in) * gain_rows[0]).astype(low_type)
    out_weight = lax.all_gather(attn_out.astype(low_type), GRID, axis=0, tiled=True)

    sliced_in, sliced_down = pack(ranks, expert_in, expert_down)

    raw = dot(normed_in, qkv_weight)
    query_raw, key_raw = raw[:, :own_width], raw[:, own_width : 2 * own_width]
    value_rows = raw[:, 2 * own_width :].astype(low_type)
    squares = jnp.stack(
        [jnp.sum(query_raw * query_raw, axis=1), jnp.sum(key_raw * key_raw, axis=1)]
    )
    scales = lax.rsqrt(sum_column(1, squares) / width + epsilon)
    query_scale, key_scale = scales[0][:, None], scales[1][:, None]
    positions = jnp.arange(seq_rows, dtype=jnp.int32)
    length_now = lengths[0]
    key_live = positions < length_now
    cosine, sine_table = angle_tables(positions)
    query_normed = query_raw * query_scale
    key_normed = key_raw * key_scale
    query_rot = rotate(query_normed * gain_own[0], cosine, sine_table).astype(low_type)
    key_rot = rotate(key_normed * gain_own[1], cosine, sine_table).astype(low_type)
    query_heads = query_rot.reshape(seq_rows, own_heads, HD)
    key_heads = key_rot.reshape(seq_rows, own_heads, HD)
    value_heads = value_rows.reshape(seq_rows, own_heads, HD)

    def per_head(spec, left, right):
        return jnp.einsum(spec, left, right, preferred_element_type=high_type)

    scores = per_head("qhd,khd->hqk", query_heads, key_heads) * score_scale
    scores = jnp.where(key_live[None, None, :], scores, masked_score)
    probs = jax.nn.softmax(scores, axis=-1)
    probs_low = probs.astype(low_type)
    attended = per_head("hqk,khd->qhd", probs_low, value_heads).astype(low_type)
    attended = exchange(depth, 2, attended.reshape(ranks, rows, own_width))
    attended = by_head(attended)

    own_positions = (z * 2 + c) * rows + jnp.arange(rows, dtype=jnp.int32)
    live_rows = (own_positions < length_now).astype(high_type)[:, None]
    input_rows = residual_in.astype(high_type)
    middle = input_rows + live_rows * dot(attended, out_weight)
    scale_mid = rms_scale(middle)
    normed_mid_f = middle * scale_mid
    normed_mid = (normed_mid_f * gain_rows[3]).astype(low_type)

    logits = dot(normed_mid, router_weight)
    named = jnp.any(
        routes[:, :, None] == jnp.arange(experts, dtype=jnp.int32)[None, None, :], axis=1
    )
    top = jnp.max(jnp.where(named, logits, -jnp.inf), axis=1, keepdims=True)
    weight_of = jnp.where(named, jnp.exp(jnp.where(named, logits - top, 0.0)), 0.0)
    gates = weight_of / jnp.sum(weight_of, axis=1, keepdims=True)

    grad_rows = cotangent.astype(high_type)
    grad_comb = live_rows * grad_rows
    own_grads, normed_mid = lax.optimization_barrier((grad_comb.astype(low_type), normed_mid))
    grads = lax.all_gather(own_grads, GRID, axis=0, tiled=True)
    tokens, gates_all, weights_in, weights_down = spread(
        depth, 3, (normed_mid, gates.T), (sliced_in, sliced_down)
    )
    weights_in, weights_down = weights_in.reshape(width, -1), weights_down.reshape(width, -1)
    tokens = tokens.reshape(-1, width)
    gates_all = lax.dynamic_slice_in_dim(gates_all, column * local_experts, local_experts, 1)
    gates_all = gates_all.transpose(0, 2, 1).reshape(-1, local_experts)
    wide = jnp.repeat(gates_all, part, axis=1)
    both_parts = dot(tokens, weights_in)
    gate_part, up_part = both_parts[:, :span], both_parts[:, span:]
    down_grad = dot(grads, weights_down)
    sigma = jax.nn.sigmoid(gate_part)
    hidden = (gate_part * sigma * up_part).astype(low_type).astype(high_type)
    gate_sums = jnp.sum((hidden * down_grad).reshape(-1, rows, local_experts, part), axis=3)
    weighted = (wide * hidden).astype(low_type)
    grad_hidden = wide * down_grad
    grad_gate = grad_hidden * up_part * sigma * (1.0 + gate_part * (1.0 - sigma))
    grad_up = grad_hidden * gate_part * sigma
    grad_both = jnp.concatenate([grad_gate, grad_up], axis=1).astype(low_type)
    grad_in = t_dot(tokens, grad_both).astype(low_type)
    grad_both, grad_in = lax.optimization_barrier((grad_both, grad_in))
    back = dot_t(grad_both, weights_in).astype(low_type)
    placed = jnp.zeros((4 * ranks, experts, rows), high_type)
    placed = lax.dynamic_update_slice(
        placed, gate_sums.transpose(0, 2, 1), (0, column * local_experts, 0)
    )
    mixed = dot_t(weighted, weights_down).astype(low_type)
    back, mixed = lax.optimization_barrier((back, mixed))
    grad_mid_norm, grad_gates = collect(depth, 4, back.reshape(-1, rows, width), placed)
    sliced = lax.all_to_all(grad_in.reshape(ranks, chunk_rows, 2 * span), SEQ, 0, 0, tiled=True)
    grad_expert_in = unpack(local_experts, sliced).reshape(
        chunk_rows, local_experts, ranks, 2, part
    )
    grad_expert_in = grad_expert_in.transpose(0, 1, 3, 2, 4).reshape(expert_in.shape)

    grad_gates = grad_gates.T
    grad_chosen = gates * (grad_gates - jnp.sum(gates * grad_gates, axis=1, keepdims=True))
    grad_logits = grad_chosen.astype(low_type)
    grad_mid_norm = grad_mid_norm + dot_t(grad_logits, router_weight)
    grad_router = t_dot(normed_mid, grad_logits)

    grad_mid_rows, grad_gain_mid = rms_back(grad_mid_norm, normed_mid_f, scale_mid, gain_rows[3])
    grad_middle = grad_rows + grad_mid_rows
    grad_branch = (live_rows * grad_middle).astype(low_type)

    grad_attended = by_rank(dot_t(grad_branch, out_weight).astype(low_type))
    grad_attended = exchange(depth, 6, grad_attended)
    grad_heads = grad_attended.reshape(seq_rows, own_heads, HD)
    grad_probs = per_head("qhd,khd->hqk", grad_heads, value_heads)
    inner_rows = jnp.sum(probs * grad_probs, axis=-1, keepdims=True)
    grad_scores = (probs * (grad_probs - inner_rows)).astype(low_type)
    grad_query = per_head("hqk,khd->qhd", grad_scores, key_heads) * score_scale
    grad_key = per_head("hqk,qhd->khd", grad_scores, query_heads) * score_scale
    grad_value = per_head("hqk,qhd->khd", probs_low, grad_heads).astype(low_type)
    grad_query = rotate(grad_query.reshape(seq_rows, own_width), cosine, -sine_table)
    grad_key = rotate(grad_key.reshape(seq_rows, own_width), cosine, -sine_table)
    query_inner = grad_query * gain_own[0]
    key_inner = grad_key * gain_own[1]
    inner = jnp.stack(
        [
            jnp.sum(query_inner * query_normed, axis=1),
            jnp.sum(key_inner * key_normed, axis=1),
        ]
    )
    inner = sum_column(7, inner) / width
    query_back = query_scale * (query_inner - query_normed * inner[0][:, None])
    key_back = key_scale * (key_inner - key_normed * inner[1][:, None])
    grad_raw = jnp.concatenate(
        [
            query_back.astype(low_type),
            key_back.astype(low_type),
            grad_value.reshape(seq_rows, own_width),
        ],
        axis=1,
    )

    share = dot_t(grad_raw, qkv_weight).astype(low_type).reshape(ranks, rows, width)
    grad_norm_in = collect_column(depth, 8, share)
    grad_norm_in, grads, attended = lax.optimization_barrier((grad_norm_in, grads, attended))
    grad_down = t_dot(grads, weighted).astype(low_type)
    sliced = lax.all_to_all(grad_down.reshape(ranks, chunk_rows, span), SEQ, 0, 0, tiled=True)
    grad_expert_down = unpack(local_experts, sliced).reshape(
        chunk_rows, ranks, local_experts, part
    )
    grad_expert_down = grad_expert_down.transpose(0, 2, 1, 3).reshape(expert_down.shape)
    scale_in = rms_scale(input_rows)
    grad_in_rows, grad_gain_in = rms_back(
        grad_norm_in, input_rows * scale_in, scale_in, gain_rows[0]
    )
    grad_input = grad_middle + grad_in_rows

    def at_heads(values):
        whole = jnp.zeros((2, own_heads, depth, HD), high_type)
        values = values.reshape(1, own_heads, 1, HD)
        return lax.dynamic_update_slice(whole, values, (c, 0, z, 0)).reshape(width)

    grad_small = jnp.concatenate(
        [
            jnp.stack(
                [
                    grad_gain_in,
                    at_heads(jnp.sum(grad_query * query_normed, axis=0)),
                    at_heads(jnp.sum(grad_key * key_normed, axis=0)),
                    grad_gain_mid,
                ]
            ).T,
            grad_router,
        ],
        axis=1,
    )
    grad_small = jnp.pad(grad_small, ((0, 0), (0, 128 - grad_small.shape[1])))
    grad_out = t_dot(attended, grad_branch).astype(low_type)
    grad_qkv = t_dot(normed_in, grad_raw).astype(low_type)
    combined, grad_out, grad_small, grad_qkv = collect(
        depth,
        5,
        mixed.reshape(-1, rows, width),
        grad_out.reshape(-1, weight_rows, width),
        grad_small.reshape(-1, weight_rows, 128),
        shared=grad_qkv.reshape(columns, -1, 3 * own_width),
    )
    output = middle + live_rows * combined
    grad_qkv = by_head(grad_qkv.reshape(ranks, weight_rows, 3, own_width))
    grad_qkv = grad_qkv.transpose(1, 0, 2).astype(high_type)
    return (
        output,
        grad_input,
        grad_qkv,
        grad_out,
        grad_small[:, :4].T,
        grad_small[:, 4 : 4 + experts],
        grad_expert_in,
        grad_expert_down,
    )


def slot_index(route_rows, experts, capacity):
    flat_routes = route_rows.reshape(-1)
    onehot = (flat_routes[:, None] == jnp.arange(experts, dtype=jnp.int32)[None, :]).astype(
        jnp.int32
    )
    rows = jnp.arange(flat_routes.shape[0], dtype=jnp.int32)
    earlier = (rows[None, :] < rows[:, None]).astype(jnp.bfloat16)
    before = jnp.dot(
        earlier, onehot.astype(jnp.bfloat16), preferred_element_type=jnp.float32
    ).astype(jnp.int32)
    rank_rows = jnp.sum(before * onehot, axis=1)
    return flat_routes * capacity + rank_rows


def head_scores(query_rot, key_all, key_live):
    row_count = query_rot.shape[0]
    query_heads = query_rot.reshape(row_count, HEADS, HD)
    key_heads = key_all.reshape(key_all.shape[0], HEADS, HD)
    raw_scores = jnp.einsum(
        "qhd,khd->hqk", query_heads, key_heads, preferred_element_type=jnp.float32
    ) * HD ** (-0.5)
    return jnp.where(key_live[None, None, :], raw_scores, masked_score)


def to_owners(buffer):
    return lax.all_to_all(buffer, "expert", split_axis=0, concat_axis=0, tiled=True)


def from_owners(buffer):
    return lax.all_to_all(buffer, "expert", split_axis=0, concat_axis=0, tiled=True)


def shards(
    residual_in,
    cotangent,
    lengths,
    routes,
    attn_qkv,
    attn_out,
    gains,
    router,
    expert_in,
    expert_down,
):
    tok_rows, model_width = residual_in.shape
    top_count = routes.shape[1]
    owners = lax.axis_size("expert")
    local_experts = expert_in.shape[1]
    experts = local_experts * owners
    capacity = tok_rows * top_count * 2 // experts
    local_slots = local_experts * capacity
    seq_rows = tok_rows * lax.axis_size("dp")
    score_scale = HD ** (-0.5)
    qkv_weights, out_weight, gain_low, router_weight = (
        lax.all_gather(attn_qkv.astype(low_type), ("expert", "dp"), axis=1, tiled=True),
        lax.all_gather(attn_out.astype(low_type), ("expert", "dp"), axis=0, tiled=True),
        lax.all_gather(gains.astype(low_type), ("expert", "dp"), axis=1, tiled=True),
        lax.all_gather(router.astype(low_type), ("expert", "dp"), axis=0, tiled=True),
    )
    gain_rows = gain_low.astype(high_type)
    input_rows = residual_in.astype(high_type)
    scale_in = rms_scale(input_rows)
    normed_in_f = input_rows * scale_in
    normed_in = (normed_in_f * gain_rows[0]).astype(low_type)
    query_raw = jnp.dot(normed_in, qkv_weights[0], preferred_element_type=high_type)
    key_raw = jnp.dot(normed_in, qkv_weights[1], preferred_element_type=high_type)
    value_rows = jnp.dot(normed_in, qkv_weights[2], preferred_element_type=high_type).astype(
        low_type
    )
    positions = lax.axis_index("dp") * tok_rows + jnp.arange(tok_rows, dtype=jnp.int32)
    length_now = lengths[0]
    live_rows = (positions < length_now).astype(high_type)[:, None]
    key_live = jnp.arange(seq_rows, dtype=jnp.int32) < length_now
    cosine, sine_table = angle_tables(positions)
    query_scale = rms_scale(query_raw)
    query_normed = query_raw * query_scale
    query_rot = rotate(query_normed * gain_rows[1], cosine, sine_table).astype(low_type)
    key_scale = rms_scale(key_raw)
    key_normed = key_raw * key_scale
    key_rot = rotate(key_normed * gain_rows[2], cosine, sine_table).astype(low_type)
    key_all = lax.all_gather(key_rot, "dp", axis=0, tiled=True)
    value_all = lax.all_gather(value_rows, "dp", axis=0, tiled=True)
    scores = head_scores(query_rot, key_all, key_live)
    top_score = jnp.max(scores, axis=-1, keepdims=True)
    exp_scores = jnp.exp(scores - top_score)
    row_total = jnp.sum(exp_scores, axis=-1, keepdims=True)
    weights_low = (exp_scores / row_total).astype(low_type)
    log_total = top_score + jnp.log(row_total)
    value_heads = value_all.reshape(seq_rows, HEADS, HD)
    attended = jnp.einsum(
        "hqk,khd->qhd", weights_low, value_heads, preferred_element_type=high_type
    )
    attended = attended.reshape(tok_rows, model_width).astype(low_type)
    branch = jnp.dot(attended, out_weight, preferred_element_type=high_type)
    middle = input_rows + live_rows * branch
    scale_mid = rms_scale(middle)
    normed_mid_f = middle * scale_mid
    normed_mid = (normed_mid_f * gain_rows[3]).astype(low_type)
    logits = jnp.dot(normed_mid, router_weight, preferred_element_type=high_type)
    selector = (routes[:, :, None] == jnp.arange(experts, dtype=jnp.int32)[None, None, :]).astype(
        high_type
    )
    chosen = jnp.einsum("te,tje->tj", logits, selector)
    gate_weights = jax.nn.softmax(chosen, axis=-1)
    slot_rows = slot_index(routes, experts, capacity)
    token_of = jnp.arange(slot_rows.shape[0], dtype=jnp.int32) // top_count
    send_rows = (
        jnp.zeros((experts * capacity, model_width), low_type)
        .at[slot_rows]
        .set(normed_mid[token_of])
    )
    rows_recv = lax.all_to_all(
        send_rows.reshape(owners, local_slots, model_width),
        "expert",
        split_axis=0,
        concat_axis=0,
        tiled=True,
    )
    rows_recv = rows_recv.reshape(owners, local_experts, capacity, model_width)
    weights_in, weights_down = (
        lax.all_gather(expert_in.astype(low_type), "dp", axis=0, tiled=True),
        lax.all_gather(expert_down.astype(low_type), "dp", axis=0, tiled=True),
    )
    both_parts = jnp.einsum(
        "sxmd,dxkf->sxmkf", rows_recv, weights_in, preferred_element_type=high_type
    )
    gate_part = both_parts[:, :, :, 0, :]
    up_part = both_parts[:, :, :, 1, :]
    hidden = (jax.nn.silu(gate_part) * up_part).astype(low_type)
    produced = jnp.einsum(
        "sxmf,dxf->sxmd", hidden, weights_down, preferred_element_type=high_type
    ).astype(low_type)
    returned = from_owners(produced.reshape(owners, local_slots, model_width))
    returned = returned.reshape(experts * capacity, model_width)
    picked = returned[slot_rows].reshape(tok_rows, top_count, model_width).astype(high_type)
    combined = jnp.sum(gate_weights[:, :, None] * picked, axis=1)
    output = middle + live_rows * combined
    grad_rows = cotangent.astype(high_type)
    grad_comb = live_rows * grad_rows
    grad_gates = jnp.einsum("tjd,td->tj", picked, grad_comb)
    grad_chosen = gate_weights * (
        grad_gates - jnp.sum(gate_weights * grad_gates, axis=-1, keepdims=True)
    )
    grad_logits = jnp.einsum("tj,tje->te", grad_chosen, selector).astype(low_type)
    grad_send = (
        (gate_weights[:, :, None] * grad_comb[:, None, :]).astype(low_type).reshape(-1, model_width)
    )
    grad_buffer = (
        jnp.zeros((experts * capacity, model_width), low_type).at[slot_rows].set(grad_send)
    )
    grad_recv = to_owners(grad_buffer.reshape(owners, local_slots, model_width))
    grad_recv = grad_recv.reshape(owners, local_experts, capacity, model_width)
    grad_hidden = jnp.einsum(
        "sxmd,dxf->sxmf", grad_recv, weights_down, preferred_element_type=high_type
    )
    sigma_gate = jax.nn.sigmoid(gate_part)
    grad_gate = grad_hidden * up_part * sigma_gate * (1.0 + gate_part * (1.0 - sigma_gate))
    grad_up = grad_hidden * gate_part * sigma_gate
    grad_both = jnp.stack([grad_gate, grad_up], axis=3).astype(low_type)
    grad_rows_out = jnp.einsum(
        "sxmkf,dxkf->sxmd", grad_both, weights_in, preferred_element_type=high_type
    ).astype(low_type)
    grad_back = from_owners(grad_rows_out.reshape(owners, local_slots, model_width))
    grad_back = grad_back.reshape(experts * capacity, model_width)
    grad_mid_norm = jnp.sum(
        grad_back[slot_rows].reshape(tok_rows, top_count, model_width).astype(high_type), axis=1
    )
    grad_mid_norm = grad_mid_norm + jnp.dot(
        grad_logits, router_weight.T, preferred_element_type=high_type
    )
    grad_router = jnp.dot(normed_mid.T, grad_logits, preferred_element_type=high_type)
    row_piece = rows_recv
    grad_expert_in = lax.psum_scatter(
        jnp.einsum(
            "sxmd,sxmkf->dxkf", row_piece, grad_both, preferred_element_type=high_type
        ).astype(jnp.bfloat16),
        "dp",
        scatter_dimension=0,
        tiled=True,
    ).astype(jnp.float32)
    row_piece = grad_recv
    grad_expert_down = lax.psum_scatter(
        jnp.einsum("sxmd,sxmf->dxf", row_piece, hidden, preferred_element_type=high_type).astype(
            jnp.bfloat16
        ),
        "dp",
        scatter_dimension=0,
        tiled=True,
    ).astype(jnp.float32)
    grad_mid_rows, grad_gain_mid = rms_back(grad_mid_norm, normed_mid_f, scale_mid, gain_rows[3])
    grad_middle = grad_rows + grad_mid_rows
    grad_branch = (live_rows * grad_middle).astype(low_type)
    grad_out_weight = jnp.dot(attended.T, grad_branch, preferred_element_type=high_type)
    grad_attended = jnp.dot(grad_branch, out_weight.T, preferred_element_type=high_type).astype(
        low_type
    )
    scores = head_scores(query_rot, key_all, key_live)
    probs_full = jnp.exp(scores - log_total)
    grad_heads = grad_attended.reshape(tok_rows, HEADS, HD)
    value_heads = value_all.reshape(seq_rows, HEADS, HD)
    key_heads = key_all.reshape(seq_rows, HEADS, HD)
    query_heads = query_rot.reshape(tok_rows, HEADS, HD)
    grad_probs = jnp.einsum(
        "qhd,khd->hqk", grad_heads, value_heads, preferred_element_type=high_type
    )
    inner_rows = jnp.sum(probs_full * grad_probs, axis=-1, keepdims=True)
    grad_scores = (probs_full * (grad_probs - inner_rows)).astype(low_type)
    grad_query = (
        jnp.einsum(
            "hqk,khd->qhd", grad_scores, key_heads, preferred_element_type=high_type
        ).reshape(tok_rows, model_width)
        * score_scale
    )
    grad_key_part = (
        jnp.einsum(
            "hqk,qhd->khd", grad_scores, query_heads, preferred_element_type=high_type
        ).reshape(seq_rows, model_width)
        * score_scale
    )
    grad_value_part = jnp.einsum(
        "hqk,qhd->khd", probs_full.astype(low_type), grad_heads, preferred_element_type=high_type
    ).reshape(seq_rows, model_width)
    grad_key_sum, grad_value_sum = (
        lax.psum_scatter(
            grad_key_part.astype(jnp.bfloat16), "dp", scatter_dimension=0, tiled=True
        ).astype(jnp.float32),
        lax.psum_scatter(
            grad_value_part.astype(jnp.bfloat16), "dp", scatter_dimension=0, tiled=True
        ).astype(jnp.float32),
    )
    grad_value = grad_value_sum.astype(low_type)
    grad_key_raw, grad_key_gain = rms_back(
        rotate(grad_key_sum, cosine, -sine_table), key_normed, key_scale, gain_rows[2]
    )
    grad_query_raw, grad_query_gain = rms_back(
        rotate(grad_query, cosine, -sine_table), query_normed, query_scale, gain_rows[1]
    )
    grad_key_raw = grad_key_raw.astype(low_type)
    grad_query_raw = grad_query_raw.astype(low_type)
    grad_norm_in = jnp.dot(grad_query_raw, qkv_weights[0].T, preferred_element_type=high_type)
    grad_norm_in = grad_norm_in + jnp.dot(
        grad_key_raw, qkv_weights[1].T, preferred_element_type=high_type
    )
    grad_norm_in = grad_norm_in + jnp.dot(
        grad_value, qkv_weights[2].T, preferred_element_type=high_type
    )
    grad_qkv_local = jnp.stack(
        [
            jnp.dot(normed_in.T, grad_query_raw, preferred_element_type=high_type),
            jnp.dot(normed_in.T, grad_key_raw, preferred_element_type=high_type),
            jnp.dot(normed_in.T, grad_value, preferred_element_type=high_type),
        ]
    )
    grad_in_rows, grad_gain_in = rms_back(grad_norm_in, normed_in_f, scale_in, gain_rows[0])
    grad_input = grad_middle + grad_in_rows
    grad_gains_local = jnp.stack([grad_gain_in, grad_query_gain, grad_key_gain, grad_gain_mid])
    summed = (
        lax.psum_scatter(grad_qkv_local, ("expert", "dp"), scatter_dimension=1, tiled=True),
        lax.psum_scatter(grad_out_weight, ("expert", "dp"), scatter_dimension=0, tiled=True),
        lax.psum_scatter(grad_gains_local, ("expert", "dp"), scatter_dimension=1, tiled=True),
        lax.psum_scatter(grad_router, ("expert", "dp"), scatter_dimension=0, tiled=True),
    )
    return (
        output,
        grad_input,
        summed[0],
        summed[1],
        summed[2],
        summed[3],
        grad_expert_in,
        grad_expert_down,
    )


def solution(mesh):
    column_count, rank_count = mesh.shape["expert"], mesh.shape["dp"]
    depth = rank_count // 2
    tiled = column_count == 4 and rank_count % 2 == 0 and HEADS == column_count * depth
    if tiled:
        mesh = Mesh(mesh.devices.reshape(2, 2, depth, 2), GRID)
        column, rank, body = ("ey", "ex"), SEQ, grid_shards
    else:
        column, rank, body = ("expert",), ("dp",), shards
    device = column + rank
    placed = (
        P(device, None),
        P(device, None),
        P(column),
        P(device, None),
        P(None, device, None),
        P(device, None),
        P(None, device),
        P(device, None),
        P(rank, column, None, None),
        P(rank, column, None),
    )
    return jax.shard_map(
        body,
        mesh=mesh,
        in_specs=placed,
        out_specs=placed[:1] * 2 + placed[4:],
        check_vma=False,
    )
```

```python
import functools

import jax
import jax.numpy as jnp
from jax import lax
from jax.experimental import pallas as pl
from jax.experimental.pallas import tpu as pltpu
from jax.sharding import Mesh
from jax.sharding import PartitionSpec as P

HEADS = 16
HD = 128

epsilon = 1e-05
rope_base = 10000.0
masked_score = -1000000000.0

low_type = jnp.bfloat16
high_type = jnp.float32


def rms_scale(values):
    return lax.rsqrt(jnp.mean(values * values, axis=-1, keepdims=True) + epsilon)


def angle_tables(positions):
    frequency = rope_base ** (-2.0 * jnp.arange(HD // 2, dtype=jnp.float32) / HD)
    angles = positions.astype(jnp.float32)[:, None] * frequency[None, :]
    return (jnp.cos(angles), jnp.sin(angles))


def rotate(values, cosine, sine_table):
    row_count, width = values.shape
    shaped = values.reshape(row_count, width // HD, 2, HD // 2)
    first_half = shaped[:, :, 0, :]
    second_half = shaped[:, :, 1, :]
    cos_rows = cosine[:, None, :]
    sin_rows = sine_table[:, None, :]
    turned = jnp.stack(
        [
            first_half * cos_rows - second_half * sin_rows,
            second_half * cos_rows + first_half * sin_rows,
        ],
        axis=2,
    )
    return turned.reshape(row_count, width)


def rms_back(grad_rows, normed, scale, gain):
    grad_normed = grad_rows * gain
    inner = jnp.mean(grad_normed * normed, axis=-1, keepdims=True)
    return (scale * grad_normed - normed * scale * inner, jnp.sum(grad_rows * normed, axis=0))


def dot(left, right):
    return jnp.dot(left, right, preferred_element_type=high_type)


def dot_t(left, right):
    return lax.dot_general(left, right, (((1,), (1,)), ((), ())), preferred_element_type=high_type)


def t_dot(left, right):
    return lax.dot_general(left, right, (((0,), (0,)), ((), ())), preferred_element_type=high_type)


GRID = ("ey", "ex", "dz", "dc")
SEQ = ("dz", "dc")


MESH_ID = pl.DeviceIdType.MESH


class Place:
    def __init__(self, depth):
        self.depth = depth
        self.y, self.x, self.z, self.c = (lax.axis_index(name) for name in GRID)

    def near_of(self, core):
        return self.y + core * (1 - 2 * self.y), self.x + (1 - core) * (1 - 2 * self.x)

    def far_of(self, core):
        return self.near_of(1 - core)

    def along(self, step):
        return lax.rem(self.z + step, self.depth)

    def next_z(self, k):
        first = self.z - 1 + 2 * lax.div(4 - self.z, 4)
        last = 3 * lax.div(3 - self.z, 2)
        return (self.z, first, 6 - self.z - first - last, last)[k]

    def block(self, column, z, core):
        return ((column[0] * 2 + column[1]) * self.depth + z) * 2 + core

    @property
    def own_column(self):
        return self.y, self.x

    @property
    def other_column(self):
        return 1 - self.y, 1 - self.x

    def core(self):
        return self.y, self.x, self.z, 1 - self.c

    def chip(self, step, core=None):
        return self.y, self.x, self.along(step), self.c if core is None else core

    def near(self):
        return (*self.near_of(self.c), self.z, self.c)

    def far(self):
        return (*self.far_of(self.c), self.z, self.c)


def meet(partners):
    barrier = pltpu.get_barrier_semaphore()
    for partner in partners:
        pl.semaphore_signal(barrier, inc=1, device_id=partner, device_id_type=MESH_ID)
    pl.semaphore_wait(barrier, len(partners))


def remote(source, target, sems, slot, partner):
    return pltpu.make_async_remote_copy(
        src_ref=source,
        dst_ref=target,
        send_sem=sems[0].at[slot],
        recv_sem=sems[1].at[slot],
        device_id=partner,
        device_id_type=MESH_ID,
    )


def pair(count):
    return [pltpu.SemaphoreType.DMA((count,)), pltpu.SemaphoreType.DMA((count,))]


def in_hbm(count):
    return [pl.BlockSpec(memory_space=pl.ANY)] * count


def spread_kernel(depth, count, extra, *refs):
    whole = count + extra
    sources, targets, sems = refs[:count], refs[whole : whole + count], refs[2 * whole :]
    extra_sources, extra_targets = refs[count:whole], refs[whole + count : 2 * whole]
    extra_sems = sems[9 * count :]
    at = Place(depth)
    others = range(1, depth)
    ranks = [(k, core) for k in range(depth) for core in range(2) if k or core]
    peers = [at.chip(k, lax.rem(at.c + core, 2)) for k, core in ranks]
    meet([at.near(), at.far()] + peers)
    started, local = [], []

    def push(n, source, index, kind, slot, partner):
        copy = remote(source, targets[n].at[index], sems[9 * n + 2 * kind :], slot, partner)
        copy.start()
        started.append(copy)

    def arrive(n, index, kind, slot):
        target = targets[n].at[index]
        remote(target, target, sems[9 * n + 2 * kind :], slot, at.core()).wait_recv()

    z_kind, near_kind, far_kind, core_kind = range(4)
    own = at.block(at.own_column, at.z, at.c)
    for n in range(count):
        push(n, sources[n], own, z_kind, at.z, (at.y, at.x, at.next_z(1), at.c))
        push(n, sources[n], own, near_kind, 0, at.near())
        push(n, sources[n], own, far_kind, 0, at.far())
        push(n, sources[n], own, core_kind, 0, at.core())
        copy = pltpu.make_async_copy(sources[n], targets[n].at[own], sems[9 * n + 8])
        copy.start()
        local.append(copy)

    inner = lax.rem(at.z, depth - 1) != 0
    onward = (at.z + 1, at.z + 1, at.z - 1, 3 * at.z - 3)

    def forward(n, source, k):
        z = at.next_z(k)
        return pltpu.make_async_remote_copy(
            src_ref=source,
            dst_ref=targets[n].at[at.block(at.own_column, z, at.c)],
            send_sem=sems[9 * n].at[z if k else depth],
            recv_sem=sems[9 * n + 1].at[z],
            device_id=(at.y, at.x, onward[k], at.c),
            device_id_type=MESH_ID,
        )

    @pl.when(inner)
    def _():
        for n in range(count):
            forward(n, sources[n], 0).start()

    for k in others:
        index = at.block(at.own_column, at.next_z(k), at.c)
        for n in range(count):
            arrive(n, index, z_kind, at.next_z(k))

        @pl.when(inner)
        def _(index=index, k=k):
            for n in range(count):
                forward(n, targets[n].at[index], k).start()

        for n in range(count):
            push(n, targets[n].at[index], index, near_kind, k, at.near())
            push(n, targets[n].at[index], index, far_kind, k, at.far())
            push(n, targets[n].at[index], index, core_kind, k, at.core())
    own_rank = at.z * 2 + at.c
    for n in range(extra):
        for slot, there in enumerate(peers):
            copy = remote(
                extra_sources[n].at[there[2] * 2 + there[3]],
                extra_targets[n].at[own_rank],
                extra_sems[3 * n :],
                slot,
                there,
            )
            copy.start()
            started.append(copy)
        copy = pltpu.make_async_copy(
            extra_sources[n].at[own_rank], extra_targets[n].at[own_rank], extra_sems[3 * n + 2]
        )
        copy.start()
        local.append(copy)
    for k in range(depth):
        index = at.block(at.near_of(at.c), at.next_z(k), at.c)
        for n in range(count):
            arrive(n, index, near_kind, k)
            push(n, targets[n].at[index], index, far_kind, depth + k, at.far())
            push(n, targets[n].at[index], index, core_kind, depth + k, at.core())
    for j in range(2 * depth):
        column = at.far_of(at.c) if j < depth else at.other_column
        index = at.block(column, at.next_z(j % depth), at.c)
        for n in range(count):
            arrive(n, index, far_kind, j)
            push(n, targets[n].at[index], index, core_kind, 2 * depth + j, at.core())
    core = 1 - at.c
    columns = [at.own_column, at.near_of(core), at.far_of(core), at.other_column]
    for j in range(4 * depth):
        index = at.block(columns[j // depth], at.next_z(j % depth), core)
        for n in range(count):
            arrive(n, index, core_kind, j)
    for n in range(extra):
        for slot, (k, core) in enumerate(ranks):
            target = extra_targets[n].at[at.along(depth - k) * 2 + lax.rem(at.c + core, 2)]
            remote(target, target, extra_sems[3 * n :], slot, at.core()).wait_recv()

    @pl.when(inner)
    def _():
        for n in range(count):
            forward(n, sources[n], 0).wait_send()
            for k in others:
                index = at.block(at.own_column, at.next_z(k), at.c)
                forward(n, targets[n].at[index], k).wait_send()

    for copy in started:
        copy.wait_send()
    for copy in local:
        copy.wait()


def spread(depth, ident, arrays, extras=()):
    sems = []
    for _ in arrays:
        sems += pair(depth + 1) + pair(depth) + pair(2 * depth) + pair(4 * depth)
        sems.append(pltpu.SemaphoreType.DMA)
    for _ in extras:
        sems += pair(2 * depth - 1) + [pltpu.SemaphoreType.DMA]
    count = len(arrays) + len(extras)
    shapes = [((8 * depth,) + a.shape, a.dtype) for a in arrays]
    shapes += [(a.shape, a.dtype) for a in extras]
    return pl.pallas_call(
        functools.partial(spread_kernel, depth, len(arrays), len(extras)),
        out_shape=[jax.ShapeDtypeStruct(*shape) for shape in shapes],
        in_specs=in_hbm(count),
        out_specs=in_hbm(count),
        scratch_shapes=sems,
        compiler_params=pltpu.CompilerParams(
            collective_id=ident, has_side_effects=True, vmem_limit_bytes=16 << 20
        ),
        cost_estimate=pl.CostEstimate(
            flops=0,
            bytes_accessed=sum(64 * depth * a.size * a.dtype.itemsize for a in arrays),
            transcendentals=0,
        ),
    )(*arrays, *extras)


def sum_rows(target, lead, terms):
    rows = target.shape[-2]
    tile = min(rows, 16)

    def body(i, carry):
        at = pl.ds(pl.multiple_of(i * tile, tile), tile)
        total = terms[0][0][(*terms[0][1], at, slice(None))].astype(high_type)
        for ref, where in terms[1:]:
            total = total + ref[(*where, at, slice(None))].astype(high_type)
        target[(*lead, at, slice(None))] = total.astype(target.dtype)
        return carry

    lax.fori_loop(0, rows // tile, body, 0)


def collect_kernel(depth, counts, *refs):
    rest = iter(refs)

    def take(count):
        return [next(rest) for _ in range(count)]

    mains, smalls, shareds, extras = (take(count) for count in counts)
    main_totals, small_totals, shared_totals, extra_outs = (take(count) for count in counts)
    main_buffers = [take(5) for _ in mains]
    small_buffers = [take(5) for _ in smalls]
    shared_buffers = [take(3) for _ in shareds]
    shared_outs = [take(1)[0] for _ in shareds]
    main_sems = [take(9) for _ in mains]
    small_sems = [take(9) for _ in smalls]
    shared_sems = [take(7) for _ in shareds]
    extra_sems = [take(3) for _ in extras]
    at = Place(depth)
    ranks = [(k, core) for k in range(depth) for core in range(2) if k or core]
    peers = [at.chip(k, lax.rem(at.c + core, 2)) for k, core in ranks]
    meet([at.near(), at.far()] + peers)
    started = []
    own_rank = at.z * 2 + at.c

    def columns(core):
        return at.other_column, at.far_of(core), at.near_of(core), at.own_column

    def number(column):
        return column[0] * 2 + column[1]

    def push(copy):
        copy.start()
        started.append(copy)

    def arrive(buffer, pair_of, slot):
        remote(buffer.at[slot], buffer.at[slot], pair_of, slot, at.core()).wait_recv()

    def piece(ref, rank):
        rows = ref.shape[0] // (2 * depth)
        return ref.at[pl.ds(pl.multiple_of(rank * rows, rows), rows)]

    def block(group, k, core):
        return at.block(columns(core)[group], at.along(1 + k), core)

    def main_load(n, group, k):
        slot = group * depth + k
        return pltpu.make_async_copy(
            mains[n].at[block(group, k, at.c)], main_buffers[n][0].at[slot], main_sems[n][8].at[slot]
        )

    def main_cross(group, k):
        slot = group * depth + k
        for n, (part, buffers, sems) in enumerate(zip(mains, main_buffers, main_sems)):
            source = part.at[block(group, k, 1 - at.c)]
            push(remote(source, buffers[1].at[slot], sems[0:2], slot, at.core()))
            main_load(n, group, k).start()

    def main_sum(n, group, k, more):
        mine, crossed = main_buffers[n][:2]
        slot = group * depth + k
        main_load(n, group, k).wait()
        arrive(crossed, main_sems[n][0:2], slot)
        terms = [(mine, (slot,)), (crossed, (slot,))] + more
        if slot < 4 * depth - 1:
            sum_rows(mine, (slot,), terms)
        else:
            sum_rows(main_totals[n], (), terms)
        return mine.at[slot]

    def main_far(k):
        for n, (buffers, sems) in enumerate(zip(main_buffers, main_sems)):
            for group in range(2):
                slot = group * depth + k
                total = main_sum(n, group, k, [])
                push(remote(total, buffers[2].at[slot], sems[2:4], slot, at.far()))

    def main_near(k):
        for n, (buffers, sems) in enumerate(zip(main_buffers, main_sems)):
            arrive(buffers[2], sems[2:4], k)
            total = main_sum(n, 2, k, [(buffers[2], (k,))])
            push(remote(total, buffers[3].at[k], sems[4:6], k, at.near()))

    def main_own(k):
        for n, (buffers, sems) in enumerate(zip(main_buffers, main_sems)):
            arrive(buffers[2], sems[2:4], depth + k)
            arrive(buffers[3], sems[4:6], k)
            total = main_sum(n, 3, k, [(buffers[2], (depth + k,)), (buffers[3], (k,))])
            if k < depth - 1:
                push(remote(total, buffers[4].at[k], sems[6:8], k, at.chip(1 + k)))

    def small_load(n, group):
        return pltpu.make_async_copy(
            smalls[n].at[at.c, number(columns(at.c)[group])],
            small_buffers[n][0].at[group],
            small_sems[n][8].at[group],
        )

    def small_cross():
        for n, (part, buffers, sems) in enumerate(zip(smalls, small_buffers, small_sems)):
            for group in range(4):
                source = part.at[1 - at.c, number(columns(1 - at.c)[group])]
                push(remote(source, buffers[1].at[group], sems[0:2], group, at.core()))
                small_load(n, group).start()

    def small_sum(n, group, more):
        mine, crossed = small_buffers[n][:2]
        small_load(n, group).wait()
        arrive(crossed, small_sems[n][0:2], group)
        for j in range(depth):
            terms = [(mine, (group, j)), (crossed, (group, j))]
            sum_rows(mine, (group, j), terms + [(ref, (i, j)) for ref, i in more])
        return mine.at[group]

    def small_far():
        for n, (buffers, sems) in enumerate(zip(small_buffers, small_sems)):
            for group in range(2):
                total = small_sum(n, group, [])
                push(remote(total, buffers[2].at[group], sems[2:4], group, at.far()))

    def small_near():
        for n, (buffers, sems) in enumerate(zip(small_buffers, small_sems)):
            arrive(buffers[2], sems[2:4], 0)
            total = small_sum(n, 2, [(buffers[2], 0)])
            push(remote(total, buffers[3].at[0], sems[4:6], 0, at.near()))

    def small_own():
        for n, (buffers, sems) in enumerate(zip(small_buffers, small_sems)):
            arrive(buffers[2], sems[2:4], 1)
            arrive(buffers[3], sems[4:6], 0)
            total = small_sum(n, 3, [(buffers[2], 1), (buffers[3], 0)])
            for k in range(1, depth):
                there = at.chip(k)
                source = total.at[there[2]]
                push(remote(source, buffers[4].at[k - 1], sems[6:8], k - 1, there))

    def shared_load(n, i):
        return pltpu.make_async_copy(
            shareds[n].at[number(columns(at.c)[2 + i])], shared_buffers[n][0].at[i], shared_sems[n][0].at[i]
        )

    def shared_far():
        for n, (part, buffers, sems) in enumerate(zip(shareds, shared_buffers, shared_sems)):
            for i in range(2):
                source = part.at[number(columns(at.c)[i])]
                push(remote(source, buffers[1].at[i], sems[1:3], i, at.far()))
                shared_load(n, i).start()

    def shared_near():
        for n, ((mine, far_in, near_in), sems) in enumerate(zip(shared_buffers, shared_sems)):
            shared_load(n, 0).wait()
            arrive(far_in, sems[1:3], 0)
            sum_rows(mine, (0,), [(mine, (0,)), (far_in, (0,))])
            push(remote(mine.at[0], near_in.at[0], sems[3:5], 0, at.near()))

    def shared_own():
        for n, ((mine, far_in, near_in), sems) in enumerate(zip(shared_buffers, shared_sems)):
            shared_load(n, 1).wait()
            arrive(far_in, sems[1:3], 1)
            arrive(near_in, sems[3:5], 0)
            sum_rows(mine, (1,), [(mine, (1,)), (far_in, (1,)), (near_in, (0,))])
            for slot, there in enumerate(peers):
                source = piece(mine.at[1], there[2] * 2 + there[3])
                push(remote(source, piece(shared_outs[n], own_rank), sems[5:7], slot, there))
            shared_kept(n).start()

    def shared_kept(n):
        mine = shared_buffers[n][0]
        return pltpu.make_async_copy(
            piece(mine.at[1], own_rank), piece(shared_outs[n], own_rank), shared_sems[n][0].at[2]
        )

    def extra_kept(n):
        return pltpu.make_async_copy(
            extras[n].at[own_rank], extra_outs[n].at[own_rank], extra_sems[n][2]
        )

    order = [(main_far, k) for k in range(2)] + [(main_near, 0)]
    for k in range(2, depth):
        order += [(main_far, k), (main_near, k - 1), (main_own, k - 2)]
    order += [(main_near, depth - 1), (main_own, depth - 2), (main_own, depth - 1)]
    groups = {main_far: (0, 1), main_near: (2,), main_own: (3,)}
    shared_far()
    small_cross()
    for stage, k in order:
        for group in groups[stage]:
            main_cross(group, k)
    for n in range(len(extras)):
        for slot, there in enumerate(peers):
            source = extras[n].at[there[2] * 2 + there[3]]
            push(remote(source, extra_outs[n].at[own_rank], extra_sems[n][:2], slot, there))
        extra_kept(n).start()
    small_far()
    for stage, k in order:
        stage(k)
        if (stage, k) == (main_near, 0):
            shared_near()
            small_near()
        if (stage, k) == (main_own, 0):
            shared_own()
            small_own()
    for n, (buffers, sems) in enumerate(zip(small_buffers, small_sems)):
        for k in range(depth - 1):
            arrive(buffers[4], sems[6:8], k)
        terms = [(buffers[0], (3, at.z))] + [(buffers[4], (k,)) for k in range(depth - 1)]
        sum_rows(small_totals[n], (), terms)
    for n, (buffers, sems) in enumerate(zip(main_buffers, main_sems)):
        for k in range(depth - 1):
            arrive(buffers[4], sems[6:8], k)
        terms = [(main_totals[n], ())] + [(buffers[4], (k,)) for k in range(depth - 1)]
        sum_rows(main_totals[n], (), terms)
    for slot, (k, core) in enumerate(ranks):
        source = at.along(depth - k) * 2 + lax.rem(at.c + core, 2)
        for n in range(len(shareds)):
            target = piece(shared_outs[n], source)
            remote(target, target, shared_sems[n][5:7], slot, at.core()).wait_recv()
        for n in range(len(extras)):
            target = extra_outs[n].at[source]
            remote(target, target, extra_sems[n][:2], slot, at.core()).wait_recv()
    for n in range(len(shareds)):
        shared_kept(n).wait()
        out, held = shared_totals[n], shared_outs[n]
        count, rows = out.shape[:2]
        heads = held.shape[1] // (count * HD)
        for rank in range(2 * depth):
            for i in range(count):
                for j in range(heads):
                    head = (rank % 2 * heads + j) * depth + rank // 2
                    value = held[rank * rows : (rank + 1) * rows, (i * heads + j) * HD :][:, :HD]
                    out[i, :, head * HD : (head + 1) * HD] = value.astype(out.dtype)
    for n in range(len(extras)):
        extra_kept(n).wait()
    for copy in started:
        copy.wait_send()


def collect(depth, ident, mains, smalls, shareds=(), extras=()):
    dma = pltpu.SemaphoreType.DMA
    peers = 2 * depth - 1

    def by_core(a):
        return a.reshape((4, depth, 2) + a.shape[1:]).transpose(2, 0, 1, 3, 4)

    smalls = [by_core(a) for a in smalls]
    buffers, sems, shapes = [], [], []
    for a in mains:
        for slots in (4 * depth, 4 * depth, 2 * depth, depth, depth - 1):
            buffers.append(pltpu.VMEM((slots,) + a.shape[1:], a.dtype))
        sems += pair(4 * depth) + pair(2 * depth) + pair(depth) + pair(depth - 1)
        sems.append(dma((4 * depth,)))
        shapes.append(jax.ShapeDtypeStruct(a.shape[1:], high_type))
    for a in smalls:
        for slots in ((4, depth), (4, depth), (2, depth), (1, depth), (depth - 1,)):
            buffers.append(pltpu.VMEM(slots + a.shape[3:], a.dtype))
        sems += pair(4) + pair(2) + pair(1) + pair(depth - 1) + [dma((4,))]
        shapes.append(jax.ShapeDtypeStruct(a.shape[3:], high_type))
    for a in shareds:
        buffers += [pltpu.VMEM((slots,) + a.shape[1:], a.dtype) for slots in (2, 2, 1)]
        buffers.append(pltpu.VMEM(a.shape[1:], a.dtype))
        sems += [dma((3,))] + pair(2) + pair(1) + pair(peers)
        shape = (3, a.shape[1] // (2 * depth), a.shape[2] // 3 * 2 * depth)
        shapes.append(jax.ShapeDtypeStruct(shape, high_type))
    for a in extras:
        sems += pair(peers) + [dma]
        shapes.append(jax.ShapeDtypeStruct(a.shape, a.dtype))
    arrays = [*mains, *smalls, *shareds, *extras]
    counts = (len(mains), len(smalls), len(shareds), len(extras))
    in_vmem = [pl.BlockSpec(memory_space=pltpu.VMEM)] * (len(arrays) - len(extras))
    return pl.pallas_call(
        functools.partial(collect_kernel, depth, counts),
        out_shape=shapes,
        in_specs=in_hbm(len(arrays)),
        out_specs=in_vmem + in_hbm(len(extras)),
        scratch_shapes=buffers + sems,
        compiler_params=pltpu.CompilerParams(
            collective_id=ident, has_side_effects=True, vmem_limit_bytes=56 << 20
        ),
        cost_estimate=pl.CostEstimate(
            flops=0,
            bytes_accessed=sum(16 * a.size * a.dtype.itemsize for a in arrays),
            transcendentals=0,
        ),
    )(*arrays)


def gather_kernel(depth, x_ref, o_ref, w_ref, s_ref, x_out, o_out, w_out, s_out, *sems):
    at = Place(depth)
    ranks = [(k, core) for k in range(depth) for core in range(2) if k or core]
    peers = [at.chip(k, lax.rem(at.c + core, 2)) for k, core in ranks]
    meet([at.near(), at.far()] + peers)
    own, column = at.z * 2 + at.c, at.y * 2 + at.x
    x_z, x_core, o_z, o_near, o_far, o_core, w_sems, s_sems, w_side, s_side = (
        sems[2 * i : 2 * i + 2] for i in range(10)
    )
    started, local = [], []
    inner = lax.rem(at.z, depth - 1) != 0
    onward = (at.z + 1, at.z + 1, at.z - 1, 3 * at.z - 3)
    own_block = at.block(at.own_column, at.z, at.c)

    def push(copy):
        copy.start()
        started.append(copy)

    def arrive(target, pair_of, slot):
        remote(target, target, pair_of, slot, at.core()).wait_recv()

    def x_place(k):
        return x_out.at[at.next_z(k) * 2 + at.c]

    def o_place(k):
        return o_out.at[at.block(at.own_column, at.next_z(k), at.c)]

    def forward(source, target, pair_of, k):
        z = at.next_z(k)
        return pltpu.make_async_remote_copy(
            src_ref=source,
            dst_ref=target,
            send_sem=pair_of[0].at[z if k else depth],
            recv_sem=pair_of[1].at[z],
            device_id=(at.y, at.x, onward[k], at.c),
            device_id_type=MESH_ID,
        )

    for slot, there in enumerate(peers):
        push(remote(s_ref, s_out.at[column, own], s_sems, slot, there))
        source = w_ref.at[there[2] * 2 + there[3]]
        push(remote(source, w_out.at[column, own], w_sems, slot, there))
    first = (at.y, at.x, at.next_z(1), at.c)
    push(remote(o_ref, o_place(0), o_z, at.z, first))
    push(remote(x_ref, x_place(0), x_z, at.z, first))

    @pl.when(inner)
    def _():
        forward(o_ref, o_place(0), o_z, 0).start()
        forward(x_ref, x_place(0), x_z, 0).start()

    push(remote(x_ref, x_place(0), x_core, 0, at.core()))
    push(remote(o_ref, o_place(0), o_near, 0, at.near()))
    push(remote(o_ref, o_place(0), o_far, 0, at.far()))
    push(remote(o_ref, o_place(0), o_core, 0, at.core()))
    for i, (source, target) in enumerate(
        (
            (x_ref, x_place(0)),
            (o_ref, o_place(0)),
            (w_ref.at[own], w_out.at[column, own]),
            (s_ref, s_out.at[column, own]),
        )
    ):
        copy = pltpu.make_async_copy(source, target, sems[20].at[i])
        copy.start()
        local.append(copy)
    near_y, near_x = at.near_of(at.c)
    far_y, far_x = at.far_of(at.c)
    beside, across = near_y * 2 + near_x, far_y * 2 + far_x
    sides = ((s_out, s_side), (w_out, w_side))
    for k in range(1, depth):
        arrive(o_place(k), o_z, at.next_z(k))

        @pl.when(inner)
        def _(k=k):
            forward(o_place(k), o_place(k), o_z, k).start()

        push(remote(o_place(k), o_place(k), o_near, k, at.near()))
        push(remote(o_place(k), o_place(k), o_far, k, at.far()))
        push(remote(o_place(k), o_place(k), o_core, k, at.core()))
        arrive(x_place(k), x_z, at.next_z(k))

        @pl.when(inner)
        def _(k=k):
            forward(x_place(k), x_place(k), x_z, k).start()

        push(remote(x_place(k), x_place(k), x_core, k, at.core()))
        if k == 1:
            for slot, (j, core) in enumerate(ranks):
                source = at.along(depth - j) * 2 + lax.rem(at.c + core, 2)
                arrive(s_out.at[column, source], s_sems, slot)
                arrive(w_out.at[column, source], w_sems, slot)
            for copy in local:
                copy.wait()
            for target, pair_of in sides:
                push(remote(target.at[column], target.at[column], pair_of, 0, at.near()))
                push(remote(target.at[column], target.at[column], pair_of, 1, at.far()))
    for target, pair_of in sides:
        arrive(target.at[beside], pair_of, 0)
        push(remote(target.at[beside], target.at[beside], pair_of, 2, at.far()))
    for k in range(depth):
        target = o_out.at[at.block(at.near_of(at.c), at.next_z(k), at.c)]
        arrive(target, o_near, k)
        push(remote(target, target, o_far, depth + k, at.far()))
        push(remote(target, target, o_core, depth + k, at.core()))
    for j in range(2 * depth):
        place = at.far_of(at.c) if j < depth else at.other_column
        target = o_out.at[at.block(place, at.next_z(j % depth), at.c)]
        arrive(target, o_far, j)
        push(remote(target, target, o_core, 2 * depth + j, at.core()))
    for target, pair_of in sides:
        arrive(target.at[across], pair_of, 1)
        arrive(target.at[3 - column], pair_of, 2)
    for k in range(depth):
        arrive(x_out.at[at.next_z(k) * 2 + 1 - at.c], x_core, k)
    core = 1 - at.c
    places = [at.own_column, at.near_of(core), at.far_of(core), at.other_column]
    for j in range(4 * depth):
        index = at.block(places[j // depth], at.next_z(j % depth), core)
        arrive(o_out.at[index], o_core, j)

    @pl.when(inner)
    def _():
        forward(x_ref, x_place(0), x_z, 0).wait_send()
        forward(o_ref, o_place(0), o_z, 0).wait_send()
        for k in range(1, depth):
            forward(x_place(k), x_place(k), x_z, k).wait_send()
            forward(o_place(k), o_place(k), o_z, k).wait_send()

    for copy in started:
        copy.wait_send()


def gather(depth, ident, x, o, w, s):
    ranks = 2 * depth
    sems = pair(depth + 1) + pair(depth) + pair(depth + 1) + pair(depth) + pair(2 * depth)
    sems += pair(4 * depth) + pair(ranks - 1) * 2 + pair(3) * 2
    sems.append(pltpu.SemaphoreType.DMA((4,)))
    return pl.pallas_call(
        functools.partial(gather_kernel, depth),
        out_shape=[
            jax.ShapeDtypeStruct((ranks,) + x.shape, x.dtype),
            jax.ShapeDtypeStruct((4 * ranks,) + o.shape, o.dtype),
            jax.ShapeDtypeStruct((4,) + w.shape, w.dtype),
            jax.ShapeDtypeStruct((4, ranks) + s.shape, s.dtype),
        ],
        in_specs=in_hbm(4),
        out_specs=in_hbm(4),
        scratch_shapes=sems,
        compiler_params=pltpu.CompilerParams(
            collective_id=ident, has_side_effects=True, vmem_limit_bytes=16 << 20
        ),
        cost_estimate=pl.CostEstimate(
            flops=0, bytes_accessed=64 * depth * x.size, transcendentals=0
        ),
    )(x, o, w, s)


def exchange_kernel(depth, same, x_ref, out_ref, send_sems, recv_sems, local_sem):
    at = Place(depth)
    ranks = [(k, core) for k in range(depth) for core in range(2) if k or core]
    peers = [at.chip(k, lax.rem(at.c + core, 2)) for k, core in ranks]
    meet(peers)
    own = at.z * 2 + at.c
    copies = []
    for slot, there in enumerate(peers):
        source = x_ref if same else x_ref.at[there[2] * 2 + there[3]]
        copy = remote(source, out_ref.at[own], (send_sems, recv_sems), slot, there)
        copy.start()
        copies.append(copy)
    local = pltpu.make_async_copy(x_ref if same else x_ref.at[own], out_ref.at[own], local_sem)
    local.start()
    for slot, (k, core) in enumerate(ranks):
        target = out_ref.at[at.along(depth - k) * 2 + lax.rem(at.c + core, 2)]
        remote(target, target, (send_sems, recv_sems), slot, at.core()).wait_recv()
    for copy in copies:
        copy.wait_send()
    local.wait()


def exchange(depth, ident, x, same=False):
    ranks = 2 * depth
    return pl.pallas_call(
        functools.partial(exchange_kernel, depth, same),
        out_shape=jax.ShapeDtypeStruct((ranks,) + x.shape if same else x.shape, x.dtype),
        in_specs=in_hbm(1),
        out_specs=in_hbm(1)[0],
        scratch_shapes=pair(ranks - 1) + [pltpu.SemaphoreType.DMA],
        compiler_params=pltpu.CompilerParams(
            collective_id=ident, has_side_effects=True, vmem_limit_bytes=16 << 20
        ),
        cost_estimate=pl.CostEstimate(
            flops=0, bytes_accessed=16 * x.size * x.dtype.itemsize, transcendentals=0
        ),
    )(x)


def column_kernel(depth, part, total, mine, crossed, z_in, z_out, *sems):
    at = Place(depth)
    meet([at.core()] + [at.chip(k) for k in range(1, depth)])
    started = []

    def push(copy):
        copy.start()
        started.append(copy)

    def local(k):
        return pltpu.make_async_copy(
            part.at[at.along(1 + k) * 2 + at.c], mine.at[k], sems[4].at[k]
        )

    def arrive(buffer, pair_of, slot):
        remote(buffer.at[slot], buffer.at[slot], pair_of, slot, at.core()).wait_recv()

    for k in range(depth):
        push(
            remote(
                part.at[at.along(1 + k) * 2 + 1 - at.c], crossed.at[k], sems[0:2], k, at.core()
            )
        )
        local(k).start()
    for k in range(depth):
        local(k).wait()
        arrive(crossed, sems[0:2], k)
        terms = [(mine, (k,)), (crossed, (k,))]
        if k < depth - 1:
            sum_rows(z_out, (k,), terms)
            push(remote(z_out.at[k], z_in.at[k], sems[2:4], k, at.chip(1 + k)))
        else:
            sum_rows(total, (), terms)
    for k in range(depth - 1):
        arrive(z_in, sems[2:4], k)
    sum_rows(total, (), [(total, ())] + [(z_in, (k,)) for k in range(depth - 1)])
    for copy in started:
        copy.wait_send()


def collect_column(depth, ident, part):
    block = part.shape[1:]
    return pl.pallas_call(
        functools.partial(column_kernel, depth),
        out_shape=jax.ShapeDtypeStruct(block, high_type),
        in_specs=in_hbm(1),
        out_specs=pl.BlockSpec(memory_space=pltpu.VMEM),
        scratch_shapes=[pltpu.VMEM((depth,) + block, part.dtype)] * 2
        + [pltpu.VMEM((depth - 1,) + block, part.dtype)] * 2
        + pair(depth)
        + pair(depth - 1)
        + [pltpu.SemaphoreType.DMA((depth,))],
        compiler_params=pltpu.CompilerParams(
            collective_id=ident, has_side_effects=True, vmem_limit_bytes=32 << 20
        ),
        cost_estimate=pl.CostEstimate(
            flops=0, bytes_accessed=16 * part.size * part.dtype.itemsize, transcendentals=0
        ),
    )(part)


def lines_in(values):
    rows, local, two, hidden = values.shape
    values = values.reshape(rows, local, two, hidden // 128, 128)
    return values.transpose(0, 1, 3, 2, 4).reshape(-1, 128)


def lines_down(values):
    rows, local, hidden = values.shape
    return values.reshape(rows, local, hidden // 128, 128).transpose(0, 2, 1, 3).reshape(-1, 128)


def places(ranks, local):
    for rank in range(ranks):
        for x in range(local):
            for k in range(2):
                yield rank, (k * local + x) * 128, (x * ranks + rank) * 2 + k, None
            yield rank, x * 128, None, rank * local + x


def pack_kernel(ranks, local, step, in_ref, down_ref, in_out, down_out):
    for rank, column, of_in, of_down in places(ranks, local):
        if of_down is None:
            value = in_ref[pl.ds(of_in, step, stride=2 * local * ranks), :]
            in_out[rank, :, column : column + 128] = value.astype(low_type)
        else:
            value = down_ref[pl.ds(of_down, step, stride=local * ranks), :]
            down_out[rank, :, column : column + 128] = value.astype(low_type)


def pack(ranks, expert_in, expert_down):
    rows, local = expert_in.shape[:2]
    step = 32
    lines = step * local * ranks
    span = local * 128
    return pl.pallas_call(
        functools.partial(pack_kernel, ranks, local, step),
        grid=(rows // step,),
        in_specs=[
            pl.BlockSpec((2 * lines, 128), lambda i: (i, 0)),
            pl.BlockSpec((lines, 128), lambda i: (i, 0)),
        ],
        out_specs=[
            pl.BlockSpec((ranks, step, 2 * span), lambda i: (0, i, 0)),
            pl.BlockSpec((ranks, step, span), lambda i: (0, i, 0)),
        ],
        out_shape=[
            jax.ShapeDtypeStruct((ranks, rows, 2 * span), low_type),
            jax.ShapeDtypeStruct((ranks, rows, span), low_type),
        ],
        compiler_params=pltpu.CompilerParams(vmem_limit_bytes=32 << 20),
    )(lines_in(expert_in), lines_down(expert_down))


def unpack_kernel(ranks, local, step, in_ref, out_ref):
    for rank, column, of_in, of_down in places(ranks, local):
        down = in_ref.shape[2] == local * 128
        if down == (of_in is None):
            first = of_down if down else of_in
            stride = (1 if down else 2) * local * ranks
            value = in_ref[rank, :, column : column + 128].astype(high_type)
            out_ref[pl.ds(first, step, stride=stride), :] = value


def unpack(local, sliced):
    ranks, rows, span = sliced.shape
    step = 32
    lines = step * ranks * span // 128
    return pl.pallas_call(
        functools.partial(unpack_kernel, ranks, local, step),
        grid=(rows // step,),
        in_specs=[pl.BlockSpec((ranks, step, span), lambda i: (0, i, 0))],
        out_specs=pl.BlockSpec((lines, 128), lambda i: (i, 0)),
        out_shape=jax.ShapeDtypeStruct((rows * ranks * span // 128, 128), high_type),
        compiler_params=pltpu.CompilerParams(vmem_limit_bytes=32 << 20),
    )(sliced)


def experts_kernel(
    local, tokens_ref, grads_ref, gates_ref, in_ref, down_ref, *outputs
):
    back_ref, mixed_ref, sums_ref, grad_in_ref, grad_down_ref, in_total, down_total = outputs
    column = lax.axis_index("ey") * 2 + lax.axis_index("ex")
    step = pl.program_id(0)
    blocks, experts, rows = gates_ref.shape
    span = down_ref.shape[1]
    width = tokens_ref.shape[2]
    units_of = (
        lax.broadcasted_iota(jnp.int32, (experts, span), 1) // 128 + column * local
        == lax.broadcasted_iota(jnp.int32, (experts, span), 0)
    ).astype(low_type)

    def terms(values, count):
        result = []
        for _ in range(count):
            result.append(values.astype(low_type))
            values = values - result[-1].astype(high_type)
        return result

    tokens = tokens_ref[...].reshape(blocks * rows, width)
    grads = grads_ref[...].reshape(blocks * rows, width)
    gates = jnp.concatenate([gates_ref[b] for b in range(blocks)], axis=1)
    gates = jnp.concatenate(terms(gates, 3), axis=0)
    wide = t_dot(gates, jnp.concatenate([units_of] * 3, axis=0))
    both = dot(tokens, in_ref[...])
    gate_part, up_part = both[:, :span], both[:, span:]
    down_grad = dot(grads, down_ref[...])
    sigma = 0.5 + 0.5 * jnp.tanh(0.5 * gate_part)
    silu = gate_part * sigma
    hidden = (silu * up_part).astype(low_type).astype(high_type)
    weighted = (wide * hidden).astype(low_type)
    inner = hidden * down_grad
    high, rest = terms(inner, 2)
    sums = dot_t(units_of, high) + dot_t(units_of, rest)
    for b in range(blocks):
        sums_ref[b] = sums[:, b * rows : (b + 1) * rows]
    grad_hidden = wide * down_grad
    grad_gate = grad_hidden * up_part * (sigma + silu * (1.0 - sigma))
    grad_both = jnp.concatenate([grad_gate, grad_hidden * silu], axis=1).astype(low_type)
    back_ref[...] = dot_t(grad_both, in_ref[...]).astype(low_type).reshape(back_ref.shape)
    mixed_ref[...] = dot_t(weighted, down_ref[...]).astype(low_type).reshape(mixed_ref.shape)

    @pl.when(step == 0)
    def _():
        in_total[...] = jnp.zeros_like(in_total)
        down_total[...] = jnp.zeros_like(down_total)

    in_total[...] += t_dot(tokens, grad_both)
    down_total[...] += t_dot(grads, weighted)

    @pl.when(step == pl.num_programs(0) - 1)
    def _():
        grad_in_ref[...] = in_total[...].astype(low_type)
        grad_down_ref[...] = down_total[...].astype(low_type)


def run_experts(local, tokens, grads, gates, weights_in, weights_down):
    devices, rows, width = tokens.shape
    experts = gates.shape[1]
    blocks = 4
    span = weights_down.shape[1]
    once = pl.Buffered(1)

    def by_step(shape):
        return pl.BlockSpec((blocks,) + shape, lambda i: (i, 0, 0))

    def whole(shape):
        return pl.BlockSpec(shape, lambda i: (0, 0), pipeline_mode=once)

    return pl.pallas_call(
        functools.partial(experts_kernel, local),
        grid=(devices // blocks,),
        in_specs=[
            by_step((rows, width)),
            by_step((rows, width)),
            by_step((experts, rows)),
            whole((width, 2 * span)),
            whole((width, span)),
        ],
        out_specs=[
            by_step((rows, width)),
            by_step((rows, width)),
            by_step((experts, rows)),
            whole((width, 2 * span)),
            whole((width, span)),
        ],
        out_shape=[
            jax.ShapeDtypeStruct((devices, rows, width), low_type),
            jax.ShapeDtypeStruct((devices, rows, width), low_type),
            jax.ShapeDtypeStruct((devices, experts, rows), high_type),
            jax.ShapeDtypeStruct((width, 2 * span), low_type),
            jax.ShapeDtypeStruct((width, span), low_type),
        ],
        scratch_shapes=[
            pltpu.VMEM((width, 2 * span), high_type),
            pltpu.VMEM((width, span), high_type),
        ],
        compiler_params=pltpu.CompilerParams(vmem_limit_bytes=60 << 20),
        cost_estimate=pl.CostEstimate(
            flops=18 * devices * rows * width * span,
            bytes_accessed=8 * devices * rows * width,
            transcendentals=devices * rows * span,
        ),
    )(tokens, grads, gates, weights_in, weights_down)


def grid_shards(
    residual_in,
    cotangent,
    lengths,
    routes,
    attn_qkv,
    attn_out,
    gains,
    router,
    expert_in,
    expert_down,
):
    rows, width = residual_in.shape
    depth = lax.axis_size("dz")
    ranks = 2 * depth
    columns = 4
    seq_rows = rows * ranks
    local_experts = expert_in.shape[1]
    experts = local_experts * columns
    hidden_width = expert_in.shape[3]
    part = hidden_width // ranks
    span = local_experts * part
    chunk_rows = expert_in.shape[0]
    weight_rows = attn_qkv.shape[1]
    score_scale = HD ** (-0.5)
    y, x, z, c = (lax.axis_index(name) for name in GRID)
    column = y * 2 + x
    own_heads = HEADS // ranks
    own_width = own_heads * HD

    def sum_column(ident, pairs):
        flat = exchange(depth, ident, pairs.reshape(-1, 128), same=True)
        return jnp.sum(flat, axis=0).reshape(pairs.shape)

    def by_rank(values):
        lead = values.shape[:-1]
        shaped = values.reshape(lead + (2, own_heads, depth, HD))
        n = len(lead)
        return shaped.transpose((n + 2, n) + tuple(range(n)) + (n + 1, n + 3)).reshape(
            (ranks,) + lead + (own_width,)
        )

    def by_head(values):
        lead = values.shape[1:-1]
        shaped = values.reshape((depth, 2) + lead + (own_heads, HD))
        n = len(lead)
        return shaped.transpose(tuple(range(2, n + 2)) + (1, n + 2, 0, n + 3)).reshape(
            lead + (width,)
        )

    small = jnp.concatenate([gains.T, router], axis=1).astype(low_type)
    small = jnp.pad(small, ((0, 0), (0, 128 - small.shape[1])))
    packed = attn_qkv.astype(low_type).transpose(1, 0, 2)
    packed = by_rank(packed).reshape(ranks, weight_rows, 3 * own_width)
    seq_input, out_weight, qkv_weight, small = gather(
        depth, 0, residual_in, attn_out.astype(low_type), packed, small
    )
    out_weight = out_weight.reshape(width, width)
    qkv_weight = qkv_weight.reshape(width, 3 * own_width)
    small = small.reshape(width, 128)
    gain_rows = small[:, :4].T.astype(high_type)
    router_weight = small[:, 4 : 4 + experts]
    gain_own = [
        lax.dynamic_index_in_dim(by_rank(gain_rows[i]), z * 2 + c, 0, keepdims=False)
        for i in (1, 2)
    ]
    normed_in = seq_input.reshape(seq_rows, width).astype(high_type)
    normed_in = (normed_in * rms_scale(normed_in) * gain_rows[0]).astype(low_type)
    sliced_in, sliced_down = pack(ranks, expert_in, expert_down)

    raw = dot(normed_in, qkv_weight)
    query_raw, key_raw = raw[:, :own_width], raw[:, own_width : 2 * own_width]
    value_rows = raw[:, 2 * own_width :].astype(low_type)
    squares = jnp.stack(
        [jnp.sum(query_raw * query_raw, axis=1), jnp.sum(key_raw * key_raw, axis=1)]
    )
    scales = lax.rsqrt(sum_column(1, squares) / width + epsilon)
    query_scale, key_scale = scales[0][:, None], scales[1][:, None]
    positions = jnp.arange(seq_rows, dtype=jnp.int32)
    length_now = lengths[0]
    key_live = positions < length_now
    cosine, sine_table = angle_tables(positions)
    query_normed = query_raw * query_scale
    key_normed = key_raw * key_scale
    query_rot = rotate(query_normed * gain_own[0], cosine, sine_table).astype(low_type)
    key_rot = rotate(key_normed * gain_own[1], cosine, sine_table).astype(low_type)
    query_heads = query_rot.reshape(seq_rows, own_heads, HD)
    key_heads = key_rot.reshape(seq_rows, own_heads, HD)
    value_heads = value_rows.reshape(seq_rows, own_heads, HD)

    def per_head(spec, left, right):
        return jnp.einsum(spec, left, right, preferred_element_type=high_type)

    scores = per_head("qhd,khd->hqk", query_heads, key_heads) * score_scale
    scores = jnp.where(key_live[None, None, :], scores, masked_score)
    probs = jax.nn.softmax(scores, axis=-1)
    probs_low = probs.astype(low_type)
    attended = per_head("hqk,khd->qhd", probs_low, value_heads).astype(low_type)
    attended = exchange(depth, 2, attended.reshape(ranks, rows, own_width))
    attended = by_head(attended)

    own_positions = (z * 2 + c) * rows + jnp.arange(rows, dtype=jnp.int32)
    live_rows = (own_positions < length_now).astype(high_type)[:, None]
    input_rows = residual_in.astype(high_type)
    middle = input_rows + live_rows * dot(attended, out_weight)
    scale_mid = rms_scale(middle)
    normed_mid_f = middle * scale_mid
    normed_mid = (normed_mid_f * gain_rows[3]).astype(low_type)

    logits = dot(normed_mid, router_weight)
    named = jnp.any(
        routes[:, :, None] == jnp.arange(experts, dtype=jnp.int32)[None, None, :], axis=1
    )
    top = jnp.max(jnp.where(named, logits, -jnp.inf), axis=1, keepdims=True)
    weight_of = jnp.where(named, jnp.exp(jnp.where(named, logits - top, 0.0)), 0.0)
    gates = weight_of / jnp.sum(weight_of, axis=1, keepdims=True)

    grad_rows = cotangent.astype(high_type)
    grad_comb = live_rows * grad_rows
    after = jnp.minimum(scales[0, 0], 0.0)
    own_grads = (grad_comb + after).astype(low_type)
    grads = lax.all_gather(own_grads, GRID, axis=0, tiled=True)
    tokens, gates_all, weights_in, weights_down = spread(
        depth, 3, (normed_mid, gates.T), (sliced_in, sliced_down)
    )
    back, mixed, gate_sums, grad_in, grad_down = run_experts(
        local_experts,
        tokens,
        grads.reshape(tokens.shape),
        gates_all,
        weights_in.reshape(width, -1),
        weights_down.reshape(width, -1),
    )
    grad_mid_norm, grad_gates, sliced_in = collect(
        depth,
        4,
        [back],
        [gate_sums],
        extras=[grad_in.reshape(ranks, chunk_rows, 2 * span)],
    )
    grad_expert_in = unpack(local_experts, sliced_in).reshape(
        chunk_rows, local_experts, ranks, 2, part
    )
    grad_expert_in = grad_expert_in.transpose(0, 1, 3, 2, 4).reshape(expert_in.shape)

    grad_gates = grad_gates.T
    grad_chosen = gates * (grad_gates - jnp.sum(gates * grad_gates, axis=1, keepdims=True))
    grad_logits = grad_chosen.astype(low_type)
    grad_mid_norm = grad_mid_norm + dot_t(grad_logits, router_weight)
    grad_router = t_dot(normed_mid, grad_logits)

    grad_mid_rows, grad_gain_mid = rms_back(grad_mid_norm, normed_mid_f, scale_mid, gain_rows[3])
    grad_middle = grad_rows + grad_mid_rows
    grad_branch = (live_rows * grad_middle).astype(low_type)

    grad_attended = by_rank(dot_t(grad_branch, out_weight).astype(low_type))
    grad_attended = exchange(depth, 6, grad_attended)
    grad_heads = grad_attended.reshape(seq_rows, own_heads, HD)
    grad_probs = per_head("qhd,khd->hqk", grad_heads, value_heads)
    inner_rows = jnp.sum(probs * grad_probs, axis=-1, keepdims=True)
    grad_scores = (probs * (grad_probs - inner_rows)).astype(low_type)
    grad_query = per_head("hqk,khd->qhd", grad_scores, key_heads) * score_scale
    grad_key = per_head("hqk,qhd->khd", grad_scores, query_heads) * score_scale
    grad_value = per_head("hqk,qhd->khd", probs_low, grad_heads).astype(low_type)
    grad_query = rotate(grad_query.reshape(seq_rows, own_width), cosine, -sine_table)
    grad_key = rotate(grad_key.reshape(seq_rows, own_width), cosine, -sine_table)
    query_inner = grad_query * gain_own[0]
    key_inner = grad_key * gain_own[1]
    inner = jnp.stack(
        [
            jnp.sum(query_inner * query_normed, axis=1),
            jnp.sum(key_inner * key_normed, axis=1),
        ]
    )
    inner = sum_column(7, inner) / width
    query_back = query_scale * (query_inner - query_normed * inner[0][:, None])
    key_back = key_scale * (key_inner - key_normed * inner[1][:, None])
    grad_raw = jnp.concatenate(
        [
            query_back.astype(low_type),
            key_back.astype(low_type),
            grad_value.reshape(seq_rows, own_width),
        ],
        axis=1,
    )

    share = dot_t(grad_raw, qkv_weight).astype(low_type).reshape(ranks, rows, width)
    grad_norm_in = collect_column(depth, 8, share)

    scale_in = rms_scale(input_rows)
    grad_in_rows, grad_gain_in = rms_back(
        grad_norm_in, input_rows * scale_in, scale_in, gain_rows[0]
    )
    grad_input = grad_middle + grad_in_rows

    def at_heads(values):
        whole = jnp.zeros((2, own_heads, depth, HD), high_type)
        values = values.reshape(1, own_heads, 1, HD)
        return lax.dynamic_update_slice(whole, values, (c, 0, z, 0)).reshape(width)

    grad_small = jnp.concatenate(
        [
            jnp.stack(
                [
                    grad_gain_in,
                    at_heads(jnp.sum(grad_query * query_normed, axis=0)),
                    at_heads(jnp.sum(grad_key * key_normed, axis=0)),
                    grad_gain_mid,
                ]
            ).T,
            grad_router,
        ],
        axis=1,
    )
    grad_small = jnp.pad(grad_small, ((0, 0), (0, 128 - grad_small.shape[1])))
    grad_out = t_dot(attended, grad_branch).astype(low_type)
    grad_qkv = t_dot(normed_in, grad_raw).astype(low_type)
    combined, grad_out, grad_small, grad_qkv, sliced_down = collect(
        depth,
        5,
        [mixed, grad_out.reshape(-1, weight_rows, width)],
        [grad_small.reshape(-1, weight_rows, 128)],
        [grad_qkv.reshape(columns, -1, 3 * own_width)],
        [grad_down.reshape(ranks, chunk_rows, span)],
    )
    grad_expert_down = unpack(local_experts, sliced_down).reshape(
        chunk_rows, ranks, local_experts, part
    )
    grad_expert_down = grad_expert_down.transpose(0, 2, 1, 3).reshape(expert_down.shape)
    output = middle + live_rows * combined
    return (
        output,
        grad_input,
        grad_qkv,
        grad_out,
        grad_small[:, :4].T,
        grad_small[:, 4 : 4 + experts],
        grad_expert_in,
        grad_expert_down,
    )


def slot_index(route_rows, experts, capacity):
    flat_routes = route_rows.reshape(-1)
    onehot = (flat_routes[:, None] == jnp.arange(experts, dtype=jnp.int32)[None, :]).astype(
        jnp.int32
    )
    rows = jnp.arange(flat_routes.shape[0], dtype=jnp.int32)
    earlier = (rows[None, :] < rows[:, None]).astype(jnp.bfloat16)
    before = jnp.dot(
        earlier, onehot.astype(jnp.bfloat16), preferred_element_type=jnp.float32
    ).astype(jnp.int32)
    rank_rows = jnp.sum(before * onehot, axis=1)
    return flat_routes * capacity + rank_rows


def head_scores(query_rot, key_all, key_live):
    row_count = query_rot.shape[0]
    query_heads = query_rot.reshape(row_count, HEADS, HD)
    key_heads = key_all.reshape(key_all.shape[0], HEADS, HD)
    raw_scores = jnp.einsum(
        "qhd,khd->hqk", query_heads, key_heads, preferred_element_type=jnp.float32
    ) * HD ** (-0.5)
    return jnp.where(key_live[None, None, :], raw_scores, masked_score)


def to_owners(buffer):
    return lax.all_to_all(buffer, "expert", split_axis=0, concat_axis=0, tiled=True)


def from_owners(buffer):
    return lax.all_to_all(buffer, "expert", split_axis=0, concat_axis=0, tiled=True)


def shards(
    residual_in,
    cotangent,
    lengths,
    routes,
    attn_qkv,
    attn_out,
    gains,
    router,
    expert_in,
    expert_down,
):
    tok_rows, model_width = residual_in.shape
    top_count = routes.shape[1]
    owners = lax.axis_size("expert")
    local_experts = expert_in.shape[1]
    experts = local_experts * owners
    capacity = tok_rows * top_count * 2 // experts
    local_slots = local_experts * capacity
    seq_rows = tok_rows * lax.axis_size("dp")
    score_scale = HD ** (-0.5)
    qkv_weights, out_weight, gain_low, router_weight = (
        lax.all_gather(attn_qkv.astype(low_type), ("expert", "dp"), axis=1, tiled=True),
        lax.all_gather(attn_out.astype(low_type), ("expert", "dp"), axis=0, tiled=True),
        lax.all_gather(gains.astype(low_type), ("expert", "dp"), axis=1, tiled=True),
        lax.all_gather(router.astype(low_type), ("expert", "dp"), axis=0, tiled=True),
    )
    gain_rows = gain_low.astype(high_type)
    input_rows = residual_in.astype(high_type)
    scale_in = rms_scale(input_rows)
    normed_in_f = input_rows * scale_in
    normed_in = (normed_in_f * gain_rows[0]).astype(low_type)
    query_raw = jnp.dot(normed_in, qkv_weights[0], preferred_element_type=high_type)
    key_raw = jnp.dot(normed_in, qkv_weights[1], preferred_element_type=high_type)
    value_rows = jnp.dot(normed_in, qkv_weights[2], preferred_element_type=high_type).astype(
        low_type
    )
    positions = lax.axis_index("dp") * tok_rows + jnp.arange(tok_rows, dtype=jnp.int32)
    length_now = lengths[0]
    live_rows = (positions < length_now).astype(high_type)[:, None]
    key_live = jnp.arange(seq_rows, dtype=jnp.int32) < length_now
    cosine, sine_table = angle_tables(positions)
    query_scale = rms_scale(query_raw)
    query_normed = query_raw * query_scale
    query_rot = rotate(query_normed * gain_rows[1], cosine, sine_table).astype(low_type)
    key_scale = rms_scale(key_raw)
    key_normed = key_raw * key_scale
    key_rot = rotate(key_normed * gain_rows[2], cosine, sine_table).astype(low_type)
    key_all = lax.all_gather(key_rot, "dp", axis=0, tiled=True)
    value_all = lax.all_gather(value_rows, "dp", axis=0, tiled=True)
    scores = head_scores(query_rot, key_all, key_live)
    top_score = jnp.max(scores, axis=-1, keepdims=True)
    exp_scores = jnp.exp(scores - top_score)
    row_total = jnp.sum(exp_scores, axis=-1, keepdims=True)
    weights_low = (exp_scores / row_total).astype(low_type)
    log_total = top_score + jnp.log(row_total)
    value_heads = value_all.reshape(seq_rows, HEADS, HD)
    attended = jnp.einsum(
        "hqk,khd->qhd", weights_low, value_heads, preferred_element_type=high_type
    )
    attended = attended.reshape(tok_rows, model_width).astype(low_type)
    branch = jnp.dot(attended, out_weight, preferred_element_type=high_type)
    middle = input_rows + live_rows * branch
    scale_mid = rms_scale(middle)
    normed_mid_f = middle * scale_mid
    normed_mid = (normed_mid_f * gain_rows[3]).astype(low_type)
    logits = jnp.dot(normed_mid, router_weight, preferred_element_type=high_type)
    selector = (routes[:, :, None] == jnp.arange(experts, dtype=jnp.int32)[None, None, :]).astype(
        high_type
    )
    chosen = jnp.einsum("te,tje->tj", logits, selector)
    gate_weights = jax.nn.softmax(chosen, axis=-1)
    slot_rows = slot_index(routes, experts, capacity)
    token_of = jnp.arange(slot_rows.shape[0], dtype=jnp.int32) // top_count
    send_rows = (
        jnp.zeros((experts * capacity, model_width), low_type)
        .at[slot_rows]
        .set(normed_mid[token_of])
    )
    rows_recv = lax.all_to_all(
        send_rows.reshape(owners, local_slots, model_width),
        "expert",
        split_axis=0,
        concat_axis=0,
        tiled=True,
    )
    rows_recv = rows_recv.reshape(owners, local_experts, capacity, model_width)
    weights_in, weights_down = (
        lax.all_gather(expert_in.astype(low_type), "dp", axis=0, tiled=True),
        lax.all_gather(expert_down.astype(low_type), "dp", axis=0, tiled=True),
    )
    both_parts = jnp.einsum(
        "sxmd,dxkf->sxmkf", rows_recv, weights_in, preferred_element_type=high_type
    )
    gate_part = both_parts[:, :, :, 0, :]
    up_part = both_parts[:, :, :, 1, :]
    hidden = (jax.nn.silu(gate_part) * up_part).astype(low_type)
    produced = jnp.einsum(
        "sxmf,dxf->sxmd", hidden, weights_down, preferred_element_type=high_type
    ).astype(low_type)
    returned = from_owners(produced.reshape(owners, local_slots, model_width))
    returned = returned.reshape(experts * capacity, model_width)
    picked = returned[slot_rows].reshape(tok_rows, top_count, model_width).astype(high_type)
    combined = jnp.sum(gate_weights[:, :, None] * picked, axis=1)
    output = middle + live_rows * combined
    grad_rows = cotangent.astype(high_type)
    grad_comb = live_rows * grad_rows
    grad_gates = jnp.einsum("tjd,td->tj", picked, grad_comb)
    grad_chosen = gate_weights * (
        grad_gates - jnp.sum(gate_weights * grad_gates, axis=-1, keepdims=True)
    )
    grad_logits = jnp.einsum("tj,tje->te", grad_chosen, selector).astype(low_type)
    grad_send = (
        (gate_weights[:, :, None] * grad_comb[:, None, :]).astype(low_type).reshape(-1, model_width)
    )
    grad_buffer = (
        jnp.zeros((experts * capacity, model_width), low_type).at[slot_rows].set(grad_send)
    )
    grad_recv = to_owners(grad_buffer.reshape(owners, local_slots, model_width))
    grad_recv = grad_recv.reshape(owners, local_experts, capacity, model_width)
    grad_hidden = jnp.einsum(
        "sxmd,dxf->sxmf", grad_recv, weights_down, preferred_element_type=high_type
    )
    sigma_gate = jax.nn.sigmoid(gate_part)
    grad_gate = grad_hidden * up_part * sigma_gate * (1.0 + gate_part * (1.0 - sigma_gate))
    grad_up = grad_hidden * gate_part * sigma_gate
    grad_both = jnp.stack([grad_gate, grad_up], axis=3).astype(low_type)
    grad_rows_out = jnp.einsum(
        "sxmkf,dxkf->sxmd", grad_both, weights_in, preferred_element_type=high_type
    ).astype(low_type)
    grad_back = from_owners(grad_rows_out.reshape(owners, local_slots, model_width))
    grad_back = grad_back.reshape(experts * capacity, model_width)
    grad_mid_norm = jnp.sum(
        grad_back[slot_rows].reshape(tok_rows, top_count, model_width).astype(high_type), axis=1
    )
    grad_mid_norm = grad_mid_norm + jnp.dot(
        grad_logits, router_weight.T, preferred_element_type=high_type
    )
    grad_router = jnp.dot(normed_mid.T, grad_logits, preferred_element_type=high_type)
    row_piece = rows_recv
    grad_expert_in = lax.psum_scatter(
        jnp.einsum(
            "sxmd,sxmkf->dxkf", row_piece, grad_both, preferred_element_type=high_type
        ).astype(jnp.bfloat16),
        "dp",
        scatter_dimension=0,
        tiled=True,
    ).astype(jnp.float32)
    row_piece = grad_recv
    grad_expert_down = lax.psum_scatter(
        jnp.einsum("sxmd,sxmf->dxf", row_piece, hidden, preferred_element_type=high_type).astype(
            jnp.bfloat16
        ),
        "dp",
        scatter_dimension=0,
        tiled=True,
    ).astype(jnp.float32)
    grad_mid_rows, grad_gain_mid = rms_back(grad_mid_norm, normed_mid_f, scale_mid, gain_rows[3])
    grad_middle = grad_rows + grad_mid_rows
    grad_branch = (live_rows * grad_middle).astype(low_type)
    grad_out_weight = jnp.dot(attended.T, grad_branch, preferred_element_type=high_type)
    grad_attended = jnp.dot(grad_branch, out_weight.T, preferred_element_type=high_type).astype(
        low_type
    )
    scores = head_scores(query_rot, key_all, key_live)
    probs_full = jnp.exp(scores - log_total)
    grad_heads = grad_attended.reshape(tok_rows, HEADS, HD)
    value_heads = value_all.reshape(seq_rows, HEADS, HD)
    key_heads = key_all.reshape(seq_rows, HEADS, HD)
    query_heads = query_rot.reshape(tok_rows, HEADS, HD)
    grad_probs = jnp.einsum(
        "qhd,khd->hqk", grad_heads, value_heads, preferred_element_type=high_type
    )
    inner_rows = jnp.sum(probs_full * grad_probs, axis=-1, keepdims=True)
    grad_scores = (probs_full * (grad_probs - inner_rows)).astype(low_type)
    grad_query = (
        jnp.einsum(
            "hqk,khd->qhd", grad_scores, key_heads, preferred_element_type=high_type
        ).reshape(tok_rows, model_width)
        * score_scale
    )
    grad_key_part = (
        jnp.einsum(
            "hqk,qhd->khd", grad_scores, query_heads, preferred_element_type=high_type
        ).reshape(seq_rows, model_width)
        * score_scale
    )
    grad_value_part = jnp.einsum(
        "hqk,qhd->khd", probs_full.astype(low_type), grad_heads, preferred_element_type=high_type
    ).reshape(seq_rows, model_width)
    grad_key_sum, grad_value_sum = (
        lax.psum_scatter(
            grad_key_part.astype(jnp.bfloat16), "dp", scatter_dimension=0, tiled=True
        ).astype(jnp.float32),
        lax.psum_scatter(
            grad_value_part.astype(jnp.bfloat16), "dp", scatter_dimension=0, tiled=True
        ).astype(jnp.float32),
    )
    grad_value = grad_value_sum.astype(low_type)
    grad_key_raw, grad_key_gain = rms_back(
        rotate(grad_key_sum, cosine, -sine_table), key_normed, key_scale, gain_rows[2]
    )
    grad_query_raw, grad_query_gain = rms_back(
        rotate(grad_query, cosine, -sine_table), query_normed, query_scale, gain_rows[1]
    )
    grad_key_raw = grad_key_raw.astype(low_type)
    grad_query_raw = grad_query_raw.astype(low_type)
    grad_norm_in = jnp.dot(grad_query_raw, qkv_weights[0].T, preferred_element_type=high_type)
    grad_norm_in = grad_norm_in + jnp.dot(
        grad_key_raw, qkv_weights[1].T, preferred_element_type=high_type
    )
    grad_norm_in = grad_norm_in + jnp.dot(
        grad_value, qkv_weights[2].T, preferred_element_type=high_type
    )
    grad_qkv_local = jnp.stack(
        [
            jnp.dot(normed_in.T, grad_query_raw, preferred_element_type=high_type),
            jnp.dot(normed_in.T, grad_key_raw, preferred_element_type=high_type),
            jnp.dot(normed_in.T, grad_value, preferred_element_type=high_type),
        ]
    )
    grad_in_rows, grad_gain_in = rms_back(grad_norm_in, normed_in_f, scale_in, gain_rows[0])
    grad_input = grad_middle + grad_in_rows
    grad_gains_local = jnp.stack([grad_gain_in, grad_query_gain, grad_key_gain, grad_gain_mid])
    summed = (
        lax.psum_scatter(grad_qkv_local, ("expert", "dp"), scatter_dimension=1, tiled=True),
        lax.psum_scatter(grad_out_weight, ("expert", "dp"), scatter_dimension=0, tiled=True),
        lax.psum_scatter(grad_gains_local, ("expert", "dp"), scatter_dimension=1, tiled=True),
        lax.psum_scatter(grad_router, ("expert", "dp"), scatter_dimension=0, tiled=True),
    )
    return (
        output,
        grad_input,
        summed[0],
        summed[1],
        summed[2],
        summed[3],
        grad_expert_in,
        grad_expert_down,
    )


def solution(mesh):
    column_count, rank_count = mesh.shape["expert"], mesh.shape["dp"]
    depth = rank_count // 2
    tiled = column_count == 4 and rank_count % 2 == 0 and HEADS == column_count * depth
    if tiled:
        mesh = Mesh(mesh.devices.reshape(2, 2, depth, 2), GRID)
        column, rank, body = ("ey", "ex"), SEQ, grid_shards
    else:
        column, rank, body = ("expert",), ("dp",), shards
    device = column + rank
    placed = (
        P(device, None),
        P(device, None),
        P(column),
        P(device, None),
        P(None, device, None),
        P(device, None),
        P(None, device),
        P(device, None),
        P(rank, column, None, None),
        P(rank, column, None),
    )
    return jax.shard_map(
        body,
        mesh=mesh,
        in_specs=placed,
        out_specs=placed[:1] * 2 + placed[4:],
        check_vma=False,
    )
```

```python
import functools

import jax
import jax.numpy as jnp
from jax import lax
from jax.experimental import pallas as pl
from jax.experimental.pallas import tpu as pltpu
from jax.sharding import Mesh
from jax.sharding import PartitionSpec as P

HEADS = 16
HD = 128

epsilon = 1e-05
rope_base = 10000.0
masked_score = -1000000000.0

low_type = jnp.bfloat16
high_type = jnp.float32


def rms_scale(values):
    return lax.rsqrt(jnp.mean(values * values, axis=-1, keepdims=True) + epsilon)


def angle_tables(positions):
    frequency = rope_base ** (-2.0 * jnp.arange(HD // 2, dtype=jnp.float32) / HD)
    angles = positions.astype(jnp.float32)[:, None] * frequency[None, :]
    return (jnp.cos(angles), jnp.sin(angles))


def rotate(values, cosine, sine_table):
    row_count, width = values.shape
    shaped = values.reshape(row_count, width // HD, 2, HD // 2)
    first_half = shaped[:, :, 0, :]
    second_half = shaped[:, :, 1, :]
    cos_rows = cosine[:, None, :]
    sin_rows = sine_table[:, None, :]
    turned = jnp.stack(
        [
            first_half * cos_rows - second_half * sin_rows,
            second_half * cos_rows + first_half * sin_rows,
        ],
        axis=2,
    )
    return turned.reshape(row_count, width)


def rms_back(grad_rows, normed, scale, gain):
    grad_normed = grad_rows * gain
    inner = jnp.mean(grad_normed * normed, axis=-1, keepdims=True)
    return (scale * grad_normed - normed * scale * inner, jnp.sum(grad_rows * normed, axis=0))


def dot(left, right):
    return jnp.dot(left, right, preferred_element_type=high_type)


def dot_t(left, right):
    return lax.dot_general(left, right, (((1,), (1,)), ((), ())), preferred_element_type=high_type)


def t_dot(left, right):
    return lax.dot_general(left, right, (((0,), (0,)), ((), ())), preferred_element_type=high_type)


GRID = ("ey", "ex", "dz", "dc")
SEQ = ("dz", "dc")


MESH_ID = pl.DeviceIdType.MESH


class Place:
    def __init__(self, depth):
        self.depth = depth
        self.y, self.x, self.z, self.c = (lax.axis_index(name) for name in GRID)

    def near_of(self, core):
        return self.y + core * (1 - 2 * self.y), self.x + (1 - core) * (1 - 2 * self.x)

    def far_of(self, core):
        return self.near_of(1 - core)

    def along(self, step):
        return lax.rem(self.z + step, self.depth)

    def next_z(self, k):
        first = self.z - 1 + 2 * lax.div(4 - self.z, 4)
        last = 3 * lax.div(3 - self.z, 2)
        return (self.z, first, 6 - self.z - first - last, last)[k]

    def block(self, column, z, core):
        return ((column[0] * 2 + column[1]) * self.depth + z) * 2 + core

    @property
    def own_column(self):
        return self.y, self.x

    @property
    def other_column(self):
        return 1 - self.y, 1 - self.x

    def core(self):
        return self.y, self.x, self.z, 1 - self.c

    def chip(self, step, core=None):
        return self.y, self.x, self.along(step), self.c if core is None else core

    def near(self):
        return (*self.near_of(self.c), self.z, self.c)

    def far(self):
        return (*self.far_of(self.c), self.z, self.c)


def meet(partners):
    barrier = pltpu.get_barrier_semaphore()
    for partner in partners:
        pl.semaphore_signal(barrier, inc=1, device_id=partner, device_id_type=MESH_ID)
    pl.semaphore_wait(barrier, len(partners))


def remote(source, target, sems, slot, partner):
    return pltpu.make_async_remote_copy(
        src_ref=source,
        dst_ref=target,
        send_sem=sems[0].at[slot],
        recv_sem=sems[1].at[slot],
        device_id=partner,
        device_id_type=MESH_ID,
    )


def pair(count):
    return [pltpu.SemaphoreType.DMA((count,)), pltpu.SemaphoreType.DMA((count,))]


def in_hbm(count):
    return [pl.BlockSpec(memory_space=pl.ANY)] * count


def spread_kernel(depth, count, extra, *refs):
    whole = count + extra
    sources, targets, sems = refs[:count], refs[whole : whole + count], refs[2 * whole :]
    extra_sources, extra_targets = refs[count:whole], refs[whole + count : 2 * whole]
    extra_sems = sems[9 * count :]
    at = Place(depth)
    others = range(1, depth)
    ranks = [(k, core) for k in range(depth) for core in range(2) if k or core]
    peers = [at.chip(k, lax.rem(at.c + core, 2)) for k, core in ranks]
    meet([at.near(), at.far()] + peers)
    started, local = [], []

    def push(n, source, index, kind, slot, partner):
        copy = remote(source, targets[n].at[index], sems[9 * n + 2 * kind :], slot, partner)
        copy.start()
        started.append(copy)

    def arrive(n, index, kind, slot):
        target = targets[n].at[index]
        remote(target, target, sems[9 * n + 2 * kind :], slot, at.core()).wait_recv()

    z_kind, near_kind, far_kind, core_kind = range(4)
    own = at.block(at.own_column, at.z, at.c)
    for n in range(count):
        push(n, sources[n], own, z_kind, at.z, (at.y, at.x, at.next_z(1), at.c))
        push(n, sources[n], own, near_kind, 0, at.near())
        push(n, sources[n], own, far_kind, 0, at.far())
        push(n, sources[n], own, core_kind, 0, at.core())
        copy = pltpu.make_async_copy(sources[n], targets[n].at[own], sems[9 * n + 8])
        copy.start()
        local.append(copy)

    inner = lax.rem(at.z, depth - 1) != 0
    onward = (at.z + 1, at.z + 1, at.z - 1, 3 * at.z - 3)

    def forward(n, source, k):
        z = at.next_z(k)
        return pltpu.make_async_remote_copy(
            src_ref=source,
            dst_ref=targets[n].at[at.block(at.own_column, z, at.c)],
            send_sem=sems[9 * n].at[z if k else depth],
            recv_sem=sems[9 * n + 1].at[z],
            device_id=(at.y, at.x, onward[k], at.c),
            device_id_type=MESH_ID,
        )

    @pl.when(inner)
    def _():
        for n in range(count):
            forward(n, sources[n], 0).start()

    for k in others:
        index = at.block(at.own_column, at.next_z(k), at.c)
        for n in range(count):
            arrive(n, index, z_kind, at.next_z(k))

        @pl.when(inner)
        def _(index=index, k=k):
            for n in range(count):
                forward(n, targets[n].at[index], k).start()

        for n in range(count):
            push(n, targets[n].at[index], index, near_kind, k, at.near())
            push(n, targets[n].at[index], index, far_kind, k, at.far())
            push(n, targets[n].at[index], index, core_kind, k, at.core())
    own_rank = at.z * 2 + at.c
    for n in range(extra):
        for slot, there in enumerate(peers):
            copy = remote(
                extra_sources[n].at[there[2] * 2 + there[3]],
                extra_targets[n].at[own_rank],
                extra_sems[3 * n :],
                slot,
                there,
            )
            copy.start()
            started.append(copy)
        copy = pltpu.make_async_copy(
            extra_sources[n].at[own_rank], extra_targets[n].at[own_rank], extra_sems[3 * n + 2]
        )
        copy.start()
        local.append(copy)
    for k in range(depth):
        index = at.block(at.near_of(at.c), at.next_z(k), at.c)
        for n in range(count):
            arrive(n, index, near_kind, k)
            push(n, targets[n].at[index], index, far_kind, depth + k, at.far())
            push(n, targets[n].at[index], index, core_kind, depth + k, at.core())
    for j in range(2 * depth):
        column = at.far_of(at.c) if j < depth else at.other_column
        index = at.block(column, at.next_z(j % depth), at.c)
        for n in range(count):
            arrive(n, index, far_kind, j)
            push(n, targets[n].at[index], index, core_kind, 2 * depth + j, at.core())
    core = 1 - at.c
    columns = [at.own_column, at.near_of(core), at.far_of(core), at.other_column]
    for j in range(4 * depth):
        index = at.block(columns[j // depth], at.next_z(j % depth), core)
        for n in range(count):
            arrive(n, index, core_kind, j)
    for n in range(extra):
        for slot, (k, core) in enumerate(ranks):
            target = extra_targets[n].at[at.along(depth - k) * 2 + lax.rem(at.c + core, 2)]
            remote(target, target, extra_sems[3 * n :], slot, at.core()).wait_recv()

    @pl.when(inner)
    def _():
        for n in range(count):
            forward(n, sources[n], 0).wait_send()
            for k in others:
                index = at.block(at.own_column, at.next_z(k), at.c)
                forward(n, targets[n].at[index], k).wait_send()

    for copy in started:
        copy.wait_send()
    for copy in local:
        copy.wait()


def spread(depth, ident, arrays, extras=()):
    sems = []
    for _ in arrays:
        sems += pair(depth + 1) + pair(depth) + pair(2 * depth) + pair(4 * depth)
        sems.append(pltpu.SemaphoreType.DMA)
    for _ in extras:
        sems += pair(2 * depth - 1) + [pltpu.SemaphoreType.DMA]
    count = len(arrays) + len(extras)
    shapes = [((8 * depth,) + a.shape, a.dtype) for a in arrays]
    shapes += [(a.shape, a.dtype) for a in extras]
    return pl.pallas_call(
        functools.partial(spread_kernel, depth, len(arrays), len(extras)),
        out_shape=[jax.ShapeDtypeStruct(*shape) for shape in shapes],
        in_specs=in_hbm(count),
        out_specs=in_hbm(count),
        scratch_shapes=sems,
        compiler_params=pltpu.CompilerParams(
            collective_id=ident, has_side_effects=True, vmem_limit_bytes=60 << 20
        ),
        cost_estimate=pl.CostEstimate(
            flops=0,
            bytes_accessed=sum(64 * depth * a.size * a.dtype.itemsize for a in arrays),
            transcendentals=0,
        ),
    )(*arrays, *extras)


def sum_rows(target, lead, terms):
    rows = target.shape[-2]
    tile = min(rows, 16)

    def body(i, carry):
        at = pl.ds(pl.multiple_of(i * tile, tile), tile)
        total = terms[0][0][(*terms[0][1], at, slice(None))].astype(high_type)
        for ref, where in terms[1:]:
            total = total + ref[(*where, at, slice(None))].astype(high_type)
        target[(*lead, at, slice(None))] = total.astype(target.dtype)
        return carry

    lax.fori_loop(0, rows // tile, body, 0)


def collect_kernel(depth, local, counts, *refs):
    rest = iter(refs)

    def take(count):
        return [next(rest) for _ in range(count)]

    mains, smalls, shareds, extras = (take(count) for count in counts)
    halves = take(2 if local else 0)
    main_totals, small_totals, shared_totals, extra_outs = (take(count) for count in counts)
    unpacked = take(1 if local else 0)
    main_buffers = [take(5) for _ in mains]
    small_buffers = [take(5) for _ in smalls]
    shared_buffers = [take(3) for _ in shareds]
    shared_outs = [take(1)[0] for _ in shareds]
    main_sems = [take(9) for _ in mains]
    small_sems = [take(9) for _ in smalls]
    shared_sems = [take(7) for _ in shareds]
    extra_sems = [take(3) for _ in extras]
    at = Place(depth)
    ranks = [(k, core) for k in range(depth) for core in range(2) if k or core]
    peers = [at.chip(k, lax.rem(at.c + core, 2)) for k, core in ranks]
    meet([at.near(), at.far()] + peers)
    started = []
    own_rank = at.z * 2 + at.c

    def columns(core):
        return at.other_column, at.far_of(core), at.near_of(core), at.own_column

    def number(column):
        return column[0] * 2 + column[1]

    def push(copy):
        copy.start()
        started.append(copy)

    def arrive(buffer, pair_of, slot):
        remote(buffer.at[slot], buffer.at[slot], pair_of, slot, at.core()).wait_recv()

    def piece(ref, rank):
        rows = ref.shape[0] // (2 * depth)
        return ref.at[pl.ds(pl.multiple_of(rank * rows, rows), rows)]

    def block(group, k, core):
        return at.block(columns(core)[group], at.along(1 + k), core)

    def main_load(n, group, k):
        slot = group * depth + k
        return pltpu.make_async_copy(
            mains[n].at[block(group, k, at.c)], main_buffers[n][0].at[slot], main_sems[n][8].at[slot]
        )

    def main_cross(n, group, k):
        slot = group * depth + k
        source = mains[n].at[block(group, k, 1 - at.c)]
        push(remote(source, main_buffers[n][1].at[slot], main_sems[n][0:2], slot, at.core()))
        main_load(n, group, k).start()

    def main_sum(n, group, k, more):
        mine, crossed = main_buffers[n][:2]
        slot = group * depth + k
        main_load(n, group, k).wait()
        arrive(crossed, main_sems[n][0:2], slot)
        terms = [(mine, (slot,)), (crossed, (slot,))] + more
        if slot < 4 * depth - 1:
            sum_rows(mine, (slot,), terms)
        else:
            sum_rows(main_totals[n], (), terms)
        return mine.at[slot]

    def main_far(n, k):
        buffers, sems = main_buffers[n], main_sems[n]
        for group in range(2):
            slot = group * depth + k
            total = main_sum(n, group, k, [])
            push(remote(total, buffers[2].at[slot], sems[2:4], slot, at.far()))

    def main_near(n, k):
        buffers, sems = main_buffers[n], main_sems[n]
        arrive(buffers[2], sems[2:4], k)
        total = main_sum(n, 2, k, [(buffers[2], (k,))])
        push(remote(total, buffers[3].at[k], sems[4:6], k, at.near()))

    def main_own(n, k):
        buffers, sems = main_buffers[n], main_sems[n]
        arrive(buffers[2], sems[2:4], depth + k)
        arrive(buffers[3], sems[4:6], k)
        total = main_sum(n, 3, k, [(buffers[2], (depth + k,)), (buffers[3], (k,))])
        if k < depth - 1:
            push(remote(total, buffers[4].at[k], sems[6:8], k, at.chip(1 + k)))

    def small_load(n, group):
        return pltpu.make_async_copy(
            smalls[n].at[at.c, number(columns(at.c)[group])],
            small_buffers[n][0].at[group],
            small_sems[n][8].at[group],
        )

    def small_cross():
        for n, (part, buffers, sems) in enumerate(zip(smalls, small_buffers, small_sems)):
            for group in range(4):
                source = part.at[1 - at.c, number(columns(1 - at.c)[group])]
                push(remote(source, buffers[1].at[group], sems[0:2], group, at.core()))
                small_load(n, group).start()

    def small_sum(n, group, more):
        mine, crossed = small_buffers[n][:2]
        small_load(n, group).wait()
        arrive(crossed, small_sems[n][0:2], group)
        for j in range(depth):
            terms = [(mine, (group, j)), (crossed, (group, j))]
            sum_rows(mine, (group, j), terms + [(ref, (i, j)) for ref, i in more])
        return mine.at[group]

    def small_far():
        for n, (buffers, sems) in enumerate(zip(small_buffers, small_sems)):
            for group in range(2):
                total = small_sum(n, group, [])
                push(remote(total, buffers[2].at[group], sems[2:4], group, at.far()))

    def small_near():
        for n, (buffers, sems) in enumerate(zip(small_buffers, small_sems)):
            arrive(buffers[2], sems[2:4], 0)
            total = small_sum(n, 2, [(buffers[2], 0)])
            push(remote(total, buffers[3].at[0], sems[4:6], 0, at.near()))

    def small_own():
        for n, (buffers, sems) in enumerate(zip(small_buffers, small_sems)):
            arrive(buffers[2], sems[2:4], 1)
            arrive(buffers[3], sems[4:6], 0)
            total = small_sum(n, 3, [(buffers[2], 1), (buffers[3], 0)])
            for k in range(1, depth):
                there = at.chip(k)
                source = total.at[there[2]]
                push(remote(source, buffers[4].at[k - 1], sems[6:8], k - 1, there))

    def shared_load(n, i):
        return pltpu.make_async_copy(
            shareds[n].at[number(columns(at.c)[2 + i])], shared_buffers[n][0].at[i], shared_sems[n][0].at[i]
        )

    def shared_far():
        for n, (part, buffers, sems) in enumerate(zip(shareds, shared_buffers, shared_sems)):
            for i in range(2):
                source = part.at[number(columns(at.c)[i])]
                push(remote(source, buffers[1].at[i], sems[1:3], i, at.far()))
                shared_load(n, i).start()

    def shared_near():
        for n, ((mine, far_in, near_in), sems) in enumerate(zip(shared_buffers, shared_sems)):
            shared_load(n, 0).wait()
            arrive(far_in, sems[1:3], 0)
            sum_rows(mine, (0,), [(mine, (0,)), (far_in, (0,))])
            push(remote(mine.at[0], near_in.at[0], sems[3:5], 0, at.near()))

    def shared_own():
        for n, ((mine, far_in, near_in), sems) in enumerate(zip(shared_buffers, shared_sems)):
            shared_load(n, 1).wait()
            arrive(far_in, sems[1:3], 1)
            arrive(near_in, sems[3:5], 0)
            sum_rows(mine, (1,), [(mine, (1,)), (far_in, (1,)), (near_in, (0,))])
            for slot, there in enumerate(peers):
                source = piece(mine.at[1], there[2] * 2 + there[3])
                push(remote(source, piece(shared_outs[n], own_rank), sems[5:7], slot, there))
            shared_kept(n).start()

    def shared_kept(n):
        mine = shared_buffers[n][0]
        return pltpu.make_async_copy(
            piece(mine.at[1], own_rank), piece(shared_outs[n], own_rank), shared_sems[n][0].at[2]
        )

    def extra_kept(n):
        return pltpu.make_async_copy(
            extras[n].at[own_rank], extra_outs[n].at[own_rank], extra_sems[n][2]
        )

    last = len(mains) - 1
    stages = [(main_far, 0), (main_far, 1), (main_near, 0), (main_own, 0)]
    for k in range(2, depth):
        stages += [(main_far, k), (main_near, k - 1), (main_own, k - 1)]
    stages += [(main_near, depth - 1), (main_own, depth - 1)]
    order = [(stage, n, k) for n in range(len(mains)) for stage, k in stages]
    for n in range(last):
        ahead = [(main_far, n + 1, k) for k in range(2)]
        order = [step for step in order if step not in ahead]
        at_end = order.index((main_near, n, depth - 1))
        order[at_end:at_end] = ahead
    groups = {main_far: (0, 1), main_near: (2,), main_own: (3,)}
    shared_far()
    small_cross()
    for stage, n, k in order:
        for group in groups[stage]:
            main_cross(n, group, k)
    for n in range(len(extras)):
        for slot, there in enumerate(peers):
            source = extras[n].at[there[2] * 2 + there[3]]
            push(remote(source, extra_outs[n].at[own_rank], extra_sems[n][:2], slot, there))
        extra_kept(n).start()
    small_far()
    for stage, n, k in order:
        stage(n, k)
        if (stage, n, k) == (main_far, last, depth - 1) and local:
            unpack_inside(local, *halves, *unpacked)
        if (stage, n, k) == (main_near, 0, 0):
            shared_near()
            small_near()
        if (stage, n, k) == (main_own, 0, 0):
            shared_own()
            small_own()
    for n, (buffers, sems) in enumerate(zip(small_buffers, small_sems)):
        for k in range(depth - 1):
            arrive(buffers[4], sems[6:8], k)
        terms = [(buffers[0], (3, at.z))] + [(buffers[4], (k,)) for k in range(depth - 1)]
        sum_rows(small_totals[n], (), terms)
    for n, (buffers, sems) in enumerate(zip(main_buffers, main_sems)):
        for k in range(depth - 1):
            arrive(buffers[4], sems[6:8], k)
        terms = [(main_totals[n], ())] + [(buffers[4], (k,)) for k in range(depth - 1)]
        sum_rows(main_totals[n], (), terms)
    for slot, (k, core) in enumerate(ranks):
        source = at.along(depth - k) * 2 + lax.rem(at.c + core, 2)
        for n in range(len(shareds)):
            target = piece(shared_outs[n], source)
            remote(target, target, shared_sems[n][5:7], slot, at.core()).wait_recv()
        for n in range(len(extras)):
            target = extra_outs[n].at[source]
            remote(target, target, extra_sems[n][:2], slot, at.core()).wait_recv()
    for n in range(len(shareds)):
        shared_kept(n).wait()
        out, held = shared_totals[n], shared_outs[n]
        count, rows = out.shape[:2]
        heads = held.shape[1] // (count * HD)
        for rank in range(2 * depth):
            for i in range(count):
                for j in range(heads):
                    head = (rank % 2 * heads + j) * depth + rank // 2
                    value = held[rank * rows : (rank + 1) * rows, (i * heads + j) * HD :][:, :HD]
                    out[i, :, head * HD : (head + 1) * HD] = value.astype(out.dtype)
    for n in range(len(extras)):
        extra_kept(n).wait()
    for copy in started:
        copy.wait_send()


def collect(depth, ident, mains, smalls, shareds=(), extras=(), to_unpack=(0,)):
    local, *halves = to_unpack
    dma = pltpu.SemaphoreType.DMA
    peers = 2 * depth - 1

    def by_core(a):
        return a.reshape((4, depth, 2) + a.shape[1:]).transpose(2, 0, 1, 3, 4)

    smalls = [by_core(a) for a in smalls]
    buffers, sems, shapes = [], [], []
    for a in mains:
        for slots in (4 * depth, 4 * depth, 2 * depth, depth, depth - 1):
            buffers.append(pltpu.VMEM((slots,) + a.shape[1:], a.dtype))
        sems += pair(4 * depth) + pair(2 * depth) + pair(depth) + pair(depth - 1)
        sems.append(dma((4 * depth,)))
        shapes.append(jax.ShapeDtypeStruct(a.shape[1:], high_type))
    for a in smalls:
        for slots in ((4, depth), (4, depth), (2, depth), (1, depth), (depth - 1,)):
            buffers.append(pltpu.VMEM(slots + a.shape[3:], a.dtype))
        sems += pair(4) + pair(2) + pair(1) + pair(depth - 1) + [dma((4,))]
        shapes.append(jax.ShapeDtypeStruct(a.shape[3:], high_type))
    for a in shareds:
        buffers += [pltpu.VMEM((slots,) + a.shape[1:], a.dtype) for slots in (2, 2, 1)]
        buffers.append(pltpu.VMEM(a.shape[1:], a.dtype))
        sems += [dma((3,))] + pair(2) + pair(1) + pair(peers)
        shape = (3, a.shape[1] // (2 * depth), a.shape[2] // 3 * 2 * depth)
        shapes.append(jax.ShapeDtypeStruct(shape, high_type))
    for a in extras:
        sems += pair(peers) + [dma]
        shapes.append(jax.ShapeDtypeStruct(a.shape, a.dtype))
    arrays = [*mains, *smalls, *shareds, *extras]
    counts = (len(mains), len(smalls), len(shareds), len(extras))
    if halves:
        lines = halves[0].size // 64
        shapes.append(jax.ShapeDtypeStruct((lines, 128), high_type))
    in_vmem = [pl.BlockSpec(memory_space=pltpu.VMEM)] * (len(arrays) - len(extras))
    return pl.pallas_call(
        functools.partial(collect_kernel, depth, local, counts),
        out_shape=shapes,
        in_specs=in_hbm(len(arrays) + len(halves)),
        out_specs=in_vmem + in_hbm(len(extras) + len(halves) // 2),
        scratch_shapes=buffers + sems,
        compiler_params=pltpu.CompilerParams(
            collective_id=ident, has_side_effects=True, vmem_limit_bytes=60 << 20
        ),
        cost_estimate=pl.CostEstimate(
            flops=0,
            bytes_accessed=sum(16 * a.size * a.dtype.itemsize for a in arrays),
            transcendentals=0,
        ),
    )(*arrays, *halves)


def gather_kernel(depth, local_experts, x_ref, o_ref, w_ref, s_ref, in_ref, down_ref, *refs):
    x_out, o_out, w_out, s_out = refs[:4]
    packed, sems = refs[4:8], refs[8:]
    at = Place(depth)
    ranks = [(k, core) for k in range(depth) for core in range(2) if k or core]
    peers = [at.chip(k, lax.rem(at.c + core, 2)) for k, core in ranks]
    meet([at.near(), at.far()] + peers)
    own, column = at.z * 2 + at.c, at.y * 2 + at.x
    x_z, x_core, o_z, o_near, o_far, o_core, w_sems, s_sems, w_side, s_side = (
        sems[2 * i : 2 * i + 2] for i in range(10)
    )
    started, local = [], []
    inner = lax.rem(at.z, depth - 1) != 0
    onward = (at.z + 1, at.z + 1, at.z - 1, 3 * at.z - 3)
    own_block = at.block(at.own_column, at.z, at.c)

    def push(copy):
        copy.start()
        started.append(copy)

    def arrive(target, pair_of, slot):
        remote(target, target, pair_of, slot, at.core()).wait_recv()

    def x_place(k):
        return x_out.at[at.next_z(k) * 2 + at.c]

    def o_place(k):
        return o_out.at[at.block(at.own_column, at.next_z(k), at.c)]

    def forward(source, target, pair_of, k):
        z = at.next_z(k)
        return pltpu.make_async_remote_copy(
            src_ref=source,
            dst_ref=target,
            send_sem=pair_of[0].at[z if k else depth],
            recv_sem=pair_of[1].at[z],
            device_id=(at.y, at.x, onward[k], at.c),
            device_id_type=MESH_ID,
        )

    for slot, there in enumerate(peers):
        push(remote(s_ref, s_out.at[column, own], s_sems, slot, there))
        source = w_ref.at[there[2] * 2 + there[3]]
        push(remote(source, w_out.at[column, own], w_sems, slot, there))
    first = (at.y, at.x, at.next_z(1), at.c)
    push(remote(o_ref, o_place(0), o_z, at.z, first))
    push(remote(x_ref, x_place(0), x_z, at.z, first))

    @pl.when(inner)
    def _():
        forward(o_ref, o_place(0), o_z, 0).start()
        forward(x_ref, x_place(0), x_z, 0).start()

    push(remote(x_ref, x_place(0), x_core, 0, at.core()))
    push(remote(o_ref, o_place(0), o_near, 0, at.near()))
    push(remote(o_ref, o_place(0), o_far, 0, at.far()))
    push(remote(o_ref, o_place(0), o_core, 0, at.core()))
    for i, (source, target) in enumerate(
        (
            (x_ref, x_place(0)),
            (o_ref, o_place(0)),
            (w_ref.at[own], w_out.at[column, own]),
            (s_ref, s_out.at[column, own]),
        )
    ):
        copy = pltpu.make_async_copy(source, target, sems[20].at[i])
        copy.start()
        local.append(copy)
    near_y, near_x = at.near_of(at.c)
    far_y, far_x = at.far_of(at.c)
    beside, across = near_y * 2 + near_x, far_y * 2 + far_x
    sides = ((s_out, s_side), (w_out, w_side))
    pack(2 * depth, local_experts, in_ref, down_ref, *packed)
    for slot, (j, core) in enumerate(ranks):
        source = at.along(depth - j) * 2 + lax.rem(at.c + core, 2)
        arrive(s_out.at[column, source], s_sems, slot)
        arrive(w_out.at[column, source], w_sems, slot)
    for copy in local:
        copy.wait()
    for target, pair_of in sides:
        push(remote(target.at[column], target.at[column], pair_of, 0, at.near()))
        push(remote(target.at[column], target.at[column], pair_of, 1, at.far()))
    for k in range(1, depth):
        arrive(o_place(k), o_z, at.next_z(k))

        @pl.when(inner)
        def _(k=k):
            forward(o_place(k), o_place(k), o_z, k).start()

        push(remote(o_place(k), o_place(k), o_near, k, at.near()))
        push(remote(o_place(k), o_place(k), o_far, k, at.far()))
        push(remote(o_place(k), o_place(k), o_core, k, at.core()))
        arrive(x_place(k), x_z, at.next_z(k))

        @pl.when(inner)
        def _(k=k):
            forward(x_place(k), x_place(k), x_z, k).start()

        push(remote(x_place(k), x_place(k), x_core, k, at.core()))
    for target, pair_of in sides:
        arrive(target.at[beside], pair_of, 0)
        push(remote(target.at[beside], target.at[beside], pair_of, 2, at.far()))
    for k in range(depth):
        target = o_out.at[at.block(at.near_of(at.c), at.next_z(k), at.c)]
        arrive(target, o_near, k)
        push(remote(target, target, o_far, depth + k, at.far()))
        push(remote(target, target, o_core, depth + k, at.core()))
    for j in range(2 * depth):
        place = at.far_of(at.c) if j < depth else at.other_column
        target = o_out.at[at.block(place, at.next_z(j % depth), at.c)]
        arrive(target, o_far, j)
        push(remote(target, target, o_core, 2 * depth + j, at.core()))
    for target, pair_of in sides:
        arrive(target.at[across], pair_of, 1)
        arrive(target.at[3 - column], pair_of, 2)
    for k in range(depth):
        arrive(x_out.at[at.next_z(k) * 2 + 1 - at.c], x_core, k)
    core = 1 - at.c
    places = [at.own_column, at.near_of(core), at.far_of(core), at.other_column]
    for j in range(4 * depth):
        index = at.block(places[j // depth], at.next_z(j % depth), core)
        arrive(o_out.at[index], o_core, j)

    @pl.when(inner)
    def _():
        forward(x_ref, x_place(0), x_z, 0).wait_send()
        forward(o_ref, o_place(0), o_z, 0).wait_send()
        for k in range(1, depth):
            forward(x_place(k), x_place(k), x_z, k).wait_send()
            forward(o_place(k), o_place(k), o_z, k).wait_send()

    for copy in started:
        copy.wait_send()


def gather(depth, ident, x, o, w, s, expert_in, expert_down):
    chunk, local = expert_in.shape[:2]
    ranks = 2 * depth
    sems = pair(depth + 1) + pair(depth) + pair(depth + 1) + pair(depth) + pair(2 * depth)
    sems += pair(4 * depth) + pair(ranks - 1) * 2 + pair(3) * 2
    sems.append(pltpu.SemaphoreType.DMA((4,)))
    return pl.pallas_call(
        functools.partial(gather_kernel, depth, local),
        out_shape=[
            jax.ShapeDtypeStruct((ranks,) + x.shape, x.dtype),
            jax.ShapeDtypeStruct((4 * ranks,) + o.shape, o.dtype),
            jax.ShapeDtypeStruct((4,) + w.shape, w.dtype),
            jax.ShapeDtypeStruct((4, ranks) + s.shape, s.dtype),
        ]
        + [jax.ShapeDtypeStruct((ranks, chunk, local * 128), low_type)] * 2
        + [jax.ShapeDtypeStruct((ranks, chunk, local * 64), low_type)] * 2,
        in_specs=in_hbm(6),
        out_specs=in_hbm(8),
        scratch_shapes=sems,
        compiler_params=pltpu.CompilerParams(
            collective_id=ident, has_side_effects=True, vmem_limit_bytes=60 << 20
        ),
        cost_estimate=pl.CostEstimate(
            flops=0, bytes_accessed=64 * depth * x.size, transcendentals=0
        ),
    )(x, o, w, s, lines_in(expert_in), lines_down(expert_down))


def exchange_kernel(depth, same, x_ref, out_ref, send_sems, recv_sems, local_sem):
    at = Place(depth)
    ranks = [(k, core) for k in range(depth) for core in range(2) if k or core]
    peers = [at.chip(k, lax.rem(at.c + core, 2)) for k, core in ranks]
    meet(peers)
    own = at.z * 2 + at.c
    copies = []
    for slot, there in enumerate(peers):
        source = x_ref if same else x_ref.at[there[2] * 2 + there[3]]
        copy = remote(source, out_ref.at[own], (send_sems, recv_sems), slot, there)
        copy.start()
        copies.append(copy)
    local = pltpu.make_async_copy(x_ref if same else x_ref.at[own], out_ref.at[own], local_sem)
    local.start()
    for slot, (k, core) in enumerate(ranks):
        target = out_ref.at[at.along(depth - k) * 2 + lax.rem(at.c + core, 2)]
        remote(target, target, (send_sems, recv_sems), slot, at.core()).wait_recv()
    for copy in copies:
        copy.wait_send()
    local.wait()


def exchange(depth, ident, x, same=False):
    ranks = 2 * depth
    return pl.pallas_call(
        functools.partial(exchange_kernel, depth, same),
        out_shape=jax.ShapeDtypeStruct((ranks,) + x.shape if same else x.shape, x.dtype),
        in_specs=in_hbm(1),
        out_specs=in_hbm(1)[0],
        scratch_shapes=pair(ranks - 1) + [pltpu.SemaphoreType.DMA],
        compiler_params=pltpu.CompilerParams(
            collective_id=ident, has_side_effects=True, vmem_limit_bytes=16 << 20
        ),
        cost_estimate=pl.CostEstimate(
            flops=0, bytes_accessed=16 * x.size * x.dtype.itemsize, transcendentals=0
        ),
    )(x)


def column_kernel(depth, part, total, mine, crossed, z_in, *sems):
    at = Place(depth)
    meet([at.core()] + [at.chip(k) for k in range(1, depth)])
    started = []
    inner = lax.rem(at.z, depth - 1) != 0
    inside = lax.div(lax.rem(at.z, depth - 1) + 1, 2)
    onto = (None, at.next_z(1), at.z + 1 - 2 * lax.div(at.z, 3), 1 + lax.rem(at.z, 2))
    slots = (
        None,
        5 - lax.div(4 - at.z, 4),
        4 * inside + (1 - inside) * at.next_z(2),
        at.next_z(3),
    )

    def local(k):
        return pltpu.make_async_copy(part.at[at.next_z(k) * 2 + at.c], mine.at[k], sems[4].at[k])

    def cross(k):
        source = part.at[at.next_z(k) * 2 + 1 - at.c]
        return remote(source, crossed.at[k], sems[0:2], k, at.core())

    def arrive(slot):
        remote(z_in.at[slot], z_in.at[slot], sems[2:4], slot, at.core()).wait_recv()

    def hand_on(k):
        return pltpu.make_async_remote_copy(
            src_ref=mine.at[k],
            dst_ref=z_in.at[slots[k]],
            send_sem=sems[2].at[k],
            recv_sem=sems[3].at[slots[k]],
            device_id=(at.y, at.x, onto[k], at.c),
            device_id_type=MESH_ID,
        )

    order = tuple(range(depth - 1, -1, -1))
    for k in order:
        cross(k).start()
        local(k).start()
    for k in order:
        local(k).wait()
        cross(k).wait_recv()
        terms = [(mine, (k,)), (crossed, (k,))]
        if k == 0:
            sum_rows(total, (), terms)
            continue

        @pl.when(inner)
        def _(terms=terms, k=k):
            arrive(at.next_z(k))
            sum_rows(mine, (k,), terms + [(z_in, (at.next_z(k),))])

        @pl.when(lax.rem(at.z, depth - 1) == 0)
        def _(terms=terms, k=k):
            sum_rows(mine, (k,), terms)

        hand_on(k).start()

    @pl.when(inner)
    def _():
        arrive(4)
        arrive(5)
        sum_rows(total, (), [(total, ()), (z_in, (4,)), (z_in, (5,))])

    @pl.when(lax.rem(at.z, depth - 1) == 0)
    def _():
        slot = 5 - lax.div(at.z, 3)
        arrive(slot)
        sum_rows(total, (), [(total, ()), (z_in, (slot,))])

    for k in order:
        cross(k).wait_send()
        if k:
            hand_on(k).wait_send()


def collect_column(depth, ident, part):
    block = part.shape[1:]
    return pl.pallas_call(
        functools.partial(column_kernel, depth),
        out_shape=jax.ShapeDtypeStruct(block, high_type),
        in_specs=in_hbm(1),
        out_specs=pl.BlockSpec(memory_space=pltpu.VMEM),
        scratch_shapes=[pltpu.VMEM((slots,) + block, part.dtype) for slots in (depth, depth, 6)]
        + pair(depth)
        + pair(6)
        + [pltpu.SemaphoreType.DMA((depth,))],
        compiler_params=pltpu.CompilerParams(
            collective_id=ident, has_side_effects=True, vmem_limit_bytes=32 << 20
        ),
        cost_estimate=pl.CostEstimate(
            flops=0, bytes_accessed=16 * part.size * part.dtype.itemsize, transcendentals=0
        ),
    )(part)


def lines_in(values):
    rows, local, two, hidden = values.shape
    values = values.reshape(rows, local, two, hidden // 128, 128)
    return values.transpose(0, 1, 3, 2, 4).reshape(-1, 128)


def lines_down(values):
    rows, local, hidden = values.shape
    return values.reshape(rows, local, hidden // 128, 128).transpose(0, 2, 1, 3).reshape(-1, 128)


def lines_of(ranks, local):
    half, of_in, of_down = local // 2, [], []
    for rank in range(ranks):
        for x in range(local):
            for k in range(2):
                line = (x * ranks + rank) * 2 + k
                columns = (k * half + x % half) * 128
                of_in.append((rank, x // half, columns, line, 2 * local * ranks))
            of_down.append((rank, x // half, x % half * 128, rank * local + x, local * ranks))
    return of_in, of_down


def pack_kernel(ranks, local, step, in_ref, down_ref, *outs):
    of_in, of_down = lines_of(ranks, local)
    for lines, ref, targets in ((of_in, in_ref, outs[:2]), (of_down, down_ref, outs[2:])):
        for rank, half, column, line, stride in lines:
            value = ref[pl.ds(line, step, stride=stride), :]
            targets[half][rank, :, column : column + 128] = value.astype(low_type)


def pack(ranks, local, in_ref, down_ref, *outs):
    step = 32
    lines = step * local * ranks

    def slices(span):
        return pl.BlockSpec((ranks, step, span), lambda i: (0, i, 0))

    pltpu.emit_pipeline(
        functools.partial(pack_kernel, ranks, local, step),
        grid=(outs[0].shape[1] // step,),
        in_specs=[
            pl.BlockSpec((2 * lines, 128), lambda i: (i, 0)),
            pl.BlockSpec((lines, 128), lambda i: (i, 0)),
        ],
        out_specs=[slices(out.shape[2]) for out in outs],
    )(in_ref, down_ref, *outs)


def unpack_kernel(ranks, local, step, first_ref, second_ref, out_ref):
    of_in, of_down = lines_of(ranks, local)
    for rank, half, column, line, stride in (
        of_in if first_ref.shape[2] == local * 128 else of_down
    ):
        value = (first_ref, second_ref)[half][rank, :, column : column + 128]
        out_ref[pl.ds(line, step, stride=stride), :] = value.astype(high_type)


def unpack_inside(local, first_ref, second_ref, out_ref):
    ranks, rows, span = first_ref.shape
    step = 32
    pltpu.emit_pipeline(
        functools.partial(unpack_kernel, ranks, local, step),
        grid=(rows // step,),
        in_specs=[pl.BlockSpec((ranks, step, span), lambda i: (0, i, 0))] * 2,
        out_specs=[pl.BlockSpec((step * ranks * span // 64, 128), lambda i: (i, 0))],
    )(first_ref, second_ref, out_ref)


def unpack(local, *halves):
    ranks, rows, span = halves[0].shape
    step = 32
    lines = step * ranks * span // 64
    return pl.pallas_call(
        functools.partial(unpack_kernel, ranks, local, step),
        grid=(rows // step,),
        in_specs=[pl.BlockSpec((ranks, step, span), lambda i: (0, i, 0))] * 2,
        out_specs=pl.BlockSpec((lines, 128), lambda i: (i, 0)),
        out_shape=jax.ShapeDtypeStruct((rows * ranks * span // 64, 128), high_type),
        compiler_params=pltpu.CompilerParams(vmem_limit_bytes=32 << 20),
    )(*halves)


def experts_kernel(first, depth, earlier, extra_count, *refs):
    rest = iter(refs)

    def take(count):
        return [next(rest) for _ in range(count)]

    tokens_ref, grads_ref, gates_ref, in_ref, down_ref = take(5)
    added = take(3) if earlier else None
    extra_refs = take(extra_count)
    back_ref, mixed_ref, sums_ref, grad_in_ref, grad_down_ref = take(5)
    extra_outs = take(extra_count)
    in_total, down_total = take(2)
    extra_sems = [take(3) for _ in extra_refs]
    column = lax.axis_index("ey") * 2 + lax.axis_index("ex")
    step, steps = pl.program_id(0), pl.num_programs(0)
    blocks, experts, rows = gates_ref.shape
    span = down_ref.shape[1]
    width = tokens_ref.shape[2]
    at = Place(depth)
    ranks = [(k, core) for k in range(depth) for core in range(2) if k or core]
    peers = [at.chip(k, lax.rem(at.c + core, 2)) for k, core in ranks]
    own_rank = at.z * 2 + at.c

    def extra_copies():
        return [
            remote(source.at[there[2] * 2 + there[3]], target.at[own_rank], sems, slot, there)
            for source, target, sems in zip(extra_refs, extra_outs, extra_sems)
            for slot, there in enumerate(peers)
        ]

    def kept():
        return [
            pltpu.make_async_copy(source.at[own_rank], target.at[own_rank], sems[2])
            for source, target, sems in zip(extra_refs, extra_outs, extra_sems)
        ]

    @pl.when(step == 0)
    def _():
        meet(peers)
        for copy in extra_copies() + kept():
            copy.start()
        in_total[...] = jnp.zeros_like(in_total)
        down_total[...] = jnp.zeros_like(down_total)

    units_of = (
        lax.broadcasted_iota(jnp.int32, (experts, span), 1) // 128 + column * 4 + first
        == lax.broadcasted_iota(jnp.int32, (experts, span), 0)
    ).astype(low_type)

    def terms(values, count):
        result = []
        for _ in range(count):
            result.append(values.astype(low_type))
            values = values - result[-1].astype(high_type)
        return result

    tokens = tokens_ref[...].reshape(blocks * rows, width)
    grads = grads_ref[...].reshape(blocks * rows, width)
    gates = jnp.concatenate([gates_ref[b] for b in range(blocks)], axis=1)
    gates = jnp.concatenate(terms(gates, 3), axis=0)
    wide = t_dot(gates, jnp.concatenate([units_of] * 3, axis=0))
    both = dot(tokens, in_ref[...])
    gate_part, up_part = both[:, :span], both[:, span:]
    down_grad = dot(grads, down_ref[...])
    sigma = 0.5 + 0.5 * jnp.tanh(0.5 * gate_part)
    silu = gate_part * sigma
    hidden = (silu * up_part).astype(low_type).astype(high_type)
    weighted = (wide * hidden).astype(low_type)
    inner = hidden * down_grad
    high, low = terms(inner, 2)
    sums = dot_t(units_of, high) + dot_t(units_of, low)
    for b in range(blocks):
        part = sums[:, b * rows : (b + 1) * rows]
        sums_ref[b] = part + added[2][b] if earlier else part
    grad_hidden = wide * down_grad
    grad_gate = grad_hidden * up_part * (sigma + silu * (1.0 - sigma))
    grad_both = jnp.concatenate([grad_gate, grad_hidden * silu], axis=1).astype(low_type)
    back = dot_t(grad_both, in_ref[...]).reshape(back_ref.shape)
    mixed = dot_t(weighted, down_ref[...]).reshape(mixed_ref.shape)
    if earlier:
        back = back + added[0][...].astype(high_type)
        mixed = mixed + added[1][...].astype(high_type)
    back_ref[...] = back.astype(low_type)
    mixed_ref[...] = mixed.astype(low_type)
    in_total[...] += t_dot(tokens, grad_both)
    down_total[...] += t_dot(grads, weighted)

    @pl.when(step == steps - 1)
    def _():
        grad_in_ref[...] = in_total[...].astype(low_type)
        grad_down_ref[...] = down_total[...].astype(low_type)
        for copy in kept() + extra_copies():
            copy.wait()


def run_experts(depth, ident, first, tokens, grads, gates, weights_in, weights_down, extras, earlier):
    devices, rows, width = tokens.shape
    experts = gates.shape[1]
    blocks = 4
    span = weights_in.shape[1] // 2

    def by_step(shape):
        return pl.BlockSpec((blocks,) + shape, lambda i: (i, 0, 0))

    def whole(shape):
        return pl.BlockSpec(shape, lambda i: (0, 0), pipeline_mode=pl.Buffered(1))

    per_token = [by_step((rows, width)), by_step((rows, width)), by_step((experts, rows))]
    sums = [jax.ShapeDtypeStruct((devices, rows, width), low_type)] * 2
    sums.append(jax.ShapeDtypeStruct((devices, experts, rows), high_type))
    return pl.pallas_call(
        functools.partial(experts_kernel, first, depth, bool(earlier), len(extras)),
        grid=(devices // blocks,),
        in_specs=per_token
        + [whole((width, 2 * span)), whole((width, span))]
        + (per_token if earlier else [])
        + in_hbm(len(extras)),
        out_specs=per_token
        + [whole((width, 2 * span)), whole((width, span))]
        + in_hbm(len(extras)),
        out_shape=sums
        + [
            jax.ShapeDtypeStruct((width, 2 * span), low_type),
            jax.ShapeDtypeStruct((width, span), low_type),
        ]
        + [jax.ShapeDtypeStruct(extra.shape, extra.dtype) for extra in extras],
        scratch_shapes=[
            pltpu.VMEM((width, 2 * span), high_type),
            pltpu.VMEM((width, span), high_type),
        ]
        + (pair(2 * depth - 1) + [pltpu.SemaphoreType.DMA]) * len(extras),
        compiler_params=pltpu.CompilerParams(
            collective_id=ident, has_side_effects=True, vmem_limit_bytes=60 << 20
        ),
        cost_estimate=pl.CostEstimate(
            flops=18 * devices * rows * width * span,
            bytes_accessed=8 * devices * rows * width,
            transcendentals=devices * rows * span,
        ),
    )(tokens, grads, gates, weights_in, weights_down, *earlier, *extras)


def grid_shards(
    residual_in,
    cotangent,
    lengths,
    routes,
    attn_qkv,
    attn_out,
    gains,
    router,
    expert_in,
    expert_down,
):
    rows, width = residual_in.shape
    depth = lax.axis_size("dz")
    ranks = 2 * depth
    columns = 4
    seq_rows = rows * ranks
    local_experts = expert_in.shape[1]
    experts = local_experts * columns
    hidden_width = expert_in.shape[3]
    part = hidden_width // ranks
    span = local_experts * part
    chunk_rows = expert_in.shape[0]
    weight_rows = attn_qkv.shape[1]
    score_scale = HD ** (-0.5)
    y, x, z, c = (lax.axis_index(name) for name in GRID)
    column = y * 2 + x
    own_heads = HEADS // ranks
    own_width = own_heads * HD

    def sum_column(ident, pairs):
        flat = exchange(depth, ident, pairs.reshape(-1, 128), same=True)
        return jnp.sum(flat, axis=0).reshape(pairs.shape)

    def by_rank(values):
        lead = values.shape[:-1]
        shaped = values.reshape(lead + (2, own_heads, depth, HD))
        n = len(lead)
        return shaped.transpose((n + 2, n) + tuple(range(n)) + (n + 1, n + 3)).reshape(
            (ranks,) + lead + (own_width,)
        )

    def by_head(values):
        lead = values.shape[1:-1]
        shaped = values.reshape((depth, 2) + lead + (own_heads, HD))
        n = len(lead)
        return shaped.transpose(tuple(range(2, n + 2)) + (1, n + 2, 0, n + 3)).reshape(
            lead + (width,)
        )

    small = jnp.concatenate([gains.T, router], axis=1).astype(low_type)
    small = jnp.pad(small, ((0, 0), (0, 128 - small.shape[1])))
    packed = attn_qkv.astype(low_type).transpose(1, 0, 2)
    packed = by_rank(packed).reshape(ranks, weight_rows, 3 * own_width)
    seq_input, out_weight, qkv_weight, small, first_in, second_in, first_down, second_down = gather(
        depth,
        0,
        residual_in,
        attn_out.astype(low_type),
        packed,
        small,
        expert_in,
        expert_down,
    )
    out_weight = out_weight.reshape(width, width)
    qkv_weight = qkv_weight.reshape(width, 3 * own_width)
    small = small.reshape(width, 128)
    gain_rows = small[:, :4].T.astype(high_type)
    router_weight = small[:, 4 : 4 + experts]
    gain_own = [
        lax.dynamic_index_in_dim(by_rank(gain_rows[i]), z * 2 + c, 0, keepdims=False)
        for i in (1, 2)
    ]
    normed_in = seq_input.reshape(seq_rows, width).astype(high_type)
    normed_in = (normed_in * rms_scale(normed_in) * gain_rows[0]).astype(low_type)
    raw = dot(normed_in, qkv_weight)
    query_raw, key_raw = raw[:, :own_width], raw[:, own_width : 2 * own_width]
    value_rows = raw[:, 2 * own_width :].astype(low_type)
    squares = jnp.stack(
        [jnp.sum(query_raw * query_raw, axis=1), jnp.sum(key_raw * key_raw, axis=1)]
    )
    scales = lax.rsqrt(sum_column(1, squares) / width + epsilon)
    query_scale, key_scale = scales[0][:, None], scales[1][:, None]
    positions = jnp.arange(seq_rows, dtype=jnp.int32)
    length_now = lengths[0]
    key_live = positions < length_now
    cosine, sine_table = angle_tables(positions)
    query_normed = query_raw * query_scale
    key_normed = key_raw * key_scale
    query_rot = rotate(query_normed * gain_own[0], cosine, sine_table).astype(low_type)
    key_rot = rotate(key_normed * gain_own[1], cosine, sine_table).astype(low_type)
    query_heads = query_rot.reshape(seq_rows, own_heads, HD)
    key_heads = key_rot.reshape(seq_rows, own_heads, HD)
    value_heads = value_rows.reshape(seq_rows, own_heads, HD)

    def per_head(spec, left, right):
        return jnp.einsum(spec, left, right, preferred_element_type=high_type)

    scores = per_head("qhd,khd->hqk", query_heads, key_heads) * score_scale
    scores = jnp.where(key_live[None, None, :], scores, masked_score)
    probs = jax.nn.softmax(scores, axis=-1)
    probs_low = probs.astype(low_type)
    attended = per_head("hqk,khd->qhd", probs_low, value_heads).astype(low_type)
    attended = exchange(depth, 2, attended.reshape(ranks, rows, own_width))
    attended = by_head(attended)

    own_positions = (z * 2 + c) * rows + jnp.arange(rows, dtype=jnp.int32)
    live_rows = (own_positions < length_now).astype(high_type)[:, None]
    input_rows = residual_in.astype(high_type)
    middle = input_rows + live_rows * dot(attended, out_weight)
    scale_mid = rms_scale(middle)
    normed_mid_f = middle * scale_mid
    normed_mid = (normed_mid_f * gain_rows[3]).astype(low_type)

    logits = dot(normed_mid, router_weight)
    named = jnp.any(
        routes[:, :, None] == jnp.arange(experts, dtype=jnp.int32)[None, None, :], axis=1
    )
    top = jnp.max(jnp.where(named, logits, -jnp.inf), axis=1, keepdims=True)
    weight_of = jnp.where(named, jnp.exp(jnp.where(named, logits - top, 0.0)), 0.0)
    gates = weight_of / jnp.sum(weight_of, axis=1, keepdims=True)

    grad_rows = cotangent.astype(high_type)
    grad_comb = live_rows * grad_rows
    after = jnp.minimum(scales[0, 0], 0.0)
    own_grads = (grad_comb + after).astype(low_type)
    grads = lax.all_gather(own_grads, GRID, axis=0, tiled=True)
    tokens, gates_all, first_in, first_down = spread(
        depth, 3, (normed_mid, gates.T), (first_in, first_down)
    )
    grads = grads.reshape(tokens.shape)

    def flat(values):
        return values.reshape(width, -1)

    def by_slice(values):
        return values.reshape(ranks, chunk_rows, -1)

    *sums, grad_first, down_first, second_in, second_down = run_experts(
        depth,
        9,
        0,
        tokens,
        grads,
        gates_all,
        flat(first_in),
        flat(first_down),
        (second_in, second_down),
        (),
    )
    back, mixed, gate_sums, grad_second, down_second, grad_first, down_first = run_experts(
        depth,
        10,
        local_experts // 2,
        tokens,
        grads,
        gates_all,
        flat(second_in),
        flat(second_down),
        (by_slice(grad_first), by_slice(down_first)),
        tuple(sums),
    )
    grad_mid_norm, combined, grad_gates, grad_second = collect(
        depth, 4, [back, mixed], [gate_sums], extras=[by_slice(grad_second)]
    )
    output = middle + live_rows * combined

    grad_gates = grad_gates.T
    grad_chosen = gates * (grad_gates - jnp.sum(gates * grad_gates, axis=1, keepdims=True))
    grad_logits = grad_chosen.astype(low_type)
    grad_mid_norm = grad_mid_norm + dot_t(grad_logits, router_weight)
    grad_router = t_dot(normed_mid, grad_logits)

    grad_mid_rows, grad_gain_mid = rms_back(grad_mid_norm, normed_mid_f, scale_mid, gain_rows[3])
    grad_middle = grad_rows + grad_mid_rows
    grad_branch = (live_rows * grad_middle).astype(low_type)

    grad_attended = by_rank(dot_t(grad_branch, out_weight).astype(low_type))
    grad_attended = exchange(depth, 6, grad_attended)
    grad_heads = grad_attended.reshape(seq_rows, own_heads, HD)
    grad_probs = per_head("qhd,khd->hqk", grad_heads, value_heads)
    inner_rows = jnp.sum(probs * grad_probs, axis=-1, keepdims=True)
    grad_scores = (probs * (grad_probs - inner_rows)).astype(low_type)
    grad_query = per_head("hqk,khd->qhd", grad_scores, key_heads) * score_scale
    grad_key = per_head("hqk,qhd->khd", grad_scores, query_heads) * score_scale
    grad_value = per_head("hqk,qhd->khd", probs_low, grad_heads).astype(low_type)
    grad_query = rotate(grad_query.reshape(seq_rows, own_width), cosine, -sine_table)
    grad_key = rotate(grad_key.reshape(seq_rows, own_width), cosine, -sine_table)
    query_inner = grad_query * gain_own[0]
    key_inner = grad_key * gain_own[1]
    inner = jnp.stack(
        [
            jnp.sum(query_inner * query_normed, axis=1),
            jnp.sum(key_inner * key_normed, axis=1),
        ]
    )
    inner = sum_column(7, inner) / width
    query_back = query_scale * (query_inner - query_normed * inner[0][:, None])
    key_back = key_scale * (key_inner - key_normed * inner[1][:, None])
    grad_raw = jnp.concatenate(
        [
            query_back.astype(low_type),
            key_back.astype(low_type),
            grad_value.reshape(seq_rows, own_width),
        ],
        axis=1,
    )

    share = dot_t(grad_raw, qkv_weight).astype(low_type).reshape(ranks, rows, width)
    grad_norm_in = collect_column(depth, 8, share)

    scale_in = rms_scale(input_rows)
    grad_in_rows, grad_gain_in = rms_back(
        grad_norm_in, input_rows * scale_in, scale_in, gain_rows[0]
    )
    grad_input = grad_middle + grad_in_rows

    def at_heads(values):
        whole = jnp.zeros((2, own_heads, depth, HD), high_type)
        values = values.reshape(1, own_heads, 1, HD)
        return lax.dynamic_update_slice(whole, values, (c, 0, z, 0)).reshape(width)

    grad_small = jnp.concatenate(
        [
            jnp.stack(
                [
                    grad_gain_in,
                    at_heads(jnp.sum(grad_query * query_normed, axis=0)),
                    at_heads(jnp.sum(grad_key * key_normed, axis=0)),
                    grad_gain_mid,
                ]
            ).T,
            grad_router,
        ],
        axis=1,
    )
    grad_small = jnp.pad(grad_small, ((0, 0), (0, 128 - grad_small.shape[1])))
    grad_out = t_dot(attended, grad_branch).astype(low_type)
    grad_qkv = t_dot(normed_in, grad_raw).astype(low_type)
    grad_out, grad_small, grad_qkv, down_second, grad_expert_in = collect(
        depth,
        5,
        [grad_out.reshape(-1, weight_rows, width)],
        [grad_small.reshape(-1, weight_rows, 128)],
        [grad_qkv.reshape(columns, -1, 3 * own_width)],
        [by_slice(down_second)],
        (local_experts, grad_first, grad_second),
    )
    grad_expert_in = grad_expert_in.reshape(chunk_rows, local_experts, ranks, 2, part)
    grad_expert_in = grad_expert_in.transpose(0, 1, 3, 2, 4).reshape(expert_in.shape)
    grad_expert_down = unpack(local_experts, down_first, down_second).reshape(
        chunk_rows, ranks, local_experts, part
    )
    grad_expert_down = grad_expert_down.transpose(0, 2, 1, 3).reshape(expert_down.shape)
    return (
        output,
        grad_input,
        grad_qkv,
        grad_out,
        grad_small[:, :4].T,
        grad_small[:, 4 : 4 + experts],
        grad_expert_in,
        grad_expert_down,
    )


def slot_index(route_rows, experts, capacity):
    flat_routes = route_rows.reshape(-1)
    onehot = (flat_routes[:, None] == jnp.arange(experts, dtype=jnp.int32)[None, :]).astype(
        jnp.int32
    )
    rows = jnp.arange(flat_routes.shape[0], dtype=jnp.int32)
    earlier = (rows[None, :] < rows[:, None]).astype(jnp.bfloat16)
    before = jnp.dot(
        earlier, onehot.astype(jnp.bfloat16), preferred_element_type=jnp.float32
    ).astype(jnp.int32)
    rank_rows = jnp.sum(before * onehot, axis=1)
    return flat_routes * capacity + rank_rows


def head_scores(query_rot, key_all, key_live):
    row_count = query_rot.shape[0]
    query_heads = query_rot.reshape(row_count, HEADS, HD)
    key_heads = key_all.reshape(key_all.shape[0], HEADS, HD)
    raw_scores = jnp.einsum(
        "qhd,khd->hqk", query_heads, key_heads, preferred_element_type=jnp.float32
    ) * HD ** (-0.5)
    return jnp.where(key_live[None, None, :], raw_scores, masked_score)


def to_owners(buffer):
    return lax.all_to_all(buffer, "expert", split_axis=0, concat_axis=0, tiled=True)


def from_owners(buffer):
    return lax.all_to_all(buffer, "expert", split_axis=0, concat_axis=0, tiled=True)


def shards(
    residual_in,
    cotangent,
    lengths,
    routes,
    attn_qkv,
    attn_out,
    gains,
    router,
    expert_in,
    expert_down,
):
    tok_rows, model_width = residual_in.shape
    top_count = routes.shape[1]
    owners = lax.axis_size("expert")
    local_experts = expert_in.shape[1]
    experts = local_experts * owners
    capacity = tok_rows * top_count * 2 // experts
    local_slots = local_experts * capacity
    seq_rows = tok_rows * lax.axis_size("dp")
    score_scale = HD ** (-0.5)
    qkv_weights, out_weight, gain_low, router_weight = (
        lax.all_gather(attn_qkv.astype(low_type), ("expert", "dp"), axis=1, tiled=True),
        lax.all_gather(attn_out.astype(low_type), ("expert", "dp"), axis=0, tiled=True),
        lax.all_gather(gains.astype(low_type), ("expert", "dp"), axis=1, tiled=True),
        lax.all_gather(router.astype(low_type), ("expert", "dp"), axis=0, tiled=True),
    )
    gain_rows = gain_low.astype(high_type)
    input_rows = residual_in.astype(high_type)
    scale_in = rms_scale(input_rows)
    normed_in_f = input_rows * scale_in
    normed_in = (normed_in_f * gain_rows[0]).astype(low_type)
    query_raw = jnp.dot(normed_in, qkv_weights[0], preferred_element_type=high_type)
    key_raw = jnp.dot(normed_in, qkv_weights[1], preferred_element_type=high_type)
    value_rows = jnp.dot(normed_in, qkv_weights[2], preferred_element_type=high_type).astype(
        low_type
    )
    positions = lax.axis_index("dp") * tok_rows + jnp.arange(tok_rows, dtype=jnp.int32)
    length_now = lengths[0]
    live_rows = (positions < length_now).astype(high_type)[:, None]
    key_live = jnp.arange(seq_rows, dtype=jnp.int32) < length_now
    cosine, sine_table = angle_tables(positions)
    query_scale = rms_scale(query_raw)
    query_normed = query_raw * query_scale
    query_rot = rotate(query_normed * gain_rows[1], cosine, sine_table).astype(low_type)
    key_scale = rms_scale(key_raw)
    key_normed = key_raw * key_scale
    key_rot = rotate(key_normed * gain_rows[2], cosine, sine_table).astype(low_type)
    key_all = lax.all_gather(key_rot, "dp", axis=0, tiled=True)
    value_all = lax.all_gather(value_rows, "dp", axis=0, tiled=True)
    scores = head_scores(query_rot, key_all, key_live)
    top_score = jnp.max(scores, axis=-1, keepdims=True)
    exp_scores = jnp.exp(scores - top_score)
    row_total = jnp.sum(exp_scores, axis=-1, keepdims=True)
    weights_low = (exp_scores / row_total).astype(low_type)
    log_total = top_score + jnp.log(row_total)
    value_heads = value_all.reshape(seq_rows, HEADS, HD)
    attended = jnp.einsum(
        "hqk,khd->qhd", weights_low, value_heads, preferred_element_type=high_type
    )
    attended = attended.reshape(tok_rows, model_width).astype(low_type)
    branch = jnp.dot(attended, out_weight, preferred_element_type=high_type)
    middle = input_rows + live_rows * branch
    scale_mid = rms_scale(middle)
    normed_mid_f = middle * scale_mid
    normed_mid = (normed_mid_f * gain_rows[3]).astype(low_type)
    logits = jnp.dot(normed_mid, router_weight, preferred_element_type=high_type)
    selector = (routes[:, :, None] == jnp.arange(experts, dtype=jnp.int32)[None, None, :]).astype(
        high_type
    )
    chosen = jnp.einsum("te,tje->tj", logits, selector)
    gate_weights = jax.nn.softmax(chosen, axis=-1)
    slot_rows = slot_index(routes, experts, capacity)
    token_of = jnp.arange(slot_rows.shape[0], dtype=jnp.int32) // top_count
    send_rows = (
        jnp.zeros((experts * capacity, model_width), low_type)
        .at[slot_rows]
        .set(normed_mid[token_of])
    )
    rows_recv = lax.all_to_all(
        send_rows.reshape(owners, local_slots, model_width),
        "expert",
        split_axis=0,
        concat_axis=0,
        tiled=True,
    )
    rows_recv = rows_recv.reshape(owners, local_experts, capacity, model_width)
    weights_in, weights_down = (
        lax.all_gather(expert_in.astype(low_type), "dp", axis=0, tiled=True),
        lax.all_gather(expert_down.astype(low_type), "dp", axis=0, tiled=True),
    )
    both_parts = jnp.einsum(
        "sxmd,dxkf->sxmkf", rows_recv, weights_in, preferred_element_type=high_type
    )
    gate_part = both_parts[:, :, :, 0, :]
    up_part = both_parts[:, :, :, 1, :]
    hidden = (jax.nn.silu(gate_part) * up_part).astype(low_type)
    produced = jnp.einsum(
        "sxmf,dxf->sxmd", hidden, weights_down, preferred_element_type=high_type
    ).astype(low_type)
    returned = from_owners(produced.reshape(owners, local_slots, model_width))
    returned = returned.reshape(experts * capacity, model_width)
    picked = returned[slot_rows].reshape(tok_rows, top_count, model_width).astype(high_type)
    combined = jnp.sum(gate_weights[:, :, None] * picked, axis=1)
    output = middle + live_rows * combined
    grad_rows = cotangent.astype(high_type)
    grad_comb = live_rows * grad_rows
    grad_gates = jnp.einsum("tjd,td->tj", picked, grad_comb)
    grad_chosen = gate_weights * (
        grad_gates - jnp.sum(gate_weights * grad_gates, axis=-1, keepdims=True)
    )
    grad_logits = jnp.einsum("tj,tje->te", grad_chosen, selector).astype(low_type)
    grad_send = (
        (gate_weights[:, :, None] * grad_comb[:, None, :]).astype(low_type).reshape(-1, model_width)
    )
    grad_buffer = (
        jnp.zeros((experts * capacity, model_width), low_type).at[slot_rows].set(grad_send)
    )
    grad_recv = to_owners(grad_buffer.reshape(owners, local_slots, model_width))
    grad_recv = grad_recv.reshape(owners, local_experts, capacity, model_width)
    grad_hidden = jnp.einsum(
        "sxmd,dxf->sxmf", grad_recv, weights_down, preferred_element_type=high_type
    )
    sigma_gate = jax.nn.sigmoid(gate_part)
    grad_gate = grad_hidden * up_part * sigma_gate * (1.0 + gate_part * (1.0 - sigma_gate))
    grad_up = grad_hidden * gate_part * sigma_gate
    grad_both = jnp.stack([grad_gate, grad_up], axis=3).astype(low_type)
    grad_rows_out = jnp.einsum(
        "sxmkf,dxkf->sxmd", grad_both, weights_in, preferred_element_type=high_type
    ).astype(low_type)
    grad_back = from_owners(grad_rows_out.reshape(owners, local_slots, model_width))
    grad_back = grad_back.reshape(experts * capacity, model_width)
    grad_mid_norm = jnp.sum(
        grad_back[slot_rows].reshape(tok_rows, top_count, model_width).astype(high_type), axis=1
    )
    grad_mid_norm = grad_mid_norm + jnp.dot(
        grad_logits, router_weight.T, preferred_element_type=high_type
    )
    grad_router = jnp.dot(normed_mid.T, grad_logits, preferred_element_type=high_type)
    row_piece = rows_recv
    grad_expert_in = lax.psum_scatter(
        jnp.einsum(
            "sxmd,sxmkf->dxkf", row_piece, grad_both, preferred_element_type=high_type
        ).astype(jnp.bfloat16),
        "dp",
        scatter_dimension=0,
        tiled=True,
    ).astype(jnp.float32)
    row_piece = grad_recv
    grad_expert_down = lax.psum_scatter(
        jnp.einsum("sxmd,sxmf->dxf", row_piece, hidden, preferred_element_type=high_type).astype(
            jnp.bfloat16
        ),
        "dp",
        scatter_dimension=0,
        tiled=True,
    ).astype(jnp.float32)
    grad_mid_rows, grad_gain_mid = rms_back(grad_mid_norm, normed_mid_f, scale_mid, gain_rows[3])
    grad_middle = grad_rows + grad_mid_rows
    grad_branch = (live_rows * grad_middle).astype(low_type)
    grad_out_weight = jnp.dot(attended.T, grad_branch, preferred_element_type=high_type)
    grad_attended = jnp.dot(grad_branch, out_weight.T, preferred_element_type=high_type).astype(
        low_type
    )
    scores = head_scores(query_rot, key_all, key_live)
    probs_full = jnp.exp(scores - log_total)
    grad_heads = grad_attended.reshape(tok_rows, HEADS, HD)
    value_heads = value_all.reshape(seq_rows, HEADS, HD)
    key_heads = key_all.reshape(seq_rows, HEADS, HD)
    query_heads = query_rot.reshape(tok_rows, HEADS, HD)
    grad_probs = jnp.einsum(
        "qhd,khd->hqk", grad_heads, value_heads, preferred_element_type=high_type
    )
    inner_rows = jnp.sum(probs_full * grad_probs, axis=-1, keepdims=True)
    grad_scores = (probs_full * (grad_probs - inner_rows)).astype(low_type)
    grad_query = (
        jnp.einsum(
            "hqk,khd->qhd", grad_scores, key_heads, preferred_element_type=high_type
        ).reshape(tok_rows, model_width)
        * score_scale
    )
    grad_key_part = (
        jnp.einsum(
            "hqk,qhd->khd", grad_scores, query_heads, preferred_element_type=high_type
        ).reshape(seq_rows, model_width)
        * score_scale
    )
    grad_value_part = jnp.einsum(
        "hqk,qhd->khd", probs_full.astype(low_type), grad_heads, preferred_element_type=high_type
    ).reshape(seq_rows, model_width)
    grad_key_sum, grad_value_sum = (
        lax.psum_scatter(
            grad_key_part.astype(jnp.bfloat16), "dp", scatter_dimension=0, tiled=True
        ).astype(jnp.float32),
        lax.psum_scatter(
            grad_value_part.astype(jnp.bfloat16), "dp", scatter_dimension=0, tiled=True
        ).astype(jnp.float32),
    )
    grad_value = grad_value_sum.astype(low_type)
    grad_key_raw, grad_key_gain = rms_back(
        rotate(grad_key_sum, cosine, -sine_table), key_normed, key_scale, gain_rows[2]
    )
    grad_query_raw, grad_query_gain = rms_back(
        rotate(grad_query, cosine, -sine_table), query_normed, query_scale, gain_rows[1]
    )
    grad_key_raw = grad_key_raw.astype(low_type)
    grad_query_raw = grad_query_raw.astype(low_type)
    grad_norm_in = jnp.dot(grad_query_raw, qkv_weights[0].T, preferred_element_type=high_type)
    grad_norm_in = grad_norm_in + jnp.dot(
        grad_key_raw, qkv_weights[1].T, preferred_element_type=high_type
    )
    grad_norm_in = grad_norm_in + jnp.dot(
        grad_value, qkv_weights[2].T, preferred_element_type=high_type
    )
    grad_qkv_local = jnp.stack(
        [
            jnp.dot(normed_in.T, grad_query_raw, preferred_element_type=high_type),
            jnp.dot(normed_in.T, grad_key_raw, preferred_element_type=high_type),
            jnp.dot(normed_in.T, grad_value, preferred_element_type=high_type),
        ]
    )
    grad_in_rows, grad_gain_in = rms_back(grad_norm_in, normed_in_f, scale_in, gain_rows[0])
    grad_input = grad_middle + grad_in_rows
    grad_gains_local = jnp.stack([grad_gain_in, grad_query_gain, grad_key_gain, grad_gain_mid])
    summed = (
        lax.psum_scatter(grad_qkv_local, ("expert", "dp"), scatter_dimension=1, tiled=True),
        lax.psum_scatter(grad_out_weight, ("expert", "dp"), scatter_dimension=0, tiled=True),
        lax.psum_scatter(grad_gains_local, ("expert", "dp"), scatter_dimension=1, tiled=True),
        lax.psum_scatter(grad_router, ("expert", "dp"), scatter_dimension=0, tiled=True),
    )
    return (
        output,
        grad_input,
        summed[0],
        summed[1],
        summed[2],
        summed[3],
        grad_expert_in,
        grad_expert_down,
    )


def solution(mesh):
    column_count, rank_count = mesh.shape["expert"], mesh.shape["dp"]
    depth = rank_count // 2
    tiled = column_count == 4 and rank_count % 2 == 0 and HEADS == column_count * depth
    if tiled:
        mesh = Mesh(mesh.devices.reshape(2, 2, depth, 2), GRID)
        column, rank, body = ("ey", "ex"), SEQ, grid_shards
    else:
        column, rank, body = ("expert",), ("dp",), shards
    device = column + rank
    placed = (
        P(device, None),
        P(device, None),
        P(column),
        P(device, None),
        P(None, device, None),
        P(device, None),
        P(None, device),
        P(device, None),
        P(rank, column, None, None),
        P(rank, column, None),
    )
    return jax.shard_map(
        body,
        mesh=mesh,
        in_specs=placed,
        out_specs=placed[:1] * 2 + placed[4:],
        check_vma=False,
    )
```

```python
import functools

import jax
import jax.numpy as jnp
from jax import lax
from jax.experimental import pallas as pl
from jax.experimental.pallas import tpu as pltpu
from jax.sharding import Mesh
from jax.sharding import PartitionSpec as P

HEADS = 16
HD = 128

epsilon = 1e-05
rope_base = 10000.0
masked_score = -1000000000.0

low_type = jnp.bfloat16
high_type = jnp.float32


def rms_scale(values):
    return lax.rsqrt(jnp.mean(values * values, axis=-1, keepdims=True) + epsilon)


def angle_tables(positions):
    frequency = rope_base ** (-2.0 * jnp.arange(HD // 2, dtype=jnp.float32) / HD)
    angles = positions.astype(jnp.float32)[:, None] * frequency[None, :]
    return (jnp.cos(angles), jnp.sin(angles))


def rotate(values, cosine, sine_table):
    row_count, width = values.shape
    shaped = values.reshape(row_count, width // HD, 2, HD // 2)
    first_half = shaped[:, :, 0, :]
    second_half = shaped[:, :, 1, :]
    cos_rows = cosine[:, None, :]
    sin_rows = sine_table[:, None, :]
    turned = jnp.stack(
        [
            first_half * cos_rows - second_half * sin_rows,
            second_half * cos_rows + first_half * sin_rows,
        ],
        axis=2,
    )
    return turned.reshape(row_count, width)


def rms_back(grad_rows, normed, scale, gain):
    grad_normed = grad_rows * gain
    inner = jnp.mean(grad_normed * normed, axis=-1, keepdims=True)
    return (scale * grad_normed - normed * scale * inner, jnp.sum(grad_rows * normed, axis=0))


def dot(left, right):
    return jnp.dot(left, right, preferred_element_type=high_type)


def dot_t(left, right):
    return lax.dot_general(left, right, (((1,), (1,)), ((), ())), preferred_element_type=high_type)


def t_dot(left, right):
    return lax.dot_general(left, right, (((0,), (0,)), ((), ())), preferred_element_type=high_type)


GRID = ("ey", "ex", "dz", "dc")
SEQ = ("dz", "dc")


MESH_ID = pl.DeviceIdType.MESH


class Place:
    def __init__(self, depth):
        self.depth = depth
        self.y, self.x, self.z, self.c = (lax.axis_index(name) for name in GRID)

    def near_of(self, core):
        return self.y + core * (1 - 2 * self.y), self.x + (1 - core) * (1 - 2 * self.x)

    def far_of(self, core):
        return self.near_of(1 - core)

    def along(self, step):
        return lax.rem(self.z + step, self.depth)

    def next_z(self, k):
        first = self.z - 1 + 2 * lax.div(4 - self.z, 4)
        last = 3 * lax.div(3 - self.z, 2)
        return (self.z, first, 6 - self.z - first - last, last)[k]

    def block(self, column, z, core):
        return ((column[0] * 2 + column[1]) * self.depth + z) * 2 + core

    @property
    def own_column(self):
        return self.y, self.x

    @property
    def other_column(self):
        return 1 - self.y, 1 - self.x

    def core(self):
        return self.y, self.x, self.z, 1 - self.c

    def chip(self, step, core=None):
        return self.y, self.x, self.along(step), self.c if core is None else core

    def near(self):
        return (*self.near_of(self.c), self.z, self.c)

    def far(self):
        return (*self.far_of(self.c), self.z, self.c)


def meet(partners):
    barrier = pltpu.get_barrier_semaphore()
    for partner in partners:
        pl.semaphore_signal(barrier, inc=1, device_id=partner, device_id_type=MESH_ID)
    pl.semaphore_wait(barrier, len(partners))


def remote(source, target, sems, slot, partner):
    return pltpu.make_async_remote_copy(
        src_ref=source,
        dst_ref=target,
        send_sem=sems[0].at[slot],
        recv_sem=sems[1].at[slot],
        device_id=partner,
        device_id_type=MESH_ID,
    )


def pair(count):
    return [pltpu.SemaphoreType.DMA((count,)), pltpu.SemaphoreType.DMA((count,))]


def in_hbm(count):
    return [pl.BlockSpec(memory_space=pl.ANY)] * count


def spread_kernel(depth, count, extra, *refs):
    whole = count + extra
    sources, targets, sems = refs[:count], refs[whole : whole + count], refs[2 * whole :]
    extra_sources, extra_targets = refs[count:whole], refs[whole + count : 2 * whole]
    extra_sems = sems[9 * count :]
    at = Place(depth)
    others = range(1, depth)
    ranks = [(k, core) for k in range(depth) for core in range(2) if k or core]
    peers = [at.chip(k, lax.rem(at.c + core, 2)) for k, core in ranks]
    meet([at.near(), at.far()] + peers)
    started, local = [], []

    def push(n, source, index, kind, slot, partner):
        copy = remote(source, targets[n].at[index], sems[9 * n + 2 * kind :], slot, partner)
        copy.start()
        started.append(copy)

    def arrive(n, index, kind, slot):
        target = targets[n].at[index]
        remote(target, target, sems[9 * n + 2 * kind :], slot, at.core()).wait_recv()

    z_kind, near_kind, far_kind, core_kind = range(4)
    own = at.block(at.own_column, at.z, at.c)
    for n in range(count):
        push(n, sources[n], own, z_kind, at.z, (at.y, at.x, at.next_z(1), at.c))
        push(n, sources[n], own, near_kind, 0, at.near())
        push(n, sources[n], own, far_kind, 0, at.far())
        push(n, sources[n], own, core_kind, 0, at.core())
        copy = pltpu.make_async_copy(sources[n], targets[n].at[own], sems[9 * n + 8])
        copy.start()
        local.append(copy)

    inner = lax.rem(at.z, depth - 1) != 0
    onward = (at.z + 1, at.z + 1, at.z - 1, 3 * at.z - 3)

    def forward(n, source, k):
        z = at.next_z(k)
        return pltpu.make_async_remote_copy(
            src_ref=source,
            dst_ref=targets[n].at[at.block(at.own_column, z, at.c)],
            send_sem=sems[9 * n].at[z if k else depth],
            recv_sem=sems[9 * n + 1].at[z],
            device_id=(at.y, at.x, onward[k], at.c),
            device_id_type=MESH_ID,
        )

    @pl.when(inner)
    def _():
        for n in range(count):
            forward(n, sources[n], 0).start()

    for k in others:
        index = at.block(at.own_column, at.next_z(k), at.c)
        for n in range(count):
            arrive(n, index, z_kind, at.next_z(k))

        @pl.when(inner)
        def _(index=index, k=k):
            for n in range(count):
                forward(n, targets[n].at[index], k).start()

        for n in range(count):
            push(n, targets[n].at[index], index, near_kind, k, at.near())
            push(n, targets[n].at[index], index, far_kind, k, at.far())
            push(n, targets[n].at[index], index, core_kind, k, at.core())
    own_rank = at.z * 2 + at.c
    for n in range(extra):
        for slot, there in enumerate(peers):
            copy = remote(
                extra_sources[n].at[there[2] * 2 + there[3]],
                extra_targets[n].at[own_rank],
                extra_sems[3 * n :],
                slot,
                there,
            )
            copy.start()
            started.append(copy)
        copy = pltpu.make_async_copy(
            extra_sources[n].at[own_rank], extra_targets[n].at[own_rank], extra_sems[3 * n + 2]
        )
        copy.start()
        local.append(copy)
    for k in range(depth):
        index = at.block(at.near_of(at.c), at.next_z(k), at.c)
        for n in range(count):
            arrive(n, index, near_kind, k)
            push(n, targets[n].at[index], index, far_kind, depth + k, at.far())
            push(n, targets[n].at[index], index, core_kind, depth + k, at.core())
    for j in range(2 * depth):
        column = at.far_of(at.c) if j < depth else at.other_column
        index = at.block(column, at.next_z(j % depth), at.c)
        for n in range(count):
            arrive(n, index, far_kind, j)
            push(n, targets[n].at[index], index, core_kind, 2 * depth + j, at.core())
    core = 1 - at.c
    columns = [at.own_column, at.near_of(core), at.far_of(core), at.other_column]
    for j in range(4 * depth):
        index = at.block(columns[j // depth], at.next_z(j % depth), core)
        for n in range(count):
            arrive(n, index, core_kind, j)
    for n in range(extra):
        for slot, (k, core) in enumerate(ranks):
            target = extra_targets[n].at[at.along(depth - k) * 2 + lax.rem(at.c + core, 2)]
            remote(target, target, extra_sems[3 * n :], slot, at.core()).wait_recv()

    @pl.when(inner)
    def _():
        for n in range(count):
            forward(n, sources[n], 0).wait_send()
            for k in others:
                index = at.block(at.own_column, at.next_z(k), at.c)
                forward(n, targets[n].at[index], k).wait_send()

    for copy in started:
        copy.wait_send()
    for copy in local:
        copy.wait()


def spread(depth, ident, arrays, extras=()):
    sems = []
    for _ in arrays:
        sems += pair(depth + 1) + pair(depth) + pair(2 * depth) + pair(4 * depth)
        sems.append(pltpu.SemaphoreType.DMA)
    for _ in extras:
        sems += pair(2 * depth - 1) + [pltpu.SemaphoreType.DMA]
    count = len(arrays) + len(extras)
    shapes = [((8 * depth,) + a.shape, a.dtype) for a in arrays]
    shapes += [(a.shape, a.dtype) for a in extras]
    return pl.pallas_call(
        functools.partial(spread_kernel, depth, len(arrays), len(extras)),
        out_shape=[jax.ShapeDtypeStruct(*shape) for shape in shapes],
        in_specs=in_hbm(count),
        out_specs=in_hbm(count),
        scratch_shapes=sems,
        compiler_params=pltpu.CompilerParams(
            collective_id=ident, has_side_effects=True, vmem_limit_bytes=60 << 20
        ),
        cost_estimate=pl.CostEstimate(
            flops=0,
            bytes_accessed=sum(64 * depth * a.size * a.dtype.itemsize for a in arrays),
            transcendentals=0,
        ),
    )(*arrays, *extras)


def sum_rows(target, lead, terms):
    rows = target.shape[-2]
    tile = min(rows, 16)

    def body(i, carry):
        at = pl.ds(pl.multiple_of(i * tile, tile), tile)
        total = terms[0][0][(*terms[0][1], at, slice(None))].astype(high_type)
        for ref, where in terms[1:]:
            total = total + ref[(*where, at, slice(None))].astype(high_type)
        target[(*lead, at, slice(None))] = total.astype(target.dtype)
        return carry

    lax.fori_loop(0, rows // tile, body, 0)


def collect_kernel(depth, local, counts, *refs):
    rest = iter(refs)

    def take(count):
        return [next(rest) for _ in range(count)]

    mains, smalls, shareds, extras = (take(count) for count in counts)
    halves = take(2 if local else 0)
    main_totals, small_totals, shared_totals, extra_outs = (take(count) for count in counts)
    unpacked = take(1 if local else 0)
    main_buffers = [take(5) for _ in mains]
    small_buffers = [take(5) for _ in smalls]
    shared_buffers = [take(3) for _ in shareds]
    shared_outs = [take(1)[0] for _ in shareds]
    main_sems = [take(9) for _ in mains]
    small_sems = [take(9) for _ in smalls]
    shared_sems = [take(7) for _ in shareds]
    extra_sems = [take(3) for _ in extras]
    at = Place(depth)
    ranks = [(k, core) for k in range(depth) for core in range(2) if k or core]
    peers = [at.chip(k, lax.rem(at.c + core, 2)) for k, core in ranks]
    meet([at.near(), at.far()] + peers)
    started = []
    own_rank = at.z * 2 + at.c

    def columns(core):
        return at.other_column, at.far_of(core), at.near_of(core), at.own_column

    def number(column):
        return column[0] * 2 + column[1]

    def push(copy):
        copy.start()
        started.append(copy)

    def arrive(buffer, pair_of, slot):
        remote(buffer.at[slot], buffer.at[slot], pair_of, slot, at.core()).wait_recv()

    def piece(ref, rank):
        rows = ref.shape[0] // (2 * depth)
        return ref.at[pl.ds(pl.multiple_of(rank * rows, rows), rows)]

    def block(group, k, core):
        return at.block(columns(core)[group], at.along(1 + k), core)

    def main_load(n, group, k):
        slot = group * depth + k
        return pltpu.make_async_copy(
            mains[n].at[block(group, k, at.c)], main_buffers[n][0].at[slot], main_sems[n][8].at[slot]
        )

    def main_cross(n, group, k):
        slot = group * depth + k
        source = mains[n].at[block(group, k, 1 - at.c)]
        push(remote(source, main_buffers[n][1].at[slot], main_sems[n][0:2], slot, at.core()))
        main_load(n, group, k).start()

    def main_sum(n, group, k, more):
        mine, crossed = main_buffers[n][:2]
        slot = group * depth + k
        main_load(n, group, k).wait()
        arrive(crossed, main_sems[n][0:2], slot)
        terms = [(mine, (slot,)), (crossed, (slot,))] + more
        if slot < 4 * depth - 1:
            sum_rows(mine, (slot,), terms)
        else:
            sum_rows(main_totals[n], (), terms)
        return mine.at[slot]

    def main_far(n, k):
        buffers, sems = main_buffers[n], main_sems[n]
        for group in range(2):
            slot = group * depth + k
            total = main_sum(n, group, k, [])
            push(remote(total, buffers[2].at[slot], sems[2:4], slot, at.far()))

    def main_near(n, k):
        buffers, sems = main_buffers[n], main_sems[n]
        arrive(buffers[2], sems[2:4], k)
        total = main_sum(n, 2, k, [(buffers[2], (k,))])
        push(remote(total, buffers[3].at[k], sems[4:6], k, at.near()))

    def main_own(n, k):
        buffers, sems = main_buffers[n], main_sems[n]
        arrive(buffers[2], sems[2:4], depth + k)
        arrive(buffers[3], sems[4:6], k)
        total = main_sum(n, 3, k, [(buffers[2], (depth + k,)), (buffers[3], (k,))])
        if k < depth - 1:
            push(remote(total, buffers[4].at[k], sems[6:8], k, at.chip(1 + k)))

    def small_load(n, group):
        return pltpu.make_async_copy(
            smalls[n].at[at.c, number(columns(at.c)[group])],
            small_buffers[n][0].at[group],
            small_sems[n][8].at[group],
        )

    def small_cross():
        for n, (part, buffers, sems) in enumerate(zip(smalls, small_buffers, small_sems)):
            for group in range(4):
                source = part.at[1 - at.c, number(columns(1 - at.c)[group])]
                push(remote(source, buffers[1].at[group], sems[0:2], group, at.core()))
                small_load(n, group).start()

    def small_sum(n, group, more):
        mine, crossed = small_buffers[n][:2]
        small_load(n, group).wait()
        arrive(crossed, small_sems[n][0:2], group)
        for j in range(depth):
            terms = [(mine, (group, j)), (crossed, (group, j))]
            sum_rows(mine, (group, j), terms + [(ref, (i, j)) for ref, i in more])
        return mine.at[group]

    def small_far():
        for n, (buffers, sems) in enumerate(zip(small_buffers, small_sems)):
            for group in range(2):
                total = small_sum(n, group, [])
                push(remote(total, buffers[2].at[group], sems[2:4], group, at.far()))

    def small_near():
        for n, (buffers, sems) in enumerate(zip(small_buffers, small_sems)):
            arrive(buffers[2], sems[2:4], 0)
            total = small_sum(n, 2, [(buffers[2], 0)])
            push(remote(total, buffers[3].at[0], sems[4:6], 0, at.near()))

    def small_own():
        for n, (buffers, sems) in enumerate(zip(small_buffers, small_sems)):
            arrive(buffers[2], sems[2:4], 1)
            arrive(buffers[3], sems[4:6], 0)
            total = small_sum(n, 3, [(buffers[2], 1), (buffers[3], 0)])
            for k in range(1, depth):
                there = at.chip(k)
                source = total.at[there[2]]
                push(remote(source, buffers[4].at[k - 1], sems[6:8], k - 1, there))

    def shared_load(n, i):
        return pltpu.make_async_copy(
            shareds[n].at[number(columns(at.c)[2 + i])], shared_buffers[n][0].at[i], shared_sems[n][0].at[i]
        )

    def shared_far():
        for n, (part, buffers, sems) in enumerate(zip(shareds, shared_buffers, shared_sems)):
            for i in range(2):
                source = part.at[number(columns(at.c)[i])]
                push(remote(source, buffers[1].at[i], sems[1:3], i, at.far()))
                shared_load(n, i).start()

    def shared_near():
        for n, ((mine, far_in, near_in), sems) in enumerate(zip(shared_buffers, shared_sems)):
            shared_load(n, 0).wait()
            arrive(far_in, sems[1:3], 0)
            sum_rows(mine, (0,), [(mine, (0,)), (far_in, (0,))])
            push(remote(mine.at[0], near_in.at[0], sems[3:5], 0, at.near()))

    def shared_own():
        for n, ((mine, far_in, near_in), sems) in enumerate(zip(shared_buffers, shared_sems)):
            shared_load(n, 1).wait()
            arrive(far_in, sems[1:3], 1)
            arrive(near_in, sems[3:5], 0)
            sum_rows(mine, (1,), [(mine, (1,)), (far_in, (1,)), (near_in, (0,))])
            for slot, there in enumerate(peers):
                source = piece(mine.at[1], there[2] * 2 + there[3])
                push(remote(source, piece(shared_outs[n], own_rank), sems[5:7], slot, there))
            shared_kept(n).start()

    def shared_kept(n):
        mine = shared_buffers[n][0]
        return pltpu.make_async_copy(
            piece(mine.at[1], own_rank), piece(shared_outs[n], own_rank), shared_sems[n][0].at[2]
        )

    def extra_kept(n):
        return pltpu.make_async_copy(
            extras[n].at[own_rank], extra_outs[n].at[own_rank], extra_sems[n][2]
        )

    last = len(mains) - 1
    stages = [(main_far, 0), (main_far, 1), (main_near, 0), (main_own, 0)]
    for k in range(2, depth):
        stages += [(main_far, k), (main_near, k - 1), (main_own, k - 1)]
    stages += [(main_near, depth - 1), (main_own, depth - 1)]
    order = [(stage, n, k) for n in range(len(mains)) for stage, k in stages]
    for n in range(last):
        ahead = [(main_far, n + 1, k) for k in range(2)]
        order = [step for step in order if step not in ahead]
        at_end = order.index((main_near, n, depth - 1))
        order[at_end:at_end] = ahead
    groups = {main_far: (0, 1), main_near: (2,), main_own: (3,)}
    shared_far()
    small_cross()
    for stage, n, k in order:
        for group in groups[stage]:
            main_cross(n, group, k)
    for n in range(len(extras)):
        for slot, there in enumerate(peers):
            source = extras[n].at[there[2] * 2 + there[3]]
            push(remote(source, extra_outs[n].at[own_rank], extra_sems[n][:2], slot, there))
        extra_kept(n).start()
    small_far()
    for stage, n, k in order:
        stage(n, k)
        if (stage, n, k) == (main_near, 0, 0):
            shared_near()
            small_near()
        if (stage, n, k) == (main_own, 0, 0):
            shared_own()
            small_own()
    if local:
        unpack_inside(local, *halves, *unpacked)
    for n, (buffers, sems) in enumerate(zip(small_buffers, small_sems)):
        for k in range(depth - 1):
            arrive(buffers[4], sems[6:8], k)
        terms = [(buffers[0], (3, at.z))] + [(buffers[4], (k,)) for k in range(depth - 1)]
        sum_rows(small_totals[n], (), terms)
    for n, (buffers, sems) in enumerate(zip(main_buffers, main_sems)):
        for k in range(depth - 1):
            arrive(buffers[4], sems[6:8], k)
        terms = [(main_totals[n], ())] + [(buffers[4], (k,)) for k in range(depth - 1)]
        sum_rows(main_totals[n], (), terms)
    for slot, (k, core) in enumerate(ranks):
        source = at.along(depth - k) * 2 + lax.rem(at.c + core, 2)
        for n in range(len(shareds)):
            target = piece(shared_outs[n], source)
            remote(target, target, shared_sems[n][5:7], slot, at.core()).wait_recv()
        for n in range(len(extras)):
            target = extra_outs[n].at[source]
            remote(target, target, extra_sems[n][:2], slot, at.core()).wait_recv()
    for n in range(len(shareds)):
        shared_kept(n).wait()
        out, held = shared_totals[n], shared_outs[n]
        count, rows = out.shape[:2]
        heads = held.shape[1] // (count * HD)
        for rank in range(2 * depth):
            for i in range(count):
                for j in range(heads):
                    head = (rank % 2 * heads + j) * depth + rank // 2
                    value = held[rank * rows : (rank + 1) * rows, (i * heads + j) * HD :][:, :HD]
                    out[i, :, head * HD : (head + 1) * HD] = value.astype(out.dtype)
    for n in range(len(extras)):
        extra_kept(n).wait()
    for copy in started:
        copy.wait_send()


def collect(depth, ident, mains, smalls, shareds=(), extras=(), to_unpack=(0,)):
    local, *halves = to_unpack
    dma = pltpu.SemaphoreType.DMA
    peers = 2 * depth - 1

    def by_core(a):
        return a.reshape((4, depth, 2) + a.shape[1:]).transpose(2, 0, 1, 3, 4)

    smalls = [by_core(a) for a in smalls]
    buffers, sems, shapes = [], [], []
    for a in mains:
        for slots in (4 * depth, 4 * depth, 2 * depth, depth, depth - 1):
            buffers.append(pltpu.VMEM((slots,) + a.shape[1:], a.dtype))
        sems += pair(4 * depth) + pair(2 * depth) + pair(depth) + pair(depth - 1)
        sems.append(dma((4 * depth,)))
        shapes.append(jax.ShapeDtypeStruct(a.shape[1:], high_type))
    for a in smalls:
        for slots in ((4, depth), (4, depth), (2, depth), (1, depth), (depth - 1,)):
            buffers.append(pltpu.VMEM(slots + a.shape[3:], a.dtype))
        sems += pair(4) + pair(2) + pair(1) + pair(depth - 1) + [dma((4,))]
        shapes.append(jax.ShapeDtypeStruct(a.shape[3:], high_type))
    for a in shareds:
        buffers += [pltpu.VMEM((slots,) + a.shape[1:], a.dtype) for slots in (2, 2, 1)]
        buffers.append(pltpu.VMEM(a.shape[1:], a.dtype))
        sems += [dma((3,))] + pair(2) + pair(1) + pair(peers)
        shape = (3, a.shape[1] // (2 * depth), a.shape[2] // 3 * 2 * depth)
        shapes.append(jax.ShapeDtypeStruct(shape, high_type))
    for a in extras:
        sems += pair(peers) + [dma]
        shapes.append(jax.ShapeDtypeStruct(a.shape, a.dtype))
    arrays = [*mains, *smalls, *shareds, *extras]
    counts = (len(mains), len(smalls), len(shareds), len(extras))
    if halves:
        lines = halves[0].size // 64
        shapes.append(jax.ShapeDtypeStruct((lines, 128), high_type))
    in_vmem = [pl.BlockSpec(memory_space=pltpu.VMEM)] * (len(arrays) - len(extras))
    return pl.pallas_call(
        functools.partial(collect_kernel, depth, local, counts),
        out_shape=shapes,
        in_specs=in_hbm(len(arrays) + len(halves)),
        out_specs=in_vmem + in_hbm(len(extras) + len(halves) // 2),
        scratch_shapes=buffers + sems,
        compiler_params=pltpu.CompilerParams(
            collective_id=ident, has_side_effects=True, vmem_limit_bytes=60 << 20
        ),
        cost_estimate=pl.CostEstimate(
            flops=0,
            bytes_accessed=sum(16 * a.size * a.dtype.itemsize for a in arrays),
            transcendentals=0,
        ),
    )(*arrays, *halves)


def gather_kernel(depth, local_experts, x_ref, o_ref, w_ref, s_ref, in_ref, down_ref, *refs):
    x_out, o_out, w_out, s_out = refs[:4]
    packed, sems = refs[4:8], refs[8:]
    at = Place(depth)
    ranks = [(k, core) for k in range(depth) for core in range(2) if k or core]
    peers = [at.chip(k, lax.rem(at.c + core, 2)) for k, core in ranks]
    meet([at.near(), at.far()] + peers)
    own, column = at.z * 2 + at.c, at.y * 2 + at.x
    x_z, x_core, o_z, o_near, o_far, o_core, w_sems, s_sems, w_side, s_side = (
        sems[2 * i : 2 * i + 2] for i in range(10)
    )
    started, local = [], []
    inner = lax.rem(at.z, depth - 1) != 0
    onward = (at.z + 1, at.z + 1, at.z - 1, 3 * at.z - 3)
    own_block = at.block(at.own_column, at.z, at.c)

    def push(copy):
        copy.start()
        started.append(copy)

    def arrive(target, pair_of, slot):
        remote(target, target, pair_of, slot, at.core()).wait_recv()

    def x_place(k):
        return x_out.at[at.next_z(k) * 2 + at.c]

    def o_place(k):
        return o_out.at[at.block(at.own_column, at.next_z(k), at.c)]

    def forward(source, target, pair_of, k):
        z = at.next_z(k)
        return pltpu.make_async_remote_copy(
            src_ref=source,
            dst_ref=target,
            send_sem=pair_of[0].at[z if k else depth],
            recv_sem=pair_of[1].at[z],
            device_id=(at.y, at.x, onward[k], at.c),
            device_id_type=MESH_ID,
        )

    for slot, there in enumerate(peers):
        push(remote(s_ref, s_out.at[column, own], s_sems, slot, there))
        source = w_ref.at[there[2] * 2 + there[3]]
        push(remote(source, w_out.at[column, own], w_sems, slot, there))
    first = (at.y, at.x, at.next_z(1), at.c)
    push(remote(o_ref, o_place(0), o_z, at.z, first))
    push(remote(x_ref, x_place(0), x_z, at.z, first))

    @pl.when(inner)
    def _():
        forward(o_ref, o_place(0), o_z, 0).start()
        forward(x_ref, x_place(0), x_z, 0).start()

    push(remote(x_ref, x_place(0), x_core, 0, at.core()))
    push(remote(o_ref, o_place(0), o_near, 0, at.near()))
    push(remote(o_ref, o_place(0), o_far, 0, at.far()))
    push(remote(o_ref, o_place(0), o_core, 0, at.core()))
    for i, (source, target) in enumerate(
        (
            (x_ref, x_place(0)),
            (o_ref, o_place(0)),
            (w_ref.at[own], w_out.at[column, own]),
            (s_ref, s_out.at[column, own]),
        )
    ):
        copy = pltpu.make_async_copy(source, target, sems[20].at[i])
        copy.start()
        local.append(copy)
    near_y, near_x = at.near_of(at.c)
    far_y, far_x = at.far_of(at.c)
    beside, across = near_y * 2 + near_x, far_y * 2 + far_x
    sides = ((s_out, s_side), (w_out, w_side))
    pack(2 * depth, local_experts, in_ref, down_ref, *packed)
    for slot, (j, core) in enumerate(ranks):
        source = at.along(depth - j) * 2 + lax.rem(at.c + core, 2)
        arrive(s_out.at[column, source], s_sems, slot)
        arrive(w_out.at[column, source], w_sems, slot)
    for copy in local:
        copy.wait()
    for target, pair_of in sides:
        push(remote(target.at[column], target.at[column], pair_of, 0, at.near()))
        push(remote(target.at[column], target.at[column], pair_of, 1, at.far()))
    for k in range(1, depth):
        arrive(o_place(k), o_z, at.next_z(k))

        @pl.when(inner)
        def _(k=k):
            forward(o_place(k), o_place(k), o_z, k).start()

        push(remote(o_place(k), o_place(k), o_near, k, at.near()))
        push(remote(o_place(k), o_place(k), o_far, k, at.far()))
        push(remote(o_place(k), o_place(k), o_core, k, at.core()))
        arrive(x_place(k), x_z, at.next_z(k))

        @pl.when(inner)
        def _(k=k):
            forward(x_place(k), x_place(k), x_z, k).start()

        push(remote(x_place(k), x_place(k), x_core, k, at.core()))
        if k == 2:
            for target, pair_of in sides:
                arrive(target.at[beside], pair_of, 0)
                push(remote(target.at[beside], target.at[beside], pair_of, 2, at.far()))
    for k in range(depth):
        target = o_out.at[at.block(at.near_of(at.c), at.next_z(k), at.c)]
        arrive(target, o_near, k)
        push(remote(target, target, o_far, depth + k, at.far()))
        push(remote(target, target, o_core, depth + k, at.core()))
    for j in range(2 * depth):
        place = at.far_of(at.c) if j < depth else at.other_column
        target = o_out.at[at.block(place, at.next_z(j % depth), at.c)]
        arrive(target, o_far, j)
        push(remote(target, target, o_core, 2 * depth + j, at.core()))
    for target, pair_of in sides:
        arrive(target.at[across], pair_of, 1)
        arrive(target.at[3 - column], pair_of, 2)
    for k in range(depth):
        arrive(x_out.at[at.next_z(k) * 2 + 1 - at.c], x_core, k)
    core = 1 - at.c
    places = [at.own_column, at.near_of(core), at.far_of(core), at.other_column]
    for j in range(4 * depth):
        index = at.block(places[j // depth], at.next_z(j % depth), core)
        arrive(o_out.at[index], o_core, j)

    @pl.when(inner)
    def _():
        forward(x_ref, x_place(0), x_z, 0).wait_send()
        forward(o_ref, o_place(0), o_z, 0).wait_send()
        for k in range(1, depth):
            forward(x_place(k), x_place(k), x_z, k).wait_send()
            forward(o_place(k), o_place(k), o_z, k).wait_send()

    for copy in started:
        copy.wait_send()


def gather(depth, ident, x, o, w, s, expert_in, expert_down):
    chunk, local = expert_in.shape[:2]
    ranks = 2 * depth
    sems = pair(depth + 1) + pair(depth) + pair(depth + 1) + pair(depth) + pair(2 * depth)
    sems += pair(4 * depth) + pair(ranks - 1) * 2 + pair(3) * 2
    sems.append(pltpu.SemaphoreType.DMA((4,)))
    return pl.pallas_call(
        functools.partial(gather_kernel, depth, local),
        out_shape=[
            jax.ShapeDtypeStruct((ranks,) + x.shape, x.dtype),
            jax.ShapeDtypeStruct((4 * ranks,) + o.shape, o.dtype),
            jax.ShapeDtypeStruct((4,) + w.shape, w.dtype),
            jax.ShapeDtypeStruct((4, ranks) + s.shape, s.dtype),
        ]
        + [jax.ShapeDtypeStruct((ranks, chunk, local * 128), low_type)] * 2
        + [jax.ShapeDtypeStruct((ranks, chunk, local * 64), low_type)] * 2,
        in_specs=in_hbm(6),
        out_specs=in_hbm(8),
        scratch_shapes=sems,
        compiler_params=pltpu.CompilerParams(
            collective_id=ident, has_side_effects=True, vmem_limit_bytes=60 << 20
        ),
        cost_estimate=pl.CostEstimate(
            flops=0, bytes_accessed=64 * depth * x.size, transcendentals=0
        ),
    )(x, o, w, s, lines_in(expert_in), lines_down(expert_down))


def exchange_kernel(depth, same, x_ref, out_ref, send_sems, recv_sems, local_sem):
    at = Place(depth)
    ranks = [(k, core) for k in range(depth) for core in range(2) if k or core]
    peers = [at.chip(k, lax.rem(at.c + core, 2)) for k, core in ranks]
    meet(peers)
    own = at.z * 2 + at.c
    copies = []
    for slot, there in enumerate(peers):
        source = x_ref if same else x_ref.at[there[2] * 2 + there[3]]
        copy = remote(source, out_ref.at[own], (send_sems, recv_sems), slot, there)
        copy.start()
        copies.append(copy)
    local = pltpu.make_async_copy(x_ref if same else x_ref.at[own], out_ref.at[own], local_sem)
    local.start()
    for slot, (k, core) in enumerate(ranks):
        target = out_ref.at[at.along(depth - k) * 2 + lax.rem(at.c + core, 2)]
        remote(target, target, (send_sems, recv_sems), slot, at.core()).wait_recv()
    for copy in copies:
        copy.wait_send()
    local.wait()


def exchange(depth, ident, x, same=False):
    ranks = 2 * depth
    return pl.pallas_call(
        functools.partial(exchange_kernel, depth, same),
        out_shape=jax.ShapeDtypeStruct((ranks,) + x.shape if same else x.shape, x.dtype),
        in_specs=in_hbm(1),
        out_specs=in_hbm(1)[0],
        scratch_shapes=pair(ranks - 1) + [pltpu.SemaphoreType.DMA],
        compiler_params=pltpu.CompilerParams(
            collective_id=ident, has_side_effects=True, vmem_limit_bytes=16 << 20
        ),
        cost_estimate=pl.CostEstimate(
            flops=0, bytes_accessed=16 * x.size * x.dtype.itemsize, transcendentals=0
        ),
    )(x)


def column_kernel(depth, part, total, mine, crossed, z_in, *sems):
    at = Place(depth)
    meet([at.core()] + [at.chip(k) for k in range(1, depth)])
    started = []
    inner = lax.rem(at.z, depth - 1) != 0
    inside = lax.div(lax.rem(at.z, depth - 1) + 1, 2)
    onto = (None, at.next_z(1), at.z + 1 - 2 * lax.div(at.z, 3), 1 + lax.rem(at.z, 2))
    slots = (
        None,
        5 - lax.div(4 - at.z, 4),
        4 * inside + (1 - inside) * at.next_z(2),
        at.next_z(3),
    )

    def local(k):
        return pltpu.make_async_copy(part.at[at.next_z(k) * 2 + at.c], mine.at[k], sems[4].at[k])

    def cross(k):
        source = part.at[at.next_z(k) * 2 + 1 - at.c]
        return remote(source, crossed.at[k], sems[0:2], k, at.core())

    def arrive(slot):
        remote(z_in.at[slot], z_in.at[slot], sems[2:4], slot, at.core()).wait_recv()

    def hand_on(k):
        return pltpu.make_async_remote_copy(
            src_ref=mine.at[k],
            dst_ref=z_in.at[slots[k]],
            send_sem=sems[2].at[k],
            recv_sem=sems[3].at[slots[k]],
            device_id=(at.y, at.x, onto[k], at.c),
            device_id_type=MESH_ID,
        )

    order = tuple(range(depth - 1, -1, -1))
    for k in order:
        cross(k).start()
        local(k).start()
    for k in order:
        local(k).wait()
        cross(k).wait_recv()
        terms = [(mine, (k,)), (crossed, (k,))]
        if k == 0:
            sum_rows(total, (), terms)
            continue

        @pl.when(inner)
        def _(terms=terms, k=k):
            arrive(at.next_z(k))
            sum_rows(mine, (k,), terms + [(z_in, (at.next_z(k),))])

        @pl.when(lax.rem(at.z, depth - 1) == 0)
        def _(terms=terms, k=k):
            sum_rows(mine, (k,), terms)

        hand_on(k).start()

    @pl.when(inner)
    def _():
        arrive(4)
        arrive(5)
        sum_rows(total, (), [(total, ()), (z_in, (4,)), (z_in, (5,))])

    @pl.when(lax.rem(at.z, depth - 1) == 0)
    def _():
        slot = 5 - lax.div(at.z, 3)
        arrive(slot)
        sum_rows(total, (), [(total, ()), (z_in, (slot,))])

    for k in order:
        cross(k).wait_send()
        if k:
            hand_on(k).wait_send()


def collect_column(depth, ident, part):
    block = part.shape[1:]
    return pl.pallas_call(
        functools.partial(column_kernel, depth),
        out_shape=jax.ShapeDtypeStruct(block, high_type),
        in_specs=in_hbm(1),
        out_specs=pl.BlockSpec(memory_space=pltpu.VMEM),
        scratch_shapes=[pltpu.VMEM((slots,) + block, part.dtype) for slots in (depth, depth, 6)]
        + pair(depth)
        + pair(6)
        + [pltpu.SemaphoreType.DMA((depth,))],
        compiler_params=pltpu.CompilerParams(
            collective_id=ident, has_side_effects=True, vmem_limit_bytes=32 << 20
        ),
        cost_estimate=pl.CostEstimate(
            flops=0, bytes_accessed=16 * part.size * part.dtype.itemsize, transcendentals=0
        ),
    )(part)


def lines_in(values):
    rows, local, two, hidden = values.shape
    values = values.reshape(rows, local, two, hidden // 128, 128)
    return values.transpose(0, 1, 3, 2, 4).reshape(-1, 128)


def lines_down(values):
    rows, local, hidden = values.shape
    return values.reshape(rows, local, hidden // 128, 128).transpose(0, 2, 1, 3).reshape(-1, 128)


def lines_of(ranks, local):
    half, of_in, of_down = local // 2, [], []
    for rank in range(ranks):
        for x in range(local):
            for k in range(2):
                line = (x * ranks + rank) * 2 + k
                columns = (k * half + x % half) * 128
                of_in.append((rank, x // half, columns, line, 2 * local * ranks))
            of_down.append((rank, x // half, x % half * 128, rank * local + x, local * ranks))
    return of_in, of_down


def pack_kernel(ranks, local, step, in_ref, down_ref, *outs):
    of_in, of_down = lines_of(ranks, local)
    for lines, ref, targets in ((of_in, in_ref, outs[:2]), (of_down, down_ref, outs[2:])):
        for rank, half, column, line, stride in lines:
            value = ref[pl.ds(line, step, stride=stride), :]
            targets[half][rank, :, column : column + 128] = value.astype(low_type)


def pack(ranks, local, in_ref, down_ref, *outs):
    step = 32
    lines = step * local * ranks

    def slices(span):
        return pl.BlockSpec((ranks, step, span), lambda i: (0, i, 0))

    pltpu.emit_pipeline(
        functools.partial(pack_kernel, ranks, local, step),
        grid=(outs[0].shape[1] // step,),
        in_specs=[
            pl.BlockSpec((2 * lines, 128), lambda i: (i, 0)),
            pl.BlockSpec((lines, 128), lambda i: (i, 0)),
        ],
        out_specs=[slices(out.shape[2]) for out in outs],
    )(in_ref, down_ref, *outs)


def unpack_kernel(ranks, local, step, first_ref, second_ref, out_ref):
    of_in, of_down = lines_of(ranks, local)
    for rank, half, column, line, stride in (
        of_in if first_ref.shape[2] == local * 128 else of_down
    ):
        value = (first_ref, second_ref)[half][rank, :, column : column + 128]
        out_ref[pl.ds(line, step, stride=stride), :] = value.astype(high_type)


def unpack_inside(local, first_ref, second_ref, out_ref):
    ranks, rows, span = first_ref.shape
    step = 32
    pltpu.emit_pipeline(
        functools.partial(unpack_kernel, ranks, local, step),
        grid=(rows // step,),
        in_specs=[pl.BlockSpec((ranks, step, span), lambda i: (0, i, 0))] * 2,
        out_specs=[pl.BlockSpec((step * ranks * span // 64, 128), lambda i: (i, 0))],
    )(first_ref, second_ref, out_ref)


def unpack(local, *halves):
    ranks, rows, span = halves[0].shape
    step = 32
    lines = step * ranks * span // 64
    return pl.pallas_call(
        functools.partial(unpack_kernel, ranks, local, step),
        grid=(rows // step,),
        in_specs=[pl.BlockSpec((ranks, step, span), lambda i: (0, i, 0))] * 2,
        out_specs=pl.BlockSpec((lines, 128), lambda i: (i, 0)),
        out_shape=jax.ShapeDtypeStruct((rows * ranks * span // 64, 128), high_type),
        compiler_params=pltpu.CompilerParams(vmem_limit_bytes=32 << 20),
    )(*halves)


def experts_kernel(first, depth, earlier, extra_count, *refs):
    rest = iter(refs)

    def take(count):
        return [next(rest) for _ in range(count)]

    tokens_ref, grads_ref, gates_ref, in_ref, down_ref = take(5)
    added = take(3) if earlier else None
    extra_refs = take(extra_count)
    back_ref, mixed_ref, sums_ref, grad_in_ref, grad_down_ref = take(5)
    extra_outs = take(extra_count)
    in_total, down_total = take(2)
    extra_sems = [take(3) for _ in extra_refs]
    column = lax.axis_index("ey") * 2 + lax.axis_index("ex")
    step, steps = pl.program_id(0), pl.num_programs(0)
    blocks, experts, rows = gates_ref.shape
    span = down_ref.shape[1]
    width = tokens_ref.shape[2]
    at = Place(depth)
    ranks = [(k, core) for k in range(depth) for core in range(2) if k or core]
    peers = [at.chip(k, lax.rem(at.c + core, 2)) for k, core in ranks]
    own_rank = at.z * 2 + at.c

    def extra_copies():
        return [
            remote(source.at[there[2] * 2 + there[3]], target.at[own_rank], sems, slot, there)
            for source, target, sems in zip(extra_refs, extra_outs, extra_sems)
            for slot, there in enumerate(peers)
        ]

    def kept():
        return [
            pltpu.make_async_copy(source.at[own_rank], target.at[own_rank], sems[2])
            for source, target, sems in zip(extra_refs, extra_outs, extra_sems)
        ]

    @pl.when(step == 0)
    def _():
        meet(peers)
        for copy in extra_copies() + kept():
            copy.start()
        in_total[...] = jnp.zeros_like(in_total)
        down_total[...] = jnp.zeros_like(down_total)

    units_of = (
        lax.broadcasted_iota(jnp.int32, (experts, span), 1) // 128 + column * 4 + first
        == lax.broadcasted_iota(jnp.int32, (experts, span), 0)
    ).astype(low_type)

    def terms(values, count):
        result = []
        for _ in range(count):
            result.append(values.astype(low_type))
            values = values - result[-1].astype(high_type)
        return result

    tokens = tokens_ref[...].reshape(blocks * rows, width)
    grads = grads_ref[...].reshape(blocks * rows, width)
    gates = jnp.concatenate([gates_ref[b] for b in range(blocks)], axis=1)
    gates = jnp.concatenate(terms(gates, 3), axis=0)
    wide = t_dot(gates, jnp.concatenate([units_of] * 3, axis=0))
    both = dot(tokens, in_ref[...])
    gate_part, up_part = both[:, :span], both[:, span:]
    down_grad = dot(grads, down_ref[...])
    sigma = 0.5 + 0.5 * jnp.tanh(0.5 * gate_part)
    silu = gate_part * sigma
    hidden = (silu * up_part).astype(low_type).astype(high_type)
    weighted = (wide * hidden).astype(low_type)
    inner = hidden * down_grad
    high, low = terms(inner, 2)
    sums = dot_t(units_of, high) + dot_t(units_of, low)
    for b in range(blocks):
        part = sums[:, b * rows : (b + 1) * rows]
        sums_ref[b] = part + added[2][b] if earlier else part
    grad_hidden = wide * down_grad
    grad_gate = grad_hidden * up_part * (sigma + silu * (1.0 - sigma))
    grad_both = jnp.concatenate([grad_gate, grad_hidden * silu], axis=1).astype(low_type)
    back = dot_t(grad_both, in_ref[...]).reshape(back_ref.shape)
    mixed = dot_t(weighted, down_ref[...]).reshape(mixed_ref.shape)
    if earlier:
        back = back + added[0][...].astype(high_type)
        mixed = mixed + added[1][...].astype(high_type)
    back_ref[...] = back.astype(low_type)
    mixed_ref[...] = mixed.astype(low_type)
    in_total[...] += t_dot(tokens, grad_both)
    down_total[...] += t_dot(grads, weighted)

    @pl.when(step == steps - 1)
    def _():
        grad_in_ref[...] = in_total[...].astype(low_type)
        grad_down_ref[...] = down_total[...].astype(low_type)
        for copy in kept() + extra_copies():
            copy.wait()


def run_experts(depth, ident, first, tokens, grads, gates, weights_in, weights_down, extras, earlier):
    devices, rows, width = tokens.shape
    experts = gates.shape[1]
    blocks = 4
    span = weights_in.shape[1] // 2

    def by_step(shape):
        return pl.BlockSpec((blocks,) + shape, lambda i: (i, 0, 0))

    def whole(shape):
        return pl.BlockSpec(shape, lambda i: (0, 0), pipeline_mode=pl.Buffered(1))

    per_token = [by_step((rows, width)), by_step((rows, width)), by_step((experts, rows))]
    sums = [jax.ShapeDtypeStruct((devices, rows, width), low_type)] * 2
    sums.append(jax.ShapeDtypeStruct((devices, experts, rows), high_type))
    return pl.pallas_call(
        functools.partial(experts_kernel, first, depth, bool(earlier), len(extras)),
        grid=(devices // blocks,),
        in_specs=per_token
        + [whole((width, 2 * span)), whole((width, span))]
        + (per_token if earlier else [])
        + in_hbm(len(extras)),
        out_specs=per_token
        + [whole((width, 2 * span)), whole((width, span))]
        + in_hbm(len(extras)),
        out_shape=sums
        + [
            jax.ShapeDtypeStruct((width, 2 * span), low_type),
            jax.ShapeDtypeStruct((width, span), low_type),
        ]
        + [jax.ShapeDtypeStruct(extra.shape, extra.dtype) for extra in extras],
        scratch_shapes=[
            pltpu.VMEM((width, 2 * span), high_type),
            pltpu.VMEM((width, span), high_type),
        ]
        + (pair(2 * depth - 1) + [pltpu.SemaphoreType.DMA]) * len(extras),
        compiler_params=pltpu.CompilerParams(
            collective_id=ident, has_side_effects=True, vmem_limit_bytes=60 << 20
        ),
        cost_estimate=pl.CostEstimate(
            flops=18 * devices * rows * width * span,
            bytes_accessed=8 * devices * rows * width,
            transcendentals=devices * rows * span,
        ),
    )(tokens, grads, gates, weights_in, weights_down, *earlier, *extras)


def grid_shards(
    residual_in,
    cotangent,
    lengths,
    routes,
    attn_qkv,
    attn_out,
    gains,
    router,
    expert_in,
    expert_down,
):
    rows, width = residual_in.shape
    depth = lax.axis_size("dz")
    ranks = 2 * depth
    columns = 4
    seq_rows = rows * ranks
    local_experts = expert_in.shape[1]
    experts = local_experts * columns
    hidden_width = expert_in.shape[3]
    part = hidden_width // ranks
    span = local_experts * part
    chunk_rows = expert_in.shape[0]
    weight_rows = attn_qkv.shape[1]
    score_scale = HD ** (-0.5)
    y, x, z, c = (lax.axis_index(name) for name in GRID)
    column = y * 2 + x
    own_heads = HEADS // ranks
    own_width = own_heads * HD

    def sum_column(ident, pairs):
        flat = exchange(depth, ident, pairs.reshape(-1, 128), same=True)
        return jnp.sum(flat, axis=0).reshape(pairs.shape)

    def by_rank(values):
        lead = values.shape[:-1]
        shaped = values.reshape(lead + (2, own_heads, depth, HD))
        n = len(lead)
        return shaped.transpose((n + 2, n) + tuple(range(n)) + (n + 1, n + 3)).reshape(
            (ranks,) + lead + (own_width,)
        )

    def by_head(values):
        lead = values.shape[1:-1]
        shaped = values.reshape((depth, 2) + lead + (own_heads, HD))
        n = len(lead)
        return shaped.transpose(tuple(range(2, n + 2)) + (1, n + 2, 0, n + 3)).reshape(
            lead + (width,)
        )

    small = jnp.concatenate([gains.T, router], axis=1).astype(low_type)
    small = jnp.pad(small, ((0, 0), (0, 128 - small.shape[1])))
    packed = attn_qkv.astype(low_type).transpose(1, 0, 2)
    packed = by_rank(packed).reshape(ranks, weight_rows, 3 * own_width)
    seq_input, out_weight, qkv_weight, small, first_in, second_in, first_down, second_down = gather(
        depth,
        0,
        residual_in,
        attn_out.astype(low_type),
        packed,
        small,
        expert_in,
        expert_down,
    )
    out_weight = out_weight.reshape(width, width)
    qkv_weight = qkv_weight.reshape(width, 3 * own_width)
    small = small.reshape(width, 128)
    gain_rows = small[:, :4].T.astype(high_type)
    router_weight = small[:, 4 : 4 + experts]
    gain_own = [
        lax.dynamic_index_in_dim(by_rank(gain_rows[i]), z * 2 + c, 0, keepdims=False)
        for i in (1, 2)
    ]
    normed_in = seq_input.reshape(seq_rows, width).astype(high_type)
    normed_in = (normed_in * rms_scale(normed_in) * gain_rows[0]).astype(low_type)
    raw = dot(normed_in, qkv_weight)
    query_raw, key_raw = raw[:, :own_width], raw[:, own_width : 2 * own_width]
    value_rows = raw[:, 2 * own_width :].astype(low_type)
    squares = jnp.stack(
        [jnp.sum(query_raw * query_raw, axis=1), jnp.sum(key_raw * key_raw, axis=1)]
    )
    scales = lax.rsqrt(sum_column(1, squares) / width + epsilon)
    query_scale, key_scale = scales[0][:, None], scales[1][:, None]
    positions = jnp.arange(seq_rows, dtype=jnp.int32)
    length_now = lengths[0]
    key_live = positions < length_now
    cosine, sine_table = angle_tables(positions)
    query_normed = query_raw * query_scale
    key_normed = key_raw * key_scale
    query_rot = rotate(query_normed * gain_own[0], cosine, sine_table).astype(low_type)
    key_rot = rotate(key_normed * gain_own[1], cosine, sine_table).astype(low_type)
    query_heads = query_rot.reshape(seq_rows, own_heads, HD)
    key_heads = key_rot.reshape(seq_rows, own_heads, HD)
    value_heads = value_rows.reshape(seq_rows, own_heads, HD)

    def per_head(spec, left, right):
        return jnp.einsum(spec, left, right, preferred_element_type=high_type)

    scores = per_head("qhd,khd->hqk", query_heads, key_heads) * score_scale
    scores = jnp.where(key_live[None, None, :], scores, masked_score)
    probs = jax.nn.softmax(scores, axis=-1)
    probs_low = probs.astype(low_type)
    attended = per_head("hqk,khd->qhd", probs_low, value_heads).astype(low_type)
    attended = exchange(depth, 2, attended.reshape(ranks, rows, own_width))
    attended = by_head(attended)

    own_positions = (z * 2 + c) * rows + jnp.arange(rows, dtype=jnp.int32)
    live_rows = (own_positions < length_now).astype(high_type)[:, None]
    input_rows = residual_in.astype(high_type)
    middle = input_rows + live_rows * dot(attended, out_weight)
    scale_mid = rms_scale(middle)
    normed_mid_f = middle * scale_mid
    normed_mid = (normed_mid_f * gain_rows[3]).astype(low_type)

    logits = dot(normed_mid, router_weight)
    named = jnp.any(
        routes[:, :, None] == jnp.arange(experts, dtype=jnp.int32)[None, None, :], axis=1
    )
    top = jnp.max(jnp.where(named, logits, -jnp.inf), axis=1, keepdims=True)
    weight_of = jnp.where(named, jnp.exp(jnp.where(named, logits - top, 0.0)), 0.0)
    gates = weight_of / jnp.sum(weight_of, axis=1, keepdims=True)

    grad_rows = cotangent.astype(high_type)
    grad_comb = live_rows * grad_rows
    after = jnp.minimum(scales[0, 0], 0.0)
    own_grads = (grad_comb + after).astype(low_type)
    grads = lax.all_gather(own_grads, GRID, axis=0, tiled=True)
    tokens, gates_all, first_in, first_down, second_down = spread(
        depth, 3, (normed_mid, gates.T), (first_in, first_down, second_down)
    )
    grads = grads.reshape(tokens.shape)

    def flat(values):
        return values.reshape(width, -1)

    def by_slice(values):
        return values.reshape(ranks, chunk_rows, -1)

    *sums, grad_first, down_first, second_in = run_experts(
        depth,
        9,
        0,
        tokens,
        grads,
        gates_all,
        flat(first_in),
        flat(first_down),
        (second_in,),
        (),
    )
    back, mixed, gate_sums, grad_second, down_second, grad_first = run_experts(
        depth,
        10,
        local_experts // 2,
        tokens,
        grads,
        gates_all,
        flat(second_in),
        flat(second_down),
        (by_slice(grad_first),),
        tuple(sums),
    )
    grad_mid_norm, combined, grad_gates, grad_second = collect(
        depth, 4, [back, mixed], [gate_sums], extras=[by_slice(grad_second)]
    )
    output = middle + live_rows * combined

    grad_gates = grad_gates.T
    grad_chosen = gates * (grad_gates - jnp.sum(gates * grad_gates, axis=1, keepdims=True))
    grad_logits = grad_chosen.astype(low_type)
    grad_mid_norm = grad_mid_norm + dot_t(grad_logits, router_weight)
    grad_router = t_dot(normed_mid, grad_logits)

    grad_mid_rows, grad_gain_mid = rms_back(grad_mid_norm, normed_mid_f, scale_mid, gain_rows[3])
    grad_middle = grad_rows + grad_mid_rows
    grad_branch = (live_rows * grad_middle).astype(low_type)

    grad_attended = by_rank(dot_t(grad_branch, out_weight).astype(low_type))
    grad_attended = exchange(depth, 6, grad_attended)
    grad_heads = grad_attended.reshape(seq_rows, own_heads, HD)
    grad_probs = per_head("qhd,khd->hqk", grad_heads, value_heads)
    inner_rows = jnp.sum(probs * grad_probs, axis=-1, keepdims=True)
    grad_scores = (probs * (grad_probs - inner_rows)).astype(low_type)
    grad_query = per_head("hqk,khd->qhd", grad_scores, key_heads) * score_scale
    grad_key = per_head("hqk,qhd->khd", grad_scores, query_heads) * score_scale
    grad_value = per_head("hqk,qhd->khd", probs_low, grad_heads).astype(low_type)
    grad_query = rotate(grad_query.reshape(seq_rows, own_width), cosine, -sine_table)
    grad_key = rotate(grad_key.reshape(seq_rows, own_width), cosine, -sine_table)
    query_inner = grad_query * gain_own[0]
    key_inner = grad_key * gain_own[1]
    inner = jnp.stack(
        [
            jnp.sum(query_inner * query_normed, axis=1),
            jnp.sum(key_inner * key_normed, axis=1),
        ]
    )
    inner = sum_column(7, inner) / width
    query_back = query_scale * (query_inner - query_normed * inner[0][:, None])
    key_back = key_scale * (key_inner - key_normed * inner[1][:, None])
    grad_raw = jnp.concatenate(
        [
            query_back.astype(low_type),
            key_back.astype(low_type),
            grad_value.reshape(seq_rows, own_width),
        ],
        axis=1,
    )

    share = dot_t(grad_raw, qkv_weight).astype(low_type).reshape(ranks, rows, width)
    grad_norm_in = collect_column(depth, 8, share)

    scale_in = rms_scale(input_rows)
    grad_in_rows, grad_gain_in = rms_back(
        grad_norm_in, input_rows * scale_in, scale_in, gain_rows[0]
    )
    grad_input = grad_middle + grad_in_rows

    def at_heads(values):
        whole = jnp.zeros((2, own_heads, depth, HD), high_type)
        values = values.reshape(1, own_heads, 1, HD)
        return lax.dynamic_update_slice(whole, values, (c, 0, z, 0)).reshape(width)

    grad_small = jnp.concatenate(
        [
            jnp.stack(
                [
                    grad_gain_in,
                    at_heads(jnp.sum(grad_query * query_normed, axis=0)),
                    at_heads(jnp.sum(grad_key * key_normed, axis=0)),
                    grad_gain_mid,
                ]
            ).T,
            grad_router,
        ],
        axis=1,
    )
    grad_small = jnp.pad(grad_small, ((0, 0), (0, 128 - grad_small.shape[1])))
    grad_out = t_dot(attended, grad_branch).astype(low_type)
    grad_qkv = t_dot(normed_in, grad_raw).astype(low_type)
    grad_out, grad_small, grad_qkv, down_first, down_second, grad_expert_in = collect(
        depth,
        5,
        [grad_out.reshape(-1, weight_rows, width)],
        [grad_small.reshape(-1, weight_rows, 128)],
        [grad_qkv.reshape(columns, -1, 3 * own_width)],
        [by_slice(down_first), by_slice(down_second)],
        (local_experts, grad_first, grad_second),
    )
    grad_expert_in = grad_expert_in.reshape(chunk_rows, local_experts, ranks, 2, part)
    grad_expert_in = grad_expert_in.transpose(0, 1, 3, 2, 4).reshape(expert_in.shape)
    grad_expert_down = unpack(local_experts, down_first, down_second).reshape(
        chunk_rows, ranks, local_experts, part
    )
    grad_expert_down = grad_expert_down.transpose(0, 2, 1, 3).reshape(expert_down.shape)
    return (
        output,
        grad_input,
        grad_qkv,
        grad_out,
        grad_small[:, :4].T,
        grad_small[:, 4 : 4 + experts],
        grad_expert_in,
        grad_expert_down,
    )


def slot_index(route_rows, experts, capacity):
    flat_routes = route_rows.reshape(-1)
    onehot = (flat_routes[:, None] == jnp.arange(experts, dtype=jnp.int32)[None, :]).astype(
        jnp.int32
    )
    rows = jnp.arange(flat_routes.shape[0], dtype=jnp.int32)
    earlier = (rows[None, :] < rows[:, None]).astype(jnp.bfloat16)
    before = jnp.dot(
        earlier, onehot.astype(jnp.bfloat16), preferred_element_type=jnp.float32
    ).astype(jnp.int32)
    rank_rows = jnp.sum(before * onehot, axis=1)
    return flat_routes * capacity + rank_rows


def head_scores(query_rot, key_all, key_live):
    row_count = query_rot.shape[0]
    query_heads = query_rot.reshape(row_count, HEADS, HD)
    key_heads = key_all.reshape(key_all.shape[0], HEADS, HD)
    raw_scores = jnp.einsum(
        "qhd,khd->hqk", query_heads, key_heads, preferred_element_type=jnp.float32
    ) * HD ** (-0.5)
    return jnp.where(key_live[None, None, :], raw_scores, masked_score)


def to_owners(buffer):
    return lax.all_to_all(buffer, "expert", split_axis=0, concat_axis=0, tiled=True)


def from_owners(buffer):
    return lax.all_to_all(buffer, "expert", split_axis=0, concat_axis=0, tiled=True)


def shards(
    residual_in,
    cotangent,
    lengths,
    routes,
    attn_qkv,
    attn_out,
    gains,
    router,
    expert_in,
    expert_down,
):
    tok_rows, model_width = residual_in.shape
    top_count = routes.shape[1]
    owners = lax.axis_size("expert")
    local_experts = expert_in.shape[1]
    experts = local_experts * owners
    capacity = tok_rows * top_count * 2 // experts
    local_slots = local_experts * capacity
    seq_rows = tok_rows * lax.axis_size("dp")
    score_scale = HD ** (-0.5)
    qkv_weights, out_weight, gain_low, router_weight = (
        lax.all_gather(attn_qkv.astype(low_type), ("expert", "dp"), axis=1, tiled=True),
        lax.all_gather(attn_out.astype(low_type), ("expert", "dp"), axis=0, tiled=True),
        lax.all_gather(gains.astype(low_type), ("expert", "dp"), axis=1, tiled=True),
        lax.all_gather(router.astype(low_type), ("expert", "dp"), axis=0, tiled=True),
    )
    gain_rows = gain_low.astype(high_type)
    input_rows = residual_in.astype(high_type)
    scale_in = rms_scale(input_rows)
    normed_in_f = input_rows * scale_in
    normed_in = (normed_in_f * gain_rows[0]).astype(low_type)
    query_raw = jnp.dot(normed_in, qkv_weights[0], preferred_element_type=high_type)
    key_raw = jnp.dot(normed_in, qkv_weights[1], preferred_element_type=high_type)
    value_rows = jnp.dot(normed_in, qkv_weights[2], preferred_element_type=high_type).astype(
        low_type
    )
    positions = lax.axis_index("dp") * tok_rows + jnp.arange(tok_rows, dtype=jnp.int32)
    length_now = lengths[0]
    live_rows = (positions < length_now).astype(high_type)[:, None]
    key_live = jnp.arange(seq_rows, dtype=jnp.int32) < length_now
    cosine, sine_table = angle_tables(positions)
    query_scale = rms_scale(query_raw)
    query_normed = query_raw * query_scale
    query_rot = rotate(query_normed * gain_rows[1], cosine, sine_table).astype(low_type)
    key_scale = rms_scale(key_raw)
    key_normed = key_raw * key_scale
    key_rot = rotate(key_normed * gain_rows[2], cosine, sine_table).astype(low_type)
    key_all = lax.all_gather(key_rot, "dp", axis=0, tiled=True)
    value_all = lax.all_gather(value_rows, "dp", axis=0, tiled=True)
    scores = head_scores(query_rot, key_all, key_live)
    top_score = jnp.max(scores, axis=-1, keepdims=True)
    exp_scores = jnp.exp(scores - top_score)
    row_total = jnp.sum(exp_scores, axis=-1, keepdims=True)
    weights_low = (exp_scores / row_total).astype(low_type)
    log_total = top_score + jnp.log(row_total)
    value_heads = value_all.reshape(seq_rows, HEADS, HD)
    attended = jnp.einsum(
        "hqk,khd->qhd", weights_low, value_heads, preferred_element_type=high_type
    )
    attended = attended.reshape(tok_rows, model_width).astype(low_type)
    branch = jnp.dot(attended, out_weight, preferred_element_type=high_type)
    middle = input_rows + live_rows * branch
    scale_mid = rms_scale(middle)
    normed_mid_f = middle * scale_mid
    normed_mid = (normed_mid_f * gain_rows[3]).astype(low_type)
    logits = jnp.dot(normed_mid, router_weight, preferred_element_type=high_type)
    selector = (routes[:, :, None] == jnp.arange(experts, dtype=jnp.int32)[None, None, :]).astype(
        high_type
    )
    chosen = jnp.einsum("te,tje->tj", logits, selector)
    gate_weights = jax.nn.softmax(chosen, axis=-1)
    slot_rows = slot_index(routes, experts, capacity)
    token_of = jnp.arange(slot_rows.shape[0], dtype=jnp.int32) // top_count
    send_rows = (
        jnp.zeros((experts * capacity, model_width), low_type)
        .at[slot_rows]
        .set(normed_mid[token_of])
    )
    rows_recv = lax.all_to_all(
        send_rows.reshape(owners, local_slots, model_width),
        "expert",
        split_axis=0,
        concat_axis=0,
        tiled=True,
    )
    rows_recv = rows_recv.reshape(owners, local_experts, capacity, model_width)
    weights_in, weights_down = (
        lax.all_gather(expert_in.astype(low_type), "dp", axis=0, tiled=True),
        lax.all_gather(expert_down.astype(low_type), "dp", axis=0, tiled=True),
    )
    both_parts = jnp.einsum(
        "sxmd,dxkf->sxmkf", rows_recv, weights_in, preferred_element_type=high_type
    )
    gate_part = both_parts[:, :, :, 0, :]
    up_part = both_parts[:, :, :, 1, :]
    hidden = (jax.nn.silu(gate_part) * up_part).astype(low_type)
    produced = jnp.einsum(
        "sxmf,dxf->sxmd", hidden, weights_down, preferred_element_type=high_type
    ).astype(low_type)
    returned = from_owners(produced.reshape(owners, local_slots, model_width))
    returned = returned.reshape(experts * capacity, model_width)
    picked = returned[slot_rows].reshape(tok_rows, top_count, model_width).astype(high_type)
    combined = jnp.sum(gate_weights[:, :, None] * picked, axis=1)
    output = middle + live_rows * combined
    grad_rows = cotangent.astype(high_type)
    grad_comb = live_rows * grad_rows
    grad_gates = jnp.einsum("tjd,td->tj", picked, grad_comb)
    grad_chosen = gate_weights * (
        grad_gates - jnp.sum(gate_weights * grad_gates, axis=-1, keepdims=True)
    )
    grad_logits = jnp.einsum("tj,tje->te", grad_chosen, selector).astype(low_type)
    grad_send = (
        (gate_weights[:, :, None] * grad_comb[:, None, :]).astype(low_type).reshape(-1, model_width)
    )
    grad_buffer = (
        jnp.zeros((experts * capacity, model_width), low_type).at[slot_rows].set(grad_send)
    )
    grad_recv = to_owners(grad_buffer.reshape(owners, local_slots, model_width))
    grad_recv = grad_recv.reshape(owners, local_experts, capacity, model_width)
    grad_hidden = jnp.einsum(
        "sxmd,dxf->sxmf", grad_recv, weights_down, preferred_element_type=high_type
    )
    sigma_gate = jax.nn.sigmoid(gate_part)
    grad_gate = grad_hidden * up_part * sigma_gate * (1.0 + gate_part * (1.0 - sigma_gate))
    grad_up = grad_hidden * gate_part * sigma_gate
    grad_both = jnp.stack([grad_gate, grad_up], axis=3).astype(low_type)
    grad_rows_out = jnp.einsum(
        "sxmkf,dxkf->sxmd", grad_both, weights_in, preferred_element_type=high_type
    ).astype(low_type)
    grad_back = from_owners(grad_rows_out.reshape(owners, local_slots, model_width))
    grad_back = grad_back.reshape(experts * capacity, model_width)
    grad_mid_norm = jnp.sum(
        grad_back[slot_rows].reshape(tok_rows, top_count, model_width).astype(high_type), axis=1
    )
    grad_mid_norm = grad_mid_norm + jnp.dot(
        grad_logits, router_weight.T, preferred_element_type=high_type
    )
    grad_router = jnp.dot(normed_mid.T, grad_logits, preferred_element_type=high_type)
    row_piece = rows_recv
    grad_expert_in = lax.psum_scatter(
        jnp.einsum(
            "sxmd,sxmkf->dxkf", row_piece, grad_both, preferred_element_type=high_type
        ).astype(jnp.bfloat16),
        "dp",
        scatter_dimension=0,
        tiled=True,
    ).astype(jnp.float32)
    row_piece = grad_recv
    grad_expert_down = lax.psum_scatter(
        jnp.einsum("sxmd,sxmf->dxf", row_piece, hidden, preferred_element_type=high_type).astype(
            jnp.bfloat16
        ),
        "dp",
        scatter_dimension=0,
        tiled=True,
    ).astype(jnp.float32)
    grad_mid_rows, grad_gain_mid = rms_back(grad_mid_norm, normed_mid_f, scale_mid, gain_rows[3])
    grad_middle = grad_rows + grad_mid_rows
    grad_branch = (live_rows * grad_middle).astype(low_type)
    grad_out_weight = jnp.dot(attended.T, grad_branch, preferred_element_type=high_type)
    grad_attended = jnp.dot(grad_branch, out_weight.T, preferred_element_type=high_type).astype(
        low_type
    )
    scores = head_scores(query_rot, key_all, key_live)
    probs_full = jnp.exp(scores - log_total)
    grad_heads = grad_attended.reshape(tok_rows, HEADS, HD)
    value_heads = value_all.reshape(seq_rows, HEADS, HD)
    key_heads = key_all.reshape(seq_rows, HEADS, HD)
    query_heads = query_rot.reshape(tok_rows, HEADS, HD)
    grad_probs = jnp.einsum(
        "qhd,khd->hqk", grad_heads, value_heads, preferred_element_type=high_type
    )
    inner_rows = jnp.sum(probs_full * grad_probs, axis=-1, keepdims=True)
    grad_scores = (probs_full * (grad_probs - inner_rows)).astype(low_type)
    grad_query = (
        jnp.einsum(
            "hqk,khd->qhd", grad_scores, key_heads, preferred_element_type=high_type
        ).reshape(tok_rows, model_width)
        * score_scale
    )
    grad_key_part = (
        jnp.einsum(
            "hqk,qhd->khd", grad_scores, query_heads, preferred_element_type=high_type
        ).reshape(seq_rows, model_width)
        * score_scale
    )
    grad_value_part = jnp.einsum(
        "hqk,qhd->khd", probs_full.astype(low_type), grad_heads, preferred_element_type=high_type
    ).reshape(seq_rows, model_width)
    grad_key_sum, grad_value_sum = (
        lax.psum_scatter(
            grad_key_part.astype(jnp.bfloat16), "dp", scatter_dimension=0, tiled=True
        ).astype(jnp.float32),
        lax.psum_scatter(
            grad_value_part.astype(jnp.bfloat16), "dp", scatter_dimension=0, tiled=True
        ).astype(jnp.float32),
    )
    grad_value = grad_value_sum.astype(low_type)
    grad_key_raw, grad_key_gain = rms_back(
        rotate(grad_key_sum, cosine, -sine_table), key_normed, key_scale, gain_rows[2]
    )
    grad_query_raw, grad_query_gain = rms_back(
        rotate(grad_query, cosine, -sine_table), query_normed, query_scale, gain_rows[1]
    )
    grad_key_raw = grad_key_raw.astype(low_type)
    grad_query_raw = grad_query_raw.astype(low_type)
    grad_norm_in = jnp.dot(grad_query_raw, qkv_weights[0].T, preferred_element_type=high_type)
    grad_norm_in = grad_norm_in + jnp.dot(
        grad_key_raw, qkv_weights[1].T, preferred_element_type=high_type
    )
    grad_norm_in = grad_norm_in + jnp.dot(
        grad_value, qkv_weights[2].T, preferred_element_type=high_type
    )
    grad_qkv_local = jnp.stack(
        [
            jnp.dot(normed_in.T, grad_query_raw, preferred_element_type=high_type),
            jnp.dot(normed_in.T, grad_key_raw, preferred_element_type=high_type),
            jnp.dot(normed_in.T, grad_value, preferred_element_type=high_type),
        ]
    )
    grad_in_rows, grad_gain_in = rms_back(grad_norm_in, normed_in_f, scale_in, gain_rows[0])
    grad_input = grad_middle + grad_in_rows
    grad_gains_local = jnp.stack([grad_gain_in, grad_query_gain, grad_key_gain, grad_gain_mid])
    summed = (
        lax.psum_scatter(grad_qkv_local, ("expert", "dp"), scatter_dimension=1, tiled=True),
        lax.psum_scatter(grad_out_weight, ("expert", "dp"), scatter_dimension=0, tiled=True),
        lax.psum_scatter(grad_gains_local, ("expert", "dp"), scatter_dimension=1, tiled=True),
        lax.psum_scatter(grad_router, ("expert", "dp"), scatter_dimension=0, tiled=True),
    )
    return (
        output,
        grad_input,
        summed[0],
        summed[1],
        summed[2],
        summed[3],
        grad_expert_in,
        grad_expert_down,
    )


def solution(mesh):
    column_count, rank_count = mesh.shape["expert"], mesh.shape["dp"]
    depth = rank_count // 2
    tiled = column_count == 4 and rank_count % 2 == 0 and HEADS == column_count * depth
    if tiled:
        mesh = Mesh(mesh.devices.reshape(2, 2, depth, 2), GRID)
        column, rank, body = ("ey", "ex"), SEQ, grid_shards
    else:
        column, rank, body = ("expert",), ("dp",), shards
    device = column + rank
    placed = (
        P(device, None),
        P(device, None),
        P(column),
        P(device, None),
        P(None, device, None),
        P(device, None),
        P(None, device),
        P(device, None),
        P(rank, column, None, None),
        P(rank, column, None),
    )
    return jax.shard_map(
        body,
        mesh=mesh,
        in_specs=placed,
        out_specs=placed[:1] * 2 + placed[4:],
        check_vma=False,
    )
```

```python
import functools

import jax
import jax.numpy as jnp
from jax import lax
from jax.experimental import pallas as pl
from jax.experimental.pallas import tpu as pltpu
from jax.sharding import Mesh
from jax.sharding import PartitionSpec as P

HEADS = 16
HD = 128

epsilon = 1e-05
rope_base = 10000.0
masked_score = -1000000000.0

low_type = jnp.bfloat16
high_type = jnp.float32


def rms_scale(values):
    return lax.rsqrt(jnp.mean(values * values, axis=-1, keepdims=True) + epsilon)


def angle_tables(positions):
    frequency = rope_base ** (-2.0 * jnp.arange(HD // 2, dtype=jnp.float32) / HD)
    angles = positions.astype(jnp.float32)[:, None] * frequency[None, :]
    return (jnp.cos(angles), jnp.sin(angles))


def rotate(values, cosine, sine_table):
    row_count, width = values.shape
    shaped = values.reshape(row_count, width // HD, 2, HD // 2)
    first_half = shaped[:, :, 0, :]
    second_half = shaped[:, :, 1, :]
    cos_rows = cosine[:, None, :]
    sin_rows = sine_table[:, None, :]
    turned = jnp.stack(
        [
            first_half * cos_rows - second_half * sin_rows,
            second_half * cos_rows + first_half * sin_rows,
        ],
        axis=2,
    )
    return turned.reshape(row_count, width)


def rms_back(grad_rows, normed, scale, gain):
    grad_normed = grad_rows * gain
    inner = jnp.mean(grad_normed * normed, axis=-1, keepdims=True)
    return (scale * grad_normed - normed * scale * inner, jnp.sum(grad_rows * normed, axis=0))


def dot(left, right):
    return jnp.dot(left, right, preferred_element_type=high_type)


def dot_t(left, right):
    return lax.dot_general(left, right, (((1,), (1,)), ((), ())), preferred_element_type=high_type)


def t_dot(left, right):
    return lax.dot_general(left, right, (((0,), (0,)), ((), ())), preferred_element_type=high_type)


GRID = ("ey", "ex", "dz", "dc")
SEQ = ("dz", "dc")


MESH_ID = pl.DeviceIdType.MESH


class Place:
    def __init__(self, depth):
        self.depth = depth
        self.y, self.x, self.z, self.c = (lax.axis_index(name) for name in GRID)

    def near_of(self, core):
        return self.y + core * (1 - 2 * self.y), self.x + (1 - core) * (1 - 2 * self.x)

    def far_of(self, core):
        return self.near_of(1 - core)

    def along(self, step):
        return lax.rem(self.z + step, self.depth)

    def next_z(self, k):
        first = self.z - 1 + 2 * lax.div(4 - self.z, 4)
        last = 3 * lax.div(3 - self.z, 2)
        return (self.z, first, 6 - self.z - first - last, last)[k]

    def block(self, column, z, core):
        return ((column[0] * 2 + column[1]) * self.depth + z) * 2 + core

    @property
    def own_column(self):
        return self.y, self.x

    @property
    def other_column(self):
        return 1 - self.y, 1 - self.x

    def core(self):
        return self.y, self.x, self.z, 1 - self.c

    def chip(self, step, core=None):
        return self.y, self.x, self.along(step), self.c if core is None else core

    def near(self):
        return (*self.near_of(self.c), self.z, self.c)

    def far(self):
        return (*self.far_of(self.c), self.z, self.c)


def meet(partners):
    barrier = pltpu.get_barrier_semaphore()
    for partner in partners:
        pl.semaphore_signal(barrier, inc=1, device_id=partner, device_id_type=MESH_ID)
    pl.semaphore_wait(barrier, len(partners))


def remote(source, target, sems, slot, partner):
    return pltpu.make_async_remote_copy(
        src_ref=source,
        dst_ref=target,
        send_sem=sems[0].at[slot],
        recv_sem=sems[1].at[slot],
        device_id=partner,
        device_id_type=MESH_ID,
    )


def pair(count):
    return [pltpu.SemaphoreType.DMA((count,)), pltpu.SemaphoreType.DMA((count,))]


def in_hbm(count):
    return [pl.BlockSpec(memory_space=pl.ANY)] * count


def spread_kernel(depth, count, extra, *refs):
    whole = count + extra
    sources, targets, sems = refs[:count], refs[whole : whole + count], refs[2 * whole :]
    extra_sources, extra_targets = refs[count:whole], refs[whole + count : 2 * whole]
    extra_sems = sems[9 * count :]
    at = Place(depth)
    others = range(1, depth)
    ranks = [(k, core) for k in range(depth) for core in range(2) if k or core]
    peers = [at.chip(k, lax.rem(at.c + core, 2)) for k, core in ranks]
    meet([at.near(), at.far()] + peers)
    started, local = [], []

    def push(n, source, index, kind, slot, partner):
        copy = remote(source, targets[n].at[index], sems[9 * n + 2 * kind :], slot, partner)
        copy.start()
        started.append(copy)

    def arrive(n, index, kind, slot):
        target = targets[n].at[index]
        remote(target, target, sems[9 * n + 2 * kind :], slot, at.core()).wait_recv()

    z_kind, near_kind, far_kind, core_kind = range(4)
    own = at.block(at.own_column, at.z, at.c)
    for n in range(count):
        push(n, sources[n], own, z_kind, at.z, (at.y, at.x, at.next_z(1), at.c))
        push(n, sources[n], own, near_kind, 0, at.near())
        push(n, sources[n], own, far_kind, 0, at.far())
        push(n, sources[n], own, core_kind, 0, at.core())
        copy = pltpu.make_async_copy(sources[n], targets[n].at[own], sems[9 * n + 8])
        copy.start()
        local.append(copy)

    inner = lax.rem(at.z, depth - 1) != 0
    onward = (at.z + 1, at.z + 1, at.z - 1, 3 * at.z - 3)

    def forward(n, source, k):
        z = at.next_z(k)
        return pltpu.make_async_remote_copy(
            src_ref=source,
            dst_ref=targets[n].at[at.block(at.own_column, z, at.c)],
            send_sem=sems[9 * n].at[z if k else depth],
            recv_sem=sems[9 * n + 1].at[z],
            device_id=(at.y, at.x, onward[k], at.c),
            device_id_type=MESH_ID,
        )

    @pl.when(inner)
    def _():
        for n in range(count):
            forward(n, sources[n], 0).start()

    for k in others:
        index = at.block(at.own_column, at.next_z(k), at.c)
        for n in range(count):
            arrive(n, index, z_kind, at.next_z(k))

        @pl.when(inner)
        def _(index=index, k=k):
            for n in range(count):
                forward(n, targets[n].at[index], k).start()

        for n in range(count):
            push(n, targets[n].at[index], index, near_kind, k, at.near())
            push(n, targets[n].at[index], index, far_kind, k, at.far())
            push(n, targets[n].at[index], index, core_kind, k, at.core())
    own_rank = at.z * 2 + at.c
    for n in range(extra):
        for slot, there in enumerate(peers):
            copy = remote(
                extra_sources[n].at[there[2] * 2 + there[3]],
                extra_targets[n].at[own_rank],
                extra_sems[3 * n :],
                slot,
                there,
            )
            copy.start()
            started.append(copy)
        copy = pltpu.make_async_copy(
            extra_sources[n].at[own_rank], extra_targets[n].at[own_rank], extra_sems[3 * n + 2]
        )
        copy.start()
        local.append(copy)
    for k in range(depth):
        index = at.block(at.near_of(at.c), at.next_z(k), at.c)
        for n in range(count):
            arrive(n, index, near_kind, k)
            push(n, targets[n].at[index], index, far_kind, depth + k, at.far())
            push(n, targets[n].at[index], index, core_kind, depth + k, at.core())
    for j in range(2 * depth):
        column = at.far_of(at.c) if j < depth else at.other_column
        index = at.block(column, at.next_z(j % depth), at.c)
        for n in range(count):
            arrive(n, index, far_kind, j)
            push(n, targets[n].at[index], index, core_kind, 2 * depth + j, at.core())
    core = 1 - at.c
    columns = [at.own_column, at.near_of(core), at.far_of(core), at.other_column]
    for j in range(4 * depth):
        index = at.block(columns[j // depth], at.next_z(j % depth), core)
        for n in range(count):
            arrive(n, index, core_kind, j)
    for n in range(extra):
        for slot, (k, core) in enumerate(ranks):
            target = extra_targets[n].at[at.along(depth - k) * 2 + lax.rem(at.c + core, 2)]
            remote(target, target, extra_sems[3 * n :], slot, at.core()).wait_recv()

    @pl.when(inner)
    def _():
        for n in range(count):
            forward(n, sources[n], 0).wait_send()
            for k in others:
                index = at.block(at.own_column, at.next_z(k), at.c)
                forward(n, targets[n].at[index], k).wait_send()

    for copy in started:
        copy.wait_send()
    for copy in local:
        copy.wait()


def spread(depth, ident, arrays, extras=()):
    sems = []
    for _ in arrays:
        sems += pair(depth + 1) + pair(depth) + pair(2 * depth) + pair(4 * depth)
        sems.append(pltpu.SemaphoreType.DMA)
    for _ in extras:
        sems += pair(2 * depth - 1) + [pltpu.SemaphoreType.DMA]
    count = len(arrays) + len(extras)
    shapes = [((8 * depth,) + a.shape, a.dtype) for a in arrays]
    shapes += [(a.shape, a.dtype) for a in extras]
    return pl.pallas_call(
        functools.partial(spread_kernel, depth, len(arrays), len(extras)),
        out_shape=[jax.ShapeDtypeStruct(*shape) for shape in shapes],
        in_specs=in_hbm(count),
        out_specs=in_hbm(count),
        scratch_shapes=sems,
        compiler_params=pltpu.CompilerParams(
            collective_id=ident, has_side_effects=True, vmem_limit_bytes=60 << 20
        ),
        cost_estimate=pl.CostEstimate(
            flops=0,
            bytes_accessed=sum(64 * depth * a.size * a.dtype.itemsize for a in arrays),
            transcendentals=0,
        ),
    )(*arrays, *extras)


def sum_rows(target, lead, terms):
    rows = target.shape[-2]
    tile = min(rows, 16)

    def body(i, carry):
        at = pl.ds(pl.multiple_of(i * tile, tile), tile)
        total = terms[0][0][(*terms[0][1], at, slice(None))].astype(high_type)
        for ref, where in terms[1:]:
            total = total + ref[(*where, at, slice(None))].astype(high_type)
        target[(*lead, at, slice(None))] = total.astype(target.dtype)
        return carry

    lax.fori_loop(0, rows // tile, body, 0)


def collect_kernel(depth, local, counts, *refs):
    rest = iter(refs)

    def take(count):
        return [next(rest) for _ in range(count)]

    mains, smalls, shareds, extras = (take(count) for count in counts)
    halves = take(2 if local else 0)
    main_totals, small_totals, shared_totals, extra_outs = (take(count) for count in counts)
    unpacked = take(1 if local else 0)
    main_buffers = [take(5) for _ in mains]
    small_buffers = [take(5) for _ in smalls]
    shared_buffers = [take(3) for _ in shareds]
    shared_outs = [take(1)[0] for _ in shareds]
    main_sems = [take(9) for _ in mains]
    small_sems = [take(9) for _ in smalls]
    shared_sems = [take(7) for _ in shareds]
    extra_sems = [take(3) for _ in extras]
    at = Place(depth)
    ranks = [(k, core) for k in range(depth) for core in range(2) if k or core]
    peers = [at.chip(k, lax.rem(at.c + core, 2)) for k, core in ranks]
    meet([at.near(), at.far()] + peers)
    started = []
    own_rank = at.z * 2 + at.c

    def columns(core):
        return at.other_column, at.far_of(core), at.near_of(core), at.own_column

    def number(column):
        return column[0] * 2 + column[1]

    def push(copy):
        copy.start()
        started.append(copy)

    def arrive(buffer, pair_of, slot):
        remote(buffer.at[slot], buffer.at[slot], pair_of, slot, at.core()).wait_recv()

    def piece(ref, rank):
        rows = ref.shape[0] // (2 * depth)
        return ref.at[pl.ds(pl.multiple_of(rank * rows, rows), rows)]

    def block(group, k, core):
        return at.block(columns(core)[group], at.along(1 + k), core)

    def main_load(n, group, k):
        slot = group * depth + k
        return pltpu.make_async_copy(
            mains[n].at[block(group, k, at.c)], main_buffers[n][0].at[slot], main_sems[n][8].at[slot]
        )

    def main_cross(n, group, k):
        slot = group * depth + k
        source = mains[n].at[block(group, k, 1 - at.c)]
        push(remote(source, main_buffers[n][1].at[slot], main_sems[n][0:2], slot, at.core()))
        main_load(n, group, k).start()

    def main_sum(n, group, k, more):
        mine, crossed = main_buffers[n][:2]
        slot = group * depth + k
        main_load(n, group, k).wait()
        arrive(crossed, main_sems[n][0:2], slot)
        terms = [(mine, (slot,)), (crossed, (slot,))] + more
        if slot < 4 * depth - 1:
            sum_rows(mine, (slot,), terms)
        else:
            sum_rows(main_totals[n], (), terms)
        return mine.at[slot]

    def main_far(n, k):
        buffers, sems = main_buffers[n], main_sems[n]
        for group in range(2):
            slot = group * depth + k
            total = main_sum(n, group, k, [])
            push(remote(total, buffers[2].at[slot], sems[2:4], slot, at.far()))

    def main_near(n, k):
        buffers, sems = main_buffers[n], main_sems[n]
        arrive(buffers[2], sems[2:4], k)
        total = main_sum(n, 2, k, [(buffers[2], (k,))])
        push(remote(total, buffers[3].at[k], sems[4:6], k, at.near()))

    def main_own(n, k):
        buffers, sems = main_buffers[n], main_sems[n]
        arrive(buffers[2], sems[2:4], depth + k)
        arrive(buffers[3], sems[4:6], k)
        total = main_sum(n, 3, k, [(buffers[2], (depth + k,)), (buffers[3], (k,))])
        if k < depth - 1:
            push(remote(total, buffers[4].at[k], sems[6:8], k, at.chip(1 + k)))

    def small_load(n, group):
        return pltpu.make_async_copy(
            smalls[n].at[at.c, number(columns(at.c)[group])],
            small_buffers[n][0].at[group],
            small_sems[n][8].at[group],
        )

    def small_cross():
        for n, (part, buffers, sems) in enumerate(zip(smalls, small_buffers, small_sems)):
            for group in range(4):
                source = part.at[1 - at.c, number(columns(1 - at.c)[group])]
                push(remote(source, buffers[1].at[group], sems[0:2], group, at.core()))
                small_load(n, group).start()

    def small_sum(n, group, more):
        mine, crossed = small_buffers[n][:2]
        small_load(n, group).wait()
        arrive(crossed, small_sems[n][0:2], group)
        for j in range(depth):
            terms = [(mine, (group, j)), (crossed, (group, j))]
            sum_rows(mine, (group, j), terms + [(ref, (i, j)) for ref, i in more])
        return mine.at[group]

    def small_far():
        for n, (buffers, sems) in enumerate(zip(small_buffers, small_sems)):
            for group in range(2):
                total = small_sum(n, group, [])
                push(remote(total, buffers[2].at[group], sems[2:4], group, at.far()))

    def small_near():
        for n, (buffers, sems) in enumerate(zip(small_buffers, small_sems)):
            arrive(buffers[2], sems[2:4], 0)
            total = small_sum(n, 2, [(buffers[2], 0)])
            push(remote(total, buffers[3].at[0], sems[4:6], 0, at.near()))

    def small_own():
        for n, (buffers, sems) in enumerate(zip(small_buffers, small_sems)):
            arrive(buffers[2], sems[2:4], 1)
            arrive(buffers[3], sems[4:6], 0)
            total = small_sum(n, 3, [(buffers[2], 1), (buffers[3], 0)])
            for k in range(1, depth):
                there = at.chip(k)
                source = total.at[there[2]]
                push(remote(source, buffers[4].at[k - 1], sems[6:8], k - 1, there))

    def shared_load(n, i):
        return pltpu.make_async_copy(
            shareds[n].at[number(columns(at.c)[2 + i])], shared_buffers[n][0].at[i], shared_sems[n][0].at[i]
        )

    def shared_far():
        for n, (part, buffers, sems) in enumerate(zip(shareds, shared_buffers, shared_sems)):
            for i in range(2):
                source = part.at[number(columns(at.c)[i])]
                push(remote(source, buffers[1].at[i], sems[1:3], i, at.far()))
                shared_load(n, i).start()

    def shared_near():
        for n, ((mine, far_in, near_in), sems) in enumerate(zip(shared_buffers, shared_sems)):
            shared_load(n, 0).wait()
            arrive(far_in, sems[1:3], 0)
            sum_rows(mine, (0,), [(mine, (0,)), (far_in, (0,))])
            push(remote(mine.at[0], near_in.at[0], sems[3:5], 0, at.near()))

    def shared_own():
        for n, ((mine, far_in, near_in), sems) in enumerate(zip(shared_buffers, shared_sems)):
            shared_load(n, 1).wait()
            arrive(far_in, sems[1:3], 1)
            arrive(near_in, sems[3:5], 0)
            sum_rows(mine, (1,), [(mine, (1,)), (far_in, (1,)), (near_in, (0,))])
            for slot, there in enumerate(peers):
                source = piece(mine.at[1], there[2] * 2 + there[3])
                push(remote(source, piece(shared_outs[n], own_rank), sems[5:7], slot, there))
            shared_kept(n).start()

    def shared_kept(n):
        mine = shared_buffers[n][0]
        return pltpu.make_async_copy(
            piece(mine.at[1], own_rank), piece(shared_outs[n], own_rank), shared_sems[n][0].at[2]
        )

    def extra_kept(n):
        return pltpu.make_async_copy(
            extras[n].at[own_rank], extra_outs[n].at[own_rank], extra_sems[n][2]
        )

    last = len(mains) - 1
    stages = [(main_far, 0), (main_far, 1), (main_near, 0), (main_own, 0)]
    for k in range(2, depth):
        stages += [(main_far, k), (main_near, k - 1), (main_own, k - 1)]
    stages += [(main_near, depth - 1), (main_own, depth - 1)]
    order = [(stage, n, k) for n in range(len(mains)) for stage, k in stages]
    for n in range(last):
        ahead = [(main_far, n + 1, k) for k in range(2)]
        order = [step for step in order if step not in ahead]
        at_end = order.index((main_near, n, depth - 1))
        order[at_end:at_end] = ahead
    groups = {main_far: (0, 1), main_near: (2,), main_own: (3,)}
    shared_far()
    small_cross()
    for stage, n, k in order:
        for group in groups[stage]:
            main_cross(n, group, k)
    for n in range(len(extras)):
        for slot, there in enumerate(peers):
            source = extras[n].at[there[2] * 2 + there[3]]
            push(remote(source, extra_outs[n].at[own_rank], extra_sems[n][:2], slot, there))
        extra_kept(n).start()
    small_far()
    for stage, n, k in order:
        stage(n, k)
        if (stage, n, k) == (main_near, 0, 0):
            shared_near()
            small_near()
        if (stage, n, k) == (main_own, 0, 0):
            shared_own()
            small_own()
    if local:
        unpack_inside(local, *halves, *unpacked)
    for n, (buffers, sems) in enumerate(zip(small_buffers, small_sems)):
        for k in range(depth - 1):
            arrive(buffers[4], sems[6:8], k)
        terms = [(buffers[0], (3, at.z))] + [(buffers[4], (k,)) for k in range(depth - 1)]
        sum_rows(small_totals[n], (), terms)
    for n, (buffers, sems) in enumerate(zip(main_buffers, main_sems)):
        for k in range(depth - 1):
            arrive(buffers[4], sems[6:8], k)
        terms = [(main_totals[n], ())] + [(buffers[4], (k,)) for k in range(depth - 1)]
        sum_rows(main_totals[n], (), terms)
    for slot, (k, core) in enumerate(ranks):
        source = at.along(depth - k) * 2 + lax.rem(at.c + core, 2)
        for n in range(len(shareds)):
            target = piece(shared_outs[n], source)
            remote(target, target, shared_sems[n][5:7], slot, at.core()).wait_recv()
        for n in range(len(extras)):
            target = extra_outs[n].at[source]
            remote(target, target, extra_sems[n][:2], slot, at.core()).wait_recv()
    for n in range(len(shareds)):
        shared_kept(n).wait()
        out, held = shared_totals[n], shared_outs[n]
        count, rows = out.shape[:2]
        heads = held.shape[1] // (count * HD)
        for rank in range(2 * depth):
            for i in range(count):
                for j in range(heads):
                    head = (rank % 2 * heads + j) * depth + rank // 2
                    value = held[rank * rows : (rank + 1) * rows, (i * heads + j) * HD :][:, :HD]
                    out[i, :, head * HD : (head + 1) * HD] = value.astype(out.dtype)
    for n in range(len(extras)):
        extra_kept(n).wait()
    for copy in started:
        copy.wait_send()


def collect(depth, ident, mains, smalls, shareds=(), extras=(), to_unpack=(0,)):
    local, *halves = to_unpack
    dma = pltpu.SemaphoreType.DMA
    peers = 2 * depth - 1

    def by_core(a):
        return a.reshape((4, depth, 2) + a.shape[1:]).transpose(2, 0, 1, 3, 4)

    smalls = [by_core(a) for a in smalls]
    buffers, sems, shapes = [], [], []
    for a in mains:
        for slots in (4 * depth, 4 * depth, 2 * depth, depth, depth - 1):
            buffers.append(pltpu.VMEM((slots,) + a.shape[1:], a.dtype))
        sems += pair(4 * depth) + pair(2 * depth) + pair(depth) + pair(depth - 1)
        sems.append(dma((4 * depth,)))
        shapes.append(jax.ShapeDtypeStruct(a.shape[1:], high_type))
    for a in smalls:
        for slots in ((4, depth), (4, depth), (2, depth), (1, depth), (depth - 1,)):
            buffers.append(pltpu.VMEM(slots + a.shape[3:], a.dtype))
        sems += pair(4) + pair(2) + pair(1) + pair(depth - 1) + [dma((4,))]
        shapes.append(jax.ShapeDtypeStruct(a.shape[3:], high_type))
    for a in shareds:
        buffers += [pltpu.VMEM((slots,) + a.shape[1:], a.dtype) for slots in (2, 2, 1)]
        buffers.append(pltpu.VMEM(a.shape[1:], a.dtype))
        sems += [dma((3,))] + pair(2) + pair(1) + pair(peers)
        shape = (3, a.shape[1] // (2 * depth), a.shape[2] // 3 * 2 * depth)
        shapes.append(jax.ShapeDtypeStruct(shape, high_type))
    for a in extras:
        sems += pair(peers) + [dma]
        shapes.append(jax.ShapeDtypeStruct(a.shape, a.dtype))
    arrays = [*mains, *smalls, *shareds, *extras]
    counts = (len(mains), len(smalls), len(shareds), len(extras))
    if halves:
        lines = halves[0].size // 64
        shapes.append(jax.ShapeDtypeStruct((lines, 128), high_type))
    in_vmem = [pl.BlockSpec(memory_space=pltpu.VMEM)] * (len(arrays) - len(extras))
    return pl.pallas_call(
        functools.partial(collect_kernel, depth, local, counts),
        out_shape=shapes,
        in_specs=in_hbm(len(arrays) + len(halves)),
        out_specs=in_vmem + in_hbm(len(extras) + len(halves) // 2),
        scratch_shapes=buffers + sems,
        compiler_params=pltpu.CompilerParams(
            collective_id=ident, has_side_effects=True, vmem_limit_bytes=60 << 20
        ),
        cost_estimate=pl.CostEstimate(
            flops=0,
            bytes_accessed=sum(16 * a.size * a.dtype.itemsize for a in arrays),
            transcendentals=0,
        ),
    )(*arrays, *halves)


def gather_kernel(depth, local_experts, x_ref, o_ref, w_ref, s_ref, in_ref, down_ref, *refs):
    x_out, o_out, w_out, s_out = refs[:4]
    packed, sems = refs[4:8], refs[8:]
    at = Place(depth)
    ranks = [(k, core) for k in range(depth) for core in range(2) if k or core]
    peers = [at.chip(k, lax.rem(at.c + core, 2)) for k, core in ranks]
    meet([at.near(), at.far()] + peers)
    own, column = at.z * 2 + at.c, at.y * 2 + at.x
    x_z, x_core, o_z, o_near, o_far, o_core, w_sems, s_sems, w_side, s_side = (
        sems[2 * i : 2 * i + 2] for i in range(10)
    )
    started, local = [], []
    inner = lax.rem(at.z, depth - 1) != 0
    onward = (at.z + 1, at.z + 1, at.z - 1, 3 * at.z - 3)
    own_block = at.block(at.own_column, at.z, at.c)

    def push(copy):
        copy.start()
        started.append(copy)

    def arrive(target, pair_of, slot):
        remote(target, target, pair_of, slot, at.core()).wait_recv()

    def x_place(k):
        return x_out.at[at.next_z(k) * 2 + at.c]

    def o_place(k):
        return o_out.at[at.block(at.own_column, at.next_z(k), at.c)]

    def forward(source, target, pair_of, k):
        z = at.next_z(k)
        return pltpu.make_async_remote_copy(
            src_ref=source,
            dst_ref=target,
            send_sem=pair_of[0].at[z if k else depth],
            recv_sem=pair_of[1].at[z],
            device_id=(at.y, at.x, onward[k], at.c),
            device_id_type=MESH_ID,
        )

    for slot, there in enumerate(peers):
        push(remote(s_ref, s_out.at[column, own], s_sems, slot, there))
        source = w_ref.at[there[2] * 2 + there[3]]
        push(remote(source, w_out.at[column, own], w_sems, slot, there))
    def w_rank(j):
        k, core = ([(0, 0)] + ranks)[j]
        return at.along(depth - k) * 2 + lax.rem(at.c + core, 2)

    all_ranks = 2 * depth

    def w_aside(source, j):
        target = w_out.at[column, w_rank(j)]
        push(remote(source, target, w_side, j, at.near()))
        push(remote(source, target, w_side, all_ranks + j, at.far()))

    w_aside(w_ref.at[own], 0)
    first = (at.y, at.x, at.next_z(1), at.c)
    push(remote(o_ref, o_place(0), o_z, at.z, first))
    push(remote(x_ref, x_place(0), x_z, at.z, first))

    @pl.when(inner)
    def _():
        forward(o_ref, o_place(0), o_z, 0).start()
        forward(x_ref, x_place(0), x_z, 0).start()

    push(remote(x_ref, x_place(0), x_core, 0, at.core()))
    push(remote(o_ref, o_place(0), o_near, 0, at.near()))
    push(remote(o_ref, o_place(0), o_far, 0, at.far()))
    push(remote(o_ref, o_place(0), o_core, 0, at.core()))
    for i, (source, target) in enumerate(
        (
            (x_ref, x_place(0)),
            (o_ref, o_place(0)),
            (w_ref.at[own], w_out.at[column, own]),
            (s_ref, s_out.at[column, own]),
        )
    ):
        copy = pltpu.make_async_copy(source, target, sems[20].at[i])
        copy.start()
        local.append(copy)
    near_y, near_x = at.near_of(at.c)
    far_y, far_x = at.far_of(at.c)
    beside, across = near_y * 2 + near_x, far_y * 2 + far_x
    pack(2 * depth, local_experts, in_ref, down_ref, *packed)
    for slot, (j, core) in enumerate(ranks):
        source = at.along(depth - j) * 2 + lax.rem(at.c + core, 2)
        arrive(s_out.at[column, source], s_sems, slot)
        arrive(w_out.at[column, source], w_sems, slot)
        w_aside(w_out.at[column, source], 1 + slot)
    for copy in local:
        copy.wait()
    push(remote(s_out.at[column], s_out.at[column], s_side, 0, at.near()))
    push(remote(s_out.at[column], s_out.at[column], s_side, 1, at.far()))
    for k in range(1, depth):
        arrive(o_place(k), o_z, at.next_z(k))

        @pl.when(inner)
        def _(k=k):
            forward(o_place(k), o_place(k), o_z, k).start()

        push(remote(o_place(k), o_place(k), o_near, k, at.near()))
        push(remote(o_place(k), o_place(k), o_far, k, at.far()))
        push(remote(o_place(k), o_place(k), o_core, k, at.core()))
        arrive(x_place(k), x_z, at.next_z(k))

        @pl.when(inner)
        def _(k=k):
            forward(x_place(k), x_place(k), x_z, k).start()

        push(remote(x_place(k), x_place(k), x_core, k, at.core()))
        if k == 2:
            arrive(s_out.at[beside], s_side, 0)
            push(remote(s_out.at[beside], s_out.at[beside], s_side, 2, at.far()))
            for j in range(all_ranks):
                target = w_out.at[beside, w_rank(j)]
                arrive(target, w_side, j)
                push(remote(target, target, w_side, 2 * all_ranks + j, at.far()))
    for k in range(depth):
        target = o_out.at[at.block(at.near_of(at.c), at.next_z(k), at.c)]
        arrive(target, o_near, k)
        push(remote(target, target, o_far, depth + k, at.far()))
        push(remote(target, target, o_core, depth + k, at.core()))
    for j in range(2 * depth):
        place = at.far_of(at.c) if j < depth else at.other_column
        target = o_out.at[at.block(place, at.next_z(j % depth), at.c)]
        arrive(target, o_far, j)
        push(remote(target, target, o_core, 2 * depth + j, at.core()))
    arrive(s_out.at[across], s_side, 1)
    arrive(s_out.at[3 - column], s_side, 2)
    for j in range(all_ranks):
        arrive(w_out.at[across, w_rank(j)], w_side, all_ranks + j)
        arrive(w_out.at[3 - column, w_rank(j)], w_side, 2 * all_ranks + j)
    for k in range(depth):
        arrive(x_out.at[at.next_z(k) * 2 + 1 - at.c], x_core, k)
    core = 1 - at.c
    places = [at.own_column, at.near_of(core), at.far_of(core), at.other_column]
    for j in range(4 * depth):
        index = at.block(places[j // depth], at.next_z(j % depth), core)
        arrive(o_out.at[index], o_core, j)

    @pl.when(inner)
    def _():
        forward(x_ref, x_place(0), x_z, 0).wait_send()
        forward(o_ref, o_place(0), o_z, 0).wait_send()
        for k in range(1, depth):
            forward(x_place(k), x_place(k), x_z, k).wait_send()
            forward(o_place(k), o_place(k), o_z, k).wait_send()

    for copy in started:
        copy.wait_send()


def gather(depth, ident, x, o, w, s, expert_in, expert_down):
    chunk, local = expert_in.shape[:2]
    ranks = 2 * depth
    sems = pair(depth + 1) + pair(depth) + pair(depth + 1) + pair(depth) + pair(2 * depth)
    sems += pair(4 * depth) + pair(ranks - 1) * 2 + pair(3 * ranks) + pair(3)
    sems.append(pltpu.SemaphoreType.DMA((4,)))
    return pl.pallas_call(
        functools.partial(gather_kernel, depth, local),
        out_shape=[
            jax.ShapeDtypeStruct((ranks,) + x.shape, x.dtype),
            jax.ShapeDtypeStruct((4 * ranks,) + o.shape, o.dtype),
            jax.ShapeDtypeStruct((4,) + w.shape, w.dtype),
            jax.ShapeDtypeStruct((4, ranks) + s.shape, s.dtype),
        ]
        + [jax.ShapeDtypeStruct((ranks, chunk, local * 128), low_type)] * 2
        + [jax.ShapeDtypeStruct((ranks, chunk, local * 64), low_type)] * 2,
        in_specs=in_hbm(6),
        out_specs=in_hbm(8),
        scratch_shapes=sems,
        compiler_params=pltpu.CompilerParams(
            collective_id=ident, has_side_effects=True, vmem_limit_bytes=60 << 20
        ),
        cost_estimate=pl.CostEstimate(
            flops=0, bytes_accessed=64 * depth * x.size, transcendentals=0
        ),
    )(x, o, w, s, lines_in(expert_in), lines_down(expert_down))


def exchange_kernel(depth, same, x_ref, out_ref, send_sems, recv_sems, local_sem):
    at = Place(depth)
    ranks = [(k, core) for k in range(depth) for core in range(2) if k or core]
    peers = [at.chip(k, lax.rem(at.c + core, 2)) for k, core in ranks]
    meet(peers)
    own = at.z * 2 + at.c
    copies = []
    for slot, there in enumerate(peers):
        source = x_ref if same else x_ref.at[there[2] * 2 + there[3]]
        copy = remote(source, out_ref.at[own], (send_sems, recv_sems), slot, there)
        copy.start()
        copies.append(copy)
    local = pltpu.make_async_copy(x_ref if same else x_ref.at[own], out_ref.at[own], local_sem)
    local.start()
    for slot, (k, core) in enumerate(ranks):
        target = out_ref.at[at.along(depth - k) * 2 + lax.rem(at.c + core, 2)]
        remote(target, target, (send_sems, recv_sems), slot, at.core()).wait_recv()
    for copy in copies:
        copy.wait_send()
    local.wait()


def exchange(depth, ident, x, same=False):
    ranks = 2 * depth
    return pl.pallas_call(
        functools.partial(exchange_kernel, depth, same),
        out_shape=jax.ShapeDtypeStruct((ranks,) + x.shape if same else x.shape, x.dtype),
        in_specs=in_hbm(1),
        out_specs=in_hbm(1)[0],
        scratch_shapes=pair(ranks - 1) + [pltpu.SemaphoreType.DMA],
        compiler_params=pltpu.CompilerParams(
            collective_id=ident, has_side_effects=True, vmem_limit_bytes=16 << 20
        ),
        cost_estimate=pl.CostEstimate(
            flops=0, bytes_accessed=16 * x.size * x.dtype.itemsize, transcendentals=0
        ),
    )(x)


def column_kernel(depth, part, total, mine, crossed, z_in, *sems):
    at = Place(depth)
    meet([at.core()] + [at.chip(k) for k in range(1, depth)])
    started = []
    inner = lax.rem(at.z, depth - 1) != 0
    inside = lax.div(lax.rem(at.z, depth - 1) + 1, 2)
    onto = (None, at.next_z(1), at.z + 1 - 2 * lax.div(at.z, 3), 1 + lax.rem(at.z, 2))
    slots = (
        None,
        5 - lax.div(4 - at.z, 4),
        4 * inside + (1 - inside) * at.next_z(2),
        at.next_z(3),
    )

    def local(k):
        return pltpu.make_async_copy(part.at[at.next_z(k) * 2 + at.c], mine.at[k], sems[4].at[k])

    def cross(k):
        source = part.at[at.next_z(k) * 2 + 1 - at.c]
        return remote(source, crossed.at[k], sems[0:2], k, at.core())

    def arrive(slot):
        remote(z_in.at[slot], z_in.at[slot], sems[2:4], slot, at.core()).wait_recv()

    def hand_on(k):
        return pltpu.make_async_remote_copy(
            src_ref=mine.at[k],
            dst_ref=z_in.at[slots[k]],
            send_sem=sems[2].at[k],
            recv_sem=sems[3].at[slots[k]],
            device_id=(at.y, at.x, onto[k], at.c),
            device_id_type=MESH_ID,
        )

    order = tuple(range(depth - 1, -1, -1))
    for k in order:
        cross(k).start()
        local(k).start()
    for k in order:
        local(k).wait()
        cross(k).wait_recv()
        terms = [(mine, (k,)), (crossed, (k,))]
        if k == 0:
            sum_rows(total, (), terms)
            continue

        @pl.when(inner)
        def _(terms=terms, k=k):
            arrive(at.next_z(k))
            sum_rows(mine, (k,), terms + [(z_in, (at.next_z(k),))])

        @pl.when(lax.rem(at.z, depth - 1) == 0)
        def _(terms=terms, k=k):
            sum_rows(mine, (k,), terms)

        hand_on(k).start()

    @pl.when(inner)
    def _():
        arrive(4)
        arrive(5)
        sum_rows(total, (), [(total, ()), (z_in, (4,)), (z_in, (5,))])

    @pl.when(lax.rem(at.z, depth - 1) == 0)
    def _():
        slot = 5 - lax.div(at.z, 3)
        arrive(slot)
        sum_rows(total, (), [(total, ()), (z_in, (slot,))])

    for k in order:
        cross(k).wait_send()
        if k:
            hand_on(k).wait_send()


def collect_column(depth, ident, part):
    block = part.shape[1:]
    return pl.pallas_call(
        functools.partial(column_kernel, depth),
        out_shape=jax.ShapeDtypeStruct(block, high_type),
        in_specs=in_hbm(1),
        out_specs=pl.BlockSpec(memory_space=pltpu.VMEM),
        scratch_shapes=[pltpu.VMEM((slots,) + block, part.dtype) for slots in (depth, depth, 6)]
        + pair(depth)
        + pair(6)
        + [pltpu.SemaphoreType.DMA((depth,))],
        compiler_params=pltpu.CompilerParams(
            collective_id=ident, has_side_effects=True, vmem_limit_bytes=32 << 20
        ),
        cost_estimate=pl.CostEstimate(
            flops=0, bytes_accessed=16 * part.size * part.dtype.itemsize, transcendentals=0
        ),
    )(part)


def lines_in(values):
    rows, local, two, hidden = values.shape
    values = values.reshape(rows, local, two, hidden // 128, 128)
    return values.transpose(0, 1, 3, 2, 4).reshape(-1, 128)


def lines_down(values):
    rows, local, hidden = values.shape
    return values.reshape(rows, local, hidden // 128, 128).transpose(0, 2, 1, 3).reshape(-1, 128)


def lines_of(ranks, local):
    half, of_in, of_down = local // 2, [], []
    for rank in range(ranks):
        for x in range(local):
            for k in range(2):
                line = (x * ranks + rank) * 2 + k
                columns = (k * half + x % half) * 128
                of_in.append((rank, x // half, columns, line, 2 * local * ranks))
            of_down.append((rank, x // half, x % half * 128, rank * local + x, local * ranks))
    return of_in, of_down


def pack_kernel(ranks, local, step, in_ref, down_ref, *outs):
    of_in, of_down = lines_of(ranks, local)
    for lines, ref, targets in ((of_in, in_ref, outs[:2]), (of_down, down_ref, outs[2:])):
        for rank, half, column, line, stride in lines:
            value = ref[pl.ds(line, step, stride=stride), :]
            targets[half][rank, :, column : column + 128] = value.astype(low_type)


def pack(ranks, local, in_ref, down_ref, *outs):
    step = 32
    lines = step * local * ranks

    def slices(span):
        return pl.BlockSpec((ranks, step, span), lambda i: (0, i, 0))

    pltpu.emit_pipeline(
        functools.partial(pack_kernel, ranks, local, step),
        grid=(outs[0].shape[1] // step,),
        in_specs=[
            pl.BlockSpec((2 * lines, 128), lambda i: (i, 0)),
            pl.BlockSpec((lines, 128), lambda i: (i, 0)),
        ],
        out_specs=[slices(out.shape[2]) for out in outs],
    )(in_ref, down_ref, *outs)


def unpack_kernel(ranks, local, step, first_ref, second_ref, out_ref):
    of_in, of_down = lines_of(ranks, local)
    for rank, half, column, line, stride in (
        of_in if first_ref.shape[2] == local * 128 else of_down
    ):
        value = (first_ref, second_ref)[half][rank, :, column : column + 128]
        out_ref[pl.ds(line, step, stride=stride), :] = value.astype(high_type)


def unpack_inside(local, first_ref, second_ref, out_ref):
    ranks, rows, span = first_ref.shape
    step = 32
    pltpu.emit_pipeline(
        functools.partial(unpack_kernel, ranks, local, step),
        grid=(rows // step,),
        in_specs=[pl.BlockSpec((ranks, step, span), lambda i: (0, i, 0))] * 2,
        out_specs=[pl.BlockSpec((step * ranks * span // 64, 128), lambda i: (i, 0))],
    )(first_ref, second_ref, out_ref)


def unpack(local, *halves):
    ranks, rows, span = halves[0].shape
    step = 32
    lines = step * ranks * span // 64
    return pl.pallas_call(
        functools.partial(unpack_kernel, ranks, local, step),
        grid=(rows // step,),
        in_specs=[pl.BlockSpec((ranks, step, span), lambda i: (0, i, 0))] * 2,
        out_specs=pl.BlockSpec((lines, 128), lambda i: (i, 0)),
        out_shape=jax.ShapeDtypeStruct((rows * ranks * span // 64, 128), high_type),
        compiler_params=pltpu.CompilerParams(vmem_limit_bytes=32 << 20),
    )(*halves)


def experts_kernel(first, depth, earlier, extra_count, *refs):
    rest = iter(refs)

    def take(count):
        return [next(rest) for _ in range(count)]

    tokens_ref, grads_ref, gates_ref, in_ref, down_ref = take(5)
    added = take(3) if earlier else None
    extra_refs = take(extra_count)
    back_ref, mixed_ref, sums_ref, grad_in_ref, grad_down_ref = take(5)
    extra_outs = take(extra_count)
    in_total, down_total = take(2)
    extra_sems = [take(3) for _ in extra_refs]
    column = lax.axis_index("ey") * 2 + lax.axis_index("ex")
    step, steps = pl.program_id(0), pl.num_programs(0)
    blocks, experts, rows = gates_ref.shape
    span = down_ref.shape[1]
    width = tokens_ref.shape[2]
    at = Place(depth)
    ranks = [(k, core) for k in range(depth) for core in range(2) if k or core]
    peers = [at.chip(k, lax.rem(at.c + core, 2)) for k, core in ranks]
    own_rank = at.z * 2 + at.c

    def extra_copies():
        return [
            remote(source.at[there[2] * 2 + there[3]], target.at[own_rank], sems, slot, there)
            for source, target, sems in zip(extra_refs, extra_outs, extra_sems)
            for slot, there in enumerate(peers)
        ]

    def kept():
        return [
            pltpu.make_async_copy(source.at[own_rank], target.at[own_rank], sems[2])
            for source, target, sems in zip(extra_refs, extra_outs, extra_sems)
        ]

    @pl.when(step == 0)
    def _():
        meet(peers)
        for copy in extra_copies() + kept():
            copy.start()
        in_total[...] = jnp.zeros_like(in_total)
        down_total[...] = jnp.zeros_like(down_total)

    units_of = (
        lax.broadcasted_iota(jnp.int32, (experts, span), 1) // 128 + column * 4 + first
        == lax.broadcasted_iota(jnp.int32, (experts, span), 0)
    ).astype(low_type)

    def terms(values, count):
        result = []
        for _ in range(count):
            result.append(values.astype(low_type))
            values = values - result[-1].astype(high_type)
        return result

    tokens = tokens_ref[...].reshape(blocks * rows, width)
    grads = grads_ref[...].reshape(blocks * rows, width)
    gates = jnp.concatenate([gates_ref[b] for b in range(blocks)], axis=1)
    gates = jnp.concatenate(terms(gates, 3), axis=0)
    wide = t_dot(gates, jnp.concatenate([units_of] * 3, axis=0))
    both = dot(tokens, in_ref[...])
    gate_part, up_part = both[:, :span], both[:, span:]
    down_grad = dot(grads, down_ref[...])
    sigma = 0.5 + 0.5 * jnp.tanh(0.5 * gate_part)
    silu = gate_part * sigma
    hidden = (silu * up_part).astype(low_type).astype(high_type)
    weighted = (wide * hidden).astype(low_type)
    inner = hidden * down_grad
    high, low = terms(inner, 2)
    sums = dot_t(units_of, high) + dot_t(units_of, low)
    for b in range(blocks):
        part = sums[:, b * rows : (b + 1) * rows]
        sums_ref[b] = part + added[2][b] if earlier else part
    grad_hidden = wide * down_grad
    grad_gate = grad_hidden * up_part * (sigma + silu * (1.0 - sigma))
    grad_both = jnp.concatenate([grad_gate, grad_hidden * silu], axis=1).astype(low_type)
    back = dot_t(grad_both, in_ref[...]).reshape(back_ref.shape)
    mixed = dot_t(weighted, down_ref[...]).reshape(mixed_ref.shape)
    if earlier:
        back = back + added[0][...].astype(high_type)
        mixed = mixed + added[1][...].astype(high_type)
    back_ref[...] = back.astype(low_type)
    mixed_ref[...] = mixed.astype(low_type)
    in_total[...] += t_dot(tokens, grad_both)
    down_total[...] += t_dot(grads, weighted)

    @pl.when(step == steps - 1)
    def _():
        grad_in_ref[...] = in_total[...].astype(low_type)
        grad_down_ref[...] = down_total[...].astype(low_type)
        for copy in kept() + extra_copies():
            copy.wait()


def run_experts(depth, ident, first, tokens, grads, gates, weights_in, weights_down, extras, earlier):
    devices, rows, width = tokens.shape
    experts = gates.shape[1]
    blocks = 4
    span = weights_in.shape[1] // 2

    def by_step(shape):
        return pl.BlockSpec((blocks,) + shape, lambda i: (i, 0, 0))

    def whole(shape):
        return pl.BlockSpec(shape, lambda i: (0, 0), pipeline_mode=pl.Buffered(1))

    per_token = [by_step((rows, width)), by_step((rows, width)), by_step((experts, rows))]
    sums = [jax.ShapeDtypeStruct((devices, rows, width), low_type)] * 2
    sums.append(jax.ShapeDtypeStruct((devices, experts, rows), high_type))
    return pl.pallas_call(
        functools.partial(experts_kernel, first, depth, bool(earlier), len(extras)),
        grid=(devices // blocks,),
        in_specs=per_token
        + [whole((width, 2 * span)), whole((width, span))]
        + (per_token if earlier else [])
        + in_hbm(len(extras)),
        out_specs=per_token
        + [whole((width, 2 * span)), whole((width, span))]
        + in_hbm(len(extras)),
        out_shape=sums
        + [
            jax.ShapeDtypeStruct((width, 2 * span), low_type),
            jax.ShapeDtypeStruct((width, span), low_type),
        ]
        + [jax.ShapeDtypeStruct(extra.shape, extra.dtype) for extra in extras],
        scratch_shapes=[
            pltpu.VMEM((width, 2 * span), high_type),
            pltpu.VMEM((width, span), high_type),
        ]
        + (pair(2 * depth - 1) + [pltpu.SemaphoreType.DMA]) * len(extras),
        compiler_params=pltpu.CompilerParams(
            collective_id=ident, has_side_effects=True, vmem_limit_bytes=60 << 20
        ),
        cost_estimate=pl.CostEstimate(
            flops=18 * devices * rows * width * span,
            bytes_accessed=8 * devices * rows * width,
            transcendentals=devices * rows * span,
        ),
    )(tokens, grads, gates, weights_in, weights_down, *earlier, *extras)


def grid_shards(
    residual_in,
    cotangent,
    lengths,
    routes,
    attn_qkv,
    attn_out,
    gains,
    router,
    expert_in,
    expert_down,
):
    rows, width = residual_in.shape
    depth = lax.axis_size("dz")
    ranks = 2 * depth
    columns = 4
    seq_rows = rows * ranks
    local_experts = expert_in.shape[1]
    experts = local_experts * columns
    hidden_width = expert_in.shape[3]
    part = hidden_width // ranks
    span = local_experts * part
    chunk_rows = expert_in.shape[0]
    weight_rows = attn_qkv.shape[1]
    score_scale = HD ** (-0.5)
    y, x, z, c = (lax.axis_index(name) for name in GRID)
    column = y * 2 + x
    own_heads = HEADS // ranks
    own_width = own_heads * HD

    def sum_column(ident, pairs):
        flat = exchange(depth, ident, pairs.reshape(-1, 128), same=True)
        return jnp.sum(flat, axis=0).reshape(pairs.shape)

    def by_rank(values):
        lead = values.shape[:-1]
        shaped = values.reshape(lead + (2, own_heads, depth, HD))
        n = len(lead)
        return shaped.transpose((n + 2, n) + tuple(range(n)) + (n + 1, n + 3)).reshape(
            (ranks,) + lead + (own_width,)
        )

    def by_head(values):
        lead = values.shape[1:-1]
        shaped = values.reshape((depth, 2) + lead + (own_heads, HD))
        n = len(lead)
        return shaped.transpose(tuple(range(2, n + 2)) + (1, n + 2, 0, n + 3)).reshape(
            lead + (width,)
        )

    small = jnp.concatenate([gains.T, router], axis=1).astype(low_type)
    small = jnp.pad(small, ((0, 0), (0, 128 - small.shape[1])))
    packed = attn_qkv.astype(low_type).transpose(1, 0, 2)
    packed = by_rank(packed).reshape(ranks, weight_rows, 3 * own_width)
    seq_input, out_weight, qkv_weight, small, first_in, second_in, first_down, second_down = gather(
        depth,
        0,
        residual_in,
        attn_out.astype(low_type),
        packed,
        small,
        expert_in,
        expert_down,
    )
    out_weight = out_weight.reshape(width, width)
    qkv_weight = qkv_weight.reshape(width, 3 * own_width)
    small = small.reshape(width, 128)
    gain_rows = small[:, :4].T.astype(high_type)
    router_weight = small[:, 4 : 4 + experts]
    gain_own = [
        lax.dynamic_index_in_dim(by_rank(gain_rows[i]), z * 2 + c, 0, keepdims=False)
        for i in (1, 2)
    ]
    normed_in = seq_input.reshape(seq_rows, width).astype(high_type)
    normed_in = (normed_in * rms_scale(normed_in) * gain_rows[0]).astype(low_type)
    normed_in = lax.optimization_barrier(normed_in)

    raw = dot(normed_in, qkv_weight)
    query_raw, key_raw = raw[:, :own_width], raw[:, own_width : 2 * own_width]
    value_rows = raw[:, 2 * own_width :].astype(low_type)
    squares = jnp.stack(
        [jnp.sum(query_raw * query_raw, axis=1), jnp.sum(key_raw * key_raw, axis=1)]
    )
    scales = lax.rsqrt(sum_column(1, squares) / width + epsilon)
    query_scale, key_scale = scales[0][:, None], scales[1][:, None]
    positions = jnp.arange(seq_rows, dtype=jnp.int32)
    length_now = lengths[0]
    key_live = positions < length_now
    cosine, sine_table = angle_tables(positions)
    query_normed = query_raw * query_scale
    key_normed = key_raw * key_scale
    query_rot = rotate(query_normed * gain_own[0], cosine, sine_table).astype(low_type)
    key_rot = rotate(key_normed * gain_own[1], cosine, sine_table).astype(low_type)
    query_heads = query_rot.reshape(seq_rows, own_heads, HD)
    key_heads = key_rot.reshape(seq_rows, own_heads, HD)
    value_heads = value_rows.reshape(seq_rows, own_heads, HD)

    def per_head(spec, left, right):
        return jnp.einsum(spec, left, right, preferred_element_type=high_type)

    scores = per_head("qhd,khd->hqk", query_heads, key_heads) * score_scale
    scores = jnp.where(key_live[None, None, :], scores, masked_score)
    probs = jax.nn.softmax(scores, axis=-1)
    probs_low = probs.astype(low_type)
    attended = per_head("hqk,khd->qhd", probs_low, value_heads).astype(low_type)
    attended = exchange(depth, 2, attended.reshape(ranks, rows, own_width))
    attended = by_head(attended)

    own_positions = (z * 2 + c) * rows + jnp.arange(rows, dtype=jnp.int32)
    live_rows = (own_positions < length_now).astype(high_type)[:, None]
    input_rows = residual_in.astype(high_type)
    middle = input_rows + live_rows * dot(attended, out_weight)
    scale_mid = rms_scale(middle)
    normed_mid_f = middle * scale_mid
    normed_mid = (normed_mid_f * gain_rows[3]).astype(low_type)

    logits = dot(normed_mid, router_weight)
    named = jnp.any(
        routes[:, :, None] == jnp.arange(experts, dtype=jnp.int32)[None, None, :], axis=1
    )
    top = jnp.max(jnp.where(named, logits, -jnp.inf), axis=1, keepdims=True)
    weight_of = jnp.where(named, jnp.exp(jnp.where(named, logits - top, 0.0)), 0.0)
    gates = weight_of / jnp.sum(weight_of, axis=1, keepdims=True)

    grad_rows = cotangent.astype(high_type)
    grad_comb = live_rows * grad_rows
    after = jnp.minimum(scales[0, 0], 0.0)
    own_grads = (grad_comb + after).astype(low_type)
    grads = lax.all_gather(own_grads, GRID, axis=0, tiled=True)
    tokens, gates_all, first_in, first_down, second_down = spread(
        depth, 3, (normed_mid, gates.T), (first_in, first_down, second_down)
    )
    grads = grads.reshape(tokens.shape)

    def flat(values):
        return values.reshape(width, -1)

    def by_slice(values):
        return values.reshape(ranks, chunk_rows, -1)

    *sums, grad_first, down_first, second_in = run_experts(
        depth,
        9,
        0,
        tokens,
        grads,
        gates_all,
        flat(first_in),
        flat(first_down),
        (second_in,),
        (),
    )
    back, mixed, gate_sums, grad_second, down_second, grad_first = run_experts(
        depth,
        10,
        local_experts // 2,
        tokens,
        grads,
        gates_all,
        flat(second_in),
        flat(second_down),
        (by_slice(grad_first),),
        tuple(sums),
    )
    grad_mid_norm, combined, grad_gates, grad_second = collect(
        depth, 4, [back, mixed], [gate_sums], extras=[by_slice(grad_second)]
    )
    output = middle + live_rows * combined

    grad_gates = grad_gates.T
    grad_chosen = gates * (grad_gates - jnp.sum(gates * grad_gates, axis=1, keepdims=True))
    grad_logits = grad_chosen.astype(low_type)
    grad_mid_norm = grad_mid_norm + dot_t(grad_logits, router_weight)
    grad_router = t_dot(normed_mid, grad_logits)

    grad_mid_rows, grad_gain_mid = rms_back(grad_mid_norm, normed_mid_f, scale_mid, gain_rows[3])
    grad_middle = grad_rows + grad_mid_rows
    grad_branch = (live_rows * grad_middle).astype(low_type)

    grad_attended = by_rank(dot_t(grad_branch, out_weight).astype(low_type))
    grad_attended = exchange(depth, 6, grad_attended)
    grad_heads = grad_attended.reshape(seq_rows, own_heads, HD)
    grad_probs = per_head("qhd,khd->hqk", grad_heads, value_heads)
    inner_rows = jnp.sum(probs * grad_probs, axis=-1, keepdims=True)
    grad_scores = (probs * (grad_probs - inner_rows)).astype(low_type)
    grad_query = per_head("hqk,khd->qhd", grad_scores, key_heads) * score_scale
    grad_key = per_head("hqk,qhd->khd", grad_scores, query_heads) * score_scale
    grad_value = per_head("hqk,qhd->khd", probs_low, grad_heads).astype(low_type)
    grad_query = rotate(grad_query.reshape(seq_rows, own_width), cosine, -sine_table)
    grad_key = rotate(grad_key.reshape(seq_rows, own_width), cosine, -sine_table)
    query_inner = grad_query * gain_own[0]
    key_inner = grad_key * gain_own[1]
    inner = jnp.stack(
        [
            jnp.sum(query_inner * query_normed, axis=1),
            jnp.sum(key_inner * key_normed, axis=1),
        ]
    )
    inner = sum_column(7, inner) / width
    query_back = query_scale * (query_inner - query_normed * inner[0][:, None])
    key_back = key_scale * (key_inner - key_normed * inner[1][:, None])
    grad_raw = jnp.concatenate(
        [
            query_back.astype(low_type),
            key_back.astype(low_type),
            grad_value.reshape(seq_rows, own_width),
        ],
        axis=1,
    )

    share = dot_t(grad_raw, qkv_weight).astype(low_type).reshape(ranks, rows, width)
    grad_norm_in = collect_column(depth, 8, share)

    scale_in = rms_scale(input_rows)
    grad_in_rows, grad_gain_in = rms_back(
        grad_norm_in, input_rows * scale_in, scale_in, gain_rows[0]
    )
    grad_input = grad_middle + grad_in_rows

    def at_heads(values):
        whole = jnp.zeros((2, own_heads, depth, HD), high_type)
        values = values.reshape(1, own_heads, 1, HD)
        return lax.dynamic_update_slice(whole, values, (c, 0, z, 0)).reshape(width)

    grad_small = jnp.concatenate(
        [
            jnp.stack(
                [
                    grad_gain_in,
                    at_heads(jnp.sum(grad_query * query_normed, axis=0)),
                    at_heads(jnp.sum(grad_key * key_normed, axis=0)),
                    grad_gain_mid,
                ]
            ).T,
            grad_router,
        ],
        axis=1,
    )
    grad_small = jnp.pad(grad_small, ((0, 0), (0, 128 - grad_small.shape[1])))
    grad_out = t_dot(attended, grad_branch).astype(low_type)
    grad_qkv = t_dot(normed_in, grad_raw).astype(low_type)
    grad_out, grad_small, grad_qkv, down_first, down_second, grad_expert_in = collect(
        depth,
        5,
        [grad_out.reshape(-1, weight_rows, width)],
        [grad_small.reshape(-1, weight_rows, 128)],
        [grad_qkv.reshape(columns, -1, 3 * own_width)],
        [by_slice(down_first), by_slice(down_second)],
        (local_experts, grad_first, grad_second),
    )
    grad_expert_in = grad_expert_in.reshape(chunk_rows, local_experts, ranks, 2, part)
    grad_expert_in = grad_expert_in.transpose(0, 1, 3, 2, 4).reshape(expert_in.shape)
    grad_expert_down = unpack(local_experts, down_first, down_second).reshape(
        chunk_rows, ranks, local_experts, part
    )
    grad_expert_down = grad_expert_down.transpose(0, 2, 1, 3).reshape(expert_down.shape)
    return (
        output,
        grad_input,
        grad_qkv,
        grad_out,
        grad_small[:, :4].T,
        grad_small[:, 4 : 4 + experts],
        grad_expert_in,
        grad_expert_down,
    )


def slot_index(route_rows, experts, capacity):
    flat_routes = route_rows.reshape(-1)
    onehot = (flat_routes[:, None] == jnp.arange(experts, dtype=jnp.int32)[None, :]).astype(
        jnp.int32
    )
    rows = jnp.arange(flat_routes.shape[0], dtype=jnp.int32)
    earlier = (rows[None, :] < rows[:, None]).astype(jnp.bfloat16)
    before = jnp.dot(
        earlier, onehot.astype(jnp.bfloat16), preferred_element_type=jnp.float32
    ).astype(jnp.int32)
    rank_rows = jnp.sum(before * onehot, axis=1)
    return flat_routes * capacity + rank_rows


def head_scores(query_rot, key_all, key_live):
    row_count = query_rot.shape[0]
    query_heads = query_rot.reshape(row_count, HEADS, HD)
    key_heads = key_all.reshape(key_all.shape[0], HEADS, HD)
    raw_scores = jnp.einsum(
        "qhd,khd->hqk", query_heads, key_heads, preferred_element_type=jnp.float32
    ) * HD ** (-0.5)
    return jnp.where(key_live[None, None, :], raw_scores, masked_score)


def to_owners(buffer):
    return lax.all_to_all(buffer, "expert", split_axis=0, concat_axis=0, tiled=True)


def from_owners(buffer):
    return lax.all_to_all(buffer, "expert", split_axis=0, concat_axis=0, tiled=True)


def shards(
    residual_in,
    cotangent,
    lengths,
    routes,
    attn_qkv,
    attn_out,
    gains,
    router,
    expert_in,
    expert_down,
):
    tok_rows, model_width = residual_in.shape
    top_count = routes.shape[1]
    owners = lax.axis_size("expert")
    local_experts = expert_in.shape[1]
    experts = local_experts * owners
    capacity = tok_rows * top_count * 2 // experts
    local_slots = local_experts * capacity
    seq_rows = tok_rows * lax.axis_size("dp")
    score_scale = HD ** (-0.5)
    qkv_weights, out_weight, gain_low, router_weight = (
        lax.all_gather(attn_qkv.astype(low_type), ("expert", "dp"), axis=1, tiled=True),
        lax.all_gather(attn_out.astype(low_type), ("expert", "dp"), axis=0, tiled=True),
        lax.all_gather(gains.astype(low_type), ("expert", "dp"), axis=1, tiled=True),
        lax.all_gather(router.astype(low_type), ("expert", "dp"), axis=0, tiled=True),
    )
    gain_rows = gain_low.astype(high_type)
    input_rows = residual_in.astype(high_type)
    scale_in = rms_scale(input_rows)
    normed_in_f = input_rows * scale_in
    normed_in = (normed_in_f * gain_rows[0]).astype(low_type)
    query_raw = jnp.dot(normed_in, qkv_weights[0], preferred_element_type=high_type)
    key_raw = jnp.dot(normed_in, qkv_weights[1], preferred_element_type=high_type)
    value_rows = jnp.dot(normed_in, qkv_weights[2], preferred_element_type=high_type).astype(
        low_type
    )
    positions = lax.axis_index("dp") * tok_rows + jnp.arange(tok_rows, dtype=jnp.int32)
    length_now = lengths[0]
    live_rows = (positions < length_now).astype(high_type)[:, None]
    key_live = jnp.arange(seq_rows, dtype=jnp.int32) < length_now
    cosine, sine_table = angle_tables(positions)
    query_scale = rms_scale(query_raw)
    query_normed = query_raw * query_scale
    query_rot = rotate(query_normed * gain_rows[1], cosine, sine_table).astype(low_type)
    key_scale = rms_scale(key_raw)
    key_normed = key_raw * key_scale
    key_rot = rotate(key_normed * gain_rows[2], cosine, sine_table).astype(low_type)
    key_all = lax.all_gather(key_rot, "dp", axis=0, tiled=True)
    value_all = lax.all_gather(value_rows, "dp", axis=0, tiled=True)
    scores = head_scores(query_rot, key_all, key_live)
    top_score = jnp.max(scores, axis=-1, keepdims=True)
    exp_scores = jnp.exp(scores - top_score)
    row_total = jnp.sum(exp_scores, axis=-1, keepdims=True)
    weights_low = (exp_scores / row_total).astype(low_type)
    log_total = top_score + jnp.log(row_total)
    value_heads = value_all.reshape(seq_rows, HEADS, HD)
    attended = jnp.einsum(
        "hqk,khd->qhd", weights_low, value_heads, preferred_element_type=high_type
    )
    attended = attended.reshape(tok_rows, model_width).astype(low_type)
    branch = jnp.dot(attended, out_weight, preferred_element_type=high_type)
    middle = input_rows + live_rows * branch
    scale_mid = rms_scale(middle)
    normed_mid_f = middle * scale_mid
    normed_mid = (normed_mid_f * gain_rows[3]).astype(low_type)
    logits = jnp.dot(normed_mid, router_weight, preferred_element_type=high_type)
    selector = (routes[:, :, None] == jnp.arange(experts, dtype=jnp.int32)[None, None, :]).astype(
        high_type
    )
    chosen = jnp.einsum("te,tje->tj", logits, selector)
    gate_weights = jax.nn.softmax(chosen, axis=-1)
    slot_rows = slot_index(routes, experts, capacity)
    token_of = jnp.arange(slot_rows.shape[0], dtype=jnp.int32) // top_count
    send_rows = (
        jnp.zeros((experts * capacity, model_width), low_type)
        .at[slot_rows]
        .set(normed_mid[token_of])
    )
    rows_recv = lax.all_to_all(
        send_rows.reshape(owners, local_slots, model_width),
        "expert",
        split_axis=0,
        concat_axis=0,
        tiled=True,
    )
    rows_recv = rows_recv.reshape(owners, local_experts, capacity, model_width)
    weights_in, weights_down = (
        lax.all_gather(expert_in.astype(low_type), "dp", axis=0, tiled=True),
        lax.all_gather(expert_down.astype(low_type), "dp", axis=0, tiled=True),
    )
    both_parts = jnp.einsum(
        "sxmd,dxkf->sxmkf", rows_recv, weights_in, preferred_element_type=high_type
    )
    gate_part = both_parts[:, :, :, 0, :]
    up_part = both_parts[:, :, :, 1, :]
    hidden = (jax.nn.silu(gate_part) * up_part).astype(low_type)
    produced = jnp.einsum(
        "sxmf,dxf->sxmd", hidden, weights_down, preferred_element_type=high_type
    ).astype(low_type)
    returned = from_owners(produced.reshape(owners, local_slots, model_width))
    returned = returned.reshape(experts * capacity, model_width)
    picked = returned[slot_rows].reshape(tok_rows, top_count, model_width).astype(high_type)
    combined = jnp.sum(gate_weights[:, :, None] * picked, axis=1)
    output = middle + live_rows * combined
    grad_rows = cotangent.astype(high_type)
    grad_comb = live_rows * grad_rows
    grad_gates = jnp.einsum("tjd,td->tj", picked, grad_comb)
    grad_chosen = gate_weights * (
        grad_gates - jnp.sum(gate_weights * grad_gates, axis=-1, keepdims=True)
    )
    grad_logits = jnp.einsum("tj,tje->te", grad_chosen, selector).astype(low_type)
    grad_send = (
        (gate_weights[:, :, None] * grad_comb[:, None, :]).astype(low_type).reshape(-1, model_width)
    )
    grad_buffer = (
        jnp.zeros((experts * capacity, model_width), low_type).at[slot_rows].set(grad_send)
    )
    grad_recv = to_owners(grad_buffer.reshape(owners, local_slots, model_width))
    grad_recv = grad_recv.reshape(owners, local_experts, capacity, model_width)
    grad_hidden = jnp.einsum(
        "sxmd,dxf->sxmf", grad_recv, weights_down, preferred_element_type=high_type
    )
    sigma_gate = jax.nn.sigmoid(gate_part)
    grad_gate = grad_hidden * up_part * sigma_gate * (1.0 + gate_part * (1.0 - sigma_gate))
    grad_up = grad_hidden * gate_part * sigma_gate
    grad_both = jnp.stack([grad_gate, grad_up], axis=3).astype(low_type)
    grad_rows_out = jnp.einsum(
        "sxmkf,dxkf->sxmd", grad_both, weights_in, preferred_element_type=high_type
    ).astype(low_type)
    grad_back = from_owners(grad_rows_out.reshape(owners, local_slots, model_width))
    grad_back = grad_back.reshape(experts * capacity, model_width)
    grad_mid_norm = jnp.sum(
        grad_back[slot_rows].reshape(tok_rows, top_count, model_width).astype(high_type), axis=1
    )
    grad_mid_norm = grad_mid_norm + jnp.dot(
        grad_logits, router_weight.T, preferred_element_type=high_type
    )
    grad_router = jnp.dot(normed_mid.T, grad_logits, preferred_element_type=high_type)
    row_piece = rows_recv
    grad_expert_in = lax.psum_scatter(
        jnp.einsum(
            "sxmd,sxmkf->dxkf", row_piece, grad_both, preferred_element_type=high_type
        ).astype(jnp.bfloat16),
        "dp",
        scatter_dimension=0,
        tiled=True,
    ).astype(jnp.float32)
    row_piece = grad_recv
    grad_expert_down = lax.psum_scatter(
        jnp.einsum("sxmd,sxmf->dxf", row_piece, hidden, preferred_element_type=high_type).astype(
            jnp.bfloat16
        ),
        "dp",
        scatter_dimension=0,
        tiled=True,
    ).astype(jnp.float32)
    grad_mid_rows, grad_gain_mid = rms_back(grad_mid_norm, normed_mid_f, scale_mid, gain_rows[3])
    grad_middle = grad_rows + grad_mid_rows
    grad_branch = (live_rows * grad_middle).astype(low_type)
    grad_out_weight = jnp.dot(attended.T, grad_branch, preferred_element_type=high_type)
    grad_attended = jnp.dot(grad_branch, out_weight.T, preferred_element_type=high_type).astype(
        low_type
    )
    scores = head_scores(query_rot, key_all, key_live)
    probs_full = jnp.exp(scores - log_total)
    grad_heads = grad_attended.reshape(tok_rows, HEADS, HD)
    value_heads = value_all.reshape(seq_rows, HEADS, HD)
    key_heads = key_all.reshape(seq_rows, HEADS, HD)
    query_heads = query_rot.reshape(tok_rows, HEADS, HD)
    grad_probs = jnp.einsum(
        "qhd,khd->hqk", grad_heads, value_heads, preferred_element_type=high_type
    )
    inner_rows = jnp.sum(probs_full * grad_probs, axis=-1, keepdims=True)
    grad_scores = (probs_full * (grad_probs - inner_rows)).astype(low_type)
    grad_query = (
        jnp.einsum(
            "hqk,khd->qhd", grad_scores, key_heads, preferred_element_type=high_type
        ).reshape(tok_rows, model_width)
        * score_scale
    )
    grad_key_part = (
        jnp.einsum(
            "hqk,qhd->khd", grad_scores, query_heads, preferred_element_type=high_type
        ).reshape(seq_rows, model_width)
        * score_scale
    )
    grad_value_part = jnp.einsum(
        "hqk,qhd->khd", probs_full.astype(low_type), grad_heads, preferred_element_type=high_type
    ).reshape(seq_rows, model_width)
    grad_key_sum, grad_value_sum = (
        lax.psum_scatter(
            grad_key_part.astype(jnp.bfloat16), "dp", scatter_dimension=0, tiled=True
        ).astype(jnp.float32),
        lax.psum_scatter(
            grad_value_part.astype(jnp.bfloat16), "dp", scatter_dimension=0, tiled=True
        ).astype(jnp.float32),
    )
    grad_value = grad_value_sum.astype(low_type)
    grad_key_raw, grad_key_gain = rms_back(
        rotate(grad_key_sum, cosine, -sine_table), key_normed, key_scale, gain_rows[2]
    )
    grad_query_raw, grad_query_gain = rms_back(
        rotate(grad_query, cosine, -sine_table), query_normed, query_scale, gain_rows[1]
    )
    grad_key_raw = grad_key_raw.astype(low_type)
    grad_query_raw = grad_query_raw.astype(low_type)
    grad_norm_in = jnp.dot(grad_query_raw, qkv_weights[0].T, preferred_element_type=high_type)
    grad_norm_in = grad_norm_in + jnp.dot(
        grad_key_raw, qkv_weights[1].T, preferred_element_type=high_type
    )
    grad_norm_in = grad_norm_in + jnp.dot(
        grad_value, qkv_weights[2].T, preferred_element_type=high_type
    )
    grad_qkv_local = jnp.stack(
        [
            jnp.dot(normed_in.T, grad_query_raw, preferred_element_type=high_type),
            jnp.dot(normed_in.T, grad_key_raw, preferred_element_type=high_type),
            jnp.dot(normed_in.T, grad_value, preferred_element_type=high_type),
        ]
    )
    grad_in_rows, grad_gain_in = rms_back(grad_norm_in, normed_in_f, scale_in, gain_rows[0])
    grad_input = grad_middle + grad_in_rows
    grad_gains_local = jnp.stack([grad_gain_in, grad_query_gain, grad_key_gain, grad_gain_mid])
    summed = (
        lax.psum_scatter(grad_qkv_local, ("expert", "dp"), scatter_dimension=1, tiled=True),
        lax.psum_scatter(grad_out_weight, ("expert", "dp"), scatter_dimension=0, tiled=True),
        lax.psum_scatter(grad_gains_local, ("expert", "dp"), scatter_dimension=1, tiled=True),
        lax.psum_scatter(grad_router, ("expert", "dp"), scatter_dimension=0, tiled=True),
    )
    return (
        output,
        grad_input,
        summed[0],
        summed[1],
        summed[2],
        summed[3],
        grad_expert_in,
        grad_expert_down,
    )


def solution(mesh):
    column_count, rank_count = mesh.shape["expert"], mesh.shape["dp"]
    depth = rank_count // 2
    tiled = column_count == 4 and rank_count % 2 == 0 and HEADS == column_count * depth
    if tiled:
        mesh = Mesh(mesh.devices.reshape(2, 2, depth, 2), GRID)
        column, rank, body = ("ey", "ex"), SEQ, grid_shards
    else:
        column, rank, body = ("expert",), ("dp",), shards
    device = column + rank
    placed = (
        P(device, None),
        P(device, None),
        P(column),
        P(device, None),
        P(None, device, None),
        P(device, None),
        P(None, device),
        P(device, None),
        P(rank, column, None, None),
        P(rank, column, None),
    )
    return jax.shard_map(
        body,
        mesh=mesh,
        in_specs=placed,
        out_specs=placed[:1] * 2 + placed[4:],
        check_vma=False,
    )
```

```python
import functools

import jax
import jax.numpy as jnp
from jax import lax
from jax.experimental import pallas as pl
from jax.experimental.pallas import tpu as pltpu
from jax.sharding import Mesh
from jax.sharding import PartitionSpec as P

HEADS = 16
HD = 128

epsilon = 1e-05
rope_base = 10000.0
masked_score = -1000000000.0

low_type = jnp.bfloat16
high_type = jnp.float32


def rms_scale(values):
    return lax.rsqrt(jnp.mean(values * values, axis=-1, keepdims=True) + epsilon)


def angle_tables(positions):
    frequency = rope_base ** (-2.0 * jnp.arange(HD // 2, dtype=jnp.float32) / HD)
    angles = positions.astype(jnp.float32)[:, None] * frequency[None, :]
    return (jnp.cos(angles), jnp.sin(angles))


def rotate(values, cosine, sine_table):
    row_count, width = values.shape
    shaped = values.reshape(row_count, width // HD, 2, HD // 2)
    first_half = shaped[:, :, 0, :]
    second_half = shaped[:, :, 1, :]
    cos_rows = cosine[:, None, :]
    sin_rows = sine_table[:, None, :]
    turned = jnp.stack(
        [
            first_half * cos_rows - second_half * sin_rows,
            second_half * cos_rows + first_half * sin_rows,
        ],
        axis=2,
    )
    return turned.reshape(row_count, width)


def rms_back(grad_rows, normed, scale, gain):
    grad_normed = grad_rows * gain
    inner = jnp.mean(grad_normed * normed, axis=-1, keepdims=True)
    return (scale * grad_normed - normed * scale * inner, jnp.sum(grad_rows * normed, axis=0))


def dot(left, right):
    return jnp.dot(left, right, preferred_element_type=high_type)


def dot_t(left, right):
    return lax.dot_general(left, right, (((1,), (1,)), ((), ())), preferred_element_type=high_type)


def t_dot(left, right):
    return lax.dot_general(left, right, (((0,), (0,)), ((), ())), preferred_element_type=high_type)


GRID = ("ey", "ex", "dz", "dc")
SEQ = ("dz", "dc")


MESH_ID = pl.DeviceIdType.MESH


class Place:
    def __init__(self, depth):
        self.depth = depth
        self.y, self.x, self.z, self.c = (lax.axis_index(name) for name in GRID)

    def near_of(self, core):
        return self.y + core * (1 - 2 * self.y), self.x + (1 - core) * (1 - 2 * self.x)

    def far_of(self, core):
        return self.near_of(1 - core)

    def along(self, step):
        return lax.rem(self.z + step, self.depth)

    def next_z(self, k):
        first = self.z - 1 + 2 * lax.div(4 - self.z, 4)
        last = 3 * lax.div(3 - self.z, 2)
        return (self.z, first, 6 - self.z - first - last, last)[k]

    def block(self, column, z, core):
        return ((column[0] * 2 + column[1]) * self.depth + z) * 2 + core

    @property
    def own_column(self):
        return self.y, self.x

    @property
    def other_column(self):
        return 1 - self.y, 1 - self.x

    def core(self):
        return self.y, self.x, self.z, 1 - self.c

    def chip(self, step, core=None):
        return self.y, self.x, self.along(step), self.c if core is None else core

    def near(self):
        return (*self.near_of(self.c), self.z, self.c)

    def far(self):
        return (*self.far_of(self.c), self.z, self.c)


def meet(partners):
    barrier = pltpu.get_barrier_semaphore()
    for partner in partners:
        pl.semaphore_signal(barrier, inc=1, device_id=partner, device_id_type=MESH_ID)
    pl.semaphore_wait(barrier, len(partners))


def remote(source, target, sems, slot, partner):
    return pltpu.make_async_remote_copy(
        src_ref=source,
        dst_ref=target,
        send_sem=sems[0].at[slot],
        recv_sem=sems[1].at[slot],
        device_id=partner,
        device_id_type=MESH_ID,
    )


def pair(count):
    return [pltpu.SemaphoreType.DMA((count,)), pltpu.SemaphoreType.DMA((count,))]


def in_hbm(count):
    return [pl.BlockSpec(memory_space=pl.ANY)] * count


def spread_kernel(depth, count, extra, *refs):
    whole = count + extra
    sources, targets, sems = refs[:count], refs[whole : whole + count], refs[2 * whole :]
    extra_sources, extra_targets = refs[count:whole], refs[whole + count : 2 * whole]
    extra_sems = sems[9 * count :]
    at = Place(depth)
    others = range(1, depth)
    ranks = [(k, core) for k in range(depth) for core in range(2) if k or core]
    peers = [at.chip(k, lax.rem(at.c + core, 2)) for k, core in ranks]
    meet([at.near(), at.far()] + peers)
    started, local = [], []

    def push(n, source, index, kind, slot, partner):
        copy = remote(source, targets[n].at[index], sems[9 * n + 2 * kind :], slot, partner)
        copy.start()
        started.append(copy)

    def arrive(n, index, kind, slot):
        target = targets[n].at[index]
        remote(target, target, sems[9 * n + 2 * kind :], slot, at.core()).wait_recv()

    z_kind, near_kind, far_kind, core_kind = range(4)
    own = at.block(at.own_column, at.z, at.c)
    for n in range(count):
        push(n, sources[n], own, z_kind, at.z, (at.y, at.x, at.next_z(1), at.c))
        push(n, sources[n], own, near_kind, 0, at.near())
        push(n, sources[n], own, far_kind, 0, at.far())
        push(n, sources[n], own, core_kind, 0, at.core())
        copy = pltpu.make_async_copy(sources[n], targets[n].at[own], sems[9 * n + 8])
        copy.start()
        local.append(copy)

    inner = lax.rem(at.z, depth - 1) != 0
    onward = (at.z + 1, at.z + 1, at.z - 1, 3 * at.z - 3)

    def forward(n, source, k):
        z = at.next_z(k)
        return pltpu.make_async_remote_copy(
            src_ref=source,
            dst_ref=targets[n].at[at.block(at.own_column, z, at.c)],
            send_sem=sems[9 * n].at[z if k else depth],
            recv_sem=sems[9 * n + 1].at[z],
            device_id=(at.y, at.x, onward[k], at.c),
            device_id_type=MESH_ID,
        )

    @pl.when(inner)
    def _():
        for n in range(count):
            forward(n, sources[n], 0).start()

    own_rank = at.z * 2 + at.c

    def extra_copies():
        return [
            remote(
                extra_sources[n].at[there[2] * 2 + there[3]],
                extra_targets[n].at[own_rank],
                extra_sems[3 * n :],
                slot,
                there,
            )
            for n in range(extra)
            for slot, there in enumerate(peers)
        ]

    def extra_kept():
        return [
            pltpu.make_async_copy(
                extra_sources[n].at[own_rank], extra_targets[n].at[own_rank], extra_sems[3 * n + 2]
            )
            for n in range(extra)
        ]

    def start_extras():
        for copy in extra_copies() + extra_kept():
            copy.start()

    @pl.when(lax.rem(at.z, depth - 1) == 0)
    def _():
        start_extras()

    for k in others:
        index = at.block(at.own_column, at.next_z(k), at.c)
        for n in range(count):
            arrive(n, index, z_kind, at.next_z(k))

        @pl.when(inner)
        def _(index=index, k=k):
            for n in range(count):
                forward(n, targets[n].at[index], k).start()

        for n in range(count):
            push(n, targets[n].at[index], index, near_kind, k, at.near())
            push(n, targets[n].at[index], index, far_kind, k, at.far())
            push(n, targets[n].at[index], index, core_kind, k, at.core())
    @pl.when(inner)
    def _():
        start_extras()

    for k in range(depth):
        index = at.block(at.near_of(at.c), at.next_z(k), at.c)
        for n in range(count):
            arrive(n, index, near_kind, k)
            push(n, targets[n].at[index], index, far_kind, depth + k, at.far())
            push(n, targets[n].at[index], index, core_kind, depth + k, at.core())
    for j in range(2 * depth):
        column = at.far_of(at.c) if j < depth else at.other_column
        index = at.block(column, at.next_z(j % depth), at.c)
        for n in range(count):
            arrive(n, index, far_kind, j)
            push(n, targets[n].at[index], index, core_kind, 2 * depth + j, at.core())
    core = 1 - at.c
    columns = [at.own_column, at.near_of(core), at.far_of(core), at.other_column]
    for j in range(4 * depth):
        index = at.block(columns[j // depth], at.next_z(j % depth), core)
        for n in range(count):
            arrive(n, index, core_kind, j)
    for n in range(extra):
        for slot, (k, core) in enumerate(ranks):
            target = extra_targets[n].at[at.along(depth - k) * 2 + lax.rem(at.c + core, 2)]
            remote(target, target, extra_sems[3 * n :], slot, at.core()).wait_recv()

    @pl.when(inner)
    def _():
        for n in range(count):
            forward(n, sources[n], 0).wait_send()
            for k in others:
                index = at.block(at.own_column, at.next_z(k), at.c)
                forward(n, targets[n].at[index], k).wait_send()

    for copy in extra_copies() + started:
        copy.wait_send()
    for copy in extra_kept() + local:
        copy.wait()


def spread(depth, ident, arrays, extras=()):
    sems = []
    for _ in arrays:
        sems += pair(depth + 1) + pair(depth) + pair(2 * depth) + pair(4 * depth)
        sems.append(pltpu.SemaphoreType.DMA)
    for _ in extras:
        sems += pair(2 * depth - 1) + [pltpu.SemaphoreType.DMA]
    count = len(arrays) + len(extras)
    shapes = [((8 * depth,) + a.shape, a.dtype) for a in arrays]
    shapes += [(a.shape, a.dtype) for a in extras]
    return pl.pallas_call(
        functools.partial(spread_kernel, depth, len(arrays), len(extras)),
        out_shape=[jax.ShapeDtypeStruct(*shape) for shape in shapes],
        in_specs=in_hbm(count),
        out_specs=in_hbm(count),
        scratch_shapes=sems,
        compiler_params=pltpu.CompilerParams(
            collective_id=ident, has_side_effects=True, vmem_limit_bytes=60 << 20
        ),
        cost_estimate=pl.CostEstimate(
            flops=0,
            bytes_accessed=sum(64 * depth * a.size * a.dtype.itemsize for a in arrays),
            transcendentals=0,
        ),
    )(*arrays, *extras)


def sum_rows(target, lead, terms):
    rows = target.shape[-2]
    tile = min(rows, 16)

    def body(i, carry):
        at = pl.ds(pl.multiple_of(i * tile, tile), tile)
        total = terms[0][0][(*terms[0][1], at, slice(None))].astype(high_type)
        for ref, where in terms[1:]:
            total = total + ref[(*where, at, slice(None))].astype(high_type)
        target[(*lead, at, slice(None))] = total.astype(target.dtype)
        return carry

    lax.fori_loop(0, rows // tile, body, 0)


def collect_kernel(depth, local, counts, *refs):
    rest = iter(refs)

    def take(count):
        return [next(rest) for _ in range(count)]

    mains, smalls, shareds, extras = (take(count) for count in counts)
    halves = take(2 if local else 0)
    main_totals, small_totals, shared_totals, extra_outs = (take(count) for count in counts)
    unpacked = take(1 if local else 0)
    main_buffers = [take(5) for _ in mains]
    small_buffers = [take(5) for _ in smalls]
    shared_buffers = [take(3) for _ in shareds]
    shared_outs = [take(1)[0] for _ in shareds]
    main_sems = [take(9) for _ in mains]
    small_sems = [take(9) for _ in smalls]
    shared_sems = [take(7) for _ in shareds]
    extra_sems = [take(3) for _ in extras]
    at = Place(depth)
    ranks = [(k, core) for k in range(depth) for core in range(2) if k or core]
    peers = [at.chip(k, lax.rem(at.c + core, 2)) for k, core in ranks]
    meet([at.near(), at.far()] + peers)
    started = []
    own_rank = at.z * 2 + at.c

    def columns(core):
        return at.other_column, at.far_of(core), at.near_of(core), at.own_column

    def number(column):
        return column[0] * 2 + column[1]

    def push(copy):
        copy.start()
        started.append(copy)

    def arrive(buffer, pair_of, slot):
        remote(buffer.at[slot], buffer.at[slot], pair_of, slot, at.core()).wait_recv()

    def piece(ref, rank):
        rows = ref.shape[0] // (2 * depth)
        return ref.at[pl.ds(pl.multiple_of(rank * rows, rows), rows)]

    def block(group, k, core):
        return at.block(columns(core)[group], at.along(1 + k), core)

    def main_load(n, group, k):
        slot = group * depth + k
        return pltpu.make_async_copy(
            mains[n].at[block(group, k, at.c)], main_buffers[n][0].at[slot], main_sems[n][8].at[slot]
        )

    def main_cross(n, group, k):
        slot = group * depth + k
        source = mains[n].at[block(group, k, 1 - at.c)]
        push(remote(source, main_buffers[n][1].at[slot], main_sems[n][0:2], slot, at.core()))
        main_load(n, group, k).start()

    def main_sum(n, group, k, more):
        mine, crossed = main_buffers[n][:2]
        slot = group * depth + k
        main_load(n, group, k).wait()
        arrive(crossed, main_sems[n][0:2], slot)
        terms = [(mine, (slot,)), (crossed, (slot,))] + more
        if slot < 4 * depth - 1:
            sum_rows(mine, (slot,), terms)
        else:
            sum_rows(main_totals[n], (), terms)
        return mine.at[slot]

    def main_far(n, k):
        buffers, sems = main_buffers[n], main_sems[n]
        for group in range(2):
            slot = group * depth + k
            total = main_sum(n, group, k, [])
            push(remote(total, buffers[2].at[slot], sems[2:4], slot, at.far()))

    def main_near(n, k):
        buffers, sems = main_buffers[n], main_sems[n]
        arrive(buffers[2], sems[2:4], k)
        total = main_sum(n, 2, k, [(buffers[2], (k,))])
        push(remote(total, buffers[3].at[k], sems[4:6], k, at.near()))

    def main_own(n, k):
        buffers, sems = main_buffers[n], main_sems[n]
        arrive(buffers[2], sems[2:4], depth + k)
        arrive(buffers[3], sems[4:6], k)
        total = main_sum(n, 3, k, [(buffers[2], (depth + k,)), (buffers[3], (k,))])
        if k < depth - 1:
            push(remote(total, buffers[4].at[k], sems[6:8], k, at.chip(1 + k)))

    def small_load(n, group):
        return pltpu.make_async_copy(
            smalls[n].at[at.c, number(columns(at.c)[group])],
            small_buffers[n][0].at[group],
            small_sems[n][8].at[group],
        )

    def small_cross():
        for n, (part, buffers, sems) in enumerate(zip(smalls, small_buffers, small_sems)):
            for group in range(4):
                source = part.at[1 - at.c, number(columns(1 - at.c)[group])]
                push(remote(source, buffers[1].at[group], sems[0:2], group, at.core()))
                small_load(n, group).start()

    def small_sum(n, group, more):
        mine, crossed = small_buffers[n][:2]
        small_load(n, group).wait()
        arrive(crossed, small_sems[n][0:2], group)
        for j in range(depth):
            terms = [(mine, (group, j)), (crossed, (group, j))]
            sum_rows(mine, (group, j), terms + [(ref, (i, j)) for ref, i in more])
        return mine.at[group]

    def small_far():
        for n, (buffers, sems) in enumerate(zip(small_buffers, small_sems)):
            for group in range(2):
                total = small_sum(n, group, [])
                push(remote(total, buffers[2].at[group], sems[2:4], group, at.far()))

    def small_near():
        for n, (buffers, sems) in enumerate(zip(small_buffers, small_sems)):
            arrive(buffers[2], sems[2:4], 0)
            total = small_sum(n, 2, [(buffers[2], 0)])
            push(remote(total, buffers[3].at[0], sems[4:6], 0, at.near()))

    def small_own():
        for n, (buffers, sems) in enumerate(zip(small_buffers, small_sems)):
            arrive(buffers[2], sems[2:4], 1)
            arrive(buffers[3], sems[4:6], 0)
            total = small_sum(n, 3, [(buffers[2], 1), (buffers[3], 0)])
            for k in range(1, depth):
                there = at.chip(k)
                source = total.at[there[2]]
                push(remote(source, buffers[4].at[k - 1], sems[6:8], k - 1, there))

    def shared_load(n, i):
        return pltpu.make_async_copy(
            shareds[n].at[number(columns(at.c)[2 + i])], shared_buffers[n][0].at[i], shared_sems[n][0].at[i]
        )

    def shared_far():
        for n, (part, buffers, sems) in enumerate(zip(shareds, shared_buffers, shared_sems)):
            for i in range(2):
                source = part.at[number(columns(at.c)[i])]
                push(remote(source, buffers[1].at[i], sems[1:3], i, at.far()))
                shared_load(n, i).start()

    def shared_near():
        for n, ((mine, far_in, near_in), sems) in enumerate(zip(shared_buffers, shared_sems)):
            shared_load(n, 0).wait()
            arrive(far_in, sems[1:3], 0)
            sum_rows(mine, (0,), [(mine, (0,)), (far_in, (0,))])
            push(remote(mine.at[0], near_in.at[0], sems[3:5], 0, at.near()))

    def shared_own():
        for n, ((mine, far_in, near_in), sems) in enumerate(zip(shared_buffers, shared_sems)):
            shared_load(n, 1).wait()
            arrive(far_in, sems[1:3], 1)
            arrive(near_in, sems[3:5], 0)
            sum_rows(mine, (1,), [(mine, (1,)), (far_in, (1,)), (near_in, (0,))])
            for slot, there in enumerate(peers):
                source = piece(mine.at[1], there[2] * 2 + there[3])
                push(remote(source, piece(shared_outs[n], own_rank), sems[5:7], slot, there))
            shared_kept(n).start()

    def shared_kept(n):
        mine = shared_buffers[n][0]
        return pltpu.make_async_copy(
            piece(mine.at[1], own_rank), piece(shared_outs[n], own_rank), shared_sems[n][0].at[2]
        )

    def extra_kept(n):
        return pltpu.make_async_copy(
            extras[n].at[own_rank], extra_outs[n].at[own_rank], extra_sems[n][2]
        )

    last = len(mains) - 1
    stages = [(main_far, 0), (main_far, 1), (main_near, 0), (main_own, 0)]
    for k in range(2, depth):
        stages += [(main_far, k), (main_near, k - 1), (main_own, k - 1)]
    stages += [(main_near, depth - 1), (main_own, depth - 1)]
    order = [(stage, n, k) for n in range(len(mains)) for stage, k in stages]
    for n in range(last):
        ahead = [(main_far, n + 1, k) for k in range(2)]
        order = [step for step in order if step not in ahead]
        at_end = order.index((main_near, n, depth - 1))
        order[at_end:at_end] = ahead
    groups = {main_far: (0, 1), main_near: (2,), main_own: (3,)}
    shared_far()
    small_cross()
    for stage, n, k in order:
        for group in groups[stage]:
            main_cross(n, group, k)
    for n in range(len(extras)):
        for slot, there in enumerate(peers):
            source = extras[n].at[there[2] * 2 + there[3]]
            push(remote(source, extra_outs[n].at[own_rank], extra_sems[n][:2], slot, there))
        extra_kept(n).start()
    small_far()
    for stage, n, k in order:
        stage(n, k)
        if (stage, n, k) == (main_near, 0, 0):
            shared_near()
            small_near()
        if (stage, n, k) == (main_own, 0, 0):
            shared_own()
            small_own()
    if local:
        unpack_inside(local, *halves, *unpacked)
    for n, (buffers, sems) in enumerate(zip(small_buffers, small_sems)):
        for k in range(depth - 1):
            arrive(buffers[4], sems[6:8], k)
        terms = [(buffers[0], (3, at.z))] + [(buffers[4], (k,)) for k in range(depth - 1)]
        sum_rows(small_totals[n], (), terms)
    for n, (buffers, sems) in enumerate(zip(main_buffers, main_sems)):
        for k in range(depth - 1):
            arrive(buffers[4], sems[6:8], k)
        terms = [(main_totals[n], ())] + [(buffers[4], (k,)) for k in range(depth - 1)]
        sum_rows(main_totals[n], (), terms)
    for slot, (k, core) in enumerate(ranks):
        source = at.along(depth - k) * 2 + lax.rem(at.c + core, 2)
        for n in range(len(shareds)):
            target = piece(shared_outs[n], source)
            remote(target, target, shared_sems[n][5:7], slot, at.core()).wait_recv()
        for n in range(len(extras)):
            target = extra_outs[n].at[source]
            remote(target, target, extra_sems[n][:2], slot, at.core()).wait_recv()
    for n in range(len(shareds)):
        shared_kept(n).wait()
        out, held = shared_totals[n], shared_outs[n]
        count, rows = out.shape[:2]
        heads = held.shape[1] // (count * HD)
        for rank in range(2 * depth):
            for i in range(count):
                for j in range(heads):
                    head = (rank % 2 * heads + j) * depth + rank // 2
                    value = held[rank * rows : (rank + 1) * rows, (i * heads + j) * HD :][:, :HD]
                    out[i, :, head * HD : (head + 1) * HD] = value.astype(out.dtype)
    for n in range(len(extras)):
        extra_kept(n).wait()
    for copy in started:
        copy.wait_send()


def collect(depth, ident, mains, smalls, shareds=(), extras=(), to_unpack=(0,)):
    local, *halves = to_unpack
    dma = pltpu.SemaphoreType.DMA
    peers = 2 * depth - 1

    def by_core(a):
        return a.reshape((4, depth, 2) + a.shape[1:]).transpose(2, 0, 1, 3, 4)

    smalls = [by_core(a) for a in smalls]
    buffers, sems, shapes = [], [], []
    for a in mains:
        for slots in (4 * depth, 4 * depth, 2 * depth, depth, depth - 1):
            buffers.append(pltpu.VMEM((slots,) + a.shape[1:], a.dtype))
        sems += pair(4 * depth) + pair(2 * depth) + pair(depth) + pair(depth - 1)
        sems.append(dma((4 * depth,)))
        shapes.append(jax.ShapeDtypeStruct(a.shape[1:], high_type))
    for a in smalls:
        for slots in ((4, depth), (4, depth), (2, depth), (1, depth), (depth - 1,)):
            buffers.append(pltpu.VMEM(slots + a.shape[3:], a.dtype))
        sems += pair(4) + pair(2) + pair(1) + pair(depth - 1) + [dma((4,))]
        shapes.append(jax.ShapeDtypeStruct(a.shape[3:], high_type))
    for a in shareds:
        buffers += [pltpu.VMEM((slots,) + a.shape[1:], a.dtype) for slots in (2, 2, 1)]
        buffers.append(pltpu.VMEM(a.shape[1:], a.dtype))
        sems += [dma((3,))] + pair(2) + pair(1) + pair(peers)
        shape = (3, a.shape[1] // (2 * depth), a.shape[2] // 3 * 2 * depth)
        shapes.append(jax.ShapeDtypeStruct(shape, high_type))
    for a in extras:
        sems += pair(peers) + [dma]
        shapes.append(jax.ShapeDtypeStruct(a.shape, a.dtype))
    arrays = [*mains, *smalls, *shareds, *extras]
    counts = (len(mains), len(smalls), len(shareds), len(extras))
    if halves:
        lines = halves[0].size // 64
        shapes.append(jax.ShapeDtypeStruct((lines, 128), high_type))
    in_vmem = [pl.BlockSpec(memory_space=pltpu.VMEM)] * (len(arrays) - len(extras))
    return pl.pallas_call(
        functools.partial(collect_kernel, depth, local, counts),
        out_shape=shapes,
        in_specs=in_hbm(len(arrays) + len(halves)),
        out_specs=in_vmem + in_hbm(len(extras) + len(halves) // 2),
        scratch_shapes=buffers + sems,
        compiler_params=pltpu.CompilerParams(
            collective_id=ident, has_side_effects=True, vmem_limit_bytes=60 << 20
        ),
        cost_estimate=pl.CostEstimate(
            flops=0,
            bytes_accessed=sum(16 * a.size * a.dtype.itemsize for a in arrays),
            transcendentals=0,
        ),
    )(*arrays, *halves)


def gather_kernel(depth, local_experts, x_ref, o_ref, w_ref, s_ref, in_ref, down_ref, *refs):
    x_out, o_out, w_out, s_out = refs[:4]
    packed, sems = refs[4:8], refs[8:]
    at = Place(depth)
    ranks = [(k, core) for k in range(depth) for core in range(2) if k or core]
    peers = [at.chip(k, lax.rem(at.c + core, 2)) for k, core in ranks]
    meet([at.near(), at.far()] + peers)
    own, column = at.z * 2 + at.c, at.y * 2 + at.x
    x_z, x_core, o_z, o_near, o_far, o_core, w_sems, s_sems, w_side, s_side = (
        sems[2 * i : 2 * i + 2] for i in range(10)
    )
    started, local = [], []
    inner = lax.rem(at.z, depth - 1) != 0
    onward = (at.z + 1, at.z + 1, at.z - 1, 3 * at.z - 3)
    own_block = at.block(at.own_column, at.z, at.c)

    def push(copy):
        copy.start()
        started.append(copy)

    def arrive(target, pair_of, slot):
        remote(target, target, pair_of, slot, at.core()).wait_recv()

    def x_place(k):
        return x_out.at[at.next_z(k) * 2 + at.c]

    def o_place(k):
        return o_out.at[at.block(at.own_column, at.next_z(k), at.c)]

    def forward(source, target, pair_of, k):
        z = at.next_z(k)
        return pltpu.make_async_remote_copy(
            src_ref=source,
            dst_ref=target,
            send_sem=pair_of[0].at[z if k else depth],
            recv_sem=pair_of[1].at[z],
            device_id=(at.y, at.x, onward[k], at.c),
            device_id_type=MESH_ID,
        )

    for slot, there in enumerate(peers):
        push(remote(s_ref, s_out.at[column, own], s_sems, slot, there))
        source = w_ref.at[there[2] * 2 + there[3]]
        push(remote(source, w_out.at[column, own], w_sems, slot, there))
    def w_rank(j):
        k, core = ([(0, 0)] + ranks)[j]
        return at.along(depth - k) * 2 + lax.rem(at.c + core, 2)

    all_ranks = 2 * depth

    def w_aside(source, j):
        target = w_out.at[column, w_rank(j)]
        push(remote(source, target, w_side, j, at.near()))
        push(remote(source, target, w_side, all_ranks + j, at.far()))

    w_aside(w_ref.at[own], 0)
    first = (at.y, at.x, at.next_z(1), at.c)
    push(remote(o_ref, o_place(0), o_z, at.z, first))
    push(remote(x_ref, x_place(0), x_z, at.z, first))

    @pl.when(inner)
    def _():
        forward(o_ref, o_place(0), o_z, 0).start()
        forward(x_ref, x_place(0), x_z, 0).start()

    push(remote(x_ref, x_place(0), x_core, 0, at.core()))
    push(remote(o_ref, o_place(0), o_near, 0, at.near()))
    push(remote(o_ref, o_place(0), o_far, 0, at.far()))
    push(remote(o_ref, o_place(0), o_core, 0, at.core()))
    for i, (source, target) in enumerate(
        (
            (x_ref, x_place(0)),
            (o_ref, o_place(0)),
            (w_ref.at[own], w_out.at[column, own]),
            (s_ref, s_out.at[column, own]),
        )
    ):
        copy = pltpu.make_async_copy(source, target, sems[20].at[i])
        copy.start()
        local.append(copy)
    near_y, near_x = at.near_of(at.c)
    far_y, far_x = at.far_of(at.c)
    beside, across = near_y * 2 + near_x, far_y * 2 + far_x
    pack(2 * depth, local_experts, in_ref, down_ref, *packed)
    for slot, (j, core) in enumerate(ranks):
        source = at.along(depth - j) * 2 + lax.rem(at.c + core, 2)
        arrive(s_out.at[column, source], s_sems, slot)
        arrive(w_out.at[column, source], w_sems, slot)
        w_aside(w_out.at[column, source], 1 + slot)
    for copy in local:
        copy.wait()
    push(remote(s_out.at[column], s_out.at[column], s_side, 0, at.near()))
    push(remote(s_out.at[column], s_out.at[column], s_side, 1, at.far()))
    for k in range(1, depth):
        arrive(o_place(k), o_z, at.next_z(k))

        @pl.when(inner)
        def _(k=k):
            forward(o_place(k), o_place(k), o_z, k).start()

        push(remote(o_place(k), o_place(k), o_near, k, at.near()))
        push(remote(o_place(k), o_place(k), o_far, k, at.far()))
        push(remote(o_place(k), o_place(k), o_core, k, at.core()))
        arrive(x_place(k), x_z, at.next_z(k))

        @pl.when(inner)
        def _(k=k):
            forward(x_place(k), x_place(k), x_z, k).start()

        push(remote(x_place(k), x_place(k), x_core, k, at.core()))
        if k == 2:
            arrive(s_out.at[beside], s_side, 0)
            push(remote(s_out.at[beside], s_out.at[beside], s_side, 2, at.far()))
            for j in range(all_ranks):
                target = w_out.at[beside, w_rank(j)]
                arrive(target, w_side, j)
                push(remote(target, target, w_side, 2 * all_ranks + j, at.far()))
    for k in range(depth):
        target = o_out.at[at.block(at.near_of(at.c), at.next_z(k), at.c)]
        arrive(target, o_near, k)
        push(remote(target, target, o_far, depth + k, at.far()))
        push(remote(target, target, o_core, depth + k, at.core()))
    for j in range(2 * depth):
        place = at.far_of(at.c) if j < depth else at.other_column
        target = o_out.at[at.block(place, at.next_z(j % depth), at.c)]
        arrive(target, o_far, j)
        push(remote(target, target, o_core, 2 * depth + j, at.core()))
    arrive(s_out.at[across], s_side, 1)
    arrive(s_out.at[3 - column], s_side, 2)
    for j in range(all_ranks):
        arrive(w_out.at[across, w_rank(j)], w_side, all_ranks + j)
        arrive(w_out.at[3 - column, w_rank(j)], w_side, 2 * all_ranks + j)
    for k in range(depth):
        arrive(x_out.at[at.next_z(k) * 2 + 1 - at.c], x_core, k)
    core = 1 - at.c
    places = [at.own_column, at.near_of(core), at.far_of(core), at.other_column]
    for j in range(4 * depth):
        index = at.block(places[j // depth], at.next_z(j % depth), core)
        arrive(o_out.at[index], o_core, j)

    @pl.when(inner)
    def _():
        forward(x_ref, x_place(0), x_z, 0).wait_send()
        forward(o_ref, o_place(0), o_z, 0).wait_send()
        for k in range(1, depth):
            forward(x_place(k), x_place(k), x_z, k).wait_send()
            forward(o_place(k), o_place(k), o_z, k).wait_send()

    for copy in started:
        copy.wait_send()


def gather(depth, ident, x, o, w, s, expert_in, expert_down):
    chunk, local = expert_in.shape[:2]
    ranks = 2 * depth
    sems = pair(depth + 1) + pair(depth) + pair(depth + 1) + pair(depth) + pair(2 * depth)
    sems += pair(4 * depth) + pair(ranks - 1) * 2 + pair(3 * ranks) + pair(3)
    sems.append(pltpu.SemaphoreType.DMA((4,)))
    return pl.pallas_call(
        functools.partial(gather_kernel, depth, local),
        out_shape=[
            jax.ShapeDtypeStruct((ranks,) + x.shape, x.dtype),
            jax.ShapeDtypeStruct((4 * ranks,) + o.shape, o.dtype),
            jax.ShapeDtypeStruct((4,) + w.shape, w.dtype),
            jax.ShapeDtypeStruct((4, ranks) + s.shape, s.dtype),
        ]
        + [jax.ShapeDtypeStruct((ranks, chunk, local * 128), low_type)] * 2
        + [jax.ShapeDtypeStruct((ranks, chunk, local * 64), low_type)] * 2,
        in_specs=in_hbm(6),
        out_specs=in_hbm(8),
        scratch_shapes=sems,
        compiler_params=pltpu.CompilerParams(
            collective_id=ident, has_side_effects=True, vmem_limit_bytes=60 << 20
        ),
        cost_estimate=pl.CostEstimate(
            flops=0, bytes_accessed=64 * depth * x.size, transcendentals=0
        ),
    )(x, o, w, s, lines_in(expert_in), lines_down(expert_down))


def exchange_kernel(depth, same, x_ref, out_ref, send_sems, recv_sems, local_sem):
    at = Place(depth)
    ranks = [(k, core) for k in range(depth) for core in range(2) if k or core]
    peers = [at.chip(k, lax.rem(at.c + core, 2)) for k, core in ranks]
    meet(peers)
    own = at.z * 2 + at.c
    copies = []
    for slot, there in enumerate(peers):
        source = x_ref if same else x_ref.at[there[2] * 2 + there[3]]
        copy = remote(source, out_ref.at[own], (send_sems, recv_sems), slot, there)
        copy.start()
        copies.append(copy)
    local = pltpu.make_async_copy(x_ref if same else x_ref.at[own], out_ref.at[own], local_sem)
    local.start()
    for slot, (k, core) in enumerate(ranks):
        target = out_ref.at[at.along(depth - k) * 2 + lax.rem(at.c + core, 2)]
        remote(target, target, (send_sems, recv_sems), slot, at.core()).wait_recv()
    for copy in copies:
        copy.wait_send()
    local.wait()


def exchange(depth, ident, x, same=False):
    ranks = 2 * depth
    return pl.pallas_call(
        functools.partial(exchange_kernel, depth, same),
        out_shape=jax.ShapeDtypeStruct((ranks,) + x.shape if same else x.shape, x.dtype),
        in_specs=in_hbm(1),
        out_specs=in_hbm(1)[0],
        scratch_shapes=pair(ranks - 1) + [pltpu.SemaphoreType.DMA],
        compiler_params=pltpu.CompilerParams(
            collective_id=ident, has_side_effects=True, vmem_limit_bytes=16 << 20
        ),
        cost_estimate=pl.CostEstimate(
            flops=0, bytes_accessed=16 * x.size * x.dtype.itemsize, transcendentals=0
        ),
    )(x)


def column_kernel(depth, part, total, mine, crossed, z_in, *sems):
    at = Place(depth)
    meet([at.core()] + [at.chip(k) for k in range(1, depth)])
    started = []
    inner = lax.rem(at.z, depth - 1) != 0
    inside = lax.div(lax.rem(at.z, depth - 1) + 1, 2)
    onto = (None, at.next_z(1), at.z + 1 - 2 * lax.div(at.z, 3), 1 + lax.rem(at.z, 2))
    slots = (
        None,
        5 - lax.div(4 - at.z, 4),
        4 * inside + (1 - inside) * at.next_z(2),
        at.next_z(3),
    )

    def local(k):
        return pltpu.make_async_copy(part.at[at.next_z(k) * 2 + at.c], mine.at[k], sems[4].at[k])

    def cross(k):
        source = part.at[at.next_z(k) * 2 + 1 - at.c]
        return remote(source, crossed.at[k], sems[0:2], k, at.core())

    def arrive(slot):
        remote(z_in.at[slot], z_in.at[slot], sems[2:4], slot, at.core()).wait_recv()

    def hand_on(k):
        return pltpu.make_async_remote_copy(
            src_ref=mine.at[k],
            dst_ref=z_in.at[slots[k]],
            send_sem=sems[2].at[k],
            recv_sem=sems[3].at[slots[k]],
            device_id=(at.y, at.x, onto[k], at.c),
            device_id_type=MESH_ID,
        )

    order = tuple(range(depth - 1, -1, -1))
    for k in order:
        cross(k).start()
        local(k).start()
    for k in order:
        local(k).wait()
        cross(k).wait_recv()
        terms = [(mine, (k,)), (crossed, (k,))]
        if k == 0:
            sum_rows(total, (), terms)
            continue

        @pl.when(inner)
        def _(terms=terms, k=k):
            arrive(at.next_z(k))
            sum_rows(mine, (k,), terms + [(z_in, (at.next_z(k),))])

        @pl.when(lax.rem(at.z, depth - 1) == 0)
        def _(terms=terms, k=k):
            sum_rows(mine, (k,), terms)

        hand_on(k).start()

    @pl.when(inner)
    def _():
        arrive(4)
        arrive(5)
        sum_rows(total, (), [(total, ()), (z_in, (4,)), (z_in, (5,))])

    @pl.when(lax.rem(at.z, depth - 1) == 0)
    def _():
        slot = 5 - lax.div(at.z, 3)
        arrive(slot)
        sum_rows(total, (), [(total, ()), (z_in, (slot,))])

    for k in order:
        cross(k).wait_send()
        if k:
            hand_on(k).wait_send()


def collect_column(depth, ident, part):
    block = part.shape[1:]
    return pl.pallas_call(
        functools.partial(column_kernel, depth),
        out_shape=jax.ShapeDtypeStruct(block, high_type),
        in_specs=in_hbm(1),
        out_specs=pl.BlockSpec(memory_space=pltpu.VMEM),
        scratch_shapes=[pltpu.VMEM((slots,) + block, part.dtype) for slots in (depth, depth, 6)]
        + pair(depth)
        + pair(6)
        + [pltpu.SemaphoreType.DMA((depth,))],
        compiler_params=pltpu.CompilerParams(
            collective_id=ident, has_side_effects=True, vmem_limit_bytes=32 << 20
        ),
        cost_estimate=pl.CostEstimate(
            flops=0, bytes_accessed=16 * part.size * part.dtype.itemsize, transcendentals=0
        ),
    )(part)


def lines_in(values):
    rows, local, two, hidden = values.shape
    values = values.reshape(rows, local, two, hidden // 128, 128)
    return values.transpose(0, 1, 3, 2, 4).reshape(-1, 128)


def lines_down(values):
    rows, local, hidden = values.shape
    return values.reshape(rows, local, hidden // 128, 128).transpose(0, 2, 1, 3).reshape(-1, 128)


def lines_of(ranks, local):
    half, of_in, of_down = local // 2, [], []
    for rank in range(ranks):
        for x in range(local):
            for k in range(2):
                line = (x * ranks + rank) * 2 + k
                columns = (k * half + x % half) * 128
                of_in.append((rank, x // half, columns, line, 2 * local * ranks))
            of_down.append((rank, x // half, x % half * 128, rank * local + x, local * ranks))
    return of_in, of_down


def pack_kernel(ranks, local, step, in_ref, down_ref, *outs):
    of_in, of_down = lines_of(ranks, local)
    for lines, ref, targets in ((of_in, in_ref, outs[:2]), (of_down, down_ref, outs[2:])):
        for rank, half, column, line, stride in lines:
            value = ref[pl.ds(line, step, stride=stride), :]
            targets[half][rank, :, column : column + 128] = value.astype(low_type)


def pack(ranks, local, in_ref, down_ref, *outs):
    step = 32
    lines = step * local * ranks

    def slices(span):
        return pl.BlockSpec((ranks, step, span), lambda i: (0, i, 0))

    pltpu.emit_pipeline(
        functools.partial(pack_kernel, ranks, local, step),
        grid=(outs[0].shape[1] // step,),
        in_specs=[
            pl.BlockSpec((2 * lines, 128), lambda i: (i, 0)),
            pl.BlockSpec((lines, 128), lambda i: (i, 0)),
        ],
        out_specs=[slices(out.shape[2]) for out in outs],
    )(in_ref, down_ref, *outs)


def unpack_kernel(ranks, local, step, first_ref, second_ref, out_ref):
    of_in, of_down = lines_of(ranks, local)
    for rank, half, column, line, stride in (
        of_in if first_ref.shape[2] == local * 128 else of_down
    ):
        value = (first_ref, second_ref)[half][rank, :, column : column + 128]
        out_ref[pl.ds(line, step, stride=stride), :] = value.astype(high_type)


def unpack_inside(local, first_ref, second_ref, out_ref):
    ranks, rows, span = first_ref.shape
    step = 32
    pltpu.emit_pipeline(
        functools.partial(unpack_kernel, ranks, local, step),
        grid=(rows // step,),
        in_specs=[pl.BlockSpec((ranks, step, span), lambda i: (0, i, 0))] * 2,
        out_specs=[pl.BlockSpec((step * ranks * span // 64, 128), lambda i: (i, 0))],
    )(first_ref, second_ref, out_ref)


def unpack(local, *halves):
    ranks, rows, span = halves[0].shape
    step = 32
    lines = step * ranks * span // 64
    return pl.pallas_call(
        functools.partial(unpack_kernel, ranks, local, step),
        grid=(rows // step,),
        in_specs=[pl.BlockSpec((ranks, step, span), lambda i: (0, i, 0))] * 2,
        out_specs=pl.BlockSpec((lines, 128), lambda i: (i, 0)),
        out_shape=jax.ShapeDtypeStruct((rows * ranks * span // 64, 128), high_type),
        compiler_params=pltpu.CompilerParams(vmem_limit_bytes=32 << 20),
    )(*halves)


def experts_kernel(first, depth, earlier, extra_count, *refs):
    rest = iter(refs)

    def take(count):
        return [next(rest) for _ in range(count)]

    tokens_ref, grads_ref, gates_ref, in_ref, down_ref = take(5)
    added = take(3) if earlier else None
    extra_refs = take(extra_count)
    back_ref, mixed_ref, sums_ref, grad_in_ref, grad_down_ref = take(5)
    extra_outs = take(extra_count)
    in_total, down_total = take(2)
    extra_sems = [take(3) for _ in extra_refs]
    column = lax.axis_index("ey") * 2 + lax.axis_index("ex")
    step, steps = pl.program_id(0), pl.num_programs(0)
    blocks, experts, rows = gates_ref.shape
    span = down_ref.shape[1]
    width = tokens_ref.shape[2]
    at = Place(depth)
    ranks = [(k, core) for k in range(depth) for core in range(2) if k or core]
    peers = [at.chip(k, lax.rem(at.c + core, 2)) for k, core in ranks]
    own_rank = at.z * 2 + at.c

    def extra_copies():
        return [
            remote(source.at[there[2] * 2 + there[3]], target.at[own_rank], sems, slot, there)
            for source, target, sems in zip(extra_refs, extra_outs, extra_sems)
            for slot, there in enumerate(peers)
        ]

    def kept():
        return [
            pltpu.make_async_copy(source.at[own_rank], target.at[own_rank], sems[2])
            for source, target, sems in zip(extra_refs, extra_outs, extra_sems)
        ]

    @pl.when(step == 0)
    def _():
        meet(peers)
        for copy in extra_copies() + kept():
            copy.start()
        in_total[...] = jnp.zeros_like(in_total)
        down_total[...] = jnp.zeros_like(down_total)

    units_of = (
        lax.broadcasted_iota(jnp.int32, (experts, span), 1) // 128 + column * 4 + first
        == lax.broadcasted_iota(jnp.int32, (experts, span), 0)
    ).astype(low_type)

    def terms(values, count):
        result = []
        for _ in range(count):
            result.append(values.astype(low_type))
            values = values - result[-1].astype(high_type)
        return result

    tokens = tokens_ref[...].reshape(blocks * rows, width)
    grads = grads_ref[...].reshape(blocks * rows, width)
    gates = jnp.concatenate([gates_ref[b] for b in range(blocks)], axis=1)
    gates = jnp.concatenate(terms(gates, 3), axis=0)
    wide = t_dot(gates, jnp.concatenate([units_of] * 3, axis=0))
    both = dot(tokens, in_ref[...])
    gate_part, up_part = both[:, :span], both[:, span:]
    down_grad = dot(grads, down_ref[...])
    sigma = 0.5 + 0.5 * jnp.tanh(0.5 * gate_part)
    silu = gate_part * sigma
    hidden = (silu * up_part).astype(low_type).astype(high_type)
    weighted = (wide * hidden).astype(low_type)
    inner = hidden * down_grad
    high, low = terms(inner, 2)
    sums = dot_t(units_of, high) + dot_t(units_of, low)
    for b in range(blocks):
        part = sums[:, b * rows : (b + 1) * rows]
        sums_ref[b] = part + added[2][b] if earlier else part
    grad_hidden = wide * down_grad
    grad_gate = grad_hidden * up_part * (sigma + silu * (1.0 - sigma))
    grad_both = jnp.concatenate([grad_gate, grad_hidden * silu], axis=1).astype(low_type)
    back = dot_t(grad_both, in_ref[...]).reshape(back_ref.shape)
    mixed = dot_t(weighted, down_ref[...]).reshape(mixed_ref.shape)
    if earlier:
        back = back + added[0][...].astype(high_type)
        mixed = mixed + added[1][...].astype(high_type)
    back_ref[...] = back.astype(low_type)
    mixed_ref[...] = mixed.astype(low_type)
    in_total[...] += t_dot(tokens, grad_both)
    down_total[...] += t_dot(grads, weighted)

    @pl.when(step == steps - 1)
    def _():
        grad_in_ref[...] = in_total[...].astype(low_type)
        grad_down_ref[...] = down_total[...].astype(low_type)
        for copy in kept() + extra_copies():
            copy.wait()


def run_experts(depth, ident, first, tokens, grads, gates, weights_in, weights_down, extras, earlier):
    devices, rows, width = tokens.shape
    experts = gates.shape[1]
    blocks = 4
    span = weights_in.shape[1] // 2

    def by_step(shape):
        return pl.BlockSpec((blocks,) + shape, lambda i: (i, 0, 0))

    def whole(shape):
        return pl.BlockSpec(shape, lambda i: (0, 0), pipeline_mode=pl.Buffered(1))

    per_token = [by_step((rows, width)), by_step((rows, width)), by_step((experts, rows))]
    sums = [jax.ShapeDtypeStruct((devices, rows, width), low_type)] * 2
    sums.append(jax.ShapeDtypeStruct((devices, experts, rows), high_type))
    return pl.pallas_call(
        functools.partial(experts_kernel, first, depth, bool(earlier), len(extras)),
        grid=(devices // blocks,),
        in_specs=per_token
        + [whole((width, 2 * span)), whole((width, span))]
        + (per_token if earlier else [])
        + in_hbm(len(extras)),
        out_specs=per_token
        + [whole((width, 2 * span)), whole((width, span))]
        + in_hbm(len(extras)),
        out_shape=sums
        + [
            jax.ShapeDtypeStruct((width, 2 * span), low_type),
            jax.ShapeDtypeStruct((width, span), low_type),
        ]
        + [jax.ShapeDtypeStruct(extra.shape, extra.dtype) for extra in extras],
        scratch_shapes=[
            pltpu.VMEM((width, 2 * span), high_type),
            pltpu.VMEM((width, span), high_type),
        ]
        + (pair(2 * depth - 1) + [pltpu.SemaphoreType.DMA]) * len(extras),
        compiler_params=pltpu.CompilerParams(
            collective_id=ident, has_side_effects=True, vmem_limit_bytes=60 << 20
        ),
        cost_estimate=pl.CostEstimate(
            flops=18 * devices * rows * width * span,
            bytes_accessed=8 * devices * rows * width,
            transcendentals=devices * rows * span,
        ),
    )(tokens, grads, gates, weights_in, weights_down, *earlier, *extras)


def grid_shards(
    residual_in,
    cotangent,
    lengths,
    routes,
    attn_qkv,
    attn_out,
    gains,
    router,
    expert_in,
    expert_down,
):
    rows, width = residual_in.shape
    depth = lax.axis_size("dz")
    ranks = 2 * depth
    columns = 4
    seq_rows = rows * ranks
    local_experts = expert_in.shape[1]
    experts = local_experts * columns
    hidden_width = expert_in.shape[3]
    part = hidden_width // ranks
    span = local_experts * part
    chunk_rows = expert_in.shape[0]
    weight_rows = attn_qkv.shape[1]
    score_scale = HD ** (-0.5)
    y, x, z, c = (lax.axis_index(name) for name in GRID)
    column = y * 2 + x
    own_heads = HEADS // ranks
    own_width = own_heads * HD

    def sum_column(ident, pairs):
        flat = exchange(depth, ident, pairs.reshape(-1, 128), same=True)
        return jnp.sum(flat, axis=0).reshape(pairs.shape)

    def by_rank(values):
        lead = values.shape[:-1]
        shaped = values.reshape(lead + (2, own_heads, depth, HD))
        n = len(lead)
        return shaped.transpose((n + 2, n) + tuple(range(n)) + (n + 1, n + 3)).reshape(
            (ranks,) + lead + (own_width,)
        )

    def by_head(values):
        lead = values.shape[1:-1]
        shaped = values.reshape((depth, 2) + lead + (own_heads, HD))
        n = len(lead)
        return shaped.transpose(tuple(range(2, n + 2)) + (1, n + 2, 0, n + 3)).reshape(
            lead + (width,)
        )

    small = jnp.concatenate([gains.T, router], axis=1).astype(low_type)
    small = jnp.pad(small, ((0, 0), (0, 128 - small.shape[1])))
    packed = attn_qkv.astype(low_type).transpose(1, 0, 2)
    packed = by_rank(packed).reshape(ranks, weight_rows, 3 * own_width)
    seq_input, out_weight, qkv_weight, small, first_in, second_in, first_down, second_down = gather(
        depth,
        0,
        residual_in,
        attn_out.astype(low_type),
        packed,
        small,
        expert_in,
        expert_down,
    )
    out_weight = out_weight.reshape(width, width)
    qkv_weight = qkv_weight.reshape(width, 3 * own_width)
    small = small.reshape(width, 128)
    gain_rows = small[:, :4].T.astype(high_type)
    router_weight = small[:, 4 : 4 + experts]
    gain_own = [
        lax.dynamic_index_in_dim(by_rank(gain_rows[i]), z * 2 + c, 0, keepdims=False)
        for i in (1, 2)
    ]
    normed_in = seq_input.reshape(seq_rows, width).astype(high_type)
    normed_in = (normed_in * rms_scale(normed_in) * gain_rows[0]).astype(low_type)
    normed_in = lax.optimization_barrier(normed_in)

    raw = dot(normed_in, qkv_weight)
    query_raw, key_raw = raw[:, :own_width], raw[:, own_width : 2 * own_width]
    value_rows = raw[:, 2 * own_width :].astype(low_type)
    squares = jnp.stack(
        [jnp.sum(query_raw * query_raw, axis=1), jnp.sum(key_raw * key_raw, axis=1)]
    )
    scales = lax.rsqrt(sum_column(1, squares) / width + epsilon)
    query_scale, key_scale = scales[0][:, None], scales[1][:, None]
    positions = jnp.arange(seq_rows, dtype=jnp.int32)
    length_now = lengths[0]
    key_live = positions < length_now
    cosine, sine_table = angle_tables(positions)
    query_normed = query_raw * query_scale
    key_normed = key_raw * key_scale
    query_rot = rotate(query_normed * gain_own[0], cosine, sine_table).astype(low_type)
    key_rot = rotate(key_normed * gain_own[1], cosine, sine_table).astype(low_type)
    query_heads = query_rot.reshape(seq_rows, own_heads, HD)
    key_heads = key_rot.reshape(seq_rows, own_heads, HD)
    value_heads = value_rows.reshape(seq_rows, own_heads, HD)

    def per_head(spec, left, right):
        return jnp.einsum(spec, left, right, preferred_element_type=high_type)

    scores = per_head("qhd,khd->hqk", query_heads, key_heads) * score_scale
    scores = jnp.where(key_live[None, None, :], scores, masked_score)
    probs = jax.nn.softmax(scores, axis=-1)
    probs_low = probs.astype(low_type)
    attended = per_head("hqk,khd->qhd", probs_low, value_heads).astype(low_type)
    attended = exchange(depth, 2, attended.reshape(ranks, rows, own_width))
    attended = by_head(attended)

    own_positions = (z * 2 + c) * rows + jnp.arange(rows, dtype=jnp.int32)
    live_rows = (own_positions < length_now).astype(high_type)[:, None]
    input_rows = residual_in.astype(high_type)
    middle = input_rows + live_rows * dot(attended, out_weight)
    scale_mid = rms_scale(middle)
    normed_mid_f = middle * scale_mid
    normed_mid = (normed_mid_f * gain_rows[3]).astype(low_type)

    logits = dot(normed_mid, router_weight)
    named = jnp.any(
        routes[:, :, None] == jnp.arange(experts, dtype=jnp.int32)[None, None, :], axis=1
    )
    top = jnp.max(jnp.where(named, logits, -jnp.inf), axis=1, keepdims=True)
    weight_of = jnp.where(named, jnp.exp(jnp.where(named, logits - top, 0.0)), 0.0)
    gates = weight_of / jnp.sum(weight_of, axis=1, keepdims=True)

    grad_rows = cotangent.astype(high_type)
    grad_comb = live_rows * grad_rows
    after = jnp.minimum(scales[0, 0], 0.0)
    own_grads = (grad_comb + after).astype(low_type)
    grads = lax.all_gather(own_grads, GRID, axis=0, tiled=True)
    tokens, gates_all, first_in, first_down, second_down = spread(
        depth, 3, (normed_mid, gates.T), (first_in, first_down, second_down)
    )
    grads = grads.reshape(tokens.shape)

    def flat(values):
        return values.reshape(width, -1)

    def by_slice(values):
        return values.reshape(ranks, chunk_rows, -1)

    *sums, grad_first, down_first, second_in = run_experts(
        depth,
        9,
        0,
        tokens,
        grads,
        gates_all,
        flat(first_in),
        flat(first_down),
        (second_in,),
        (),
    )
    back, mixed, gate_sums, grad_second, down_second, grad_first = run_experts(
        depth,
        10,
        local_experts // 2,
        tokens,
        grads,
        gates_all,
        flat(second_in),
        flat(second_down),
        (by_slice(grad_first),),
        tuple(sums),
    )
    grad_mid_norm, combined, grad_gates, grad_second = collect(
        depth, 4, [back, mixed], [gate_sums], extras=[by_slice(grad_second)]
    )
    output = middle + live_rows * combined

    grad_gates = grad_gates.T
    grad_chosen = gates * (grad_gates - jnp.sum(gates * grad_gates, axis=1, keepdims=True))
    grad_logits = grad_chosen.astype(low_type)
    grad_mid_norm = grad_mid_norm + dot_t(grad_logits, router_weight)
    grad_router = t_dot(normed_mid, grad_logits)

    grad_mid_rows, grad_gain_mid = rms_back(grad_mid_norm, normed_mid_f, scale_mid, gain_rows[3])
    grad_middle = grad_rows + grad_mid_rows
    grad_branch = (live_rows * grad_middle).astype(low_type)

    grad_attended = by_rank(dot_t(grad_branch, out_weight).astype(low_type))
    grad_attended = exchange(depth, 6, grad_attended)
    grad_heads = grad_attended.reshape(seq_rows, own_heads, HD)
    grad_probs = per_head("qhd,khd->hqk", grad_heads, value_heads)
    inner_rows = jnp.sum(probs * grad_probs, axis=-1, keepdims=True)
    grad_scores = (probs * (grad_probs - inner_rows)).astype(low_type)
    grad_query = per_head("hqk,khd->qhd", grad_scores, key_heads) * score_scale
    grad_key = per_head("hqk,qhd->khd", grad_scores, query_heads) * score_scale
    grad_value = per_head("hqk,qhd->khd", probs_low, grad_heads).astype(low_type)
    grad_query = rotate(grad_query.reshape(seq_rows, own_width), cosine, -sine_table)
    grad_key = rotate(grad_key.reshape(seq_rows, own_width), cosine, -sine_table)
    query_inner = grad_query * gain_own[0]
    key_inner = grad_key * gain_own[1]
    inner = jnp.stack(
        [
            jnp.sum(query_inner * query_normed, axis=1),
            jnp.sum(key_inner * key_normed, axis=1),
        ]
    )
    inner = sum_column(7, inner) / width
    query_back = query_scale * (query_inner - query_normed * inner[0][:, None])
    key_back = key_scale * (key_inner - key_normed * inner[1][:, None])
    grad_raw = jnp.concatenate(
        [
            query_back.astype(low_type),
            key_back.astype(low_type),
            grad_value.reshape(seq_rows, own_width),
        ],
        axis=1,
    )

    share = dot_t(grad_raw, qkv_weight).astype(low_type).reshape(ranks, rows, width)
    grad_norm_in = collect_column(depth, 8, share)

    scale_in = rms_scale(input_rows)
    grad_in_rows, grad_gain_in = rms_back(
        grad_norm_in, input_rows * scale_in, scale_in, gain_rows[0]
    )
    grad_input = grad_middle + grad_in_rows

    def at_heads(values):
        whole = jnp.zeros((2, own_heads, depth, HD), high_type)
        values = values.reshape(1, own_heads, 1, HD)
        return lax.dynamic_update_slice(whole, values, (c, 0, z, 0)).reshape(width)

    grad_small = jnp.concatenate(
        [
            jnp.stack(
                [
                    grad_gain_in,
                    at_heads(jnp.sum(grad_query * query_normed, axis=0)),
                    at_heads(jnp.sum(grad_key * key_normed, axis=0)),
                    grad_gain_mid,
                ]
            ).T,
            grad_router,
        ],
        axis=1,
    )
    grad_small = jnp.pad(grad_small, ((0, 0), (0, 128 - grad_small.shape[1])))
    grad_out = t_dot(attended, grad_branch).astype(low_type)
    grad_qkv = t_dot(normed_in, grad_raw).astype(low_type)
    grad_out, grad_small, grad_qkv, down_first, down_second, grad_expert_in = collect(
        depth,
        5,
        [grad_out.reshape(-1, weight_rows, width)],
        [grad_small.reshape(-1, weight_rows, 128)],
        [grad_qkv.reshape(columns, -1, 3 * own_width)],
        [by_slice(down_first), by_slice(down_second)],
        (local_experts, grad_first, grad_second),
    )
    grad_expert_in = grad_expert_in.reshape(chunk_rows, local_experts, ranks, 2, part)
    grad_expert_in = grad_expert_in.transpose(0, 1, 3, 2, 4).reshape(expert_in.shape)
    grad_expert_down = unpack(local_experts, down_first, down_second).reshape(
        chunk_rows, ranks, local_experts, part
    )
    grad_expert_down = grad_expert_down.transpose(0, 2, 1, 3).reshape(expert_down.shape)
    return (
        output,
        grad_input,
        grad_qkv,
        grad_out,
        grad_small[:, :4].T,
        grad_small[:, 4 : 4 + experts],
        grad_expert_in,
        grad_expert_down,
    )


def slot_index(route_rows, experts, capacity):
    flat_routes = route_rows.reshape(-1)
    onehot = (flat_routes[:, None] == jnp.arange(experts, dtype=jnp.int32)[None, :]).astype(
        jnp.int32
    )
    rows = jnp.arange(flat_routes.shape[0], dtype=jnp.int32)
    earlier = (rows[None, :] < rows[:, None]).astype(jnp.bfloat16)
    before = jnp.dot(
        earlier, onehot.astype(jnp.bfloat16), preferred_element_type=jnp.float32
    ).astype(jnp.int32)
    rank_rows = jnp.sum(before * onehot, axis=1)
    return flat_routes * capacity + rank_rows


def head_scores(query_rot, key_all, key_live):
    row_count = query_rot.shape[0]
    query_heads = query_rot.reshape(row_count, HEADS, HD)
    key_heads = key_all.reshape(key_all.shape[0], HEADS, HD)
    raw_scores = jnp.einsum(
        "qhd,khd->hqk", query_heads, key_heads, preferred_element_type=jnp.float32
    ) * HD ** (-0.5)
    return jnp.where(key_live[None, None, :], raw_scores, masked_score)


def to_owners(buffer):
    return lax.all_to_all(buffer, "expert", split_axis=0, concat_axis=0, tiled=True)


def from_owners(buffer):
    return lax.all_to_all(buffer, "expert", split_axis=0, concat_axis=0, tiled=True)


def shards(
    residual_in,
    cotangent,
    lengths,
    routes,
    attn_qkv,
    attn_out,
    gains,
    router,
    expert_in,
    expert_down,
):
    tok_rows, model_width = residual_in.shape
    top_count = routes.shape[1]
    owners = lax.axis_size("expert")
    local_experts = expert_in.shape[1]
    experts = local_experts * owners
    capacity = tok_rows * top_count * 2 // experts
    local_slots = local_experts * capacity
    seq_rows = tok_rows * lax.axis_size("dp")
    score_scale = HD ** (-0.5)
    qkv_weights, out_weight, gain_low, router_weight = (
        lax.all_gather(attn_qkv.astype(low_type), ("expert", "dp"), axis=1, tiled=True),
        lax.all_gather(attn_out.astype(low_type), ("expert", "dp"), axis=0, tiled=True),
        lax.all_gather(gains.astype(low_type), ("expert", "dp"), axis=1, tiled=True),
        lax.all_gather(router.astype(low_type), ("expert", "dp"), axis=0, tiled=True),
    )
    gain_rows = gain_low.astype(high_type)
    input_rows = residual_in.astype(high_type)
    scale_in = rms_scale(input_rows)
    normed_in_f = input_rows * scale_in
    normed_in = (normed_in_f * gain_rows[0]).astype(low_type)
    query_raw = jnp.dot(normed_in, qkv_weights[0], preferred_element_type=high_type)
    key_raw = jnp.dot(normed_in, qkv_weights[1], preferred_element_type=high_type)
    value_rows = jnp.dot(normed_in, qkv_weights[2], preferred_element_type=high_type).astype(
        low_type
    )
    positions = lax.axis_index("dp") * tok_rows + jnp.arange(tok_rows, dtype=jnp.int32)
    length_now = lengths[0]
    live_rows = (positions < length_now).astype(high_type)[:, None]
    key_live = jnp.arange(seq_rows, dtype=jnp.int32) < length_now
    cosine, sine_table = angle_tables(positions)
    query_scale = rms_scale(query_raw)
    query_normed = query_raw * query_scale
    query_rot = rotate(query_normed * gain_rows[1], cosine, sine_table).astype(low_type)
    key_scale = rms_scale(key_raw)
    key_normed = key_raw * key_scale
    key_rot = rotate(key_normed * gain_rows[2], cosine, sine_table).astype(low_type)
    key_all = lax.all_gather(key_rot, "dp", axis=0, tiled=True)
    value_all = lax.all_gather(value_rows, "dp", axis=0, tiled=True)
    scores = head_scores(query_rot, key_all, key_live)
    top_score = jnp.max(scores, axis=-1, keepdims=True)
    exp_scores = jnp.exp(scores - top_score)
    row_total = jnp.sum(exp_scores, axis=-1, keepdims=True)
    weights_low = (exp_scores / row_total).astype(low_type)
    log_total = top_score + jnp.log(row_total)
    value_heads = value_all.reshape(seq_rows, HEADS, HD)
    attended = jnp.einsum(
        "hqk,khd->qhd", weights_low, value_heads, preferred_element_type=high_type
    )
    attended = attended.reshape(tok_rows, model_width).astype(low_type)
    branch = jnp.dot(attended, out_weight, preferred_element_type=high_type)
    middle = input_rows + live_rows * branch
    scale_mid = rms_scale(middle)
    normed_mid_f = middle * scale_mid
    normed_mid = (normed_mid_f * gain_rows[3]).astype(low_type)
    logits = jnp.dot(normed_mid, router_weight, preferred_element_type=high_type)
    selector = (routes[:, :, None] == jnp.arange(experts, dtype=jnp.int32)[None, None, :]).astype(
        high_type
    )
    chosen = jnp.einsum("te,tje->tj", logits, selector)
    gate_weights = jax.nn.softmax(chosen, axis=-1)
    slot_rows = slot_index(routes, experts, capacity)
    token_of = jnp.arange(slot_rows.shape[0], dtype=jnp.int32) // top_count
    send_rows = (
        jnp.zeros((experts * capacity, model_width), low_type)
        .at[slot_rows]
        .set(normed_mid[token_of])
    )
    rows_recv = lax.all_to_all(
        send_rows.reshape(owners, local_slots, model_width),
        "expert",
        split_axis=0,
        concat_axis=0,
        tiled=True,
    )
    rows_recv = rows_recv.reshape(owners, local_experts, capacity, model_width)
    weights_in, weights_down = (
        lax.all_gather(expert_in.astype(low_type), "dp", axis=0, tiled=True),
        lax.all_gather(expert_down.astype(low_type), "dp", axis=0, tiled=True),
    )
    both_parts = jnp.einsum(
        "sxmd,dxkf->sxmkf", rows_recv, weights_in, preferred_element_type=high_type
    )
    gate_part = both_parts[:, :, :, 0, :]
    up_part = both_parts[:, :, :, 1, :]
    hidden = (jax.nn.silu(gate_part) * up_part).astype(low_type)
    produced = jnp.einsum(
        "sxmf,dxf->sxmd", hidden, weights_down, preferred_element_type=high_type
    ).astype(low_type)
    returned = from_owners(produced.reshape(owners, local_slots, model_width))
    returned = returned.reshape(experts * capacity, model_width)
    picked = returned[slot_rows].reshape(tok_rows, top_count, model_width).astype(high_type)
    combined = jnp.sum(gate_weights[:, :, None] * picked, axis=1)
    output = middle + live_rows * combined
    grad_rows = cotangent.astype(high_type)
    grad_comb = live_rows * grad_rows
    grad_gates = jnp.einsum("tjd,td->tj", picked, grad_comb)
    grad_chosen = gate_weights * (
        grad_gates - jnp.sum(gate_weights * grad_gates, axis=-1, keepdims=True)
    )
    grad_logits = jnp.einsum("tj,tje->te", grad_chosen, selector).astype(low_type)
    grad_send = (
        (gate_weights[:, :, None] * grad_comb[:, None, :]).astype(low_type).reshape(-1, model_width)
    )
    grad_buffer = (
        jnp.zeros((experts * capacity, model_width), low_type).at[slot_rows].set(grad_send)
    )
    grad_recv = to_owners(grad_buffer.reshape(owners, local_slots, model_width))
    grad_recv = grad_recv.reshape(owners, local_experts, capacity, model_width)
    grad_hidden = jnp.einsum(
        "sxmd,dxf->sxmf", grad_recv, weights_down, preferred_element_type=high_type
    )
    sigma_gate = jax.nn.sigmoid(gate_part)
    grad_gate = grad_hidden * up_part * sigma_gate * (1.0 + gate_part * (1.0 - sigma_gate))
    grad_up = grad_hidden * gate_part * sigma_gate
    grad_both = jnp.stack([grad_gate, grad_up], axis=3).astype(low_type)
    grad_rows_out = jnp.einsum(
        "sxmkf,dxkf->sxmd", grad_both, weights_in, preferred_element_type=high_type
    ).astype(low_type)
    grad_back = from_owners(grad_rows_out.reshape(owners, local_slots, model_width))
    grad_back = grad_back.reshape(experts * capacity, model_width)
    grad_mid_norm = jnp.sum(
        grad_back[slot_rows].reshape(tok_rows, top_count, model_width).astype(high_type), axis=1
    )
    grad_mid_norm = grad_mid_norm + jnp.dot(
        grad_logits, router_weight.T, preferred_element_type=high_type
    )
    grad_router = jnp.dot(normed_mid.T, grad_logits, preferred_element_type=high_type)
    row_piece = rows_recv
    grad_expert_in = lax.psum_scatter(
        jnp.einsum(
            "sxmd,sxmkf->dxkf", row_piece, grad_both, preferred_element_type=high_type
        ).astype(jnp.bfloat16),
        "dp",
        scatter_dimension=0,
        tiled=True,
    ).astype(jnp.float32)
    row_piece = grad_recv
    grad_expert_down = lax.psum_scatter(
        jnp.einsum("sxmd,sxmf->dxf", row_piece, hidden, preferred_element_type=high_type).astype(
            jnp.bfloat16
        ),
        "dp",
        scatter_dimension=0,
        tiled=True,
    ).astype(jnp.float32)
    grad_mid_rows, grad_gain_mid = rms_back(grad_mid_norm, normed_mid_f, scale_mid, gain_rows[3])
    grad_middle = grad_rows + grad_mid_rows
    grad_branch = (live_rows * grad_middle).astype(low_type)
    grad_out_weight = jnp.dot(attended.T, grad_branch, preferred_element_type=high_type)
    grad_attended = jnp.dot(grad_branch, out_weight.T, preferred_element_type=high_type).astype(
        low_type
    )
    scores = head_scores(query_rot, key_all, key_live)
    probs_full = jnp.exp(scores - log_total)
    grad_heads = grad_attended.reshape(tok_rows, HEADS, HD)
    value_heads = value_all.reshape(seq_rows, HEADS, HD)
    key_heads = key_all.reshape(seq_rows, HEADS, HD)
    query_heads = query_rot.reshape(tok_rows, HEADS, HD)
    grad_probs = jnp.einsum(
        "qhd,khd->hqk", grad_heads, value_heads, preferred_element_type=high_type
    )
    inner_rows = jnp.sum(probs_full * grad_probs, axis=-1, keepdims=True)
    grad_scores = (probs_full * (grad_probs - inner_rows)).astype(low_type)
    grad_query = (
        jnp.einsum(
            "hqk,khd->qhd", grad_scores, key_heads, preferred_element_type=high_type
        ).reshape(tok_rows, model_width)
        * score_scale
    )
    grad_key_part = (
        jnp.einsum(
            "hqk,qhd->khd", grad_scores, query_heads, preferred_element_type=high_type
        ).reshape(seq_rows, model_width)
        * score_scale
    )
    grad_value_part = jnp.einsum(
        "hqk,qhd->khd", probs_full.astype(low_type), grad_heads, preferred_element_type=high_type
    ).reshape(seq_rows, model_width)
    grad_key_sum, grad_value_sum = (
        lax.psum_scatter(
            grad_key_part.astype(jnp.bfloat16), "dp", scatter_dimension=0, tiled=True
        ).astype(jnp.float32),
        lax.psum_scatter(
            grad_value_part.astype(jnp.bfloat16), "dp", scatter_dimension=0, tiled=True
        ).astype(jnp.float32),
    )
    grad_value = grad_value_sum.astype(low_type)
    grad_key_raw, grad_key_gain = rms_back(
        rotate(grad_key_sum, cosine, -sine_table), key_normed, key_scale, gain_rows[2]
    )
    grad_query_raw, grad_query_gain = rms_back(
        rotate(grad_query, cosine, -sine_table), query_normed, query_scale, gain_rows[1]
    )
    grad_key_raw = grad_key_raw.astype(low_type)
    grad_query_raw = grad_query_raw.astype(low_type)
    grad_norm_in = jnp.dot(grad_query_raw, qkv_weights[0].T, preferred_element_type=high_type)
    grad_norm_in = grad_norm_in + jnp.dot(
        grad_key_raw, qkv_weights[1].T, preferred_element_type=high_type
    )
    grad_norm_in = grad_norm_in + jnp.dot(
        grad_value, qkv_weights[2].T, preferred_element_type=high_type
    )
    grad_qkv_local = jnp.stack(
        [
            jnp.dot(normed_in.T, grad_query_raw, preferred_element_type=high_type),
            jnp.dot(normed_in.T, grad_key_raw, preferred_element_type=high_type),
            jnp.dot(normed_in.T, grad_value, preferred_element_type=high_type),
        ]
    )
    grad_in_rows, grad_gain_in = rms_back(grad_norm_in, normed_in_f, scale_in, gain_rows[0])
    grad_input = grad_middle + grad_in_rows
    grad_gains_local = jnp.stack([grad_gain_in, grad_query_gain, grad_key_gain, grad_gain_mid])
    summed = (
        lax.psum_scatter(grad_qkv_local, ("expert", "dp"), scatter_dimension=1, tiled=True),
        lax.psum_scatter(grad_out_weight, ("expert", "dp"), scatter_dimension=0, tiled=True),
        lax.psum_scatter(grad_gains_local, ("expert", "dp"), scatter_dimension=1, tiled=True),
        lax.psum_scatter(grad_router, ("expert", "dp"), scatter_dimension=0, tiled=True),
    )
    return (
        output,
        grad_input,
        summed[0],
        summed[1],
        summed[2],
        summed[3],
        grad_expert_in,
        grad_expert_down,
    )


def solution(mesh):
    column_count, rank_count = mesh.shape["expert"], mesh.shape["dp"]
    depth = rank_count // 2
    tiled = column_count == 4 and rank_count % 2 == 0 and HEADS == column_count * depth
    if tiled:
        mesh = Mesh(mesh.devices.reshape(2, 2, depth, 2), GRID)
        column, rank, body = ("ey", "ex"), SEQ, grid_shards
    else:
        column, rank, body = ("expert",), ("dp",), shards
    device = column + rank
    placed = (
        P(device, None),
        P(device, None),
        P(column),
        P(device, None),
        P(None, device, None),
        P(device, None),
        P(None, device),
        P(device, None),
        P(rank, column, None, None),
        P(rank, column, None),
    )
    return jax.shard_map(
        body,
        mesh=mesh,
        in_specs=placed,
        out_specs=placed[:1] * 2 + placed[4:],
        check_vma=False,
    )
```
